32 devices in a mesh: dom: 32 (over z, y, x, core).
Axes of the slice: x: 2, y: 2, z: 4, core: 2. Of those that a mesh axis runs over, the one named last changes fastest.
Arguments:
- adjoint_start: float32 [3, 221184], P(None, 'dom'), may hold values from -6 to 6
- adjoint_source: float32 [3, 221184], P(None, 'dom'), may hold values from -6 to 6
- inverse_diagonal: float32 [3, 221184], P(None, 'dom'), may hold values from 0.05 to 0.3
- primal_field: float32 [3, 221184], P(None, 'dom'), may hold values from -6 to 6
- cell_load: float32 [192, 8192], P(None, 'dom'), may hold values from -6 to 6
- modulus: float32 [8192], P('dom'), may hold values from 0.5 to 4
- stiffness: float32 [192, 192], replicated
- connectivity: int32 [64, 8192], P(None, 'dom'), may hold values from 0 to 16368
- hang_node: int32 [4096], P('dom'), may hold values from 0 to 16368, as said below
- hang_master: int32 [16, 4096], P(None, 'dom'), may hold values from 0 to 16368
- hang_weight: float32 [16, 4096], P(None, 'dom'), may hold values from -0.25 to 0.45
- ghost_lists: int32 [8, 8192], P(None, 'dom'), may hold values from 0 to 16368
- subface_cell: int32 [8, 4096], P(None, 'dom'), may hold values from 0 to 255
- subface_face: int32 [8, 4096], P(None, 'dom'), may hold values from 0 to 5
- subface_owner: int32 [8, 4096], P(None, 'dom'), may hold values from 0 to 256, as said below
Outputs:
- adjoint: float32 [3, 221184], P(None, 'dom')
- indicator: float32 [8192], P('dom')
The draws below stay inside these ranges and needn't reach their ends.
Inputs may be any that keep to these rules, and one draw needn't show every extreme that they name: `hang_node`: on each partition the live hanging slots come first and hold distinct codes under min(16368, 6912); all slots after them hold 16368; between half and all of a partition's slots are live. `subface_owner`: 256 marks an unused slot; between half and all of each neighbour slot's entries are live.
All inputs are finite; a program needn't handle non-finite values.
Results may differ from the reference program's by a relative error of at most 0.0003.
Values sent between devices are 32-bit elements; how exact they have to be, the bound alone decides.
No kernel may reach another device: no remote copies, remote signals or barrier semaphores. Data moves between devices by JAX's collectives and lax.ppermute only.
A program may use at most 64 MiB of HBM per device.

```python
import math
import jax
import jax.numpy as jnp
from jax import lax

C = 256
LOC = 192
MASTERS = 16
REACH = 4
SWEEPS = 2
NODES_DEV = 6912
GHOST = 256
SUBS = 128
HANG = 128
EXT = 8960
CELLS = 8192
NODES = 221184
N_DOM = 32


def draw_stiffness(key, part):
    key = jax.random.fold_in(key, 11)
    first_key, second_key = jax.random.split(key)
    diagonal = jax.random.uniform(first_key, (LOC, LOC), jnp.float32, 1.5, 2.5)
    spread = jax.random.normal(second_key, (LOC, LOC), jnp.float32) * (0.8 / LOC ** 0.5)
    rows = lax.broadcasted_iota(jnp.int32, (LOC, LOC), 0)
    cols = lax.broadcasted_iota(jnp.int32, (LOC, LOC), 1)
    return jnp.where(rows == cols, diagonal, spread)


def draw_hang_node(key, part):
    key = jax.random.fold_in(key, 12)
    keys = jax.random.split(key, N_DOM + 1)
    bound = min(16368, NODES_DEV)

    def pick_one(single):
        return jax.random.permutation(single, bound)[:HANG].astype(jnp.int32)
    picks = jax.vmap(pick_one)(keys[1:])
    counts = jax.random.randint(keys[0], (N_DOM,), HANG // 2, HANG)
    counts = counts.at[0].set(HANG // 2)
    slots = jnp.arange(HANG, dtype=jnp.int32)
    chosen = jnp.where(slots[None, :] < counts[:, None], picks, 16368)
    return chosen.reshape(-1).astype(jnp.int32)


def draw_subface_owner(key, part):
    key = jax.random.fold_in(key, 13)
    first_key, second_key = jax.random.split(key)
    owners = jax.random.randint(first_key, (N_DOM, 2 * REACH, SUBS), 0, C)
    counts = jax.random.randint(second_key, (N_DOM, 2 * REACH), SUBS // 2, SUBS + 1)
    counts = counts.at[0, 0].set(SUBS // 2).at[1, 0].set(SUBS)
    slots = jnp.arange(SUBS, dtype=jnp.int32)
    chosen = jnp.where(slots[None, None, :] < counts[:, :, None], owners, C)
    return jnp.transpose(chosen, (1, 0, 2)).reshape(2 * REACH, N_DOM * SUBS).astype(jnp.int32)


def plant(values, stream_key, low, largest):
    place = [jax.random.randint(jax.random.fold_in(stream_key, axis), (), 0, length) for axis, length in enumerate(values.shape)]
    longest = values.shape.index(max(values.shape))
    next_to = place[:longest] + [(place[longest] + 1) % values.shape[longest]] + place[longest + 1:]
    return values.at[tuple(place)].set(low).at[tuple(next_to)].set(largest)


def steps_of(rng, extent, cuts, least, top_value):
    level, own = 1.0, jax.random.fold_in(rng, 6)
    for dim, shards_of in cuts:
        heights = jnp.exp(jax.random.uniform(jax.random.fold_in(own, dim), (shards_of,), jnp.float32, least / len(cuts), top_value / len(cuts)))
        level = level * jnp.repeat(heights, extent[dim] // shards_of).reshape([-1 if axis == dim else 1 for axis in range(len(extent))])
    return level


def scatter_about(stream_key, shape, deviation, reach, cuts=(), kind=jnp.bfloat16):
    result = jax.random.normal(stream_key, shape, jnp.float32) * deviation
    if len(cuts) > 0:
        result = steps_of(stream_key, shape, cuts, -0.22, 0.18) * result
    return jnp.clip(result, min=-reach, max=reach).astype(kind)


def setup_inputs(seed: int = 0) -> dict:
    key_of = jax.random.split(jax.random.key(seed), 16)
    adjoint_start = scatter_about(key_of[0], (3, NODES), 1.0, 6.0, ((1, 32),), jnp.float32)
    adjoint_source = scatter_about(key_of[1], (3, NODES), 1.0, 6.0, ((1, 32),), jnp.float32)
    inverse_diagonal = jnp.clip(jnp.exp(math.log(0.3) - 1.7917595 * jax.random.uniform(key_of[2], (3, NODES), jnp.float32) ** steps_of(key_of[2], (3, NODES), ((1, 32),), -0.2, 0.2)), 0.05, 0.3)
    primal_field = scatter_about(key_of[3], (3, NODES), 1.0, 6.0, ((1, 32),), jnp.float32)
    cell_load = scatter_about(key_of[4], (LOC, CELLS), 1.0, 6.0, ((1, 32),), jnp.float32)
    modulus = jnp.clip(jnp.exp(math.log(4.0) - 2.0794415 * jax.random.uniform(key_of[5], (CELLS,), jnp.float32) ** steps_of(key_of[5], (CELLS,), ((0, 32),), -0.2, 0.2)), 0.5, 4.0)
    stiffness = draw_stiffness(jax.random.fold_in(key_of[15], 71), 0)
    connectivity = plant(jax.random.randint(key_of[7], (64, CELLS), 0, 16369), jax.random.fold_in(key_of[7], 1), 0, 16368).astype(jnp.int32)
    hang_node = draw_hang_node(jax.random.fold_in(key_of[15], 71), 0)
    hang_master = plant(jax.random.randint(key_of[9], (MASTERS, HANG * N_DOM), 0, 16369), jax.random.fold_in(key_of[9], 1), 0, 16368).astype(jnp.int32)
    hang_weight = jnp.clip(-0.25 + 0.7 * jax.random.uniform(key_of[10], (MASTERS, HANG * N_DOM), jnp.float32) ** steps_of(key_of[10], (MASTERS, HANG * N_DOM), ((1, 32),), -0.2, 0.2), -0.25, 0.45)
    ghost_lists = plant(jax.random.randint(key_of[11], (2 * REACH, GHOST * N_DOM), 0, 16369), jax.random.fold_in(key_of[11], 1), 0, 16368).astype(jnp.int32)
    subface_cell = plant(jax.random.randint(key_of[12], (2 * REACH, SUBS * N_DOM), 0, C), jax.random.fold_in(key_of[12], 1), 0, C - 1).astype(jnp.int32)
    subface_face = plant(jax.random.randint(key_of[13], (2 * REACH, SUBS * N_DOM), 0, 6), jax.random.fold_in(key_of[13], 1), 0, 5).astype(jnp.int32)
    subface_owner = draw_subface_owner(jax.random.fold_in(key_of[15], 71), 0)
    return {"adjoint_start": adjoint_start, "adjoint_source": adjoint_source, "inverse_diagonal": inverse_diagonal, "primal_field": primal_field, "cell_load": cell_load, "modulus": modulus, "stiffness": stiffness, "connectivity": connectivity, "hang_node": hang_node, "hang_master": hang_master, "hang_weight": hang_weight, "ghost_lists": ghost_lists, "subface_cell": subface_cell, "subface_face": subface_face, "subface_owner": subface_owner}


relaxation = 0.7
scale_down = 16.0
pad_code = 16368


def neighbour_offsets():
    return [step + 1 for step in range(REACH)] + [-(step + 1) for step in range(REACH)]


def by_device(array):
    lead = array.shape[:-1]
    width = array.shape[-1] // N_DOM
    return jnp.moveaxis(array.reshape(lead + (N_DOM, width)), -2, 0)


def to_global(array):
    moved = jnp.moveaxis(array, 0, -2)
    return moved.reshape(moved.shape[:-2] + (-1,))


def decode_connect(codes):
    cells = jnp.arange(codes.shape[-1], dtype=jnp.int32)
    return ((27 * cells + 17 * codes) % EXT).astype(jnp.int32)


def decode_master(codes):
    slots = jnp.arange(codes.shape[-1], dtype=jnp.int32)
    return ((17 * codes + 8 * slots) % EXT).astype(jnp.int32)


def decode_node(codes):
    return jnp.where(codes == pad_code, EXT, (13 * codes) % NODES_DEV).astype(jnp.int32)


def decode_lists(codes):
    slots = jnp.arange(codes.shape[-1], dtype=jnp.int32)
    return ((17 * codes + slots) % NODES_DEV).astype(jnp.int32)


def move_along(blocks, direction):
    pieces = []
    for slot, offset in enumerate(neighbour_offsets()):
        amount = direction * offset
        block = blocks[:, slot]
        empty = jnp.zeros_like(block[:abs(amount)])
        if amount > 0:
            pieces.append(jnp.concatenate([empty, block[:-amount]], 0))
        else:
            pieces.append(jnp.concatenate([block[-amount:], empty], 0))
    return jnp.stack(pieces, 1)


def face_table(width):
    node = jnp.arange(width, dtype=jnp.int32) % 64
    first = node // 16
    second = (node // 4) % 4
    third = node % 4
    rows = [first == 0, first == 3, second == 0, second == 3, third == 0, third == 3]
    return jnp.stack(rows).astype(jnp.float32)


def constrain(extended, node, master, weight):
    padded = jnp.concatenate([extended, jnp.zeros((extended.shape[0], 1), extended.dtype)], 1)
    values = jnp.sum(weight[None] * padded[:, master], axis=1)
    padded = padded.at[:, node].set(values)
    return padded[:, :-1]


def release(totals, node, master, weight):
    padded = jnp.concatenate([totals, jnp.zeros((totals.shape[0], 1), totals.dtype)], 1)
    held = padded[:, node]
    padded = padded.at[:, node].set(0.0)
    spread = weight[None] * held[:, None, :]
    padded = padded.at[:, master.reshape(-1)].add(spread.reshape(totals.shape[0], -1))
    return padded[:, :-1]


def local_product(extended, connect, modulus, stiffness, node, master, weight):
    fixed = constrain(extended, node, master, weight)
    cells = fixed[:, connect].reshape(3 * connect.shape[0], -1)
    image = modulus[None] * lax.dot_general(stiffness, cells, (((0,), (0,)), ((), ())), precision=lax.Precision.HIGHEST)
    totals = jnp.zeros_like(fixed).at[:, connect].add(image.reshape(3, connect.shape[0], -1))
    return release(totals, node, master, weight)


def cell_section(adjoint_ext, primal_ext, connect, modulus, stiffness, node, master, weight, load, sub_cell, sub_face):
    adjoint_cells = constrain(adjoint_ext, node, master, weight)[:, connect].reshape(3 * connect.shape[0], -1)
    primal_cells = constrain(primal_ext, node, master, weight)[:, connect].reshape(3 * connect.shape[0], -1)
    applied = modulus[None] * jnp.dot(stiffness, primal_cells, precision=lax.Precision.HIGHEST)
    cell_term = jnp.sum(adjoint_cells * (load - applied), axis=0)
    flux = jnp.dot(face_table(applied.shape[0]), applied * adjoint_cells, precision=lax.Precision.HIGHEST)
    count = connect.shape[1]
    sent = flux.reshape(-1)[sub_face * count + sub_cell]
    return cell_term, sent


def reference(adjoint_start, adjoint_source, inverse_diagonal, primal_field, cell_load, modulus, stiffness, connectivity, hang_node, hang_master, hang_weight, ghost_lists, subface_cell, subface_face, subface_owner):
    adjoint = by_device(adjoint_start)
    source = by_device(adjoint_source)
    inverse = by_device(inverse_diagonal)
    primal = by_device(primal_field)
    load = by_device(cell_load)
    moduli = by_device(modulus)
    connect = decode_connect(by_device(connectivity))
    node = decode_node(by_device(hang_node))
    master = decode_master(by_device(hang_master))
    weight = by_device(hang_weight)
    lists = decode_lists(by_device(ghost_lists))
    sub_cell = by_device(subface_cell)
    sub_face = by_device(subface_face)
    sub_owner = by_device(subface_owner)
    owned_count = adjoint.shape[2]
    ghost_count = lists.shape[2]

    def import_all(owned):
        blocks = jax.vmap(lambda values, rows: jnp.moveaxis(values[:, rows], 1, 0))(owned, lists)
        ghosts = move_along(blocks, 1)
        ghosts = jnp.moveaxis(ghosts, 1, 2).reshape(N_DOM, owned.shape[1], -1)
        return jnp.concatenate([owned, ghosts], 2)

    def product_one(items):
        return local_product(items[0], items[1], items[2], stiffness, items[3], items[4], items[5])

    for sweep in range(SWEEPS):
        extended = import_all(adjoint)
        totals = lax.map(product_one, (extended, connect, moduli, node, master, weight))
        owned_part = totals[:, :, :owned_count]
        ghost_part = jnp.moveaxis(totals[:, :, owned_count:].reshape(N_DOM, 3, 2 * REACH, ghost_count), 2, 1)
        back = move_along(ghost_part, -1)

        def add_back(values, rows, returned):
            return values.at[:, rows.reshape(-1)].add(jnp.moveaxis(returned, 0, 1).reshape(3, -1))

        applied = jax.vmap(add_back)(owned_part, lists, back)
        adjoint = adjoint + relaxation * inverse * (source - applied)

    adjoint_ext = import_all(adjoint)
    primal_ext = import_all(primal)

    def section_one(items):
        return cell_section(items[0], items[1], items[2], items[3], stiffness, items[4], items[5], items[6], items[7], items[8], items[9])

    cell_term, sent = lax.map(section_one, (adjoint_ext, primal_ext, connect, moduli, node, master, weight, load, sub_cell, sub_face))
    received = move_along(sent, 1)
    cell_count = connect.shape[2]

    def collect(owners, values):
        return jnp.zeros((cell_count + 1,), values.dtype).at[owners.reshape(-1)].add(values.reshape(-1))[:cell_count]

    face_term = jax.vmap(collect)(sub_owner, received)
    indicator = (jnp.abs(cell_term) + jnp.abs(face_term)) / scale_down
    return to_global(adjoint), indicator.reshape(-1)
```

```python
import functools

import jax
import jax.numpy as jnp
from jax import lax
from jax.experimental import pallas as pl
from jax.experimental.pallas import tpu as pltpu
from jax.sharding import PartitionSpec as P

REACH = 4
SWEEPS = 2
WIDE = 256
OWN = 32
EDGE = 16
NOWHERE = 63

relaxation = 0.7
scale_down = 16.0
pad_code = 16368

f32 = jnp.float32
bf16 = jnp.bfloat16
i16 = jnp.int16
i32 = jnp.int32


def from_behind(block, axis, distance):
    devices = range(lax.axis_size(axis))
    route = [(i - distance, i) for i in devices if i - distance in devices]
    return lax.ppermute(block, axis, route)


def neighbour_offsets():
    return [step + 1 for step in range(REACH)] + [-(step + 1) for step in range(REACH)]


def pieces(x):
    high = x.astype(bf16)
    return high, (x - high.astype(f32)).astype(bf16)


def match16(row, count):
    width = row.shape[1]
    wide = jnp.broadcast_to(row, (16, width)).astype(i16)
    numbers = lax.broadcasted_iota(i16, (count, width), 0).reshape(count // 16, 16, width)
    return numbers == wide[None]


def one_hot(row, count):
    mask = match16(row, count)
    ones = jnp.ones(mask.shape, bf16)
    return jnp.where(mask, ones, jnp.zeros_like(ones)).reshape(count, row.shape[1])


def spread16(mask, row):
    wide = jnp.broadcast_to(row, (16, row.shape[1])).astype(bf16)[None]
    out = jnp.where(mask, jnp.broadcast_to(wide, mask.shape), jnp.zeros(mask.shape, bf16))
    return out.reshape(mask.shape[0] * 16, row.shape[1])


def gather_rows(table, rows, parts, at_row, at_column):
    hot = one_hot(at_column, WIDE)
    found = jnp.dot(table, jnp.concatenate([hot, hot], 0), preferred_element_type=f32)
    mask = lax.broadcasted_iota(i32, (rows, at_row.shape[1]), 0) == at_row
    return [
        jnp.sum(jnp.where(mask, found[part * rows : (part + 1) * rows], 0.0), 0, keepdims=True)
        for part in range(parts)
    ]


def gather_cells(table_ref, rows, parts, row_ref, column_ref, out_ref):
    count = row_ref.shape[0]

    def body(block, carry):
        start = pl.multiple_of(block * 8, 8)
        at_row = row_ref[pl.ds(start, 8), :]
        at_column = column_ref[pl.ds(start, 8), :]
        for j in range(8):
            found = gather_rows(
                table_ref[...], rows, parts, at_row[j : j + 1], at_column[j : j + 1]
            )
            for part in range(parts):
                out_ref[pl.ds(part * count + start + j, 1), :] = found[part]
        return carry

    lax.fori_loop(0, count // 8, body, 0)


def scatter_block(values, rows, at_row, at_column):
    count = at_row.shape[0]
    masks = [match16(at_row[j : j + 1], rows) for j in range(count)]
    hot = jnp.concatenate([one_hot(at_column[j : j + 1], WIDE) for j in range(count)], 1)
    stacked = []
    for piece in range(2):
        for part in range(3):
            stacked.append(
                jnp.concatenate(
                    [spread16(masks[j], values[piece][part][j : j + 1]) for j in range(count)], 1
                )
            )
    return lax.dot_general(
        jnp.concatenate(stacked, 0), hot, (((1,), (1,)), ((), ())), preferred_element_type=f32
    )


def split32(x):
    high = x.astype(bf16).astype(f32)
    return high, x - high


def scatter_cells(image_ref, rows, row_ref, column_ref, sum_ref):
    count = row_ref.shape[0]
    sum_ref[...] = jnp.zeros_like(sum_ref)

    def body(block, carry):
        start = pl.multiple_of(block * 8, 8)
        values = [split32(image_ref[pl.ds(part * count + start, 8), :]) for part in range(3)]
        values = list(zip(*values))
        sum_ref[...] += scatter_block(
            values, rows, row_ref[pl.ds(start, 8), :], column_ref[pl.ds(start, 8), :]
        )
        return carry

    lax.fori_loop(0, count // 8, body, 0)


def add_pieces(sums):
    half = sums.shape[0] // 2
    return sums[:half] + sums[half:]


def spread_hanging(held, weight, rows, at_row, at_column):
    both = jnp.concatenate([held, held], 1)
    values = [split32(weight * both[part : part + 1]) for part in range(3)]
    return add_pieces(scatter_block(list(zip(*values)), rows, at_row, at_column))


def sum_masters(table, rows, parts, weight, at_row, at_column):
    total = [jnp.zeros((1, WIDE), f32)] * parts
    for j in range(8):
        found = gather_rows(table, rows, parts, at_row[j : j + 1], at_column[j : j + 1])
        total = [total[part] + weight[j : j + 1] * found[part] for part in range(parts)]
    half = WIDE // 2
    return [x[:, :half] + x[:, half:] for x in total]


def fill_table(x_ref, out_ref):
    count = x_ref.shape[1] // WIDE
    out_ref[...] = jnp.zeros_like(out_ref)
    for row in range(count):
        block = x_ref[:, row * WIDE : (row + 1) * WIDE]
        for part in range(3):
            out_ref[part * OWN + row : part * OWN + row + 1, :] = block[part : part + 1]


def export_rows(table, parts, at_row, at_column, out_refs):
    for slot, out_ref in enumerate(out_refs):
        found = gather_rows(
            table, OWN, parts, at_row[slot : slot + 1], at_column[slot : slot + 1]
        )
        for part in range(parts):
            out_ref[part : part + 1, :] = found[part]


def first_export(adjoint_ref, primal_ref, list_ref, tab_a, tab_p, row_ref, column_ref, *out_refs):
    owned = adjoint_ref.shape[1]
    fill_table(adjoint_ref, tab_a)
    fill_table(primal_ref, tab_p)
    codes = list_ref[...]
    node = lax.rem(17 * codes + lax.broadcasted_iota(i32, codes.shape, 1), owned)
    row_ref[...] = node >> 8
    column_ref[...] = node & 255
    table = jnp.concatenate([tab_a[...], tab_p[...]], 0)
    table = jnp.concatenate(pieces(table), 1)
    export_rows(table, 6, node >> 8, node & 255, out_refs)


def setup(
    connect_ref,
    node_ref,
    master_ref,
    weight_ref,
    source_ref,
    inverse_ref,
    row_own,
    column_own,
    row_edge,
    column_edge,
    master_own,
    master_edge,
    master_column,
    weight_out,
    tab_source,
    tab_inverse,
    found_ref,
):
    owned = source_ref.shape[1]
    extent = owned + 2 * REACH * WIDE
    fill_table(source_ref, tab_source)
    fill_table(inverse_ref, tab_inverse)
    half = WIDE // 2
    codes = master_ref[...]
    master = lax.rem(17 * codes + 8 * lax.broadcasted_iota(i32, codes.shape, 1), extent)
    count = codes.shape[0] // 2
    master = jnp.concatenate([master[:count], master[count:]], 1)
    weight = weight_ref[...]
    weight_out[...] = jnp.concatenate([weight[:count], weight[count:]], 1)
    last = owned // WIDE
    row = master >> 8
    master_own[...] = jnp.where(row < last, row, NOWHERE)
    master_edge[...] = jnp.where(row < last, NOWHERE, row - last)
    master_column[...] = master & 255

    codes = node_ref[...]
    node = jnp.where(codes == pad_code, extent, lax.rem(13 * codes, owned))
    hot = one_hot(node & 255, WIDE)
    slot = (lax.broadcasted_iota(i32, codes.shape, 1) + 1).astype(f32)
    where = spread16(match16(node >> 8, OWN), slot)
    table = lax.dot_general(where, hot, (((1,), (1,)), ((), ())), preferred_element_type=f32)
    table = table.astype(bf16)

    codes = connect_ref[...]
    cells = lax.broadcasted_iota(i32, codes.shape, 1)
    slots = lax.rem(27 * cells + 17 * codes, extent)
    row_own[...] = slots >> 8
    column_own[...] = slots & 255

    def body(block, carry):
        start = pl.multiple_of(block * 8, 8)
        at_row = row_own[pl.ds(start, 8), :]
        at_column = column_own[pl.ds(start, 8), :]
        for j in range(8):
            found = jnp.dot(
                table, one_hot(at_column[j : j + 1], WIDE), preferred_element_type=f32
            )
            mask = lax.broadcasted_iota(i32, (OWN, WIDE), 0) == at_row[j : j + 1]
            found_ref[pl.ds(start + j, 1), :] = jnp.sum(
                jnp.where(mask, found, 0.0), 0, keepdims=True
            )
        return carry

    lax.fori_loop(0, codes.shape[0] // 8, body, 0)
    slot = found_ref[...].astype(i32)
    row = slots >> 8
    hanging = slot > 0
    outside = row >= last
    row_own[...] = jnp.where(hanging | outside, NOWHERE, row)
    row_edge[...] = jnp.where(
        hanging, 2 * REACH, jnp.where(outside, row - last, NOWHERE)
    )
    column_edge[...] = jnp.where(hanging, slot - 1, slots & 255)


def own_gather(
    tab_ref, row_ref, column_ref, master_row, master_column, weight_ref, cells_ref, hang_ref, table_ref
):
    table_ref[...] = jnp.concatenate(pieces(tab_ref[...]), 1)
    found = sum_masters(
        table_ref[...], OWN, 3, weight_ref[...], master_row[...], master_column[...]
    )
    for part in range(3):
        hang_ref[part : part + 1, :] = found[part]
    gather_cells(table_ref, OWN, 3, row_ref, column_ref, cells_ref)


def edge_gather(
    ghost_refs, first, hang_ref, row_ref, column_ref, master_row, master_column, weight_ref,
    edge_ref, table_ref, out_ref,
):
    edge_ref[...] = jnp.zeros_like(edge_ref)
    for slot, ghost_ref in enumerate(ghost_refs):
        for part in range(3):
            edge_ref[part * EDGE + slot : part * EDGE + slot + 1, :] = ghost_ref[
                first + part : first + part + 1, :
            ]
    found = sum_masters(
        jnp.concatenate(pieces(edge_ref[...]), 1),
        EDGE,
        3,
        weight_ref[...],
        master_row[...],
        master_column[...],
    )
    slots = len(ghost_refs)
    for part in range(3):
        edge_ref[part * EDGE + slots : part * EDGE + slots + 1, : WIDE // 2] = (
            found[part] + hang_ref[part : part + 1, :]
        )
    table_ref[...] = jnp.concatenate(pieces(edge_ref[...]), 1)
    gather_cells(table_ref, EDGE, 3, row_ref, column_ref, out_ref)


def edge_product(first, *refs):
    ghost_refs = refs[: 2 * REACH]
    (
        cells_ref, hang_ref, row_ref, column_ref, master_row, master_column, weight_ref,
        modulus_ref, stiffness_ref,
    ) = refs[2 * REACH : 2 * REACH + 9]
    rest = refs[2 * REACH + 9 :]
    out_refs = rest[: 2 * REACH]
    image_ref, held_ref, edge_ref, table_ref, more_ref, sum_ref = rest[2 * REACH :]
    edge_gather(
        ghost_refs, first, hang_ref, row_ref, column_ref, master_row, master_column, weight_ref,
        edge_ref, table_ref, more_ref,
    )
    image_ref[...] = modulus_ref[...] * lax.dot_general(
        stiffness_ref[...],
        cells_ref[...] + more_ref[...],
        (((0,), (0,)), ((), ())),
        precision=lax.Precision.HIGHEST,
        preferred_element_type=f32,
    )
    scatter_cells(image_ref, EDGE, row_ref, column_ref, sum_ref)
    edge_ref[...] = add_pieces(sum_ref[...])
    slots = 2 * REACH
    held = jnp.concatenate(
        [edge_ref[part * EDGE + slots : part * EDGE + slots + 1, : WIDE // 2] for part in range(3)],
        0,
    )
    held_ref[...] = held
    edge_ref[...] += spread_hanging(
        held, weight_ref[...], EDGE, master_row[...], master_column[...]
    )
    for slot, out_ref in enumerate(out_refs):
        for part in range(3):
            out_ref[part : part + 1, :] = edge_ref[part * EDGE + slot : part * EDGE + slot + 1, :]


def own_sums(
    image_ref, held_ref, row_ref, column_ref, master_row, master_column, weight_ref,
    tab_ref, source_ref, inverse_ref, out_ref, sum_ref,
):
    scatter_cells(image_ref, OWN, row_ref, column_ref, sum_ref)
    applied = add_pieces(sum_ref[...]) + spread_hanging(
        held_ref[...], weight_ref[...], OWN, master_row[...], master_column[...]
    )
    out_ref[...] = tab_ref[...] + relaxation * inverse_ref[...] * (source_ref[...] - applied)


def update(last, *refs):
    back_refs = refs[: 2 * REACH]
    row_ref, column_ref, partial_ref, inverse_ref = refs[2 * REACH : 2 * REACH + 4]
    rest = refs[2 * REACH + 4 :]
    out_refs = rest[: 2 * REACH]
    tab_ref = rest[2 * REACH]
    values = []
    for part in range(3):
        block = jnp.concatenate([ref[part : part + 1, :] for ref in back_refs], 0)
        values.append(split32(block))
    returned = add_pieces(
        scatter_block(list(zip(*values)), OWN, row_ref[...], column_ref[...])
    )
    fresh = partial_ref[...] - relaxation * inverse_ref[...] * returned
    tab_ref[...] = fresh
    table = jnp.concatenate(pieces(fresh), 1)
    export_rows(table, 3, row_ref[...], column_ref[...], out_refs)
    if last:
        final_ref = rest[2 * REACH + 1]
        for row in range(final_ref.shape[1] // WIDE):
            for part in range(3):
                final_ref[part : part + 1, row * WIDE : (row + 1) * WIDE] = tab_ref[
                    part * OWN + row : part * OWN + row + 1, :
                ]


def primal_product(first, *refs):
    ghost_refs = refs[: 2 * REACH]
    (
        cells_ref, hang_ref, row_ref, column_ref, master_row, master_column, weight_ref,
        modulus_ref, stiffness_ref, out_ref, edge_ref, table_ref, more_ref,
    ) = refs[2 * REACH :]
    edge_gather(
        ghost_refs, first, hang_ref, row_ref, column_ref, master_row, master_column, weight_ref,
        edge_ref, table_ref, more_ref,
    )
    out_ref[...] = modulus_ref[...] * jnp.dot(
        stiffness_ref[...],
        cells_ref[...] + more_ref[...],
        precision=lax.Precision.HIGHEST,
        preferred_element_type=f32,
    )


def fluxes(*refs):
    ghost_refs = refs[: 2 * REACH]
    (
        cells_ref, hang_ref, row_ref, column_ref, master_row, master_column, weight_ref,
        ku_ref, load_ref, sub_cell, sub_face,
    ) = refs[2 * REACH : 2 * REACH + 11]
    rest = refs[2 * REACH + 11 :]
    out_refs = rest[: 2 * REACH]
    term_ref, edge_ref, table_ref, more_ref = rest[2 * REACH :]
    edge_gather(
        ghost_refs, 0, hang_ref, row_ref, column_ref, master_row, master_column, weight_ref,
        edge_ref, table_ref, more_ref,
    )
    cells = cells_ref[...] + more_ref[...]
    ku = ku_ref[...]
    term_ref[...] = jnp.sum(cells * (load_ref[...] - ku), 0, keepdims=True)
    face = lax.broadcasted_iota(i32, (8, ku.shape[0]), 0)
    node = lax.broadcasted_iota(i32, (8, ku.shape[0]), 1) & 63
    index = jnp.where(face < 2, node >> 4, jnp.where(face < 4, (node >> 2) & 3, node & 3))
    member = jnp.where((face < 6) & (index == 3 * (face & 1)), 1.0, 0.0).astype(f32)
    flux = jnp.dot(
        member, ku * cells, precision=lax.Precision.HIGHEST, preferred_element_type=f32
    )
    table = jnp.concatenate(pieces(flux), 1)
    for slot, out_ref in enumerate(out_refs):
        out_ref[...] = gather_rows(
            table, 8, 1, sub_face[slot : slot + 1, :], sub_cell[slot : slot + 1, :]
        )[0]


def collect(*refs):
    got_refs = refs[: 2 * REACH]
    owner_ref, term_ref, out_ref = refs[2 * REACH :]
    count = term_ref.shape[1]
    got = jnp.concatenate([ref[...] for ref in got_refs], 1)
    hot = jnp.concatenate(
        [one_hot(owner_ref[slot : slot + 1, :], count) for slot in range(2 * REACH)], 1
    )
    high, low = split32(got)
    values = jnp.concatenate(
        [jnp.broadcast_to(x, (16, got.shape[1])).astype(bf16) for x in (high, low)], 0
    )
    sums = lax.dot_general(values, hot, (((1,), (1,)), ((), ())), preferred_element_type=f32)
    face_term = sums[0:1] + sums[16:17]
    out_ref[...] = (jnp.abs(term_ref[...]) + jnp.abs(face_term)) / scale_down


def call(kernel, outs, scratch=()):
    return pl.pallas_call(
        kernel,
        out_shape=[jax.ShapeDtypeStruct(shape, kind) for shape, kind in outs],
        scratch_shapes=[pltpu.VMEM(shape, kind) for shape, kind in scratch],
        compiler_params=pltpu.CompilerParams(vmem_limit_bytes=40 * 1024 * 1024),
    )


def local(
    adjoint_start,
    adjoint_source,
    inverse_diagonal,
    primal_field,
    cell_load,
    modulus,
    stiffness,
    connectivity,
    hang_node,
    hang_master,
    hang_weight,
    ghost_lists,
    subface_cell,
    subface_face,
    subface_owner,
):
    offsets = neighbour_offsets()
    slots = len(offsets)
    local_values, cell_count = cell_load.shape
    nodes = connectivity.shape[0]
    moduli = modulus.reshape(1, cell_count)
    table = ((3 * OWN, WIDE), f32)
    index = ((nodes, cell_count), i32)
    block = ((3, WIDE), f32)
    cells_shape = ((local_values, cell_count), f32)
    hang_shape = ((3, hang_node.shape[0]), f32)
    master_shape = ((8, WIDE), i32)
    own_table = ((3 * OWN, 2 * WIDE), bf16)
    edge = [((3 * EDGE, WIDE), f32), ((3 * EDGE, 2 * WIDE), bf16), cells_shape]

    def send(blocks, sign):
        return [from_behind(b, "dom", sign * o) for b, o in zip(blocks, offsets)]

    tab, tab_primal, list_row, list_column, *blocks = call(
        first_export,
        [table, table, (ghost_lists.shape, i32), (ghost_lists.shape, i32)]
        + [((6, WIDE), f32)] * slots,
    )(adjoint_start, primal_field, ghost_lists)
    ghosts = first_ghosts = send(blocks, 1)
    (
        row_own, column_own, row_edge, column_edge, master_own, master_edge, master_column,
        weight, source, inverse,
    ) = call(
        setup,
        [index] * 4 + [master_shape] * 3 + [((8, WIDE), f32), table, table],
        [((nodes, cell_count), f32)],
    )(
        connectivity, hang_node.reshape(1, -1), hang_master, hang_weight, adjoint_source,
        inverse_diagonal,
    )

    def gather_own(values):
        return call(own_gather, [cells_shape, hang_shape], [own_table])(
            values, row_own, column_own, master_own, master_column, weight
        )

    on_edge = (row_edge, column_edge, master_edge, master_column, weight)
    ku = None
    for sweep in range(SWEEPS):
        cells, hang = gather_own(tab)
        *blocks, image, held = call(
            functools.partial(edge_product, 0),
            [block] * slots + [cells_shape, hang_shape],
            edge + [((6 * EDGE, WIDE), f32)],
        )(*ghosts, cells, hang, *on_edge, moduli, stiffness)
        returned = send(blocks, -1)
        (partial,) = call(own_sums, [table], [((6 * OWN, WIDE), f32)])(
            image, held, row_own, column_own, master_own, master_column, weight, tab, source,
            inverse,
        )
        if sweep == 0:
            cells, hang = gather_own(tab_primal)
            (ku,) = call(functools.partial(primal_product, 3), [cells_shape], edge)(
                *first_ghosts, cells, hang, *on_edge, moduli, stiffness
            )
        last = sweep == SWEEPS - 1
        *blocks, tab = call(
            functools.partial(update, last),
            [block] * slots + [table] + ([(adjoint_start.shape, f32)] if last else []),
        )(*returned, list_row, list_column, partial, inverse)
        if last:
            adjoint = tab
            tab = blocks.pop()
        ghosts = send(blocks, 1)
    cells, hang = gather_own(tab)
    *sent, term = call(
        fluxes,
        [((1, subface_cell.shape[1]), f32)] * slots + [((1, cell_count), f32)],
        edge,
    )(*ghosts, cells, hang, *on_edge, ku, cell_load, subface_cell, subface_face)
    received = send(sent, 1)
    (indicator,) = call(collect, [((1, cell_count), f32)])(*received, subface_owner, term)
    return (adjoint, indicator.reshape(cell_count))


def solution(mesh):
    placed = (
        P(None, "dom"),
        P(None, "dom"),
        P(None, "dom"),
        P(None, "dom"),
        P(None, "dom"),
        P("dom"),
        P(),
        P(None, "dom"),
        P("dom"),
        P(None, "dom"),
        P(None, "dom"),
        P(None, "dom"),
        P(None, "dom"),
        P(None, "dom"),
        P(None, "dom"),
    )
    return jax.shard_map(
        local, mesh=mesh, in_specs=placed, out_specs=(P(None, "dom"), P("dom")), check_vma=False
    )
```

```python
import functools

import jax
import jax.numpy as jnp
from jax import lax
from jax.experimental import pallas as pl
from jax.experimental.pallas import tpu as pltpu
from jax.sharding import PartitionSpec as P

REACH = 4
SWEEPS = 2
WIDE = 256
OWN = 32
EDGE = 16
NOWHERE = 63

relaxation = 0.7
scale_down = 16.0
pad_code = 16368

f32 = jnp.float32
bf16 = jnp.bfloat16
i16 = jnp.int16
i32 = jnp.int32


def neighbour_offsets():
    return [step + 1 for step in range(REACH)] + [-(step + 1) for step in range(REACH)]


def pieces(x):
    high = x.astype(bf16)
    return high, (x - high.astype(f32)).astype(bf16)


def match16(row, count):
    width = row.shape[1]
    wide = jnp.broadcast_to(row, (16, width)).astype(i16)
    numbers = lax.broadcasted_iota(i16, (count, width), 0).reshape(count // 16, 16, width)
    return numbers == wide[None]


def one_hot(row, count):
    mask = match16(row, count)
    ones = jnp.ones(mask.shape, bf16)
    return jnp.where(mask, ones, jnp.zeros_like(ones)).reshape(count, row.shape[1])


def spread16(mask, row):
    wide = jnp.broadcast_to(row, (16, row.shape[1])).astype(bf16)[None]
    out = jnp.where(mask, jnp.broadcast_to(wide, mask.shape), jnp.zeros(mask.shape, bf16))
    return out.reshape(mask.shape[0] * 16, row.shape[1])


def gather_rows(table, rows, parts, at_row, at_column):
    hot = one_hot(at_column, WIDE)
    found = jnp.dot(table, jnp.concatenate([hot, hot], 0), preferred_element_type=f32)
    mask = lax.broadcasted_iota(i32, (rows, at_row.shape[1]), 0) == at_row
    return [
        jnp.sum(jnp.where(mask, found[part * rows : (part + 1) * rows], 0.0), 0, keepdims=True)
        for part in range(parts)
    ]


def gather_cells(table_ref, rows, parts, row_ref, column_ref, out_ref):
    count = row_ref.shape[0]

    def body(block, carry):
        start = pl.multiple_of(block * 8, 8)
        at_row = row_ref[pl.ds(start, 8), :]
        at_column = column_ref[pl.ds(start, 8), :]
        for j in range(8):
            found = gather_rows(
                table_ref[...], rows, parts, at_row[j : j + 1], at_column[j : j + 1]
            )
            for part in range(parts):
                out_ref[pl.ds(part * count + start + j, 1), :] = found[part]
        return carry

    lax.fori_loop(0, count // 8, body, 0)


def scatter_block(values, rows, at_row, at_column):
    count = at_row.shape[0]
    masks = [match16(at_row[j : j + 1], rows) for j in range(count)]
    hot = jnp.concatenate([one_hot(at_column[j : j + 1], WIDE) for j in range(count)], 1)
    stacked = []
    for piece in range(2):
        for part in range(3):
            stacked.append(
                jnp.concatenate(
                    [spread16(masks[j], values[piece][part][j : j + 1]) for j in range(count)], 1
                )
            )
    return lax.dot_general(
        jnp.concatenate(stacked, 0), hot, (((1,), (1,)), ((), ())), preferred_element_type=f32
    )


def split32(x):
    high = x.astype(bf16).astype(f32)
    return high, x - high


def scatter_cells(image_ref, rows, row_ref, column_ref, sum_ref):
    count = row_ref.shape[0]
    sum_ref[...] = jnp.zeros_like(sum_ref)

    def body(block, carry):
        start = pl.multiple_of(block * 8, 8)
        values = [split32(image_ref[pl.ds(part * count + start, 8), :]) for part in range(3)]
        values = list(zip(*values))
        sum_ref[...] += scatter_block(
            values, rows, row_ref[pl.ds(start, 8), :], column_ref[pl.ds(start, 8), :]
        )
        return carry

    lax.fori_loop(0, count // 8, body, 0)


def add_pieces(sums):
    half = sums.shape[0] // 2
    return sums[:half] + sums[half:]


def spread_hanging(held, weight, rows, at_row, at_column):
    both = jnp.concatenate([held, held], 1)
    values = [split32(weight * both[part : part + 1]) for part in range(3)]
    return add_pieces(scatter_block(list(zip(*values)), rows, at_row, at_column))


def sum_masters(table, rows, parts, weight, at_row, at_column):
    total = [jnp.zeros((1, WIDE), f32)] * parts
    for j in range(8):
        found = gather_rows(table, rows, parts, at_row[j : j + 1], at_column[j : j + 1])
        total = [total[part] + weight[j : j + 1] * found[part] for part in range(parts)]
    half = WIDE // 2
    return [x[:, :half] + x[:, half:] for x in total]


def fill_table(x_ref, out_ref):
    count = x_ref.shape[1] // WIDE
    out_ref[...] = jnp.zeros_like(out_ref)
    for row in range(count):
        block = x_ref[:, row * WIDE : (row + 1) * WIDE]
        for part in range(3):
            out_ref[part * OWN + row : part * OWN + row + 1, :] = block[part : part + 1]


def export_rows(table, parts, at_row, at_column, out_ref):
    slots = 2 * REACH
    for slot in range(slots):
        found = gather_rows(
            table, OWN, parts, at_row[slot : slot + 1], at_column[slot : slot + 1]
        )
        for part in range(parts):
            out_ref[part * slots + slot : part * slots + slot + 1, :] = found[part]


def fetch_blocks(place_ref, sign, all_ref, land_ref, sems):
    place, count = place_ref[0], all_ref.shape[0]
    sources = [place - sign * offset for offset in neighbour_offsets()]
    copies = [
        pltpu.make_async_copy(
            all_ref.at[jnp.clip(source, 0, count - 1)], land_ref.at[slot], sems.at[slot]
        )
        for slot, source in enumerate(sources)
    ]
    for copy in copies:
        copy.start()
    for copy in copies:
        copy.wait()
    for slot, source in enumerate(sources):

        @pl.when((source < 0) | (source >= count))
        def _():
            land_ref[slot] = jnp.zeros(land_ref.shape[1:], land_ref.dtype)


def landed(land_ref, first=0):
    slots = 2 * REACH
    return [
        [
            land_ref[slot, (first + part) * slots + slot : (first + part) * slots + slot + 1, :]
            for part in range(3)
        ]
        for slot in range(slots)
    ]


def first_export(adjoint_ref, primal_ref, list_ref, tab_a, tab_p, row_ref, column_ref, out_ref):
    owned = adjoint_ref.shape[1]
    fill_table(adjoint_ref, tab_a)
    fill_table(primal_ref, tab_p)
    codes = list_ref[...]
    node = lax.rem(17 * codes + lax.broadcasted_iota(i32, codes.shape, 1), owned)
    row_ref[...] = node >> 8
    column_ref[...] = node & 255
    table = jnp.concatenate([tab_a[...], tab_p[...]], 0)
    table = jnp.concatenate(pieces(table), 1)
    export_rows(table, 6, node >> 8, node & 255, out_ref)


def setup(
    connect_ref,
    node_ref,
    master_ref,
    weight_ref,
    source_ref,
    inverse_ref,
    row_own,
    column_own,
    row_edge,
    column_edge,
    master_own,
    master_edge,
    master_column,
    weight_out,
    tab_source,
    tab_inverse,
    found_ref,
):
    owned = source_ref.shape[1]
    extent = owned + 2 * REACH * WIDE
    fill_table(source_ref, tab_source)
    fill_table(inverse_ref, tab_inverse)
    half = WIDE // 2
    codes = master_ref[...]
    master = lax.rem(17 * codes + 8 * lax.broadcasted_iota(i32, codes.shape, 1), extent)
    count = codes.shape[0] // 2
    master = jnp.concatenate([master[:count], master[count:]], 1)
    weight = weight_ref[...]
    weight_out[...] = jnp.concatenate([weight[:count], weight[count:]], 1)
    last = owned // WIDE
    row = master >> 8
    master_own[...] = jnp.where(row < last, row, NOWHERE)
    master_edge[...] = jnp.where(row < last, NOWHERE, row - last)
    master_column[...] = master & 255

    codes = node_ref[...]
    node = jnp.where(codes == pad_code, extent, lax.rem(13 * codes, owned))
    hot = one_hot(node & 255, WIDE)
    slot = (lax.broadcasted_iota(i32, codes.shape, 1) + 1).astype(f32)
    where = spread16(match16(node >> 8, OWN), slot)
    table = lax.dot_general(where, hot, (((1,), (1,)), ((), ())), preferred_element_type=f32)
    table = table.astype(bf16)

    codes = connect_ref[...]
    cells = lax.broadcasted_iota(i32, codes.shape, 1)
    slots = lax.rem(27 * cells + 17 * codes, extent)
    row_own[...] = slots >> 8
    column_own[...] = slots & 255

    def body(block, carry):
        start = pl.multiple_of(block * 8, 8)
        at_row = row_own[pl.ds(start, 8), :]
        at_column = column_own[pl.ds(start, 8), :]
        for j in range(8):
            found = jnp.dot(
                table, one_hot(at_column[j : j + 1], WIDE), preferred_element_type=f32
            )
            mask = lax.broadcasted_iota(i32, (OWN, WIDE), 0) == at_row[j : j + 1]
            found_ref[pl.ds(start + j, 1), :] = jnp.sum(
                jnp.where(mask, found, 0.0), 0, keepdims=True
            )
        return carry

    lax.fori_loop(0, codes.shape[0] // 8, body, 0)
    slot = found_ref[...].astype(i32)
    row = slots >> 8
    hanging = slot > 0
    outside = row >= last
    row_own[...] = jnp.where(hanging | outside, NOWHERE, row)
    row_edge[...] = jnp.where(
        hanging, 2 * REACH, jnp.where(outside, row - last, NOWHERE)
    )
    column_edge[...] = jnp.where(hanging, slot - 1, slots & 255)


def own_gather(
    tab_ref, row_ref, column_ref, master_row, master_column, weight_ref, cells_ref, hang_ref, table_ref
):
    table_ref[...] = jnp.concatenate(pieces(tab_ref[...]), 1)
    found = sum_masters(
        table_ref[...], OWN, 3, weight_ref[...], master_row[...], master_column[...]
    )
    for part in range(3):
        hang_ref[part : part + 1, :] = found[part]
    gather_cells(table_ref, OWN, 3, row_ref, column_ref, cells_ref)


def edge_gather(
    ghosts, hang_ref, row_ref, column_ref, master_row, master_column, weight_ref,
    edge_ref, table_ref, out_ref,
):
    edge_ref[...] = jnp.zeros_like(edge_ref)
    for slot, ghost in enumerate(ghosts):
        for part in range(3):
            edge_ref[part * EDGE + slot : part * EDGE + slot + 1, :] = ghost[part]
    found = sum_masters(
        jnp.concatenate(pieces(edge_ref[...]), 1),
        EDGE,
        3,
        weight_ref[...],
        master_row[...],
        master_column[...],
    )
    slots = len(ghosts)
    for part in range(3):
        edge_ref[part * EDGE + slots : part * EDGE + slots + 1, : WIDE // 2] = (
            found[part] + hang_ref[part : part + 1, :]
        )
    table_ref[...] = jnp.concatenate(pieces(edge_ref[...]), 1)
    gather_cells(table_ref, EDGE, 3, row_ref, column_ref, out_ref)


def edge_product(
    place_ref, all_ref, cells_ref, hang_ref, row_ref, column_ref, master_row, master_column,
    weight_ref, modulus_ref, stiffness_ref, out_ref, image_ref, held_ref, edge_ref, table_ref,
    more_ref, sum_ref, land_ref, sems,
):
    fetch_blocks(place_ref, 1, all_ref, land_ref, sems)
    edge_gather(
        landed(land_ref), hang_ref, row_ref, column_ref, master_row, master_column, weight_ref,
        edge_ref, table_ref, more_ref,
    )
    image_ref[...] = modulus_ref[...] * lax.dot_general(
        stiffness_ref[...],
        cells_ref[...] + more_ref[...],
        (((0,), (0,)), ((), ())),
        precision=lax.Precision.HIGHEST,
        preferred_element_type=f32,
    )
    scatter_cells(image_ref, EDGE, row_ref, column_ref, sum_ref)
    edge_ref[...] = add_pieces(sum_ref[...])
    slots = 2 * REACH
    held = jnp.concatenate(
        [edge_ref[part * EDGE + slots : part * EDGE + slots + 1, : WIDE // 2] for part in range(3)],
        0,
    )
    held_ref[...] = held
    edge_ref[...] += spread_hanging(
        held, weight_ref[...], EDGE, master_row[...], master_column[...]
    )
    for part in range(3):
        out_ref[part * slots : (part + 1) * slots, :] = edge_ref[
            part * EDGE : part * EDGE + slots, :
        ]


def own_sums(
    image_ref, held_ref, row_ref, column_ref, master_row, master_column, weight_ref,
    tab_ref, source_ref, inverse_ref, out_ref, sum_ref,
):
    scatter_cells(image_ref, OWN, row_ref, column_ref, sum_ref)
    applied = add_pieces(sum_ref[...]) + spread_hanging(
        held_ref[...], weight_ref[...], OWN, master_row[...], master_column[...]
    )
    out_ref[...] = tab_ref[...] + relaxation * inverse_ref[...] * (source_ref[...] - applied)


def update(
    last, place_ref, all_ref, row_ref, column_ref, partial_ref, inverse_ref, out_ref, tab_ref, *rest
):
    land_ref, sems = rest[-2:]
    fetch_blocks(place_ref, -1, all_ref, land_ref, sems)
    back = landed(land_ref)
    values = [
        split32(jnp.concatenate([block[part] for block in back], 0)) for part in range(3)
    ]
    returned = add_pieces(
        scatter_block(list(zip(*values)), OWN, row_ref[...], column_ref[...])
    )
    fresh = partial_ref[...] - relaxation * inverse_ref[...] * returned
    tab_ref[...] = fresh
    table = jnp.concatenate(pieces(fresh), 1)
    export_rows(table, 3, row_ref[...], column_ref[...], out_ref)
    if last:
        final_ref = rest[0]
        for row in range(final_ref.shape[1] // WIDE):
            for part in range(3):
                final_ref[part : part + 1, row * WIDE : (row + 1) * WIDE] = tab_ref[
                    part * OWN + row : part * OWN + row + 1, :
                ]


def primal_product(
    place_ref, all_ref, cells_ref, hang_ref, row_ref, column_ref, master_row, master_column,
    weight_ref, modulus_ref, stiffness_ref, out_ref, edge_ref, table_ref, more_ref, land_ref, sems,
):
    fetch_blocks(place_ref, 1, all_ref, land_ref, sems)
    edge_gather(
        landed(land_ref, 3), hang_ref, row_ref, column_ref, master_row, master_column, weight_ref,
        edge_ref, table_ref, more_ref,
    )
    out_ref[...] = modulus_ref[...] * jnp.dot(
        stiffness_ref[...],
        cells_ref[...] + more_ref[...],
        precision=lax.Precision.HIGHEST,
        preferred_element_type=f32,
    )


def fluxes(
    place_ref, all_ref, cells_ref, hang_ref, row_ref, column_ref, master_row, master_column,
    weight_ref, ku_ref, load_ref, sub_cell, sub_face, out_ref, term_ref, edge_ref, table_ref,
    more_ref, land_ref, sems,
):
    fetch_blocks(place_ref, 1, all_ref, land_ref, sems)
    edge_gather(
        landed(land_ref), hang_ref, row_ref, column_ref, master_row, master_column, weight_ref,
        edge_ref, table_ref, more_ref,
    )
    cells = cells_ref[...] + more_ref[...]
    ku = ku_ref[...]
    term_ref[...] = jnp.sum(cells * (load_ref[...] - ku), 0, keepdims=True)
    face = lax.broadcasted_iota(i32, (8, ku.shape[0]), 0)
    node = lax.broadcasted_iota(i32, (8, ku.shape[0]), 1) & 63
    index = jnp.where(face < 2, node >> 4, jnp.where(face < 4, (node >> 2) & 3, node & 3))
    member = jnp.where((face < 6) & (index == 3 * (face & 1)), 1.0, 0.0).astype(f32)
    flux = jnp.dot(
        member, ku * cells, precision=lax.Precision.HIGHEST, preferred_element_type=f32
    )
    table = jnp.concatenate(pieces(flux), 1)
    for slot in range(2 * REACH):
        out_ref[slot : slot + 1, :] = gather_rows(
            table, 8, 1, sub_face[slot : slot + 1, :], sub_cell[slot : slot + 1, :]
        )[0]


def collect(place_ref, all_ref, owner_ref, term_ref, out_ref, land_ref, sems):
    fetch_blocks(place_ref, 1, all_ref, land_ref, sems)
    count = term_ref.shape[1]
    got = jnp.concatenate([land_ref[slot, slot : slot + 1, :] for slot in range(2 * REACH)], 1)
    hot = jnp.concatenate(
        [one_hot(owner_ref[slot : slot + 1, :], count) for slot in range(2 * REACH)], 1
    )
    high, low = split32(got)
    values = jnp.concatenate(
        [jnp.broadcast_to(x, (16, got.shape[1])).astype(bf16) for x in (high, low)], 0
    )
    sums = lax.dot_general(values, hot, (((1,), (1,)), ((), ())), preferred_element_type=f32)
    face_term = sums[0:1] + sums[16:17]
    out_ref[...] = (jnp.abs(term_ref[...]) + jnp.abs(face_term)) / scale_down


def call(kernel, outs, scratch=(), gathered=None):
    specs = {}
    scratch = [pltpu.VMEM(shape, kind) for shape, kind in scratch]
    if gathered is not None:
        scratch += [
            pltpu.VMEM((2 * REACH,) + gathered, f32),
            pltpu.SemaphoreType.DMA((2 * REACH,)),
        ]

    def run(*args):
        if gathered is not None:
            specs["in_specs"] = [
                pl.BlockSpec(memory_space=pltpu.SMEM),
                pl.BlockSpec(memory_space=pl.ANY),
            ] + [pl.BlockSpec(memory_space=pltpu.VMEM)] * (len(args) - 2)
        return pl.pallas_call(
            kernel,
            out_shape=[jax.ShapeDtypeStruct(shape, kind) for shape, kind in outs],
            scratch_shapes=scratch,
            compiler_params=pltpu.CompilerParams(vmem_limit_bytes=40 * 1024 * 1024),
            **specs,
        )(*args)

    return run


def local(
    adjoint_start,
    adjoint_source,
    inverse_diagonal,
    primal_field,
    cell_load,
    modulus,
    stiffness,
    connectivity,
    hang_node,
    hang_master,
    hang_weight,
    ghost_lists,
    subface_cell,
    subface_face,
    subface_owner,
):
    slots = 2 * REACH
    local_values, cell_count = cell_load.shape
    nodes = connectivity.shape[0]
    moduli = modulus.reshape(1, cell_count)
    table = ((3 * OWN, WIDE), f32)
    index = ((nodes, cell_count), i32)
    cells_shape = ((local_values, cell_count), f32)
    hang_shape = ((3, hang_node.shape[0]), f32)
    master_shape = ((8, WIDE), i32)
    own_table = ((3 * OWN, 2 * WIDE), bf16)
    edge = [((3 * EDGE, WIDE), f32), ((3 * EDGE, 2 * WIDE), bf16), cells_shape]

    def share(blocks):
        return lax.all_gather(blocks, "dom")

    place = lax.axis_index("dom").reshape(1).astype(i32)
    block = ((3 * slots, WIDE), f32)
    landing = block[0]
    tab, tab_primal, list_row, list_column, blocks = call(
        first_export,
        [table, table, (ghost_lists.shape, i32), (ghost_lists.shape, i32)]
        + [((6 * slots, WIDE), f32)],
    )(adjoint_start, primal_field, ghost_lists)
    ghosts = first_ghosts = share(blocks)
    first_landing = (6 * slots, WIDE)
    (
        row_own, column_own, row_edge, column_edge, master_own, master_edge, master_column,
        weight, source, inverse,
    ) = call(
        setup,
        [index] * 4 + [master_shape] * 3 + [((8, WIDE), f32), table, table],
        [((nodes, cell_count), f32)],
    )(
        connectivity, hang_node.reshape(1, -1), hang_master, hang_weight, adjoint_source,
        inverse_diagonal,
    )

    def gather_own(values):
        return call(own_gather, [cells_shape, hang_shape], [own_table])(
            values, row_own, column_own, master_own, master_column, weight
        )

    on_edge = (row_edge, column_edge, master_edge, master_column, weight)
    ku = None
    for sweep in range(SWEEPS):
        cells, hang = gather_own(tab)
        blocks, image, held = call(
            edge_product,
            [block, cells_shape, hang_shape],
            edge + [((6 * EDGE, WIDE), f32)],
            first_landing if sweep == 0 else landing,
        )(place, ghosts, cells, hang, *on_edge, moduli, stiffness)
        returned = share(blocks)
        (partial,) = call(own_sums, [table], [((6 * OWN, WIDE), f32)])(
            image, held, row_own, column_own, master_own, master_column, weight, tab, source,
            inverse,
        )
        if sweep == 0:
            cells, hang = gather_own(tab_primal)
            (ku,) = call(primal_product, [cells_shape], edge, first_landing)(
                place, first_ghosts, cells, hang, *on_edge, moduli, stiffness
            )
        last = sweep == SWEEPS - 1
        blocks, tab, *final = call(
            functools.partial(update, last),
            [block, table] + ([(adjoint_start.shape, f32)] if last else []),
            gathered=landing,
        )(place, returned, list_row, list_column, partial, inverse)
        ghosts = share(blocks)
    cells, hang = gather_own(tab)
    sent, term = call(
        fluxes,
        [(subface_cell.shape, f32), ((1, cell_count), f32)],
        edge,
        landing,
    )(place, ghosts, cells, hang, *on_edge, ku, cell_load, subface_cell, subface_face)
    received = share(sent)
    (indicator,) = call(collect, [((1, cell_count), f32)], gathered=subface_cell.shape)(
        place, received, subface_owner, term
    )
    return (final[0], indicator.reshape(cell_count))


def solution(mesh):
    placed = (
        P(None, "dom"),
        P(None, "dom"),
        P(None, "dom"),
        P(None, "dom"),
        P(None, "dom"),
        P("dom"),
        P(),
        P(None, "dom"),
        P("dom"),
        P(None, "dom"),
        P(None, "dom"),
        P(None, "dom"),
        P(None, "dom"),
        P(None, "dom"),
        P(None, "dom"),
    )
    return jax.shard_map(
        local, mesh=mesh, in_specs=placed, out_specs=(P(None, "dom"), P("dom")), check_vma=False
    )
```

```python
import functools

import jax
import jax.numpy as jnp
from jax import lax
from jax.experimental import pallas as pl
from jax.experimental.pallas import tpu as pltpu
from jax.sharding import PartitionSpec as P

REACH = 4
SWEEPS = 2
LANES = 128
WIDE = 2 * LANES
OWN = 32
EDGE = 16
NOWHERE = 126

relaxation = 0.7
scale_down = 16.0
pad_code = 16368

f32 = jnp.float32
bf16 = jnp.bfloat16
i32 = jnp.int32


def neighbour_offsets():
    return [step + 1 for step in range(REACH)] + [-(step + 1) for step in range(REACH)]


def exchange(packed):
    return lax.all_to_all(packed, "dom", 0, 0, tiled=True)


def pack(place, sign, rows, pack_ref, out_ref):
    count = out_ref.shape[0]
    pack_ref[...] = jnp.zeros_like(pack_ref)
    for slot, offset in enumerate(neighbour_offsets()):
        target = place + sign * offset
        at = jnp.where((target >= 0) & (target < count), target, count)
        for number, row in enumerate(rows[slot]):
            pack_ref[at, number : number + 1, :] = row
    out_ref[...] = pack_ref[:count]


def landed(place, sign, got_ref, number):
    count = got_ref.shape[0]
    rows = []
    for offset in neighbour_offsets():
        source = place - sign * offset
        row = got_ref[jnp.clip(source, 0, count - 1), number : number + 1, :]
        there = jnp.broadcast_to((source >= 0) & (source < count), row.shape)
        rows.append(jnp.where(there, row, 0.0))
    return rows


def landed_wide(place, sign, got_ref, part):
    halves = [
        jnp.concatenate(landed(place, sign, got_ref, 2 * part + half), 0) for half in range(2)
    ]
    return jnp.concatenate(halves, 1)


def match16(row, count):
    width = row.shape[1]
    wide = jnp.broadcast_to(row.astype(f32), (16, width)).astype(bf16)
    numbers = lax.broadcasted_iota(i32, (count, width), 0).astype(f32).astype(bf16)
    numbers = numbers.reshape(count // 16, 16, width)
    return numbers == wide[None]


def one_hot(row, count):
    mask = match16(row, count)
    ones = jnp.ones(mask.shape, bf16)
    return jnp.where(mask, ones, jnp.zeros_like(ones)).reshape(count, row.shape[1])


def spread16(mask, row):
    wide = jnp.broadcast_to(row, (16, row.shape[1])).astype(bf16)[None]
    out = jnp.where(mask, jnp.broadcast_to(wide, mask.shape), jnp.zeros(mask.shape, bf16))
    return out.reshape(mask.shape[0] * 16, row.shape[1])


def look_up(table, tops, half_rows, where, lane, totals=None):
    tiles = range(len(where))
    if totals is None:
        totals = [[jnp.zeros(where[0].shape, f32) for _ in tiles] for _ in tops]
    for half_row in range(half_rows):
        row, half = half_row // 2, half_row % 2
        masks = [where[tile] == half_row for tile in tiles]
        for part, top in enumerate(tops):
            line = jnp.broadcast_to(
                table[top + row : top + row + 1, half * LANES : (half + 1) * LANES],
                where[0].shape,
            )
            for tile in tiles:
                found = jnp.take_along_axis(line, lane[tile], axis=1, mode="promise_in_bounds")
                totals[part][tile] = jnp.where(masks[tile], found, totals[part][tile])
    return totals


def halves(x):
    return [x[:, :LANES], x[:, LANES:]]


def gather_cells(table, tops, half_rows, where_ref, lane_ref, out_ref, start_ref=None):
    count = where_ref.shape[0]
    high = 32

    def body(group, carry):
        start = pl.multiple_of(group * high, high)
        places = [
            (start + 8 * (tile // 2), slice(LANES * (tile % 2), LANES * (tile % 2 + 1)))
            for tile in range(high // 4)
        ]
        where = [where_ref[pl.ds(row, 8), columns] for row, columns in places]
        lane = [lane_ref[pl.ds(row, 8), columns] for row, columns in places]
        totals = None
        if start_ref is not None:
            totals = [
                [start_ref[pl.ds(part * count + row, 8), columns] for row, columns in places]
                for part in range(len(tops))
            ]
        totals = look_up(table, tops, half_rows, where, lane, totals)
        for part in range(len(tops)):
            for tile, (row, columns) in enumerate(places):
                out_ref[pl.ds(part * count + row, 8), columns] = totals[part][tile]
        return carry

    lax.fori_loop(0, count // high, body, 0)


def tops_of(rows, parts=3):
    return [part * rows for part in range(parts)]


def rows_and_columns(where, lane):
    return where >> 1, (where & 1) * LANES + lane


def scatter_block(values, rows, where, lane):
    at_row, at_column = rows_and_columns(where, lane)
    count = at_row.shape[0]
    masks = [match16(at_row[j : j + 1], rows) for j in range(count)]
    hot = jnp.concatenate([one_hot(at_column[j : j + 1], WIDE) for j in range(count)], 1)
    stacked = []
    for piece in range(2):
        for part in range(3):
            stacked.append(
                jnp.concatenate(
                    [spread16(masks[j], values[piece][part][j : j + 1]) for j in range(count)], 1
                )
            )
    return lax.dot_general(
        jnp.concatenate(stacked, 0), hot, (((1,), (1,)), ((), ())), preferred_element_type=f32
    )


def split32(x):
    high = x.astype(bf16).astype(f32)
    return high, x - high


def scatter_cells(image_ref, rows, where_ref, lane_ref, sum_ref):
    count = where_ref.shape[0]
    sum_ref[...] = jnp.zeros_like(sum_ref)

    def body(block, carry):
        start = pl.multiple_of(block * 8, 8)
        values = [split32(image_ref[pl.ds(part * count + start, 8), :]) for part in range(3)]
        values = list(zip(*values))
        sum_ref[...] += scatter_block(
            values, rows, where_ref[pl.ds(start, 8), :], lane_ref[pl.ds(start, 8), :]
        )
        return carry

    lax.fori_loop(0, count // 8, body, 0)


def add_pieces(sums):
    half = sums.shape[0] // 2
    return sums[:half] + sums[half:]


def spread_hanging(held, weight, rows, where, lane):
    both = jnp.concatenate([held, held], 1)
    values = [split32(weight * both[part : part + 1]) for part in range(3)]
    return add_pieces(scatter_block(list(zip(*values)), rows, where, lane))


def sum_masters(table, tops, half_rows, weight, where, lane):
    found = look_up(table, tops, half_rows, halves(where), halves(lane))
    weight = halves(weight)
    return [
        jnp.sum(weight[0] * tiles[0] + weight[1] * tiles[1], 0, keepdims=True) for tiles in found
    ]


def fill_table(x_ref, out_ref):
    count = x_ref.shape[1] // WIDE
    for part in range(3):
        out_ref[part * OWN + count : (part + 1) * OWN, :] = jnp.zeros((OWN - count, WIDE), f32)
    for row in range(count):
        block = x_ref[:, row * WIDE : (row + 1) * WIDE]
        for part in range(3):
            out_ref[part * OWN + row : part * OWN + row + 1, :] = block[part : part + 1]


def export_rows(tables, half_rows, where, lane):
    rows = [[] for _ in range(2 * REACH)]
    for table in tables:
        found = look_up(table, tops_of(OWN), half_rows, halves(where), halves(lane))
        for tiles in found:
            for tile in tiles:
                for slot in range(2 * REACH):
                    rows[slot].append(tile[slot : slot + 1])
    return rows


def copy_in(pairs, sems):
    copies = [
        pltpu.make_async_copy(source, target, sems.at[number])
        for number, (source, target) in enumerate(pairs)
    ]
    for copy in copies:
        copy.start()
    for copy in copies:
        copy.wait()


def first_export(
    place_ref, adjoint_hbm, primal_hbm, list_hbm, tab_a, tab_p, where_ref, lane_ref,
    out_ref, pack_ref, adjoint_ref, primal_ref, list_ref, sems,
):
    copy_in(
        [(adjoint_hbm, adjoint_ref), (primal_hbm, primal_ref), (list_hbm, list_ref)], sems
    )
    owned = adjoint_ref.shape[1]
    fill_table(adjoint_ref, tab_a)
    fill_table(primal_ref, tab_p)
    codes = list_ref[...]
    node = lax.rem(17 * codes + lax.broadcasted_iota(i32, codes.shape, 1), owned)
    where_ref[...] = node >> 7
    lane_ref[...] = node & 127
    rows = export_rows([tab_a, tab_p], owned // LANES, node >> 7, node & 127)
    pack(place_ref[0], 1, rows, pack_ref, out_ref)


def setup(
    connect_hbm, node_hbm, master_hbm, weight_hbm, source_hbm, inverse_hbm,
    own_where, edge_where, lane_ref, master_own, master_edge, master_lane, weight_out,
    tab_source, tab_inverse,
    connect_ref, node_ref, master_ref, weight_ref, source_ref, inverse_ref, map_ref, found_ref,
    sems,
):
    copy_in(
        [
            (connect_hbm, connect_ref),
            (node_hbm, node_ref),
            (master_hbm, master_ref),
            (weight_hbm, weight_ref),
            (source_hbm, source_ref),
            (inverse_hbm, inverse_ref),
        ],
        sems,
    )
    owned = source_ref.shape[1]
    extent = owned + 2 * REACH * WIDE
    fill_table(source_ref, tab_source)
    fill_table(inverse_ref, tab_inverse)
    codes = master_ref[...]
    master = lax.rem(17 * codes + 8 * lax.broadcasted_iota(i32, codes.shape, 1), extent)
    count = codes.shape[0] // 2
    master = jnp.concatenate([master[:count], master[count:]], 1)
    weight = weight_ref[...]
    weight_out[...] = jnp.concatenate([weight[:count], weight[count:]], 1)
    last = owned // LANES
    where = master >> 7
    master_own[...] = jnp.where(where < last, where, NOWHERE)
    master_edge[...] = jnp.where(where < last, NOWHERE, where - last)
    master_lane[...] = master & 127

    codes = node_ref[...]
    node = jnp.where(codes == pad_code, extent, lax.rem(13 * codes, owned))
    slot = (lax.broadcasted_iota(i32, codes.shape, 1) + 1).astype(f32)
    map_ref[...] = lax.dot_general(
        spread16(match16(node >> 8, OWN), slot),
        one_hot(node & 255, WIDE),
        (((1,), (1,)), ((), ())),
        preferred_element_type=f32,
    )

    codes = connect_ref[...]
    cells = lax.broadcasted_iota(i32, codes.shape, 1)
    slots = lax.rem(27 * cells + 17 * codes, extent)
    own_where[...] = slots >> 7
    lane_ref[...] = slots & 127
    gather_cells(map_ref, [0], last, own_where, lane_ref, found_ref)
    slot = found_ref[...].astype(i32)
    where = slots >> 7
    hanging = slot > 0
    outside = where >= last
    own_where[...] = jnp.where(hanging | outside, NOWHERE, where)
    edge_where[...] = jnp.where(
        hanging, 4 * REACH, jnp.where(outside, where - last, NOWHERE)
    )
    lane_ref[...] = jnp.where(hanging, slot - 1, slots & 127)


def pieces(x):
    high = x.astype(bf16)
    return high, (x - high.astype(f32)).astype(bf16)


def gather_own_cells(tab_ref, half_rows, where_ref, lane_ref, out_ref, tall_ref):
    count = where_ref.shape[0]
    tall = -(-half_rows // 8) * 8
    tall_ref[...] = jnp.zeros_like(tall_ref)
    for part in range(3):
        for half_row in range(half_rows):
            row, half = part * OWN + half_row // 2, half_row % 2
            tall_ref[part * tall + half_row : part * tall + half_row + 1, :] = tab_ref[
                row : row + 1, half * LANES : (half + 1) * LANES
            ]
    table = jnp.concatenate(pieces(tall_ref[...]), 1)

    def body(block, carry):
        start = pl.multiple_of(block * 8, 8)
        where = where_ref[pl.ds(start, 8), :]
        lane = lane_ref[pl.ds(start, 8), :]
        for j in range(8):
            hot = one_hot(lane[j : j + 1], LANES)
            found = jnp.dot(table, jnp.concatenate([hot, hot], 0), preferred_element_type=f32)
            mask = lax.broadcasted_iota(i32, (tall, WIDE), 0) == where[j : j + 1]
            for part in range(3):
                out_ref[pl.ds(part * count + start + j, 1), :] = jnp.sum(
                    jnp.where(mask, found[part * tall : (part + 1) * tall], 0.0), 0, keepdims=True
                )
        return carry

    lax.fori_loop(0, count // 8, body, 0)


def own_gather(
    half_rows, tab_ref, where_ref, lane_ref, master_where, master_lane, weight_ref, cells_ref,
    hang_ref, tall_ref,
):
    found = sum_masters(
        tab_ref, tops_of(OWN), half_rows, weight_ref[...], master_where[...], master_lane[...]
    )
    for part in range(3):
        hang_ref[part : part + 1, :] = found[part]
    gather_own_cells(tab_ref, half_rows, where_ref, lane_ref, cells_ref, tall_ref)


def edge_gather(
    place, got_ref, first, cells_ref, hang_ref, where_ref, lane_ref, master_where, master_lane,
    weight_ref, edge_ref, out_ref,
):
    slots = 2 * REACH
    for part in range(3):
        edge_ref[part * EDGE : part * EDGE + slots, :] = landed_wide(
            place, 1, got_ref, first + part
        )
    found = sum_masters(
        edge_ref, tops_of(EDGE), 2 * slots, weight_ref[...], master_where[...], master_lane[...]
    )
    for part in range(3):
        edge_ref[part * EDGE + slots : part * EDGE + slots + 1, :LANES] = (
            found[part] + hang_ref[part : part + 1, :]
        )
    gather_cells(
        edge_ref, tops_of(EDGE), 2 * slots + 1, where_ref, lane_ref, out_ref, cells_ref
    )


def edge_product(
    place_ref, got_ref, cells_ref, hang_ref, where_ref, lane_ref, master_where,
    master_lane, weight_ref, modulus_ref, stiffness_ref, out_ref,
    image_ref, held_ref, pack_ref, edge_ref, full_ref, sum_ref,
):
    place = place_ref[0]
    edge_gather(
        place, got_ref, 0, cells_ref, hang_ref, where_ref, lane_ref,
        master_where, master_lane, weight_ref, edge_ref, full_ref,
    )
    image_ref[...] = modulus_ref[...] * lax.dot_general(
        stiffness_ref[...],
        full_ref[...],
        (((0,), (0,)), ((), ())),
        precision=lax.Precision.HIGHEST,
        preferred_element_type=f32,
    )
    scatter_cells(image_ref, EDGE, where_ref, lane_ref, sum_ref)
    sums = add_pieces(sum_ref[...])
    slots = 2 * REACH
    held = jnp.concatenate(
        [sums[part * EDGE + slots : part * EDGE + slots + 1, :LANES] for part in range(3)], 0
    )
    held_ref[...] = held
    edge_ref[...] = sums + spread_hanging(
        held, weight_ref[...], EDGE, master_where[...], master_lane[...]
    )
    rows = [
        [
            edge_ref[part * EDGE + slot : part * EDGE + slot + 1, half * LANES : (half + 1) * LANES]
            for part in range(3)
            for half in range(2)
        ]
        for slot in range(slots)
    ]
    pack(place, -1, rows, pack_ref, out_ref)


def own_sums(
    image_ref, held_ref, where_ref, lane_ref, master_where, master_lane, weight_ref,
    tab_ref, source_ref, inverse_ref, out_ref, sum_ref,
):
    scatter_cells(image_ref, OWN, where_ref, lane_ref, sum_ref)
    applied = add_pieces(sum_ref[...]) + spread_hanging(
        held_ref[...], weight_ref[...], OWN, master_where[...], master_lane[...]
    )
    out_ref[...] = tab_ref[...] + relaxation * inverse_ref[...] * (source_ref[...] - applied)


def update(
    half_rows, place_ref, got_ref, where_ref, lane_ref, partial_ref, inverse_ref,
    out_ref, tab_ref, *rest,
):
    pack_ref = rest[-1]
    place = place_ref[0]
    values = [split32(landed_wide(place, -1, got_ref, part)) for part in range(3)]
    returned = add_pieces(
        scatter_block(list(zip(*values)), OWN, where_ref[...], lane_ref[...])
    )
    tab_ref[...] = partial_ref[...] - relaxation * inverse_ref[...] * returned
    rows = export_rows([tab_ref], half_rows, where_ref[...], lane_ref[...])
    pack(place, 1, rows, pack_ref, out_ref)
    if len(rest) > 1:
        final_ref = rest[0]
        for row in range(final_ref.shape[1] // WIDE):
            for part in range(3):
                final_ref[part : part + 1, row * WIDE : (row + 1) * WIDE] = tab_ref[
                    part * OWN + row : part * OWN + row + 1, :
                ]


def primal_product(
    place_ref, got_ref, cells_ref, hang_ref, where_ref, lane_ref, master_where,
    master_lane, weight_ref, modulus_ref, stiffness_ref, out_ref, edge_ref, full_ref,
):
    edge_gather(
        place_ref[0], got_ref, 3, cells_ref, hang_ref, where_ref, lane_ref,
        master_where, master_lane, weight_ref, edge_ref, full_ref,
    )
    out_ref[...] = modulus_ref[...] * jnp.dot(
        stiffness_ref[...],
        full_ref[...],
        precision=lax.Precision.HIGHEST,
        preferred_element_type=f32,
    )


def fluxes(
    place_ref, got_ref, cells_ref, hang_ref, where_ref, lane_ref, master_where,
    master_lane, weight_ref, ku_ref, load_ref, sub_cell, sub_face, out_ref,
    term_ref, pack_ref, edge_ref, full_ref, flux_ref,
):
    place = place_ref[0]
    edge_gather(
        place, got_ref, 0, cells_ref, hang_ref, where_ref, lane_ref,
        master_where, master_lane, weight_ref, edge_ref, full_ref,
    )
    cells = full_ref[...]
    ku = ku_ref[...]
    term_ref[...] = jnp.sum(cells * (load_ref[...] - ku), 0, keepdims=True)
    face = lax.broadcasted_iota(i32, (8, ku.shape[0]), 0)
    node = lax.broadcasted_iota(i32, (8, ku.shape[0]), 1) & 63
    index = jnp.where(face < 2, node >> 4, jnp.where(face < 4, (node >> 2) & 3, node & 3))
    member = jnp.where((face < 6) & (index == 3 * (face & 1)), 1.0, 0.0).astype(f32)
    flux_ref[...] = jnp.dot(
        member, ku * cells, precision=lax.Precision.HIGHEST, preferred_element_type=f32
    )
    cell = sub_cell[...]
    found = look_up(flux_ref, [0], 12, [2 * sub_face[...] + (cell >> 7)], [cell & 127])[0][0]
    rows = [[found[slot : slot + 1]] for slot in range(2 * REACH)]
    pack(place, 1, rows, pack_ref, out_ref)


def collect(place_ref, got_ref, owner_ref, term_ref, out_ref):
    count = term_ref.shape[1]
    got = jnp.concatenate(landed(place_ref[0], 1, got_ref, 0), 1)
    hot = jnp.concatenate(
        [one_hot(owner_ref[slot : slot + 1, :], count) for slot in range(2 * REACH)], 1
    )
    values = jnp.concatenate(
        [jnp.broadcast_to(x, (16, got.shape[1])).astype(bf16) for x in split32(got)], 0
    )
    sums = lax.dot_general(values, hot, (((1,), (1,)), ((), ())), preferred_element_type=f32)
    face_term = sums[0:1] + sums[16:17]
    out_ref[...] = (jnp.abs(term_ref[...]) + jnp.abs(face_term)) / scale_down


SMALL = pl.BlockSpec(memory_space=pltpu.SMEM)
FAST = pl.BlockSpec(memory_space=pltpu.VMEM)
FAR = pl.BlockSpec(memory_space=pl.ANY)


def call(kernel, outs, scratch=(), specs=None, sems=0):
    scratch = [pltpu.VMEM(shape, kind) for shape, kind in scratch]
    if sems:
        scratch.append(pltpu.SemaphoreType.DMA((sems,)))

    def run(*args):
        return pl.pallas_call(
            kernel,
            out_shape=[jax.ShapeDtypeStruct(shape, kind) for shape, kind in outs],
            in_specs=specs or [SMALL] + [FAST] * (len(args) - 1),
            scratch_shapes=scratch,
            compiler_params=pltpu.CompilerParams(vmem_limit_bytes=40 * 1024 * 1024),
        )(*args)

    return run


def local(
    adjoint_start,
    adjoint_source,
    inverse_diagonal,
    primal_field,
    cell_load,
    modulus,
    stiffness,
    connectivity,
    hang_node,
    hang_master,
    hang_weight,
    ghost_lists,
    subface_cell,
    subface_face,
    subface_owner,
):
    slots = 2 * REACH
    local_values, cell_count = cell_load.shape
    nodes = connectivity.shape[0]
    half_rows = adjoint_start.shape[1] // LANES
    moduli = modulus.reshape(1, cell_count)
    place = lax.axis_index("dom").reshape(1).astype(i32)
    table = ((3 * OWN, WIDE), f32)
    index = ((nodes, cell_count), i32)
    cells_shape = ((local_values, cell_count), f32)
    hang_shape = ((3, hang_node.shape[0]), f32)
    master_shape = ((8, WIDE), i32)
    edge = ((3 * EDGE, WIDE), f32)

    count = lax.axis_size("dom")

    def packed(height):
        return [((count, height, LANES), f32)]

    def room(height):
        return ((count + 1, height, LANES), f32)

    tab, tab_primal, list_where, list_lane, blocks = call(
        first_export,
        [table, table] + [(ghost_lists.shape, i32)] * 2 + packed(16),
        [
            room(16),
            (adjoint_start.shape, f32),
            (primal_field.shape, f32),
            (ghost_lists.shape, i32),
        ],
        [SMALL, FAR, FAR, FAR],
        sems=3,
    )(place, adjoint_start, primal_field, ghost_lists)
    ghosts = first_ghosts = exchange(blocks)
    hang_node = hang_node.reshape(1, -1)
    far = (
        connectivity, hang_node, hang_master, hang_weight, adjoint_source, inverse_diagonal
    )
    (
        own_where, edge_where, lane, master_own, master_edge, master_lane, weight, source, inverse,
    ) = call(
        setup,
        [index] * 3 + [master_shape] * 3 + [((8, WIDE), f32), table, table],
        [(x.shape, x.dtype) for x in far] + [((OWN, WIDE), f32), ((nodes, cell_count), f32)],
        [FAR] * 6,
        sems=6,
    )(*far)

    def gather_own(values):
        return call(
            functools.partial(own_gather, half_rows),
            [cells_shape, hang_shape],
            [((3 * (-(-half_rows // 8) * 8), LANES), f32)],
            specs=[FAST] * 6,
        )(values, own_where, lane, master_own, master_lane, weight)

    on_edge = (edge_where, lane, master_edge, master_lane, weight)
    ku = None
    for sweep in range(SWEEPS):
        cells, hang = gather_own(tab)
        blocks, image, held = call(
            edge_product,
            packed(8) + [cells_shape, hang_shape],
            [room(8), edge, cells_shape, ((6 * EDGE, WIDE), f32)],
        )(place, ghosts, cells, hang, *on_edge, moduli, stiffness)
        returned = exchange(blocks)
        (partial,) = call(
            own_sums, [table], [((6 * OWN, WIDE), f32)], specs=[FAST] * 10
        )(image, held, own_where, lane, master_own, master_lane, weight, tab, source, inverse)
        if sweep == 0:
            cells, hang = gather_own(tab_primal)
            (ku,) = call(primal_product, [cells_shape], [edge, cells_shape])(
                place, first_ghosts, cells, hang, *on_edge, moduli, stiffness
            )
        last = sweep == SWEEPS - 1
        blocks, tab, *final = call(
            functools.partial(update, half_rows),
            packed(8) + [table] + ([(adjoint_start.shape, f32)] if last else []),
            [room(8)],
        )(place, returned, list_where, list_lane, partial, inverse)
        ghosts = exchange(blocks)
    cells, hang = gather_own(tab)
    blocks, term = call(
        fluxes,
        packed(1) + [((1, cell_count), f32)],
        [room(1), edge, cells_shape, ((8, cell_count), f32)],
    )(place, ghosts, cells, hang, *on_edge, ku, cell_load, subface_cell, subface_face)
    received = exchange(blocks)
    (indicator,) = call(collect, [((1, cell_count), f32)])(
        place, received, subface_owner, term
    )
    return (final[0], indicator.reshape(cell_count))


def solution(mesh):
    placed = (
        P(None, "dom"),
        P(None, "dom"),
        P(None, "dom"),
        P(None, "dom"),
        P(None, "dom"),
        P("dom"),
        P(),
        P(None, "dom"),
        P("dom"),
        P(None, "dom"),
        P(None, "dom"),
        P(None, "dom"),
        P(None, "dom"),
        P(None, "dom"),
        P(None, "dom"),
    )
    return jax.shard_map(
        local, mesh=mesh, in_specs=placed, out_specs=(P(None, "dom"), P("dom")), check_vma=False
    )
```

```python
import functools

import jax
import jax.numpy as jnp
from jax import lax
from jax.experimental import pallas as pl
from jax.experimental.pallas import tpu as pltpu
from jax.sharding import PartitionSpec as P

REACH = 4
SWEEPS = 2
LANES = 128
WIDE = 2 * LANES
OWN = 32
EDGE = 16
TALL = 24
NOWHERE = 126

relaxation = 0.7
scale_down = 16.0
pad_code = 16368

f32 = jnp.float32
bf16 = jnp.bfloat16
i32 = jnp.int32


def neighbour_offsets():
    return [step + 1 for step in range(REACH)] + [-(step + 1) for step in range(REACH)]


def exchange(packed):
    return lax.all_to_all(packed, "dom", 0, 0, tiled=True)


def pack(place, sign, rows, pack_ref, out_ref):
    count = out_ref.shape[0]
    pack_ref[...] = jnp.zeros_like(pack_ref)
    for slot, offset in enumerate(neighbour_offsets()):
        target = place + sign * offset
        at = jnp.where((target >= 0) & (target < count), target, count)
        for number, row in enumerate(rows[slot]):
            pack_ref[at, number : number + 1, :] = row
    out_ref[...] = pack_ref[:count]


def landed(place, sign, got_ref, number):
    count = got_ref.shape[0]
    rows = []
    for offset in neighbour_offsets():
        source = place - sign * offset
        row = got_ref[jnp.clip(source, 0, count - 1), number : number + 1, :]
        there = jnp.broadcast_to((source >= 0) & (source < count), row.shape)
        rows.append(jnp.where(there, row, 0.0))
    return rows


def landed_wide(place, sign, got_ref, part):
    halves = [
        jnp.concatenate(landed(place, sign, got_ref, 2 * part + half), 0) for half in range(2)
    ]
    return jnp.concatenate(halves, 1)


def match16(row, count):
    width = row.shape[1]
    wide = jnp.broadcast_to(row.astype(f32), (16, width)).astype(bf16)
    numbers = lax.broadcasted_iota(i32, (count, width), 0).astype(f32).astype(bf16)
    numbers = numbers.reshape(count // 16, 16, width)
    return numbers == wide[None]


def one_hot(row, count):
    mask = match16(row, count)
    ones = jnp.ones(mask.shape, bf16)
    return jnp.where(mask, ones, jnp.zeros_like(ones)).reshape(count, row.shape[1])


def spread16(mask, row):
    wide = jnp.broadcast_to(row, (16, row.shape[1])).astype(bf16)[None]
    out = jnp.where(mask, jnp.broadcast_to(wide, mask.shape), jnp.zeros(mask.shape, bf16))
    return out.reshape(mask.shape[0] * 16, row.shape[1])


def pieces(x):
    high = x.astype(bf16)
    return high, (x - high.astype(f32)).astype(bf16)


def gather(table, tall, parts, where_ref, lane_ref, sums_ref):
    count = where_ref.shape[0]
    width = where_ref.shape[1]
    numbers = lax.broadcasted_iota(i32, (tall, width), 0)

    def body(block, carry):
        start = pl.multiple_of(block * 8, 8)
        for j in range(8):
            hot = one_hot(lane_ref[pl.ds(start + j, 1), :], LANES)
            found = jnp.dot(table, jnp.concatenate([hot, hot], 0), preferred_element_type=f32)
            mask = numbers == jnp.broadcast_to(where_ref[pl.ds(start + j, 1), :], numbers.shape)
            for part in range(parts):
                kept = jnp.where(mask, found[part * tall : (part + 1) * tall], 0.0)
                kept = jnp.sum(kept.reshape(tall // 8, 8, width), 0)
                for half in range(width // LANES):
                    sums_ref[half, pl.ds(part * count * 8 + start * 8 + j * 8, 8), :] = kept[
                        :, half * LANES : (half + 1) * LANES
                    ]
        return carry

    lax.fori_loop(0, count // 8, body, 0)


def gathered(sums_ref, count, part):
    totals = []
    for half in range(sums_ref.shape[0]):
        rows = [sums_ref[half, pl.ds(part * count * 8 + s, count, stride=8), :] for s in range(8)]
        while len(rows) > 1:
            rows = [a + b for a, b in zip(rows[::2], rows[1::2])]
        totals.append(rows[0])
    return jnp.concatenate(totals, 1)


def halves(x):
    return [x[:, :LANES], x[:, LANES:]]


def rows_and_columns(where, lane):
    return where >> 1, (where & 1) * LANES + lane


def scatter(high_ref, low_ref, rows, row_ref, column_ref, sum_ref, deep):
    count = row_ref.shape[0]
    sum_ref[...] = jnp.zeros_like(sum_ref)

    def body(block, carry):
        start = pl.multiple_of(block * 8, 8)
        for first in range(0, 8, deep):
            steps = range(first, first + deep)
            masks = [match16(row_ref[pl.ds(start + j, 1), :], rows) for j in steps]
            hot = jnp.concatenate(
                [one_hot(column_ref[pl.ds(start + j, 1), :], WIDE) for j in steps], 1
            )
            stacked = [
                jnp.concatenate(
                    [
                        spread16(mask, piece_ref[pl.ds(part * count + start + j, 1), :])
                        for mask, j in zip(masks, steps)
                    ],
                    1,
                )
                for piece_ref in (high_ref, low_ref)
                for part in range(3)
            ]
            sum_ref[...] += lax.dot_general(
                jnp.concatenate(stacked, 0),
                hot,
                (((1,), (1,)), ((), ())),
                preferred_element_type=f32,
            )
        return carry

    lax.fori_loop(0, count // 8, body, 0)


def split32(x):
    high = x.astype(bf16).astype(f32)
    return high, x - high


def add_pieces(sums):
    half = sums.shape[0] // 2
    return sums[:half] + sums[half:]


def scatter_few(values, rows, where, lane, scratch):
    high_ref, low_ref, row_ref, column_ref, sum_ref = scratch
    row_ref[...], column_ref[...] = rows_and_columns(where, lane)
    for part in range(3):
        high_ref[part * 8 : part * 8 + 8, :], low_ref[part * 8 : part * 8 + 8, :] = split32(
            values[part]
        )
    scatter(high_ref, low_ref, rows, row_ref, column_ref, sum_ref, 8)
    return add_pieces(sum_ref[...])


def few(rows):
    return [((24, WIDE), f32)] * 2 + [((8, WIDE), i32)] * 2 + [((6 * rows, WIDE), f32)]


def spread_hanging(held, weight, rows, where, lane, scratch):
    both = jnp.concatenate([held, held], 1)
    values = [weight * both[part : part + 1] for part in range(3)]
    return scatter_few(values, rows, where, lane, scratch)


def sum_masters(table, tall, weight, where_ref, lane_ref, sums_ref):
    gather(table, tall, 3, where_ref, lane_ref, sums_ref)
    totals = []
    for part in range(3):
        left, right = halves(weight * gathered(sums_ref, 8, part))
        totals.append(jnp.sum(left + right, 0, keepdims=True))
    return totals


def fill_table(x_ref, out_ref):
    count = x_ref.shape[1] // WIDE
    for part in range(3):
        out_ref[part * OWN + count : (part + 1) * OWN, :] = jnp.zeros((OWN - count, WIDE), f32)
    for row in range(count):
        block = x_ref[:, row * WIDE : (row + 1) * WIDE]
        for part in range(3):
            out_ref[part * OWN + row : part * OWN + row + 1, :] = block[part : part + 1]


def tall_table(tab_refs, half_rows, tall_ref):
    tall = up8(half_rows)
    tall_ref[...] = jnp.zeros_like(tall_ref)
    for number, tab_ref in enumerate(tab_refs):
        for part in range(3):
            for half_row in range(half_rows):
                row, half = part * OWN + half_row // 2, half_row % 2
                at = (3 * number + part) * tall + half_row
                tall_ref[at : at + 1, :] = tab_ref[
                    row : row + 1, half * LANES : (half + 1) * LANES
                ]
    return jnp.concatenate(pieces(tall_ref[...]), 1)


def up8(count):
    return -(-count // 8) * 8


def export_rows(table, tall, parts, where_ref, lane_ref, sums_ref):
    gather(table, tall, parts, where_ref, lane_ref, sums_ref)
    rows = [[] for _ in range(2 * REACH)]
    for part in range(parts):
        for tile in halves(gathered(sums_ref, 8, part)):
            for slot in range(2 * REACH):
                rows[slot].append(tile[slot : slot + 1])
    return rows


def copy_in(pairs, sems):
    copies = [
        pltpu.make_async_copy(source, target, sems.at[number])
        for number, (source, target) in enumerate(pairs)
    ]
    for copy in copies:
        copy.start()
    for copy in copies:
        copy.wait()


def first_export(
    place_ref, adjoint_hbm, primal_hbm, list_hbm, tab_a, tab_p, where_ref, lane_ref,
    out_ref, pack_ref, adjoint_ref, primal_ref, list_ref, tall_ref, sums_ref, sems,
):
    copy_in(
        [(adjoint_hbm, adjoint_ref), (primal_hbm, primal_ref), (list_hbm, list_ref)], sems
    )
    owned = adjoint_ref.shape[1]
    fill_table(adjoint_ref, tab_a)
    fill_table(primal_ref, tab_p)
    codes = list_ref[...]
    node = lax.rem(17 * codes + lax.broadcasted_iota(i32, codes.shape, 1), owned)
    where_ref[...] = node >> 7
    lane_ref[...] = node & 127
    half_rows = owned // LANES
    table = tall_table([tab_a, tab_p], half_rows, tall_ref)
    rows = export_rows(table, up8(half_rows), 6, where_ref, lane_ref, sums_ref)
    pack(place_ref[0], 1, rows, pack_ref, out_ref)


def setup(
    connect_hbm, node_hbm, master_hbm, weight_hbm, source_hbm, inverse_hbm,
    own_where, own_row, edge_where, edge_row, lane_ref, column_ref, edge_column, master_own, master_edge,
    master_lane, weight_out,
    tab_source, tab_inverse,
    connect_ref, node_ref, master_ref, weight_ref, source_ref, inverse_ref, map_ref, tall_ref, sums_ref,
    sems,
):
    copy_in(
        [
            (connect_hbm, connect_ref),
            (node_hbm, node_ref),
            (master_hbm, master_ref),
            (weight_hbm, weight_ref),
            (source_hbm, source_ref),
            (inverse_hbm, inverse_ref),
        ],
        sems,
    )
    owned = source_ref.shape[1]
    extent = owned + 2 * REACH * WIDE
    fill_table(source_ref, tab_source)
    fill_table(inverse_ref, tab_inverse)
    codes = master_ref[...]
    master = lax.rem(17 * codes + 8 * lax.broadcasted_iota(i32, codes.shape, 1), extent)
    count = codes.shape[0] // 2
    master = jnp.concatenate([master[:count], master[count:]], 1)
    weight = weight_ref[...]
    weight_out[...] = jnp.concatenate([weight[:count], weight[count:]], 1)
    last = owned // LANES
    where = master >> 7
    master_own[...] = jnp.where(where < last, where, NOWHERE)
    master_edge[...] = jnp.where(where < last, NOWHERE, where - last)
    master_lane[...] = master & 127

    codes = node_ref[...]
    node = jnp.where(codes == pad_code, extent, lax.rem(13 * codes, owned))
    slot = (lax.broadcasted_iota(i32, codes.shape, 1) + 1).astype(f32)
    map_ref[...] = lax.dot_general(
        spread16(match16(node >> 8, OWN), slot),
        one_hot(node & 255, WIDE),
        (((1,), (1,)), ((), ())),
        preferred_element_type=f32,
    )

    codes = connect_ref[...]
    cells = lax.broadcasted_iota(i32, codes.shape, 1)
    slots = lax.rem(27 * cells + 17 * codes, extent)
    own_where[...] = slots >> 7
    lane_ref[...] = slots & 127
    tall_ref[...] = jnp.zeros_like(tall_ref)
    for half_row in range(last):
        row, half = half_row // 2, half_row % 2
        tall_ref[half_row : half_row + 1, :] = map_ref[
            row : row + 1, half * LANES : (half + 1) * LANES
        ]
    table = jnp.concatenate(pieces(tall_ref[...]), 1)
    gather(table, tall_ref.shape[0], 1, own_where, lane_ref, sums_ref)
    slot = gathered(sums_ref, codes.shape[0], 0).astype(i32)
    where = slots >> 7
    hanging = slot > 0
    outside = where >= last
    lane = jnp.where(hanging, slot - 1, slots & 127)
    lane_ref[...] = lane
    where_own = jnp.where(hanging | outside, NOWHERE, where)
    own_where[...] = where_own
    own_row[...], column_ref[...] = rows_and_columns(where_own, lane)
    where_edge = jnp.where(hanging, 4 * REACH, jnp.where(outside, where - last, NOWHERE))
    edge_where[...] = where_edge
    edge_row[...], edge_column[...] = rows_and_columns(where_edge, lane)


def own_gather(
    half_rows, tab_ref, where_ref, lane_ref, master_where, master_lane, weight_ref, cells_ref,
    hang_ref, tall_ref, sums_ref,
):
    table = tall_table([tab_ref], half_rows, tall_ref)
    tall = up8(half_rows)
    found = sum_masters(table, tall, weight_ref[...], master_where, master_lane, sums_ref)
    for part in range(3):
        hang_ref[part : part + 1, :] = found[part]
    gather(table, tall, 3, where_ref, lane_ref, sums_ref)
    count = where_ref.shape[0]
    for part in range(3):
        cells_ref[part * count : (part + 1) * count, :] = gathered(sums_ref, count, part)


def edge_gather(
    place, got_ref, first, cells_ref, hang_ref, where_ref, lane_ref, master_where, master_lane,
    weight_ref, edge_ref, sums_ref, out_ref,
):
    slots = 2 * REACH
    edge_ref[...] = jnp.zeros_like(edge_ref)
    for part in range(3):
        for half in range(2):
            lines = landed(place, 1, got_ref, 2 * (first + part) + half)
            for slot in range(slots):
                at = part * TALL + 2 * slot + half
                edge_ref[at : at + 1, :] = lines[slot]
    table = jnp.concatenate(pieces(edge_ref[...]), 1)
    found = sum_masters(table, TALL, weight_ref[...], master_where, master_lane, sums_ref)
    for part in range(3):
        at = part * TALL + 2 * slots
        edge_ref[at : at + 1, :] = found[part] + hang_ref[part : part + 1, :]
    table = jnp.concatenate(pieces(edge_ref[...]), 1)
    gather(table, TALL, 3, where_ref, lane_ref, sums_ref)
    count = where_ref.shape[0]
    for part in range(3):
        rows = slice(part * count, (part + 1) * count)
        out_ref[rows, :] = cells_ref[rows, :] + gathered(sums_ref, count, part)


def edge_product(
    place_ref, got_ref, cells_ref, hang_ref, where_ref, lane_ref, master_where, master_lane,
    weight_ref, row_ref, column_ref, modulus_ref, stiffness_ref, out_ref,
    image_ref, held_ref, pack_ref, edge_ref, sums_ref, full_ref, low_ref, sum_ref, *scratch,
):
    place = place_ref[0]
    edge_gather(
        place, got_ref, 0, cells_ref, hang_ref, where_ref, lane_ref,
        master_where, master_lane, weight_ref, edge_ref, sums_ref, full_ref,
    )
    image = modulus_ref[...] * lax.dot_general(
        stiffness_ref[...],
        full_ref[...],
        (((0,), (0,)), ((), ())),
        precision=lax.Precision.HIGHEST,
        preferred_element_type=f32,
    )
    image_ref[...] = image
    full_ref[...], low_ref[...] = split32(image)
    scatter(full_ref, low_ref, EDGE, row_ref, column_ref, sum_ref, 2)
    sums = add_pieces(sum_ref[...])
    slots = 2 * REACH
    held = jnp.concatenate(
        [sums[part * EDGE + slots : part * EDGE + slots + 1, :LANES] for part in range(3)], 0
    )
    held_ref[...] = held
    sums += spread_hanging(
        held, weight_ref[...], EDGE, master_where[...], master_lane[...], scratch
    )
    rows = [
        [
            sums[part * EDGE + slot : part * EDGE + slot + 1, half * LANES : (half + 1) * LANES]
            for part in range(3)
            for half in range(2)
        ]
        for slot in range(slots)
    ]
    pack(place, -1, rows, pack_ref, out_ref)


def own_sums(
    image_ref, held_ref, row_ref, column_ref, master_where, master_lane, weight_ref,
    tab_ref, source_ref, inverse_ref, out_ref, high_ref, low_ref, sum_ref, *scratch,
):
    high_ref[...], low_ref[...] = split32(image_ref[...])
    scatter(high_ref, low_ref, OWN, row_ref, column_ref, sum_ref, 8)
    applied = add_pieces(sum_ref[...]) + spread_hanging(
        held_ref[...], weight_ref[...], OWN, master_where[...], master_lane[...], scratch
    )
    out_ref[...] = tab_ref[...] + relaxation * inverse_ref[...] * (source_ref[...] - applied)


def update(
    half_rows, place_ref, got_ref, where_ref, lane_ref, partial_ref, inverse_ref,
    out_ref, tab_ref, *rest,
):
    *final_ref, pack_ref, tall_ref, sums_ref = rest[:-5]
    place = place_ref[0]
    values = [landed_wide(place, -1, got_ref, part) for part in range(3)]
    returned = scatter_few(values, OWN, where_ref[...], lane_ref[...], rest[-5:])
    tab_ref[...] = partial_ref[...] - relaxation * inverse_ref[...] * returned
    table = tall_table([tab_ref], half_rows, tall_ref)
    rows = export_rows(table, up8(half_rows), 3, where_ref, lane_ref, sums_ref)
    pack(place, 1, rows, pack_ref, out_ref)
    if final_ref:
        final_ref = final_ref[0]
        for row in range(final_ref.shape[1] // WIDE):
            for part in range(3):
                final_ref[part : part + 1, row * WIDE : (row + 1) * WIDE] = tab_ref[
                    part * OWN + row : part * OWN + row + 1, :
                ]


def primal_product(
    place_ref, got_ref, cells_ref, hang_ref, where_ref, lane_ref, master_where,
    master_lane, weight_ref, modulus_ref, stiffness_ref, out_ref, edge_ref, sums_ref, full_ref,
):
    edge_gather(
        place_ref[0], got_ref, 3, cells_ref, hang_ref, where_ref, lane_ref,
        master_where, master_lane, weight_ref, edge_ref, sums_ref, full_ref,
    )
    out_ref[...] = modulus_ref[...] * jnp.dot(
        stiffness_ref[...],
        full_ref[...],
        precision=lax.Precision.HIGHEST,
        preferred_element_type=f32,
    )


def fluxes(
    place_ref, got_ref, cells_ref, hang_ref, where_ref, lane_ref, master_where,
    master_lane, weight_ref, ku_ref, load_ref, sub_cell, sub_face, out_ref,
    term_ref, pack_ref, edge_ref, sums_ref, full_ref, tall_ref, code_ref, few_ref,
):
    place = place_ref[0]
    edge_gather(
        place, got_ref, 0, cells_ref, hang_ref, where_ref, lane_ref,
        master_where, master_lane, weight_ref, edge_ref, sums_ref, full_ref,
    )
    cells = full_ref[...]
    ku = ku_ref[...]
    term_ref[...] = jnp.sum(cells * (load_ref[...] - ku), 0, keepdims=True)
    face = lax.broadcasted_iota(i32, (8, ku.shape[0]), 0)
    node = lax.broadcasted_iota(i32, (8, ku.shape[0]), 1) & 63
    index = jnp.where(face < 2, node >> 4, jnp.where(face < 4, (node >> 2) & 3, node & 3))
    member = jnp.where((face < 6) & (index == 3 * (face & 1)), 1.0, 0.0).astype(f32)
    flux = jnp.dot(
        member, ku * cells, precision=lax.Precision.HIGHEST, preferred_element_type=f32
    )
    tall_ref[...] = jnp.zeros_like(tall_ref)
    for number in range(6):
        for half in range(2):
            at = 2 * number + half
            tall_ref[at : at + 1, :] = flux[
                number : number + 1, half * LANES : (half + 1) * LANES
            ]
    cell = sub_cell[...]
    code_ref[:8, :] = 2 * sub_face[...] + (cell >> 7)
    code_ref[8:, :] = cell & 127
    table = jnp.concatenate(pieces(tall_ref[...]), 1)
    gather(table, 16, 1, code_ref.at[:8, :], code_ref.at[8:, :], few_ref)
    found = gathered(few_ref, 8, 0)
    rows = [[found[slot : slot + 1]] for slot in range(2 * REACH)]
    pack(place, 1, rows, pack_ref, out_ref)


def collect(place_ref, got_ref, owner_ref, term_ref, out_ref):
    count = term_ref.shape[1]
    got = jnp.concatenate(landed(place_ref[0], 1, got_ref, 0), 1)
    hot = jnp.concatenate(
        [one_hot(owner_ref[slot : slot + 1, :], count) for slot in range(2 * REACH)], 1
    )
    values = jnp.concatenate(
        [jnp.broadcast_to(x, (16, got.shape[1])).astype(bf16) for x in split32(got)], 0
    )
    sums = lax.dot_general(values, hot, (((1,), (1,)), ((), ())), preferred_element_type=f32)
    face_term = sums[0:1] + sums[16:17]
    out_ref[...] = (jnp.abs(term_ref[...]) + jnp.abs(face_term)) / scale_down


SMALL = pl.BlockSpec(memory_space=pltpu.SMEM)
FAST = pl.BlockSpec(memory_space=pltpu.VMEM)
FAR = pl.BlockSpec(memory_space=pl.ANY)


def away(*arrays):
    return [pltpu.with_memory_space_constraint(x, pltpu.HBM) for x in arrays]


def call(kernel, outs, scratch=(), specs=None, sems=0):
    scratch = [pltpu.VMEM(shape, kind) for shape, kind in scratch]
    if sems:
        scratch.append(pltpu.SemaphoreType.DMA((sems,)))

    def run(*args):
        return pl.pallas_call(
            kernel,
            out_shape=[jax.ShapeDtypeStruct(shape, kind) for shape, kind in outs],
            in_specs=specs or [SMALL] + [FAST] * (len(args) - 1),
            scratch_shapes=scratch,
            compiler_params=pltpu.CompilerParams(vmem_limit_bytes=40 * 1024 * 1024),
        )(*args)

    return run


def local(
    adjoint_start,
    adjoint_source,
    inverse_diagonal,
    primal_field,
    cell_load,
    modulus,
    stiffness,
    connectivity,
    hang_node,
    hang_master,
    hang_weight,
    ghost_lists,
    subface_cell,
    subface_face,
    subface_owner,
):
    slots = 2 * REACH
    local_values, cell_count = cell_load.shape
    nodes = connectivity.shape[0]
    half_rows = adjoint_start.shape[1] // LANES
    moduli = modulus.reshape(1, cell_count)
    place = lax.axis_index("dom").reshape(1).astype(i32)
    table = ((3 * OWN, WIDE), f32)
    index = ((nodes, cell_count), i32)
    cells_shape = ((local_values, cell_count), f32)
    hang_shape = ((3, hang_node.shape[0]), f32)
    master_shape = ((8, WIDE), i32)

    count = lax.axis_size("dom")

    def packed(height):
        return [((count, height, LANES), f32)]

    def room(height):
        return ((count + 1, height, LANES), f32)

    tall = up8(half_rows)
    few_sums = ((2, 3 * 64, LANES), f32)
    many_sums = ((2, local_values * 8, LANES), f32)
    own_tall = ((3 * tall, LANES), f32)
    edge = [((3 * TALL, LANES), f32), many_sums, cells_shape]
    tab, tab_primal, list_where, list_lane, blocks = call(
        first_export,
        [table, table] + [(ghost_lists.shape, i32)] * 2 + packed(16),
        [
            room(16),
            (adjoint_start.shape, f32),
            (primal_field.shape, f32),
            (ghost_lists.shape, i32),
            ((6 * tall, LANES), f32),
            ((2, 6 * 64, LANES), f32),
        ],
        [SMALL, FAR, FAR, FAR],
        sems=3,
    )(place, *away(adjoint_start, primal_field, ghost_lists))
    ghosts = first_ghosts = exchange(blocks)
    far = (
        connectivity, hang_node.reshape(1, -1), hang_master, hang_weight, adjoint_source,
        inverse_diagonal,
    )
    (
        own_where, own_row, edge_where, edge_row, lane, own_column, edge_column, master_own,
        master_edge, master_lane, weight, source, inverse,
    ) = call(
        setup,
        [index] * 7 + [master_shape] * 3 + [((8, WIDE), f32), table, table],
        [(x.shape, x.dtype) for x in far]
        + [((OWN, WIDE), f32), ((tall, LANES), f32), ((2, nodes * 8, LANES), f32)],
        [FAR] * 6,
        sems=6,
    )(*away(*far))

    def gather_own(values):
        return call(
            functools.partial(own_gather, half_rows),
            [cells_shape, hang_shape],
            [own_tall, many_sums],
            specs=[FAST] * 6,
        )(values, own_where, lane, master_own, master_lane, weight)

    on_edge = (edge_where, lane, master_edge, master_lane, weight)
    for sweep in range(SWEEPS):
        cells, hang = gather_own(tab)
        if sweep == 1:
            (ku,) = call(primal_product, [cells_shape], edge)(
                place, first_ghosts, *primal_cells, *on_edge, moduli, stiffness
            )
            cells, ku = lax.optimization_barrier((cells, ku))
        blocks, image, held = call(
            edge_product,
            packed(8) + [cells_shape, hang_shape],
            [room(8)] + edge + [cells_shape, ((6 * EDGE, WIDE), f32)] + few(EDGE),
        )(place, ghosts, cells, hang, *on_edge, edge_row, edge_column, moduli, stiffness)
        returned = exchange(blocks)
        (partial,) = call(
            own_sums,
            [table],
            [cells_shape, cells_shape, ((6 * OWN, WIDE), f32)] + few(OWN),
            specs=[FAST] * 10,
        )(image, held, own_row, own_column, master_own, master_lane, weight, tab, source, inverse)
        if sweep == 0:
            tab_primal, image = lax.optimization_barrier((tab_primal, image))
            primal_cells = gather_own(tab_primal)
            partial, *primal_cells = lax.optimization_barrier((partial, *primal_cells))
        last = sweep == SWEEPS - 1
        blocks, tab, *final = call(
            functools.partial(update, half_rows),
            packed(8) + [table] + ([(adjoint_start.shape, f32)] if last else []),
            [room(8), own_tall, few_sums] + few(OWN),
        )(place, returned, list_where, list_lane, partial, inverse)
        ghosts = exchange(blocks)
    cells, hang = gather_own(tab)
    blocks, term = call(
        fluxes,
        packed(1) + [((1, cell_count), f32)],
        [room(1)]
        + edge
        + [
            ((16, LANES), f32),
            ((16, subface_cell.shape[1]), i32),
            ((1, 64, LANES), f32),
        ],
    )(place, ghosts, cells, hang, *on_edge, ku, cell_load, subface_cell, subface_face)
    received = exchange(blocks)
    (indicator,) = call(collect, [((1, cell_count), f32)])(
        place, received, subface_owner, term
    )
    return (final[0], indicator.reshape(cell_count))


def solution(mesh):
    placed = (
        P(None, "dom"),
        P(None, "dom"),
        P(None, "dom"),
        P(None, "dom"),
        P(None, "dom"),
        P("dom"),
        P(),
        P(None, "dom"),
        P("dom"),
        P(None, "dom"),
        P(None, "dom"),
        P(None, "dom"),
        P(None, "dom"),
        P(None, "dom"),
        P(None, "dom"),
    )
    return jax.shard_map(
        local, mesh=mesh, in_specs=placed, out_specs=(P(None, "dom"), P("dom")), check_vma=False
    )
```

```python
import jax
import jax.numpy as jnp
from jax import lax
from jax.experimental import pallas as pl
from jax.experimental.pallas import tpu as pltpu
from jax.sharding import PartitionSpec as P

REACH = 4
SWEEPS = 2
LANES = 128
WIDE = 2 * LANES
OWN = 32
EDGE = 16
NOWHERE = 63

relaxation = 0.7
scale_down = 16.0
pad_code = 16368

f32 = jnp.float32
bf16 = jnp.bfloat16
i32 = jnp.int32


def neighbour_offsets():
    return [step + 1 for step in range(REACH)] + [-(step + 1) for step in range(REACH)]


def exchange(packed):
    return lax.all_to_all(packed, "dom", 0, 0, tiled=True)


def pack(place, sign, rows, pack_ref, out_ref):
    count = out_ref.shape[0]
    pack_ref[...] = jnp.zeros_like(pack_ref)
    for slot, offset in enumerate(neighbour_offsets()):
        target = place + sign * offset
        at = jnp.where((target >= 0) & (target < count), target, count)
        for number, row in enumerate(rows[slot]):
            pack_ref[at, number : number + 1, :] = row
    out_ref[...] = pack_ref[:count]


def landed(place, sign, got_ref, number):
    count = got_ref.shape[0]
    rows = []
    for offset in neighbour_offsets():
        source = place - sign * offset
        row = got_ref[jnp.clip(source, 0, count - 1), number : number + 1, :]
        there = jnp.broadcast_to((source >= 0) & (source < count), row.shape)
        rows.append(jnp.where(there, row, 0.0))
    return rows


def landed_wide(place, sign, got_ref, part):
    halves = [
        jnp.concatenate(landed(place, sign, got_ref, 2 * part + half), 0) for half in range(2)
    ]
    return jnp.concatenate(halves, 1)


def match16(row, count):
    width = row.shape[1]
    wide = jnp.broadcast_to(row.astype(f32), (16, width)).astype(bf16)
    numbers = lax.broadcasted_iota(i32, (count, width), 0).astype(f32).astype(bf16)
    numbers = numbers.reshape(count // 16, 16, width)
    return numbers == wide[None]


def one_hot(row, count):
    mask = match16(row, count)
    ones = jnp.ones(mask.shape, bf16)
    return jnp.where(mask, ones, jnp.zeros_like(ones)).reshape(count, row.shape[1])


def spread16(mask, row):
    wide = jnp.broadcast_to(row, (16, row.shape[1])).astype(bf16)[None]
    out = jnp.where(mask, jnp.broadcast_to(wide, mask.shape), jnp.zeros(mask.shape, bf16))
    return out.reshape(mask.shape[0] * 16, row.shape[1])


def pieces(x):
    high = x.astype(bf16)
    return high, (x - high.astype(f32)).astype(bf16)


def build_hot(column_ref, hot_ref):
    def body(block, carry):
        start = pl.multiple_of(block * 8, 8)
        for j in range(8):
            at = pl.multiple_of((start + j) * WIDE, WIDE)
            hot_ref[pl.ds(at, WIDE), :] = one_hot(column_ref[pl.ds(start + j, 1), :], WIDE)
        return carry

    lax.fori_loop(0, column_ref.shape[0] // 8, body, 0)


def hot_of(hot_ref, number):
    return hot_ref[pl.ds(pl.multiple_of(number * WIDE, WIDE), WIDE), :]


def two_pieces(table):
    return jnp.concatenate(pieces(table), 0)


def gather(table, rows, parts, row_ref, hot_ref, sums_ref):
    count, width = row_ref.shape
    numbers = lax.broadcasted_iota(i32, (rows, width), 0)
    half_table = parts * rows

    def body(block, carry):
        start = pl.multiple_of(block * 8, 8)
        for j in range(8):
            found = jnp.dot(table, hot_of(hot_ref, start + j), preferred_element_type=f32)
            found = found[:half_table] + found[half_table:]
            mask = numbers == jnp.broadcast_to(row_ref[pl.ds(start + j, 1), :], numbers.shape)
            for part in range(parts):
                kept = jnp.where(mask, found[part * rows : (part + 1) * rows], 0.0)
                kept = jnp.sum(kept.reshape(rows // 8, 8, width), 0)
                for half in range(width // LANES):
                    sums_ref[half, pl.ds(part * count * 8 + start * 8 + j * 8, 8), :] = kept[
                        :, half * LANES : (half + 1) * LANES
                    ]
        return carry

    lax.fori_loop(0, count // 8, body, 0)


def gathered(sums_ref, count, part):
    totals = []
    for half in range(sums_ref.shape[0]):
        rows = [sums_ref[half, pl.ds(part * count * 8 + s, count, stride=8), :] for s in range(8)]
        while len(rows) > 1:
            rows = [a + b for a, b in zip(rows[::2], rows[1::2])]
        totals.append(rows[0])
    return jnp.concatenate(totals, 1)


def halves(x):
    return [x[:, :LANES], x[:, LANES:]]


def scatter(high_ref, low_ref, rows, row_ref, hot_ref, sum_ref):
    count = row_ref.shape[0]
    sum_ref[...] = jnp.zeros_like(sum_ref)

    def body(block, carry):
        start = pl.multiple_of(block * 8, 8)
        masks = [match16(row_ref[pl.ds(start + j, 1), :], rows) for j in range(8)]
        hot = jnp.concatenate([hot_of(hot_ref, start + j) for j in range(8)], 1)
        stacked = [
            jnp.concatenate(
                [
                    spread16(mask, piece_ref[pl.ds(part * count + start + j, 1), :])
                    for j, mask in enumerate(masks)
                ],
                1,
            )
            for piece_ref in (high_ref, low_ref)
            for part in range(3)
        ]
        sum_ref[...] += lax.dot_general(
            jnp.concatenate(stacked, 0), hot, (((1,), (1,)), ((), ())), preferred_element_type=f32
        )
        return carry

    lax.fori_loop(0, count // 8, body, 0)


def split32(x):
    high = x.astype(bf16).astype(f32)
    return high, x - high


def add_pieces(sums):
    half = sums.shape[0] // 2
    return sums[:half] + sums[half:]


def scatter_few(values, rows, row_ref, hot_ref, scratch):
    high_ref, low_ref, sum_ref = scratch
    for part in range(3):
        high_ref[part * 8 : part * 8 + 8, :], low_ref[part * 8 : part * 8 + 8, :] = split32(
            values[part]
        )
    scatter(high_ref, low_ref, rows, row_ref, hot_ref, sum_ref)
    return add_pieces(sum_ref[...])


def few(rows):
    return [((24, WIDE), f32)] * 2 + [((6 * rows, WIDE), f32)]


def spread_hanging(held, weight, rows, row_ref, hot_ref, scratch):
    both = jnp.concatenate([held, held], 1)
    values = [weight * both[part : part + 1] for part in range(3)]
    return scatter_few(values, rows, row_ref, hot_ref, scratch)


def sum_masters(table, rows, weight, row_ref, hot_ref, sums_ref):
    gather(table, rows, 3, row_ref, hot_ref, sums_ref)
    totals = []
    for part in range(3):
        left, right = halves(weight * gathered(sums_ref, 8, part))
        totals.append(jnp.sum(left + right, 0, keepdims=True))
    return totals


def fill_table(x_ref, out_ref):
    count = x_ref.shape[1] // WIDE
    for part in range(3):
        out_ref[part * OWN + count : (part + 1) * OWN, :] = jnp.zeros((OWN - count, WIDE), f32)
    for row in range(count):
        block = x_ref[:, row * WIDE : (row + 1) * WIDE]
        for part in range(3):
            out_ref[part * OWN + row : part * OWN + row + 1, :] = block[part : part + 1]


def export_rows(table, parts, row_ref, hot_ref, sums_ref):
    gather(table, OWN, parts, row_ref, hot_ref, sums_ref)
    rows = [[] for _ in range(2 * REACH)]
    for part in range(parts):
        for tile in halves(gathered(sums_ref, 8, part)):
            for slot in range(2 * REACH):
                rows[slot].append(tile[slot : slot + 1])
    return rows


def copy_in(pairs, sems):
    copies = [
        pltpu.make_async_copy(source, target, sems.at[number])
        for number, (source, target) in enumerate(pairs)
    ]
    for copy in copies:
        copy.start()
    for copy in copies:
        copy.wait()


def first_export(
    place_ref, adjoint_hbm, primal_hbm, list_hbm, tab_a, tab_p, row_ref, hot_ref,
    out_ref, pack_ref, adjoint_ref, primal_ref, list_ref, column_ref, sums_ref, sems,
):
    copy_in(
        [(adjoint_hbm, adjoint_ref), (primal_hbm, primal_ref), (list_hbm, list_ref)], sems
    )
    owned = adjoint_ref.shape[1]
    fill_table(adjoint_ref, tab_a)
    fill_table(primal_ref, tab_p)
    codes = list_ref[...]
    node = lax.rem(17 * codes + lax.broadcasted_iota(i32, codes.shape, 1), owned)
    row_ref[...] = node >> 8
    column_ref[...] = node & 255
    build_hot(column_ref, hot_ref)
    table = two_pieces(jnp.concatenate([tab_a[...], tab_p[...]], 0))
    rows = export_rows(table, 6, row_ref, hot_ref, sums_ref)
    pack(place_ref[0], 1, rows, pack_ref, out_ref)


def setup(
    connect_hbm, node_hbm, master_hbm, weight_hbm, source_hbm, inverse_hbm,
    own_row, edge_row, hot_ref, master_own, master_edge, master_hot, weight_out,
    tab_source, tab_inverse,
    connect_ref, node_ref, master_ref, weight_ref, source_ref, inverse_ref, column_ref,
    master_column, sums_ref, sems,
):
    copy_in(
        [
            (connect_hbm, connect_ref),
            (node_hbm, node_ref),
            (master_hbm, master_ref),
            (weight_hbm, weight_ref),
            (source_hbm, source_ref),
            (inverse_hbm, inverse_ref),
        ],
        sems,
    )
    owned = source_ref.shape[1]
    extent = owned + 2 * REACH * WIDE
    fill_table(source_ref, tab_source)
    fill_table(inverse_ref, tab_inverse)
    codes = master_ref[...]
    master = lax.rem(17 * codes + 8 * lax.broadcasted_iota(i32, codes.shape, 1), extent)
    count = codes.shape[0] // 2
    master = jnp.concatenate([master[:count], master[count:]], 1)
    weight = weight_ref[...]
    weight_out[...] = jnp.concatenate([weight[:count], weight[count:]], 1)
    last = owned // WIDE
    row = master >> 8
    master_own[...] = jnp.where(row < last, row, NOWHERE)
    master_edge[...] = jnp.where(row < last, NOWHERE, row - last)
    master_column[...] = master & 255
    build_hot(master_column, master_hot)

    codes = node_ref[...]
    node = jnp.where(codes == pad_code, extent, lax.rem(13 * codes, owned))
    slot = (lax.broadcasted_iota(i32, codes.shape, 1) + 1).astype(f32)
    table = lax.dot_general(
        spread16(match16(node >> 8, OWN), slot),
        one_hot(node & 255, WIDE),
        (((1,), (1,)), ((), ())),
        preferred_element_type=f32,
    ).astype(bf16)

    codes = connect_ref[...]
    cells = lax.broadcasted_iota(i32, codes.shape, 1)
    slots = lax.rem(27 * cells + 17 * codes, extent)
    own_row[...] = slots >> 8
    column_ref[...] = slots & 255
    numbers = lax.broadcasted_iota(i32, (OWN, WIDE), 0)

    def body(block, carry):
        start = pl.multiple_of(block * 8, 8)
        for j in range(8):
            hot = one_hot(column_ref[pl.ds(start + j, 1), :], WIDE)
            found = jnp.dot(table, hot, preferred_element_type=f32)
            mask = numbers == jnp.broadcast_to(own_row[pl.ds(start + j, 1), :], numbers.shape)
            kept = jnp.sum(jnp.where(mask, found, 0.0).reshape(OWN // 8, 8, WIDE), 0)
            for half in range(2):
                sums_ref[half, pl.ds(start * 8 + j * 8, 8), :] = halves(kept)[half]
        return carry

    lax.fori_loop(0, codes.shape[0] // 8, body, 0)
    slot = gathered(sums_ref, codes.shape[0], 0).astype(i32)
    row = slots >> 8
    hanging = slot > 0
    outside = row >= last
    own_row[...] = jnp.where(hanging | outside, NOWHERE, row)
    edge_row[...] = jnp.where(hanging, 2 * REACH, jnp.where(outside, row - last, NOWHERE))
    column_ref[...] = jnp.where(hanging, slot - 1, slots & 255)
    build_hot(column_ref, hot_ref)


def own_gather(
    tab_ref, row_ref, hot_ref, master_row, master_hot, weight_ref, cells_ref, hang_ref, sums_ref
):
    table = two_pieces(tab_ref[...])
    found = sum_masters(table, OWN, weight_ref[...], master_row, master_hot, sums_ref)
    for part in range(3):
        hang_ref[part : part + 1, :] = found[part]
    gather(table, OWN, 3, row_ref, hot_ref, sums_ref)
    count = row_ref.shape[0]
    for part in range(3):
        cells_ref[part * count : (part + 1) * count, :] = gathered(sums_ref, count, part)


def edge_gather(
    place, got_ref, first, cells_ref, hang_ref, row_ref, hot_ref, master_row, master_hot,
    weight_ref, edge_ref, sums_ref, out_ref,
):
    slots = 2 * REACH
    edge_ref[...] = jnp.zeros_like(edge_ref)
    for part in range(3):
        edge_ref[part * EDGE : part * EDGE + slots, :] = landed_wide(
            place, 1, got_ref, first + part
        )
    found = sum_masters(
        two_pieces(edge_ref[...]), EDGE, weight_ref[...], master_row, master_hot, sums_ref
    )
    for part in range(3):
        at = part * EDGE + slots
        edge_ref[at : at + 1, :LANES] = found[part] + hang_ref[part : part + 1, :]
    gather(two_pieces(edge_ref[...]), EDGE, 3, row_ref, hot_ref, sums_ref)
    count = row_ref.shape[0]
    for part in range(3):
        rows = slice(part * count, (part + 1) * count)
        out_ref[rows, :] = cells_ref[rows, :] + gathered(sums_ref, count, part)


def edge_product(
    place_ref, got_ref, cells_ref, hang_ref, row_ref, hot_ref, master_row, master_hot,
    weight_ref, modulus_ref, stiffness_ref, out_ref,
    image_ref, held_ref, pack_ref, edge_ref, sums_ref, full_ref, low_ref, sum_ref, *scratch,
):
    place = place_ref[0]
    edge_gather(
        place, got_ref, 0, cells_ref, hang_ref, row_ref, hot_ref,
        master_row, master_hot, weight_ref, edge_ref, sums_ref, full_ref,
    )
    image = modulus_ref[...] * lax.dot_general(
        stiffness_ref[...],
        full_ref[...],
        (((0,), (0,)), ((), ())),
        precision=lax.Precision.HIGHEST,
        preferred_element_type=f32,
    )
    image_ref[...] = image
    full_ref[...], low_ref[...] = split32(image)
    scatter(full_ref, low_ref, EDGE, row_ref, hot_ref, sum_ref)
    sums = add_pieces(sum_ref[...])
    slots = 2 * REACH
    held = jnp.concatenate(
        [sums[part * EDGE + slots : part * EDGE + slots + 1, :LANES] for part in range(3)], 0
    )
    held_ref[...] = held
    sums += spread_hanging(held, weight_ref[...], EDGE, master_row, master_hot, scratch)
    rows = [
        [
            sums[part * EDGE + slot : part * EDGE + slot + 1, half * LANES : (half + 1) * LANES]
            for part in range(3)
            for half in range(2)
        ]
        for slot in range(slots)
    ]
    pack(place, -1, rows, pack_ref, out_ref)


def own_sums(
    image_ref, held_ref, row_ref, hot_ref, master_row, master_hot, weight_ref,
    tab_ref, source_ref, inverse_ref, out_ref, high_ref, low_ref, sum_ref, *scratch,
):
    high_ref[...], low_ref[...] = split32(image_ref[...])
    scatter(high_ref, low_ref, OWN, row_ref, hot_ref, sum_ref)
    applied = add_pieces(sum_ref[...]) + spread_hanging(
        held_ref[...], weight_ref[...], OWN, master_row, master_hot, scratch
    )
    out_ref[...] = tab_ref[...] + relaxation * inverse_ref[...] * (source_ref[...] - applied)


def update(
    place_ref, got_ref, row_ref, hot_ref, partial_ref, inverse_ref,
    out_ref, tab_ref, *rest,
):
    *final_ref, pack_ref, sums_ref = rest[:-3]
    place = place_ref[0]
    values = [landed_wide(place, -1, got_ref, part) for part in range(3)]
    returned = scatter_few(values, OWN, row_ref, hot_ref, rest[-3:])
    tab_ref[...] = partial_ref[...] - relaxation * inverse_ref[...] * returned
    rows = export_rows(two_pieces(tab_ref[...]), 3, row_ref, hot_ref, sums_ref)
    pack(place, 1, rows, pack_ref, out_ref)
    if final_ref:
        final_ref = final_ref[0]
        for row in range(final_ref.shape[1] // WIDE):
            for part in range(3):
                final_ref[part : part + 1, row * WIDE : (row + 1) * WIDE] = tab_ref[
                    part * OWN + row : part * OWN + row + 1, :
                ]


def primal_product(
    place_ref, got_ref, cells_ref, hang_ref, row_ref, hot_ref, master_row,
    master_hot, weight_ref, modulus_ref, stiffness_ref, out_ref, edge_ref, sums_ref, full_ref,
):
    edge_gather(
        place_ref[0], got_ref, 3, cells_ref, hang_ref, row_ref, hot_ref,
        master_row, master_hot, weight_ref, edge_ref, sums_ref, full_ref,
    )
    out_ref[...] = modulus_ref[...] * jnp.dot(
        stiffness_ref[...],
        full_ref[...],
        precision=lax.Precision.HIGHEST,
        preferred_element_type=f32,
    )


def fluxes(
    place_ref, got_ref, cells_ref, hang_ref, row_ref, hot_ref, master_row,
    master_hot, weight_ref, ku_ref, load_ref, sub_cell, sub_face, out_ref,
    term_ref, pack_ref, edge_ref, sums_ref, full_ref, face_hot, few_ref,
):
    place = place_ref[0]
    edge_gather(
        place, got_ref, 0, cells_ref, hang_ref, row_ref, hot_ref,
        master_row, master_hot, weight_ref, edge_ref, sums_ref, full_ref,
    )
    cells = full_ref[...]
    ku = ku_ref[...]
    term_ref[...] = jnp.sum(cells * (load_ref[...] - ku), 0, keepdims=True)
    face = lax.broadcasted_iota(i32, (8, ku.shape[0]), 0)
    node = lax.broadcasted_iota(i32, (8, ku.shape[0]), 1) & 63
    index = jnp.where(face < 2, node >> 4, jnp.where(face < 4, (node >> 2) & 3, node & 3))
    member = jnp.where((face < 6) & (index == 3 * (face & 1)), 1.0, 0.0).astype(f32)
    flux = jnp.dot(
        member, ku * cells, precision=lax.Precision.HIGHEST, preferred_element_type=f32
    )
    build_hot(sub_cell, face_hot)
    gather(two_pieces(flux), 8, 1, sub_face, face_hot, few_ref)
    found = gathered(few_ref, 8, 0)
    rows = [[found[slot : slot + 1]] for slot in range(2 * REACH)]
    pack(place, 1, rows, pack_ref, out_ref)


def collect(place_ref, got_ref, owner_ref, term_ref, out_ref):
    count = term_ref.shape[1]
    got = jnp.concatenate(landed(place_ref[0], 1, got_ref, 0), 1)
    hot = jnp.concatenate(
        [one_hot(owner_ref[slot : slot + 1, :], count) for slot in range(2 * REACH)], 1
    )
    values = jnp.concatenate(
        [jnp.broadcast_to(x, (16, got.shape[1])).astype(bf16) for x in split32(got)], 0
    )
    sums = lax.dot_general(values, hot, (((1,), (1,)), ((), ())), preferred_element_type=f32)
    face_term = sums[0:1] + sums[16:17]
    out_ref[...] = (jnp.abs(term_ref[...]) + jnp.abs(face_term)) / scale_down


SMALL = pl.BlockSpec(memory_space=pltpu.SMEM)
FAST = pl.BlockSpec(memory_space=pltpu.VMEM)
FAR = pl.BlockSpec(memory_space=pl.ANY)


def away(*arrays):
    return [pltpu.with_memory_space_constraint(x, pltpu.HBM) for x in arrays]


def call(kernel, outs, scratch=(), specs=None, sems=0):
    scratch = [pltpu.VMEM(shape, kind) for shape, kind in scratch]
    if sems:
        scratch.append(pltpu.SemaphoreType.DMA((sems,)))

    def run(*args):
        return pl.pallas_call(
            kernel,
            out_shape=[jax.ShapeDtypeStruct(shape, kind) for shape, kind in outs],
            in_specs=specs or [SMALL] + [FAST] * (len(args) - 1),
            scratch_shapes=scratch,
            compiler_params=pltpu.CompilerParams(vmem_limit_bytes=24 * 1024 * 1024),
        )(*args)

    return run


def local(
    adjoint_start,
    adjoint_source,
    inverse_diagonal,
    primal_field,
    cell_load,
    modulus,
    stiffness,
    connectivity,
    hang_node,
    hang_master,
    hang_weight,
    ghost_lists,
    subface_cell,
    subface_face,
    subface_owner,
):
    slots = 2 * REACH
    local_values, cell_count = cell_load.shape
    nodes = connectivity.shape[0]
    moduli = modulus.reshape(1, cell_count)
    place = lax.axis_index("dom").reshape(1).astype(i32)
    table = ((3 * OWN, WIDE), f32)
    index = ((nodes, cell_count), i32)
    cells_shape = ((local_values, cell_count), f32)
    hang_shape = ((3, hang_node.shape[0]), f32)
    master_shape = ((8, WIDE), i32)

    count = lax.axis_size("dom")

    def packed(height):
        return [((count, height, LANES), f32)]

    def room(height):
        return ((count + 1, height, LANES), f32)

    few_sums = ((2, 3 * 64, LANES), f32)
    many_sums = ((2, local_values * 8, LANES), f32)
    few_hot = ((8 * WIDE, WIDE), bf16)
    edge = [((3 * EDGE, WIDE), f32), many_sums, cells_shape]
    tab, tab_primal, list_row, list_hot, blocks = call(
        first_export,
        [table, table, (ghost_lists.shape, i32), few_hot] + packed(16),
        [
            room(16),
            (adjoint_start.shape, f32),
            (primal_field.shape, f32),
            (ghost_lists.shape, i32),
            (ghost_lists.shape, i32),
            ((2, 6 * 64, LANES), f32),
        ],
        [SMALL, FAR, FAR, FAR],
        sems=3,
    )(place, *away(adjoint_start, primal_field, ghost_lists))
    ghosts = first_ghosts = exchange(blocks)
    far = (
        connectivity, hang_node.reshape(1, -1), hang_master, hang_weight, adjoint_source,
        inverse_diagonal,
    )
    (
        own_row, edge_row, hot, master_own, master_edge, master_hot, weight, source, inverse,
    ) = call(
        setup,
        [index, index, ((nodes * WIDE, cell_count), bf16), master_shape, master_shape, few_hot]
        + [((8, WIDE), f32), table, table],
        [(x.shape, x.dtype) for x in far]
        + [index, master_shape, ((2, nodes * 8, LANES), f32)],
        [FAR] * 6,
        sems=6,
    )(*away(*far))

    def gather_own(values):
        return call(own_gather, [cells_shape, hang_shape], [many_sums], specs=[FAST] * 6)(
            values, own_row, hot, master_own, master_hot, weight
        )

    on_edge = (edge_row, hot, master_edge, master_hot, weight)
    for sweep in range(SWEEPS):
        cells, hang = gather_own(tab)
        if sweep == 1:
            (ku,) = call(primal_product, [cells_shape], edge)(
                place, first_ghosts, *primal_cells, *on_edge, moduli, stiffness
            )
            cells, ku = lax.optimization_barrier((cells, ku))
        blocks, image, held = call(
            edge_product,
            packed(8) + [cells_shape, hang_shape],
            [room(8)] + edge + [cells_shape, ((6 * EDGE, WIDE), f32)] + few(EDGE),
        )(place, ghosts, cells, hang, *on_edge, moduli, stiffness)
        returned = exchange(blocks)
        (partial,) = call(
            own_sums,
            [table],
            [cells_shape, cells_shape, ((6 * OWN, WIDE), f32)] + few(OWN),
            specs=[FAST] * 10,
        )(image, held, own_row, hot, master_own, master_hot, weight, tab, source, inverse)
        if sweep == 0:
            tab_primal, image = lax.optimization_barrier((tab_primal, image))
            primal_cells = gather_own(tab_primal)
            partial, *primal_cells = lax.optimization_barrier((partial, *primal_cells))
        last = sweep == SWEEPS - 1
        blocks, tab, *final = call(
            update,
            packed(8) + [table] + ([(adjoint_start.shape, f32)] if last else []),
            [room(8), few_sums] + few(OWN),
        )(place, returned, list_row, list_hot, partial, inverse)
        ghosts = exchange(blocks)
    cells, hang = gather_own(tab)
    blocks, term = call(
        fluxes,
        packed(1) + [((1, cell_count), f32)],
        [room(1)]
        + edge
        + [((8 * WIDE, subface_cell.shape[1]), bf16), ((1, 64, LANES), f32)],
    )(place, ghosts, cells, hang, *on_edge, ku, cell_load, subface_cell, subface_face)
    received = exchange(blocks)
    (indicator,) = call(collect, [((1, cell_count), f32)])(
        place, received, subface_owner, term
    )
    return (final[0], indicator.reshape(cell_count))


def solution(mesh):
    placed = (
        P(None, "dom"),
        P(None, "dom"),
        P(None, "dom"),
        P(None, "dom"),
        P(None, "dom"),
        P("dom"),
        P(),
        P(None, "dom"),
        P("dom"),
        P(None, "dom"),
        P(None, "dom"),
        P(None, "dom"),
        P(None, "dom"),
        P(None, "dom"),
        P(None, "dom"),
    )
    return jax.shard_map(
        local, mesh=mesh, in_specs=placed, out_specs=(P(None, "dom"), P("dom")), check_vma=False
    )
```

```python
import functools

import jax
import jax.numpy as jnp
from jax import lax
from jax.experimental import pallas as pl
from jax.experimental.pallas import tpu as pltpu
from jax.sharding import PartitionSpec as P

REACH = 4
SWEEPS = 2
LANES = 128
WIDE = 2 * LANES
OWN = 32
EDGE = 16
TALL = 24
NOWHERE = 126

relaxation = 0.7
scale_down = 16.0
pad_code = 16368

f32 = jnp.float32
bf16 = jnp.bfloat16
i32 = jnp.int32


def neighbour_offsets():
    return [step + 1 for step in range(REACH)] + [-(step + 1) for step in range(REACH)]


def exchange(packed):
    return lax.all_to_all(packed, "dom", 0, 0, tiled=True)


def pack(place, sign, rows, pack_ref, out_ref):
    count = out_ref.shape[0]
    pack_ref[...] = jnp.zeros_like(pack_ref)
    for slot, offset in enumerate(neighbour_offsets()):
        target = place + sign * offset
        at = jnp.where((target >= 0) & (target < count), target, count)
        for number, row in enumerate(rows[slot]):
            pack_ref[at, number : number + 1, :] = row
    out_ref[...] = pack_ref[:count]


def landed(place, sign, got_ref, number):
    count = got_ref.shape[0]
    rows = []
    for offset in neighbour_offsets():
        source = place - sign * offset
        row = got_ref[jnp.clip(source, 0, count - 1), number : number + 1, :]
        there = jnp.broadcast_to((source >= 0) & (source < count), row.shape)
        rows.append(jnp.where(there, row, 0.0))
    return rows


def landed_wide(place, sign, got_ref, part):
    halves = [
        jnp.concatenate(landed(place, sign, got_ref, 2 * part + half), 0) for half in range(2)
    ]
    return jnp.concatenate(halves, 1)


def match16(row, count):
    width = row.shape[1]
    wide = jnp.broadcast_to(row.astype(f32), (16, width)).astype(bf16)
    numbers = lax.broadcasted_iota(i32, (count, width), 0).astype(f32).astype(bf16)
    numbers = numbers.reshape(count // 16, 16, width)
    return numbers == wide[None]


def one_hot(row, count):
    mask = match16(row, count)
    ones = jnp.ones(mask.shape, bf16)
    return jnp.where(mask, ones, jnp.zeros_like(ones)).reshape(count, row.shape[1])


def spread16(mask, row):
    wide = jnp.broadcast_to(row, (16, row.shape[1])).astype(bf16)[None]
    out = jnp.where(mask, jnp.broadcast_to(wide, mask.shape), jnp.zeros(mask.shape, bf16))
    return out.reshape(mask.shape[0] * 16, row.shape[1])


def pieces(x):
    high = x.astype(bf16)
    return high, (x - high.astype(f32)).astype(bf16)


def gather(table, rows, parts, row_ref, column_ref, sums_ref, wide=False):
    count, width = row_ref.shape
    step = min(count, 32)
    numbers = lax.broadcasted_iota(i32, (rows, width), 0)

    def body(block, carry):
        start = pl.multiple_of(block * step, step)
        for j in range(step):
            hot = one_hot(column_ref[pl.ds(start + j, 1), :], WIDE if wide else LANES)
            if not wide:
                hot = jnp.concatenate([hot, hot], 0)
            found = jnp.dot(table, hot, preferred_element_type=f32)
            if wide:
                found = found[: parts * rows] + found[parts * rows :]
            mask = numbers == jnp.broadcast_to(row_ref[pl.ds(start + j, 1), :], numbers.shape)
            for part in range(parts):
                kept = jnp.where(mask, found[part * rows : (part + 1) * rows], 0.0)
                kept = jnp.sum(kept.reshape(rows // 8, 8, width), 0)
                for half in range(width // LANES):
                    sums_ref[half, pl.ds(part * count * 8 + start * 8 + j * 8, 8), :] = kept[
                        :, half * LANES : (half + 1) * LANES
                    ]
        return carry

    if count == step:
        body(0, 0)
    else:
        lax.fori_loop(0, count // step, body, 0)


def gathered(sums_ref, count, part):
    totals = []
    for half in range(sums_ref.shape[0]):
        rows = [sums_ref[half, pl.ds(part * count * 8 + s, count, stride=8), :] for s in range(8)]
        while len(rows) > 1:
            rows = [a + b for a, b in zip(rows[::2], rows[1::2])]
        totals.append(rows[0])
    return jnp.concatenate(totals, 1)


def halves(x):
    return [x[:, :LANES], x[:, LANES:]]


def rows_and_columns(where, lane):
    return where >> 1, (where & 1) * LANES + lane


def scatter(high_ref, low_ref, rows, row_ref, column_ref, sum_ref):
    count = row_ref.shape[0]
    step = min(count, 16)

    def product(start):
        masks = [match16(row_ref[pl.ds(start + j, 1), :], rows) for j in range(8)]
        hot = jnp.concatenate(
            [one_hot(column_ref[pl.ds(start + j, 1), :], WIDE) for j in range(8)], 1
        )
        stacked = [
            jnp.concatenate(
                [
                    spread16(mask, piece_ref[pl.ds(part * count + start + j, 1), :])
                    for j, mask in enumerate(masks)
                ],
                1,
            )
            for piece_ref in (high_ref, low_ref)
            for part in range(3)
        ]
        return lax.dot_general(
            jnp.concatenate(stacked, 0), hot, (((1,), (1,)), ((), ())), preferred_element_type=f32
        )

    if count == 8:
        sum_ref[...] = product(0)
        return
    sum_ref[...] = jnp.zeros_like(sum_ref)

    def body(block, carry):
        start = pl.multiple_of(block * step, step)
        total = product(start)
        for first in range(8, step, 8):
            total += product(start + first)
        sum_ref[...] += total
        return carry

    lax.fori_loop(0, count // step, body, 0)


def split32(x):
    high = x.astype(bf16).astype(f32)
    return high, x - high


def add_pieces(sums):
    half = sums.shape[0] // 2
    return sums[:half] + sums[half:]


def scatter_few(values, rows, row_ref, column_ref, scratch):
    high_ref, low_ref, sum_ref = scratch
    for part in range(3):
        high_ref[part * 8 : part * 8 + 8, :], low_ref[part * 8 : part * 8 + 8, :] = split32(
            values[part]
        )
    scatter(high_ref, low_ref, rows, row_ref, column_ref, sum_ref)
    return add_pieces(sum_ref[...])


def few(rows):
    return [((24, WIDE), f32)] * 2 + [((6 * rows, WIDE), f32)]


def spread_hanging(held, weight, rows, row_ref, column_ref, scratch):
    both = jnp.concatenate([held, held], 1)
    values = [weight * both[part : part + 1] for part in range(3)]
    return scatter_few(values, rows, row_ref, column_ref, scratch)


def sum_masters(table, tall, weight, where_ref, lane_ref, sums_ref):
    gather(table, tall, 3, where_ref, lane_ref, sums_ref)
    totals = []
    for part in range(3):
        left, right = halves(weight * gathered(sums_ref, 8, part))
        totals.append(jnp.sum(left + right, 0, keepdims=True))
    return totals


def fill_table(x_ref, out_ref):
    count = x_ref.shape[1] // WIDE
    for part in range(3):
        out_ref[part * OWN + count : (part + 1) * OWN, :] = jnp.zeros((OWN - count, WIDE), f32)
    for row in range(count):
        block = x_ref[:, row * WIDE : (row + 1) * WIDE]
        for part in range(3):
            out_ref[part * OWN + row : part * OWN + row + 1, :] = block[part : part + 1]


def tall_table(tab_refs, half_rows, tall_ref):
    tall = up8(half_rows)
    tall_ref[...] = jnp.zeros_like(tall_ref)
    for number, tab_ref in enumerate(tab_refs):
        for part in range(3):
            for half_row in range(half_rows):
                row, half = part * OWN + half_row // 2, half_row % 2
                at = (3 * number + part) * tall + half_row
                tall_ref[at : at + 1, :] = tab_ref[
                    row : row + 1, half * LANES : (half + 1) * LANES
                ]
    return jnp.concatenate(pieces(tall_ref[...]), 1)


def up8(count):
    return -(-count // 8) * 8


def export_rows(table, parts, row_ref, column_ref, sums_ref):
    table = jnp.concatenate(pieces(table), 0)
    gather(table, OWN, parts, row_ref, column_ref, sums_ref, wide=True)
    rows = [[] for _ in range(2 * REACH)]
    for part in range(parts):
        for tile in halves(gathered(sums_ref, 8, part)):
            for slot in range(2 * REACH):
                rows[slot].append(tile[slot : slot + 1])
    return rows


def copy_in(pairs, sems):
    copies = [
        pltpu.make_async_copy(source, target, sems.at[number])
        for number, (source, target) in enumerate(pairs)
    ]
    for copy in copies:
        copy.start()
    for copy in copies:
        copy.wait()


def first_export(
    place_ref, adjoint_hbm, primal_hbm, list_hbm, tab_a, tab_p, row_ref, column_ref,
    out_ref, pack_ref, adjoint_ref, primal_ref, list_ref, sums_ref, sems,
):
    copy_in(
        [(adjoint_hbm, adjoint_ref), (primal_hbm, primal_ref), (list_hbm, list_ref)], sems
    )
    owned = adjoint_ref.shape[1]
    fill_table(adjoint_ref, tab_a)
    fill_table(primal_ref, tab_p)
    codes = list_ref[...]
    node = lax.rem(17 * codes + lax.broadcasted_iota(i32, codes.shape, 1), owned)
    row_ref[...] = node >> 8
    column_ref[...] = node & 255
    table = jnp.concatenate([tab_a[...], tab_p[...]], 0)
    rows = export_rows(table, 6, row_ref, column_ref, sums_ref)
    pack(place_ref[0], 1, rows, pack_ref, out_ref)


def setup(
    connect_hbm, node_hbm, master_hbm, weight_hbm, source_hbm, inverse_hbm, modulus_hbm,
    own_where, own_row, edge_where, edge_row, lane_ref, column_ref, edge_column, master_own, master_own_row,
    master_edge, master_edge_row, master_lane, master_column, weight_out, tab_source, tab_inverse,
    modulus_out,
    connect_ref, node_ref, master_ref, weight_ref, source_ref, inverse_ref, map_ref, tall_ref, sums_ref,
    sems,
):
    copy_in(
        [
            (connect_hbm, connect_ref),
            (node_hbm, node_ref),
            (master_hbm, master_ref),
            (weight_hbm, weight_ref),
            (source_hbm, source_ref),
            (inverse_hbm, inverse_ref),
            (modulus_hbm, modulus_out),
        ],
        sems,
    )
    owned = source_ref.shape[1]
    extent = owned + 2 * REACH * WIDE
    fill_table(source_ref, tab_source)
    fill_table(inverse_ref, tab_inverse)
    codes = master_ref[...]
    master = lax.rem(17 * codes + 8 * lax.broadcasted_iota(i32, codes.shape, 1), extent)
    count = codes.shape[0] // 2
    master = jnp.concatenate([master[:count], master[count:]], 1)
    weight = weight_ref[...]
    weight_out[...] = jnp.concatenate([weight[:count], weight[count:]], 1)
    last = owned // LANES
    where = master >> 7
    master_own[...] = jnp.where(where < last, where, NOWHERE)
    master_edge[...] = jnp.where(where < last, NOWHERE, where - last)
    master_lane[...] = master & 127
    row = master >> 8
    master_own_row[...] = jnp.where(where < last, row, NOWHERE)
    master_edge_row[...] = jnp.where(where < last, NOWHERE, row - last // 2)
    master_column[...] = master & 255

    codes = node_ref[...]
    node = jnp.where(codes == pad_code, extent, lax.rem(13 * codes, owned))
    slot = (lax.broadcasted_iota(i32, codes.shape, 1) + 1).astype(f32)
    map_ref[...] = lax.dot_general(
        spread16(match16(node >> 8, OWN), slot),
        one_hot(node & 255, WIDE),
        (((1,), (1,)), ((), ())),
        preferred_element_type=f32,
    )

    codes = connect_ref[...]
    cells = lax.broadcasted_iota(i32, codes.shape, 1)
    slots = lax.rem(27 * cells + 17 * codes, extent)
    own_where[...] = slots >> 7
    lane_ref[...] = slots & 127
    tall_ref[...] = jnp.zeros_like(tall_ref)
    for half_row in range(last):
        row, half = half_row // 2, half_row % 2
        tall_ref[half_row : half_row + 1, :] = map_ref[
            row : row + 1, half * LANES : (half + 1) * LANES
        ]
    table = jnp.concatenate(pieces(tall_ref[...]), 1)
    gather(table, tall_ref.shape[0], 1, own_where, lane_ref, sums_ref)
    slot = gathered(sums_ref, codes.shape[0], 0).astype(i32)
    where = slots >> 7
    hanging = slot > 0
    outside = where >= last
    lane = jnp.where(hanging, slot - 1, slots & 127)
    lane_ref[...] = lane
    where_own = jnp.where(hanging | outside, NOWHERE, where)
    own_where[...] = where_own
    own_row[...], column_ref[...] = rows_and_columns(where_own, lane)
    where_edge = jnp.where(hanging, 4 * REACH, jnp.where(outside, where - last, NOWHERE))
    edge_where[...] = where_edge
    edge_row[...], edge_column[...] = rows_and_columns(where_edge, lane)


def own_gather(
    half_rows, tab_ref, where_ref, lane_ref, master_where, master_lane, weight_ref, cells_ref,
    hang_ref, *rest,
):
    *final_ref, tall_ref, sums_ref = rest
    table = tall_table([tab_ref], half_rows, tall_ref)
    tall = up8(half_rows)
    found = sum_masters(table, tall, weight_ref[...], master_where, master_lane, sums_ref)
    for part in range(3):
        hang_ref[part : part + 1, :] = found[part]
    gather(table, tall, 3, where_ref, lane_ref, sums_ref)
    count = where_ref.shape[0]
    for part in range(3):
        cells_ref[part * count : (part + 1) * count, :] = gathered(sums_ref, count, part)
    if final_ref:
        final_ref = final_ref[0]
        for row in range(final_ref.shape[1] // WIDE):
            for part in range(3):
                final_ref[part : part + 1, row * WIDE : (row + 1) * WIDE] = tab_ref[
                    part * OWN + row : part * OWN + row + 1, :
                ]


def edge_gather(
    place, got_ref, first, cells_ref, hang_ref, where_ref, lane_ref, master_where, master_lane,
    weight_ref, edge_ref, sums_ref, out_ref,
):
    slots = 2 * REACH
    edge_ref[...] = jnp.zeros_like(edge_ref)
    for part in range(3):
        for half in range(2):
            lines = landed(place, 1, got_ref, 2 * (first + part) + half)
            for slot in range(slots):
                at = part * TALL + 2 * slot + half
                edge_ref[at : at + 1, :] = lines[slot]
    table = jnp.concatenate(pieces(edge_ref[...]), 1)
    found = sum_masters(table, TALL, weight_ref[...], master_where, master_lane, sums_ref)
    for part in range(3):
        at = part * TALL + 2 * slots
        edge_ref[at : at + 1, :] = found[part] + hang_ref[part : part + 1, :]
    table = jnp.concatenate(pieces(edge_ref[...]), 1)
    gather(table, TALL, 3, where_ref, lane_ref, sums_ref)
    count = where_ref.shape[0]
    for part in range(3):
        rows = slice(part * count, (part + 1) * count)
        out_ref[rows, :] = cells_ref[rows, :] + gathered(sums_ref, count, part)


def edge_product(
    place_ref, got_ref, cells_ref, hang_ref, where_ref, lane_ref, master_where, master_lane,
    weight_ref, row_ref, column_ref, master_row, master_column, modulus_ref, stiffness_ref, out_ref,
    image_ref, held_ref, pack_ref, edge_ref, sums_ref, full_ref, low_ref, sum_ref, *scratch,
):
    place = place_ref[0]
    edge_gather(
        place, got_ref, 0, cells_ref, hang_ref, where_ref, lane_ref,
        master_where, master_lane, weight_ref, edge_ref, sums_ref, full_ref,
    )
    image = modulus_ref[...] * lax.dot_general(
        stiffness_ref[...],
        full_ref[...],
        (((0,), (0,)), ((), ())),
        precision=lax.Precision.HIGHEST,
        preferred_element_type=f32,
    )
    image_ref[...] = image
    full_ref[...], low_ref[...] = split32(image)
    scatter(full_ref, low_ref, EDGE, row_ref, column_ref, sum_ref)
    sums = add_pieces(sum_ref[...])
    slots = 2 * REACH
    held = jnp.concatenate(
        [sums[part * EDGE + slots : part * EDGE + slots + 1, :LANES] for part in range(3)], 0
    )
    held_ref[...] = held
    sums += spread_hanging(held, weight_ref[...], EDGE, master_row, master_column, scratch)
    rows = [
        [
            sums[part * EDGE + slot : part * EDGE + slot + 1, half * LANES : (half + 1) * LANES]
            for part in range(3)
            for half in range(2)
        ]
        for slot in range(slots)
    ]
    pack(place, -1, rows, pack_ref, out_ref)


def own_sums(
    image_ref, held_ref, row_ref, column_ref, master_row, master_column, weight_ref,
    tab_ref, source_ref, inverse_ref, out_ref, high_ref, low_ref, sum_ref, *scratch,
):
    high_ref[...], low_ref[...] = split32(image_ref[...])
    scatter(high_ref, low_ref, OWN, row_ref, column_ref, sum_ref)
    applied = add_pieces(sum_ref[...]) + spread_hanging(
        held_ref[...], weight_ref[...], OWN, master_row, master_column, scratch
    )
    out_ref[...] = tab_ref[...] + relaxation * inverse_ref[...] * (source_ref[...] - applied)


def update(
    place_ref, got_ref, row_ref, column_ref, partial_ref, inverse_ref, out_ref, tab_ref,
    pack_ref, sums_ref, *scratch,
):
    place = place_ref[0]
    values = [landed_wide(place, -1, got_ref, part) for part in range(3)]
    returned = scatter_few(values, OWN, row_ref, column_ref, scratch)
    fresh = partial_ref[...] - relaxation * inverse_ref[...] * returned
    tab_ref[...] = fresh
    rows = export_rows(fresh, 3, row_ref, column_ref, sums_ref)
    pack(place, 1, rows, pack_ref, out_ref)


def primal_product(
    place_ref, got_ref, cells_ref, hang_ref, where_ref, lane_ref, master_where,
    master_lane, weight_ref, modulus_ref, stiffness_ref, out_ref, edge_ref, sums_ref, full_ref,
):
    edge_gather(
        place_ref[0], got_ref, 3, cells_ref, hang_ref, where_ref, lane_ref,
        master_where, master_lane, weight_ref, edge_ref, sums_ref, full_ref,
    )
    out_ref[...] = modulus_ref[...] * jnp.dot(
        stiffness_ref[...],
        full_ref[...],
        precision=lax.Precision.HIGHEST,
        preferred_element_type=f32,
    )


def fluxes(
    place_ref, got_ref, cells_ref, hang_ref, where_ref, lane_ref, master_where,
    master_lane, weight_ref, ku_ref, load_ref, sub_cell, sub_face, out_ref,
    term_ref, pack_ref, edge_ref, sums_ref, full_ref, tall_ref, code_ref, few_ref,
):
    place = place_ref[0]
    edge_gather(
        place, got_ref, 0, cells_ref, hang_ref, where_ref, lane_ref,
        master_where, master_lane, weight_ref, edge_ref, sums_ref, full_ref,
    )
    cells = full_ref[...]
    ku = ku_ref[...]
    term_ref[...] = jnp.sum(cells * (load_ref[...] - ku), 0, keepdims=True)
    face = lax.broadcasted_iota(i32, (8, ku.shape[0]), 0)
    node = lax.broadcasted_iota(i32, (8, ku.shape[0]), 1) & 63
    index = jnp.where(face < 2, node >> 4, jnp.where(face < 4, (node >> 2) & 3, node & 3))
    member = jnp.where((face < 6) & (index == 3 * (face & 1)), 1.0, 0.0).astype(f32)
    flux = jnp.dot(
        member, ku * cells, precision=lax.Precision.HIGHEST, preferred_element_type=f32
    )
    tall_ref[...] = jnp.zeros_like(tall_ref)
    for number in range(6):
        for half in range(2):
            at = 2 * number + half
            tall_ref[at : at + 1, :] = flux[
                number : number + 1, half * LANES : (half + 1) * LANES
            ]
    cell = sub_cell[...]
    code_ref[:8, :] = 2 * sub_face[...] + (cell >> 7)
    code_ref[8:, :] = cell & 127
    table = jnp.concatenate(pieces(tall_ref[...]), 1)
    gather(table, 16, 1, code_ref.at[:8, :], code_ref.at[8:, :], few_ref)
    found = gathered(few_ref, 8, 0)
    rows = [[found[slot : slot + 1]] for slot in range(2 * REACH)]
    pack(place, 1, rows, pack_ref, out_ref)


def collect(place_ref, got_ref, owner_ref, term_ref, out_ref):
    count = term_ref.shape[1]
    got = jnp.concatenate(landed(place_ref[0], 1, got_ref, 0), 1)
    hot = jnp.concatenate(
        [one_hot(owner_ref[slot : slot + 1, :], count) for slot in range(2 * REACH)], 1
    )
    values = jnp.concatenate(
        [jnp.broadcast_to(x, (16, got.shape[1])).astype(bf16) for x in split32(got)], 0
    )
    sums = lax.dot_general(values, hot, (((1,), (1,)), ((), ())), preferred_element_type=f32)
    face_term = sums[0:1] + sums[16:17]
    out_ref[...] = (jnp.abs(term_ref[...]) + jnp.abs(face_term)) / scale_down


SMALL = pl.BlockSpec(memory_space=pltpu.SMEM)
FAST = pl.BlockSpec(memory_space=pltpu.VMEM)
FAR = pl.BlockSpec(memory_space=pl.ANY)


def away(*arrays):
    return [pltpu.with_memory_space_constraint(x, pltpu.HBM) for x in arrays]


def call(kernel, outs, scratch=(), specs=None, sems=0):
    scratch = [pltpu.VMEM(shape, kind) for shape, kind in scratch]
    if sems:
        scratch.append(pltpu.SemaphoreType.DMA((sems,)))

    def run(*args):
        return pl.pallas_call(
            kernel,
            out_shape=[jax.ShapeDtypeStruct(shape, kind) for shape, kind in outs],
            in_specs=specs or [SMALL] + [FAST] * (len(args) - 1),
            scratch_shapes=scratch,
            compiler_params=pltpu.CompilerParams(vmem_limit_bytes=40 * 1024 * 1024),
        )(*args)

    return run


def local(
    adjoint_start,
    adjoint_source,
    inverse_diagonal,
    primal_field,
    cell_load,
    modulus,
    stiffness,
    connectivity,
    hang_node,
    hang_master,
    hang_weight,
    ghost_lists,
    subface_cell,
    subface_face,
    subface_owner,
):
    slots = 2 * REACH
    local_values, cell_count = cell_load.shape
    nodes = connectivity.shape[0]
    half_rows = adjoint_start.shape[1] // LANES
    place = lax.axis_index("dom").reshape(1).astype(i32)
    table = ((3 * OWN, WIDE), f32)
    index = ((nodes, cell_count), i32)
    cells_shape = ((local_values, cell_count), f32)
    hang_shape = ((3, hang_node.shape[0]), f32)
    master_shape = ((8, WIDE), i32)

    count = lax.axis_size("dom")

    def packed(height):
        return [((count, height, LANES), f32)]

    def room(height):
        return ((count + 1, height, LANES), f32)

    tall = up8(half_rows)
    few_sums = ((2, 3 * 64, LANES), f32)
    many_sums = ((2, local_values * 8, LANES), f32)
    own_tall = ((3 * tall, LANES), f32)
    edge = [((3 * TALL, LANES), f32), many_sums, cells_shape]
    tab, tab_primal, list_row, list_column, blocks = call(
        first_export,
        [table, table] + [(ghost_lists.shape, i32)] * 2 + packed(16),
        [
            room(16),
            (adjoint_start.shape, f32),
            (primal_field.shape, f32),
            (ghost_lists.shape, i32),
            ((2, 6 * 64, LANES), f32),
        ],
        [SMALL, FAR, FAR, FAR],
        sems=3,
    )(place, *away(adjoint_start, primal_field, ghost_lists))
    ghosts = first_ghosts = exchange(blocks)
    far = (
        connectivity, hang_node.reshape(1, -1), hang_master, hang_weight, adjoint_source,
        inverse_diagonal,
    )
    (
        own_where, own_row, edge_where, edge_row, lane, own_column, edge_column, master_own,
        master_own_row, master_edge, master_edge_row, master_lane, master_column, weight, source,
        inverse, moduli,
    ) = call(
        setup,
        [index] * 7 + [master_shape] * 6
        + [((8, WIDE), f32), table, table, ((1, cell_count), f32)],
        [(x.shape, x.dtype) for x in far]
        + [((OWN, WIDE), f32), ((tall, LANES), f32), ((2, nodes * 8, LANES), f32)],
        [FAR] * 7,
        sems=7,
    )(*away(*far, modulus.reshape(1, cell_count)))

    def gather_own(values, final=()):
        return call(
            functools.partial(own_gather, half_rows),
            [cells_shape, hang_shape, *final],
            [own_tall, many_sums],
            specs=[FAST] * 6,
        )(values, own_where, lane, master_own, master_lane, weight)

    on_edge = (edge_where, lane, master_edge, master_lane, weight)
    for sweep in range(SWEEPS):
        cells, hang = gather_own(tab)
        if sweep == 1:
            (ku,) = call(primal_product, [cells_shape], edge)(
                place, first_ghosts, *primal_cells, *on_edge, moduli, stiffness
            )
            cells, ku = lax.optimization_barrier((cells, ku))
        blocks, image, held = call(
            edge_product,
            packed(8) + [cells_shape, hang_shape],
            [room(8)] + edge + [cells_shape, ((6 * EDGE, WIDE), f32)] + few(EDGE),
        )(
            place, ghosts, cells, hang, *on_edge, edge_row, edge_column, master_edge_row,
            master_column, moduli, stiffness,
        )
        returned = exchange(blocks)
        (partial,) = call(
            own_sums,
            [table],
            [cells_shape, cells_shape, ((6 * OWN, WIDE), f32)] + few(OWN),
            specs=[FAST] * 10,
        )(
            image, held, own_row, own_column, master_own_row, master_column, weight, tab, source,
            inverse,
        )
        if sweep == 0:
            tab_primal, image = lax.optimization_barrier((tab_primal, image))
            primal_cells = gather_own(tab_primal)
            partial, *primal_cells = lax.optimization_barrier((partial, *primal_cells))
        blocks, tab = call(update, packed(8) + [table], [room(8), few_sums] + few(OWN))(
            place, returned, list_row, list_column, partial, inverse
        )
        ghosts = exchange(blocks)
    cells, hang, adjoint = gather_own(tab, [(adjoint_start.shape, f32)])
    blocks, term = call(
        fluxes,
        packed(1) + [((1, cell_count), f32)],
        [room(1)]
        + edge
        + [
            ((16, LANES), f32),
            ((16, subface_cell.shape[1]), i32),
            ((1, 64, LANES), f32),
        ],
    )(place, ghosts, cells, hang, *on_edge, ku, cell_load, subface_cell, subface_face)
    received = exchange(blocks)
    (indicator,) = call(collect, [((1, cell_count), f32)])(
        place, received, subface_owner, term
    )
    return (adjoint, indicator.reshape(cell_count))


def solution(mesh):
    placed = (
        P(None, "dom"),
        P(None, "dom"),
        P(None, "dom"),
        P(None, "dom"),
        P(None, "dom"),
        P("dom"),
        P(),
        P(None, "dom"),
        P("dom"),
        P(None, "dom"),
        P(None, "dom"),
        P(None, "dom"),
        P(None, "dom"),
        P(None, "dom"),
        P(None, "dom"),
    )
    return jax.shard_map(
        local, mesh=mesh, in_specs=placed, out_specs=(P(None, "dom"), P("dom")), check_vma=False
    )
```

```python
import functools

import jax
import jax.numpy as jnp
from jax import lax
from jax.experimental import pallas as pl
from jax.experimental.pallas import tpu as pltpu
from jax.sharding import PartitionSpec as P

REACH = 4
SWEEPS = 2
LANES = 128
WIDE = 2 * LANES
OWN = 32
EDGE = 16
TALL = 24
NOWHERE = 126

relaxation = 0.7
scale_down = 16.0
pad_code = 16368

f32 = jnp.float32
bf16 = jnp.bfloat16
i32 = jnp.int32


def neighbour_offsets():
    return [step + 1 for step in range(REACH)] + [-(step + 1) for step in range(REACH)]


def exchange(packed):
    return lax.all_to_all(packed, "dom", 0, 0, tiled=True)


def pack(place, sign, rows, pack_ref, out_ref):
    count = out_ref.shape[0]
    pack_ref[...] = jnp.zeros_like(pack_ref)
    for slot, offset in enumerate(neighbour_offsets()):
        target = place + sign * offset
        at = jnp.where((target >= 0) & (target < count), target, count)
        for number, row in enumerate(rows[slot]):
            pack_ref[at, number : number + 1, :] = row
    out_ref[...] = pack_ref[:count]


def landed(place, sign, got_ref, number):
    count = got_ref.shape[0]
    rows = []
    for offset in neighbour_offsets():
        source = place - sign * offset
        row = got_ref[jnp.clip(source, 0, count - 1), number : number + 1, :]
        there = jnp.broadcast_to((source >= 0) & (source < count), row.shape)
        rows.append(jnp.where(there, row, 0.0))
    return rows


def landed_wide(place, sign, got_ref, part):
    halves = [
        jnp.concatenate(landed(place, sign, got_ref, 2 * part + half), 0) for half in range(2)
    ]
    return jnp.concatenate(halves, 1)


def wide16(row):
    return jnp.broadcast_to(row, (16, row.shape[1])).astype(bf16)[None]


def one_hot(row, count):
    width = row.shape[1]
    numbers = lax.broadcasted_iota(i32, (count, width), 0).astype(f32).astype(bf16)
    off = numbers.reshape(count // 16, 16, width) - wide16(row.astype(f32))
    hot = jnp.maximum(jnp.ones_like(off) - off * off, jnp.zeros_like(off))
    return hot.reshape(count, width)


def spread16(hot, row):
    count, width = hot.shape
    return (hot.reshape(count // 16, 16, width) * wide16(row)).reshape(count, width)


def pieces(x):
    high = x.astype(bf16)
    return high, (x - high.astype(f32)).astype(bf16)


def gather(table, rows, parts, row_ref, column_ref, sums_ref, wide=False):
    count, width = row_ref.shape
    step = min(count, 32)
    numbers = lax.broadcasted_iota(i32, (rows, width), 0)

    def body(block, carry):
        start = pl.multiple_of(block * step, step)
        for j in range(step):
            hot = one_hot(column_ref[pl.ds(start + j, 1), :], WIDE if wide else LANES)
            if not wide:
                hot = jnp.concatenate([hot, hot], 0)
            found = jnp.dot(table, hot, preferred_element_type=f32)
            if wide:
                found = found[: parts * rows] + found[parts * rows :]
            mask = numbers == jnp.broadcast_to(row_ref[pl.ds(start + j, 1), :], numbers.shape)
            for part in range(parts):
                kept = jnp.where(mask, found[part * rows : (part + 1) * rows], 0.0)
                kept = jnp.sum(kept.reshape(rows // 8, 8, width), 0)
                for half in range(width // LANES):
                    sums_ref[half, pl.ds(part * count * 8 + start * 8 + j * 8, 8), :] = kept[
                        :, half * LANES : (half + 1) * LANES
                    ]
        return carry

    if count == step:
        body(0, 0)
    else:
        lax.fori_loop(0, count // step, body, 0)


def gathered(sums_ref, count, part):
    totals = []
    for half in range(sums_ref.shape[0]):
        rows = [sums_ref[half, pl.ds(part * count * 8 + s, count, stride=8), :] for s in range(8)]
        while len(rows) > 1:
            rows = [a + b for a, b in zip(rows[::2], rows[1::2])]
        totals.append(rows[0])
    return jnp.concatenate(totals, 1)


def halves(x):
    return [x[:, :LANES], x[:, LANES:]]


def rows_and_columns(where, lane):
    return where >> 1, (where & 1) * LANES + lane


def scatter(high_ref, low_ref, rows, row_ref, column_ref, sum_ref):
    count = row_ref.shape[0]
    step = min(count, 16)

    def product(start):
        masks = [one_hot(row_ref[pl.ds(start + j, 1), :], rows) for j in range(8)]
        hot = jnp.concatenate(
            [one_hot(column_ref[pl.ds(start + j, 1), :], WIDE) for j in range(8)], 1
        )
        stacked = [
            jnp.concatenate(
                [
                    spread16(mask, piece_ref[pl.ds(part * count + start + j, 1), :])
                    for j, mask in enumerate(masks)
                ],
                1,
            )
            for piece_ref in (high_ref, low_ref)
            for part in range(3)
        ]
        return lax.dot_general(
            jnp.concatenate(stacked, 0), hot, (((1,), (1,)), ((), ())), preferred_element_type=f32
        )

    if count == 8:
        sum_ref[...] = product(0)
        return
    sum_ref[...] = jnp.zeros_like(sum_ref)

    def body(block, carry):
        start = pl.multiple_of(block * step, step)
        total = product(start)
        for first in range(8, step, 8):
            total += product(start + first)
        sum_ref[...] += total
        return carry

    lax.fori_loop(0, count // step, body, 0)


def split32(x):
    high = x.astype(bf16).astype(f32)
    return high, x - high


def add_pieces(sums):
    half = sums.shape[0] // 2
    return sums[:half] + sums[half:]


def scatter_few(values, rows, row_ref, column_ref, scratch):
    high_ref, low_ref, sum_ref = scratch
    for part in range(3):
        high_ref[part * 8 : part * 8 + 8, :], low_ref[part * 8 : part * 8 + 8, :] = split32(
            values[part]
        )
    scatter(high_ref, low_ref, rows, row_ref, column_ref, sum_ref)
    return add_pieces(sum_ref[...])


def few(rows):
    return [((24, WIDE), f32)] * 2 + [((6 * rows, WIDE), f32)]


def spread_hanging(held, weight, rows, row_ref, column_ref, scratch):
    both = jnp.concatenate([held, held], 1)
    values = [weight * both[part : part + 1] for part in range(3)]
    return scatter_few(values, rows, row_ref, column_ref, scratch)


def sum_masters(table, tall, weight, where_ref, lane_ref, sums_ref):
    gather(table, tall, 3, where_ref, lane_ref, sums_ref)
    totals = []
    for part in range(3):
        left, right = halves(weight * gathered(sums_ref, 8, part))
        totals.append(jnp.sum(left + right, 0, keepdims=True))
    return totals


def fill_table(x_ref, out_ref):
    count = x_ref.shape[1] // WIDE
    for part in range(3):
        out_ref[part * OWN + count : (part + 1) * OWN, :] = jnp.zeros((OWN - count, WIDE), f32)
    for row in range(count):
        block = x_ref[:, row * WIDE : (row + 1) * WIDE]
        for part in range(3):
            out_ref[part * OWN + row : part * OWN + row + 1, :] = block[part : part + 1]


def tall_table(tab_refs, half_rows, tall_ref):
    tall = up8(half_rows)
    tall_ref[...] = jnp.zeros_like(tall_ref)
    for number, tab_ref in enumerate(tab_refs):
        for part in range(3):
            for half_row in range(half_rows):
                row, half = part * OWN + half_row // 2, half_row % 2
                at = (3 * number + part) * tall + half_row
                tall_ref[at : at + 1, :] = tab_ref[
                    row : row + 1, half * LANES : (half + 1) * LANES
                ]
    return jnp.concatenate(pieces(tall_ref[...]), 1)


def up8(count):
    return -(-count // 8) * 8


def export_tiles(table, row_ref, column_ref, sums_ref):
    table = jnp.concatenate(pieces(table), 0)
    gather(table, OWN, 3, row_ref, column_ref, sums_ref, wide=True)
    return [tile for part in range(3) for tile in halves(gathered(sums_ref, 8, part))]


def export_rows(table, row_ref, column_ref, sums_ref):
    tiles = export_tiles(table, row_ref, column_ref, sums_ref)
    return [[tile[slot : slot + 1] for tile in tiles] for slot in range(2 * REACH)]


def add_primal(rows, sign, part, extra_ref):
    slots = 2 * REACH
    for slot in range(slots):
        export = slot if sign > 0 else (slot + REACH) % slots
        for half in range(2):
            rows[slot].append(extra_ref[2 * part + half, export : export + 1, :])


def copy_in(pairs, sems):
    copies = [
        pltpu.make_async_copy(source, target, sems.at[number])
        for number, (source, target) in enumerate(pairs)
    ]
    for copy in copies:
        copy.start()
    for copy in copies:
        copy.wait()


def first_export(
    place_ref, adjoint_hbm, list_hbm, tab_ref, row_ref, column_ref,
    out_ref, pack_ref, adjoint_ref, list_ref, sums_ref, sems,
):
    copy_in([(adjoint_hbm, adjoint_ref), (list_hbm, list_ref)], sems)
    owned = adjoint_ref.shape[1]
    fill_table(adjoint_ref, tab_ref)
    codes = list_ref[...]
    node = lax.rem(17 * codes + lax.broadcasted_iota(i32, codes.shape, 1), owned)
    row_ref[...] = node >> 8
    column_ref[...] = node & 255
    rows = export_rows(tab_ref[...], row_ref, column_ref, sums_ref)
    pack(place_ref[0], 1, rows, pack_ref, out_ref)


def primal_export(
    primal_hbm, row_ref, column_ref, tab_ref, out_ref, primal_ref, sums_ref, sems
):
    copy_in([(primal_hbm, primal_ref)], sems)
    fill_table(primal_ref, tab_ref)
    tiles = export_tiles(tab_ref[...], row_ref, column_ref, sums_ref)
    for number, tile in enumerate(tiles):
        out_ref[number] = tile


def setup(
    connect_hbm, node_hbm, master_hbm, weight_hbm, source_hbm, inverse_hbm, modulus_hbm,
    own_where, own_row, edge_where, edge_row, lane_ref, column_ref, edge_column, master_own, master_own_row,
    master_edge, master_edge_row, master_lane, master_column, weight_out, tab_source, tab_inverse,
    modulus_out,
    connect_ref, node_ref, master_ref, weight_ref, source_ref, inverse_ref, map_ref, tall_ref, sums_ref,
    sems,
):
    copy_in(
        [
            (connect_hbm, connect_ref),
            (node_hbm, node_ref),
            (master_hbm, master_ref),
            (weight_hbm, weight_ref),
            (source_hbm, source_ref),
            (inverse_hbm, inverse_ref),
            (modulus_hbm, modulus_out),
        ],
        sems,
    )
    owned = source_ref.shape[1]
    extent = owned + 2 * REACH * WIDE
    fill_table(source_ref, tab_source)
    fill_table(inverse_ref, tab_inverse)
    codes = master_ref[...]
    master = lax.rem(17 * codes + 8 * lax.broadcasted_iota(i32, codes.shape, 1), extent)
    count = codes.shape[0] // 2
    master = jnp.concatenate([master[:count], master[count:]], 1)
    weight = weight_ref[...]
    weight_out[...] = jnp.concatenate([weight[:count], weight[count:]], 1)
    last = owned // LANES
    where = master >> 7
    master_own[...] = jnp.where(where < last, where, NOWHERE)
    master_edge[...] = jnp.where(where < last, NOWHERE, where - last)
    master_lane[...] = master & 127
    row = master >> 8
    master_own_row[...] = jnp.where(where < last, row, NOWHERE)
    master_edge_row[...] = jnp.where(where < last, NOWHERE, row - last // 2)
    master_column[...] = master & 255

    codes = node_ref[...]
    node = jnp.where(codes == pad_code, extent, lax.rem(13 * codes, owned))
    slot = (lax.broadcasted_iota(i32, codes.shape, 1) + 1).astype(f32)
    map_ref[...] = lax.dot_general(
        spread16(one_hot(node >> 8, OWN), slot),
        one_hot(node & 255, WIDE),
        (((1,), (1,)), ((), ())),
        preferred_element_type=f32,
    )

    codes = connect_ref[...]
    cells = lax.broadcasted_iota(i32, codes.shape, 1)
    slots = lax.rem(27 * cells + 17 * codes, extent)
    own_where[...] = slots >> 7
    lane_ref[...] = slots & 127
    tall_ref[...] = jnp.zeros_like(tall_ref)
    for half_row in range(last):
        row, half = half_row // 2, half_row % 2
        tall_ref[half_row : half_row + 1, :] = map_ref[
            row : row + 1, half * LANES : (half + 1) * LANES
        ]
    table = jnp.concatenate(pieces(tall_ref[...]), 1)
    gather(table, tall_ref.shape[0], 1, own_where, lane_ref, sums_ref)
    slot = gathered(sums_ref, codes.shape[0], 0).astype(i32)
    where = slots >> 7
    hanging = slot > 0
    outside = where >= last
    lane = jnp.where(hanging, slot - 1, slots & 127)
    lane_ref[...] = lane
    where_own = jnp.where(hanging | outside, NOWHERE, where)
    own_where[...] = where_own
    own_row[...], column_ref[...] = rows_and_columns(where_own, lane)
    where_edge = jnp.where(hanging, 4 * REACH, jnp.where(outside, where - last, NOWHERE))
    edge_where[...] = where_edge
    edge_row[...], edge_column[...] = rows_and_columns(where_edge, lane)


def own_gather(
    half_rows, tab_ref, where_ref, lane_ref, master_where, master_lane, weight_ref, cells_ref,
    hang_ref, *rest,
):
    *final_ref, tall_ref, sums_ref = rest
    table = tall_table([tab_ref], half_rows, tall_ref)
    tall = up8(half_rows)
    found = sum_masters(table, tall, weight_ref[...], master_where, master_lane, sums_ref)
    for part in range(3):
        hang_ref[part : part + 1, :] = found[part]
    gather(table, tall, 3, where_ref, lane_ref, sums_ref)
    count = where_ref.shape[0]
    for part in range(3):
        cells_ref[part * count : (part + 1) * count, :] = gathered(sums_ref, count, part)
    if final_ref:
        final_ref = final_ref[0]
        for row in range(final_ref.shape[1] // WIDE):
            for part in range(3):
                final_ref[part : part + 1, row * WIDE : (row + 1) * WIDE] = tab_ref[
                    part * OWN + row : part * OWN + row + 1, :
                ]


def edge_gather(
    place, got_refs, first, cells_ref, hang_ref, where_ref, lane_ref, master_where, master_lane,
    weight_ref, edge_ref, sums_ref, out_ref,
):
    slots = 2 * REACH
    edge_ref[...] = jnp.zeros_like(edge_ref)
    for part in range(3):
        for half in range(2):
            lines = landed(place, 1, got_refs[part], first[part] + half)
            for slot in range(slots):
                at = part * TALL + 2 * slot + half
                edge_ref[at : at + 1, :] = lines[slot]
    table = jnp.concatenate(pieces(edge_ref[...]), 1)
    found = sum_masters(table, TALL, weight_ref[...], master_where, master_lane, sums_ref)
    for part in range(3):
        at = part * TALL + 2 * slots
        edge_ref[at : at + 1, :] = found[part] + hang_ref[part : part + 1, :]
    table = jnp.concatenate(pieces(edge_ref[...]), 1)
    gather(table, TALL, 3, where_ref, lane_ref, sums_ref)
    count = where_ref.shape[0]
    for part in range(3):
        rows = slice(part * count, (part + 1) * count)
        out_ref[rows, :] = cells_ref[rows, :] + gathered(sums_ref, count, part)


def edge_product(
    primal_part, place_ref, got_ref, cells_ref, hang_ref, where_ref, lane_ref, master_where, master_lane,
    weight_ref, row_ref, column_ref, master_row, master_column, extra_ref, modulus_ref,
    stiffness_ref, out_ref,
    image_ref, held_ref, pack_ref, edge_ref, sums_ref, full_ref, low_ref, sum_ref, *scratch,
):
    place = place_ref[0]
    edge_gather(
        place, [got_ref] * 3, (0, 2, 4), cells_ref, hang_ref, where_ref, lane_ref,
        master_where, master_lane, weight_ref, edge_ref, sums_ref, full_ref,
    )
    image = modulus_ref[...] * lax.dot_general(
        stiffness_ref[...],
        full_ref[...],
        (((0,), (0,)), ((), ())),
        precision=lax.Precision.HIGHEST,
        preferred_element_type=f32,
    )
    image_ref[...] = image
    full_ref[...], low_ref[...] = split32(image)
    scatter(full_ref, low_ref, EDGE, row_ref, column_ref, sum_ref)
    sums = add_pieces(sum_ref[...])
    slots = 2 * REACH
    held = jnp.concatenate(
        [sums[part * EDGE + slots : part * EDGE + slots + 1, :LANES] for part in range(3)], 0
    )
    held_ref[...] = held
    sums += spread_hanging(held, weight_ref[...], EDGE, master_row, master_column, scratch)
    rows = [
        [
            sums[part * EDGE + slot : part * EDGE + slot + 1, half * LANES : (half + 1) * LANES]
            for part in range(3)
            for half in range(2)
        ]
        for slot in range(slots)
    ]
    add_primal(rows, -1, primal_part, extra_ref)
    pack(place, -1, rows, pack_ref, out_ref)


def own_sums(
    image_ref, held_ref, row_ref, column_ref, master_row, master_column, weight_ref,
    tab_ref, source_ref, inverse_ref, out_ref, high_ref, low_ref, sum_ref, *scratch,
):
    high_ref[...], low_ref[...] = split32(image_ref[...])
    scatter(high_ref, low_ref, OWN, row_ref, column_ref, sum_ref)
    applied = add_pieces(sum_ref[...]) + spread_hanging(
        held_ref[...], weight_ref[...], OWN, master_row, master_column, scratch
    )
    out_ref[...] = tab_ref[...] + relaxation * inverse_ref[...] * (source_ref[...] - applied)


def update(
    primal_part, place_ref, got_ref, row_ref, column_ref, partial_ref, inverse_ref, extra_ref,
    out_ref, tab_ref,
    pack_ref, sums_ref, *scratch,
):
    place = place_ref[0]
    values = [landed_wide(place, -1, got_ref, part) for part in range(3)]
    returned = scatter_few(values, OWN, row_ref, column_ref, scratch)
    fresh = partial_ref[...] - relaxation * inverse_ref[...] * returned
    tab_ref[...] = fresh
    rows = export_rows(fresh, row_ref, column_ref, sums_ref)
    if primal_part is not None:
        add_primal(rows, 1, primal_part, extra_ref)
    pack(place, 1, rows, pack_ref, out_ref)


def primal_product(
    place_ref, got_a, got_b, got_c, cells_ref, hang_ref, where_ref, lane_ref, master_where,
    master_lane, weight_ref, modulus_ref, stiffness_ref, out_ref, edge_ref, sums_ref, full_ref,
):
    edge_gather(
        place_ref[0], (got_a, got_b, got_c), (6, 6, 6), cells_ref, hang_ref, where_ref, lane_ref,
        master_where, master_lane, weight_ref, edge_ref, sums_ref, full_ref,
    )
    out_ref[...] = modulus_ref[...] * jnp.dot(
        stiffness_ref[...],
        full_ref[...],
        precision=lax.Precision.HIGHEST,
        preferred_element_type=f32,
    )


def fluxes(
    place_ref, got_ref, cells_ref, hang_ref, where_ref, lane_ref, master_where,
    master_lane, weight_ref, ku_ref, load_ref, sub_cell, sub_face, out_ref,
    term_ref, pack_ref, edge_ref, sums_ref, full_ref, tall_ref, code_ref, few_ref,
):
    place = place_ref[0]
    edge_gather(
        place, [got_ref] * 3, (0, 2, 4), cells_ref, hang_ref, where_ref, lane_ref,
        master_where, master_lane, weight_ref, edge_ref, sums_ref, full_ref,
    )
    cells = full_ref[...]
    ku = ku_ref[...]
    term_ref[...] = jnp.sum(cells * (load_ref[...] - ku), 0, keepdims=True)
    face = lax.broadcasted_iota(i32, (8, ku.shape[0]), 0)
    node = lax.broadcasted_iota(i32, (8, ku.shape[0]), 1) & 63
    index = jnp.where(face < 2, node >> 4, jnp.where(face < 4, (node >> 2) & 3, node & 3))
    member = jnp.where((face < 6) & (index == 3 * (face & 1)), 1.0, 0.0).astype(f32)
    flux = jnp.dot(
        member, ku * cells, precision=lax.Precision.HIGHEST, preferred_element_type=f32
    )
    tall_ref[...] = jnp.zeros_like(tall_ref)
    for number in range(6):
        for half in range(2):
            at = 2 * number + half
            tall_ref[at : at + 1, :] = flux[
                number : number + 1, half * LANES : (half + 1) * LANES
            ]
    cell = sub_cell[...]
    code_ref[:8, :] = 2 * sub_face[...] + (cell >> 7)
    code_ref[8:, :] = cell & 127
    table = jnp.concatenate(pieces(tall_ref[...]), 1)
    gather(table, 16, 1, code_ref.at[:8, :], code_ref.at[8:, :], few_ref)
    found = gathered(few_ref, 8, 0)
    rows = [[found[slot : slot + 1]] for slot in range(2 * REACH)]
    pack(place, 1, rows, pack_ref, out_ref)


def collect(place_ref, got_ref, owner_ref, term_ref, out_ref):
    count = term_ref.shape[1]
    got = jnp.concatenate(landed(place_ref[0], 1, got_ref, 0), 1)
    hot = jnp.concatenate(
        [one_hot(owner_ref[slot : slot + 1, :], count) for slot in range(2 * REACH)], 1
    )
    values = jnp.concatenate(
        [jnp.broadcast_to(x, (16, got.shape[1])).astype(bf16) for x in split32(got)], 0
    )
    sums = lax.dot_general(values, hot, (((1,), (1,)), ((), ())), preferred_element_type=f32)
    face_term = sums[0:1] + sums[16:17]
    out_ref[...] = (jnp.abs(term_ref[...]) + jnp.abs(face_term)) / scale_down


SMALL = pl.BlockSpec(memory_space=pltpu.SMEM)
FAST = pl.BlockSpec(memory_space=pltpu.VMEM)
FAR = pl.BlockSpec(memory_space=pl.ANY)


def away(*arrays):
    return [pltpu.with_memory_space_constraint(x, pltpu.HBM) for x in arrays]


def call(kernel, outs, scratch=(), specs=None, sems=0):
    scratch = [pltpu.VMEM(shape, kind) for shape, kind in scratch]
    if sems:
        scratch.append(pltpu.SemaphoreType.DMA((sems,)))

    def run(*args):
        return pl.pallas_call(
            kernel,
            out_shape=[jax.ShapeDtypeStruct(shape, kind) for shape, kind in outs],
            in_specs=specs or [SMALL] + [FAST] * (len(args) - 1),
            scratch_shapes=scratch,
            compiler_params=pltpu.CompilerParams(vmem_limit_bytes=40 * 1024 * 1024),
        )(*args)

    return run


def local(
    adjoint_start,
    adjoint_source,
    inverse_diagonal,
    primal_field,
    cell_load,
    modulus,
    stiffness,
    connectivity,
    hang_node,
    hang_master,
    hang_weight,
    ghost_lists,
    subface_cell,
    subface_face,
    subface_owner,
):
    slots = 2 * REACH
    local_values, cell_count = cell_load.shape
    nodes = connectivity.shape[0]
    half_rows = adjoint_start.shape[1] // LANES
    place = lax.axis_index("dom").reshape(1).astype(i32)
    table = ((3 * OWN, WIDE), f32)
    index = ((nodes, cell_count), i32)
    cells_shape = ((local_values, cell_count), f32)
    hang_shape = ((3, hang_node.shape[0]), f32)
    master_shape = ((8, WIDE), i32)

    count = lax.axis_size("dom")

    def packed(height):
        return [((count, height, LANES), f32)]

    def room(height):
        return ((count + 1, height, LANES), f32)

    tall = up8(half_rows)
    few_sums = ((2, 3 * 64, LANES), f32)
    many_sums = ((2, local_values * 8, LANES), f32)
    own_tall = ((3 * tall, LANES), f32)
    edge = [((3 * TALL, LANES), f32), many_sums, cells_shape]
    tab, list_row, list_column, blocks = call(
        first_export,
        [table] + [(ghost_lists.shape, i32)] * 2 + packed(8),
        [room(8), (adjoint_start.shape, f32), (ghost_lists.shape, i32), few_sums],
        [SMALL, FAR, FAR],
        sems=2,
    )(place, *away(adjoint_start, ghost_lists))
    ghosts = exchange(blocks)
    tab_primal, extra = call(
        primal_export,
        [table, ((6, slots, LANES), f32)],
        [(primal_field.shape, f32), few_sums],
        [FAR, FAST, FAST],
        sems=1,
    )(*away(primal_field), list_row, list_column)
    far = (
        connectivity, hang_node.reshape(1, -1), hang_master, hang_weight, adjoint_source,
        inverse_diagonal,
    )
    (
        own_where, own_row, edge_where, edge_row, lane, own_column, edge_column, master_own,
        master_own_row, master_edge, master_edge_row, master_lane, master_column, weight, source,
        inverse, moduli,
    ) = call(
        setup,
        [index] * 7 + [master_shape] * 6
        + [((8, WIDE), f32), table, table, ((1, cell_count), f32)],
        [(x.shape, x.dtype) for x in far]
        + [((OWN, WIDE), f32), ((tall, LANES), f32), ((2, nodes * 8, LANES), f32)],
        [FAR] * 7,
        sems=7,
    )(*away(*far, modulus.reshape(1, cell_count)))

    def gather_own(values, final=()):
        return call(
            functools.partial(own_gather, half_rows),
            [cells_shape, hang_shape, *final],
            [own_tall, many_sums],
            specs=[FAST] * 6,
        )(values, own_where, lane, master_own, master_lane, weight)

    on_edge = (edge_where, lane, master_edge, master_lane, weight)
    landings = []
    for sweep in range(SWEEPS):
        cells, hang = gather_own(tab)
        if sweep == 1:
            tab_primal, tab = lax.optimization_barrier((tab_primal, tab))
            primal_cells = gather_own(tab_primal)
            cells, *primal_cells = lax.optimization_barrier((cells, *primal_cells))
        blocks, image, held = call(
            functools.partial(edge_product, 2 * sweep),
            packed(8) + [cells_shape, hang_shape],
            [room(8)] + edge + [cells_shape, ((6 * EDGE, WIDE), f32)] + few(EDGE),
        )(
            place, ghosts, cells, hang, *on_edge, edge_row, edge_column, master_edge_row,
            master_column, extra, moduli, stiffness,
        )
        returned = exchange(blocks)
        landings.append(returned)
        (partial,) = call(
            own_sums,
            [table],
            [cells_shape, cells_shape, ((6 * OWN, WIDE), f32)] + few(OWN),
            specs=[FAST] * 10,
        )(
            image, held, own_row, own_column, master_own_row, master_column, weight, tab, source,
            inverse,
        )
        blocks, tab = call(
            functools.partial(update, 1 if sweep == 0 else None),
            packed(8) + [table],
            [room(8), few_sums] + few(OWN),
        )(place, returned, list_row, list_column, partial, inverse, extra)
        ghosts = exchange(blocks)
        landings.append(ghosts)
    cells, hang, adjoint = gather_own(tab, [(adjoint_start.shape, f32)])
    tab, *primal_cells = lax.optimization_barrier((tab, *primal_cells))
    (ku,) = call(primal_product, [cells_shape], edge)(
        place, *landings[:3], *primal_cells, *on_edge, moduli, stiffness
    )
    blocks, term = call(
        fluxes,
        packed(1) + [((1, cell_count), f32)],
        [room(1)]
        + edge
        + [
            ((16, LANES), f32),
            ((16, subface_cell.shape[1]), i32),
            ((1, 64, LANES), f32),
        ],
    )(place, ghosts, cells, hang, *on_edge, ku, cell_load, subface_cell, subface_face)
    received = exchange(blocks)
    (indicator,) = call(collect, [((1, cell_count), f32)])(
        place, received, subface_owner, term
    )
    return (adjoint, indicator.reshape(cell_count))


def solution(mesh):
    placed = (
        P(None, "dom"),
        P(None, "dom"),
        P(None, "dom"),
        P(None, "dom"),
        P(None, "dom"),
        P("dom"),
        P(),
        P(None, "dom"),
        P("dom"),
        P(None, "dom"),
        P(None, "dom"),
        P(None, "dom"),
        P(None, "dom"),
        P(None, "dom"),
        P(None, "dom"),
    )
    return jax.shard_map(
        local, mesh=mesh, in_specs=placed, out_specs=(P(None, "dom"), P("dom")), check_vma=False
    )
```

```python
import functools

import jax
import jax.numpy as jnp
from jax import lax
from jax.experimental import pallas as pl
from jax.experimental.pallas import tpu as pltpu
from jax.sharding import PartitionSpec as P

REACH = 4
SWEEPS = 2
LANES = 128
WIDE = 2 * LANES
OWN = 32
EDGE = 16
TALL = 24
NOWHERE = 126

relaxation = 0.7
scale_down = 16.0
pad_code = 16368

f32 = jnp.float32
bf16 = jnp.bfloat16
i32 = jnp.int32


def neighbour_offsets():
    return [step + 1 for step in range(REACH)] + [-(step + 1) for step in range(REACH)]


def exchange(packed):
    return lax.all_to_all(packed, "dom", 0, 0, tiled=True)


def pack(place, sign, rows, pack_ref, out_ref):
    count = out_ref.shape[0]
    pack_ref[...] = jnp.zeros_like(pack_ref)
    for slot, offset in enumerate(neighbour_offsets()):
        target = place + sign * offset
        at = jnp.where((target >= 0) & (target < count), target, count)
        for number, row in enumerate(rows[slot]):
            pack_ref[at, number : number + 1, :] = row
    out_ref[...] = pack_ref[:count]


def landed(place, sign, got_ref, number):
    count = got_ref.shape[0]
    rows = []
    for offset in neighbour_offsets():
        source = place - sign * offset
        row = got_ref[jnp.clip(source, 0, count - 1), number : number + 1, :]
        there = jnp.broadcast_to((source >= 0) & (source < count), row.shape)
        rows.append(jnp.where(there, row, 0.0))
    return rows


def landed_wide(place, sign, got_ref, part):
    halves = [
        jnp.concatenate(landed(place, sign, got_ref, 2 * part + half), 0) for half in range(2)
    ]
    return jnp.concatenate(halves, 1)


def one_hot(row, count):
    shape = (count, row.shape[1])
    mask = lax.broadcasted_iota(i32, shape, 0) == jnp.broadcast_to(row, shape)
    return jnp.where(mask, 1.0, 0.0).astype(bf16)


def match16(row, count):
    width = row.shape[1]
    wide = jnp.broadcast_to(row.astype(f32), (16, width)).astype(bf16)
    numbers = lax.broadcasted_iota(i32, (count, width), 0).astype(f32).astype(bf16)
    return numbers.reshape(count // 16, 16, width) == wide[None]


def spread16(mask, row):
    wide = jnp.broadcast_to(row, (16, row.shape[1])).astype(bf16)[None]
    out = jnp.where(mask, jnp.broadcast_to(wide, mask.shape), jnp.zeros(mask.shape, bf16))
    return out.reshape(mask.shape[0] * 16, row.shape[1])


def pieces(x):
    high = x.astype(bf16)
    return high, (x - high.astype(f32)).astype(bf16)


def gather(table, rows, parts, row_ref, column_ref, sums_ref, wide=False):
    count, width = row_ref.shape
    step = min(count, 64)
    numbers = lax.broadcasted_iota(i32, (rows, width), 0)

    def body(block, carry):
        start = pl.multiple_of(block * step, step)
        for j in range(step):
            hot = one_hot(column_ref[pl.ds(start + j, 1), :], WIDE if wide else LANES)
            if not wide:
                hot = jnp.concatenate([hot, hot], 0)
            found = jnp.dot(table, hot, preferred_element_type=f32)
            if wide:
                found = found[: parts * rows] + found[parts * rows :]
            mask = numbers == jnp.broadcast_to(row_ref[pl.ds(start + j, 1), :], numbers.shape)
            for part in range(parts):
                kept = jnp.where(mask, found[part * rows : (part + 1) * rows], 0.0)
                kept = jnp.sum(kept.reshape(rows // 8, 8, width), 0)
                for half in range(width // LANES):
                    sums_ref[half, pl.ds(part * count * 8 + start * 8 + j * 8, 8), :] = kept[
                        :, half * LANES : (half + 1) * LANES
                    ]
        return carry

    if count == step:
        body(0, 0)
    else:
        lax.fori_loop(0, count // step, body, 0)


def gathered(sums_ref, count, part):
    totals = []
    for half in range(sums_ref.shape[0]):
        rows = [sums_ref[half, pl.ds(part * count * 8 + s, count, stride=8), :] for s in range(8)]
        while len(rows) > 1:
            rows = [a + b for a, b in zip(rows[::2], rows[1::2])]
        totals.append(rows[0])
    return jnp.concatenate(totals, 1)


def halves(x):
    return [x[:, :LANES], x[:, LANES:]]


def rows_and_columns(where, lane):
    return where >> 1, (where & 1) * LANES + lane


def scatter(high_ref, low_ref, rows, row_ref, column_ref, sum_ref):
    count = row_ref.shape[0]
    step = min(count, 32)

    def product(start):
        masks = [match16(row_ref[pl.ds(start + j, 1), :], rows) for j in range(8)]
        hot = jnp.concatenate(
            [one_hot(column_ref[pl.ds(start + j, 1), :], WIDE) for j in range(8)], 1
        )
        stacked = [
            jnp.concatenate(
                [
                    spread16(mask, piece_ref[pl.ds(part * count + start + j, 1), :])
                    for j, mask in enumerate(masks)
                ],
                1,
            )
            for piece_ref in (high_ref, low_ref)
            for part in range(3)
        ]
        return lax.dot_general(
            jnp.concatenate(stacked, 0), hot, (((1,), (1,)), ((), ())), preferred_element_type=f32
        )

    if count == 8:
        sum_ref[...] = product(0)
        return
    sum_ref[...] = jnp.zeros_like(sum_ref)

    def body(block, carry):
        start = pl.multiple_of(block * step, step)
        total = product(start)
        for first in range(8, step, 8):
            total += product(start + first)
        sum_ref[...] += total
        return carry

    lax.fori_loop(0, count // step, body, 0)


def split32(x):
    high = x.astype(bf16).astype(f32)
    return high, x - high


def add_pieces(sums):
    half = sums.shape[0] // 2
    return sums[:half] + sums[half:]


def scatter_few(values, rows, row_ref, column_ref, scratch):
    high_ref, low_ref, sum_ref = scratch
    for part in range(3):
        high_ref[part * 8 : part * 8 + 8, :], low_ref[part * 8 : part * 8 + 8, :] = split32(
            values[part]
        )
    scatter(high_ref, low_ref, rows, row_ref, column_ref, sum_ref)
    return add_pieces(sum_ref[...])


def few(rows):
    return [((24, WIDE), f32)] * 2 + [((6 * rows, WIDE), f32)]


def spread_hanging(held, weight, rows, row_ref, column_ref, scratch):
    both = jnp.concatenate([held, held], 1)
    values = [weight * both[part : part + 1] for part in range(3)]
    return scatter_few(values, rows, row_ref, column_ref, scratch)


def sum_masters(table, tall, weight, where_ref, lane_ref, sums_ref):
    gather(table, tall, 3, where_ref, lane_ref, sums_ref)
    totals = []
    for part in range(3):
        left, right = halves(weight * gathered(sums_ref, 8, part))
        totals.append(jnp.sum(left + right, 0, keepdims=True))
    return totals


def fill_table(x_ref, out_ref):
    count = x_ref.shape[1] // WIDE
    for part in range(3):
        out_ref[part * OWN + count : (part + 1) * OWN, :] = jnp.zeros((OWN - count, WIDE), f32)
    for row in range(count):
        block = x_ref[:, row * WIDE : (row + 1) * WIDE]
        for part in range(3):
            out_ref[part * OWN + row : part * OWN + row + 1, :] = block[part : part + 1]


def tall_table(tab_refs, half_rows, tall_ref):
    tall = up8(half_rows)
    tall_ref[...] = jnp.zeros_like(tall_ref)
    for number, tab_ref in enumerate(tab_refs):
        for part in range(3):
            for half_row in range(half_rows):
                row, half = part * OWN + half_row // 2, half_row % 2
                at = (3 * number + part) * tall + half_row
                tall_ref[at : at + 1, :] = tab_ref[
                    row : row + 1, half * LANES : (half + 1) * LANES
                ]
    return jnp.concatenate(pieces(tall_ref[...]), 1)


def up8(count):
    return -(-count // 8) * 8


def export_tiles(table, parts, row_ref, column_ref, sums_ref):
    table = jnp.concatenate(pieces(table), 0)
    gather(table, OWN, parts, row_ref, column_ref, sums_ref, wide=True)
    return [tile for part in range(parts) for tile in halves(gathered(sums_ref, 8, part))]


def rows_of(tiles):
    return [[tile[slot : slot + 1] for tile in tiles] for slot in range(2 * REACH)]


def add_primal(rows, sign, part, extra_ref):
    slots = 2 * REACH
    for slot in range(slots):
        export = slot if sign > 0 else (slot + REACH) % slots
        for half in range(2):
            rows[slot].append(extra_ref[2 * part + half, export : export + 1, :])


def copy_in(pairs, sems):
    copies = [
        pltpu.make_async_copy(source, target, sems.at[number])
        for number, (source, target) in enumerate(pairs)
    ]
    for copy in copies:
        copy.start()
    for copy in copies:
        copy.wait()


def first_export(
    place_ref, adjoint_hbm, primal_hbm, list_hbm, tab_a, tab_p, row_ref, column_ref, extra_ref,
    out_ref, pack_ref, adjoint_ref, primal_ref, list_ref, sums_ref, sems,
):
    copy_in(
        [(adjoint_hbm, adjoint_ref), (primal_hbm, primal_ref), (list_hbm, list_ref)], sems
    )
    owned = adjoint_ref.shape[1]
    fill_table(adjoint_ref, tab_a)
    fill_table(primal_ref, tab_p)
    codes = list_ref[...]
    node = lax.rem(17 * codes + lax.broadcasted_iota(i32, codes.shape, 1), owned)
    row_ref[...] = node >> 8
    column_ref[...] = node & 255
    table = jnp.concatenate([tab_a[...], tab_p[...]], 0)
    tiles = export_tiles(table, 6, row_ref, column_ref, sums_ref)
    for number in range(6):
        extra_ref[number] = tiles[6 + number]
    pack(place_ref[0], 1, rows_of(tiles[:6]), pack_ref, out_ref)


def setup(
    connect_hbm, node_hbm, master_hbm, weight_hbm, source_hbm, inverse_hbm, modulus_hbm,
    own_where, own_row, edge_where, edge_row, lane_ref, column_ref, edge_column, master_own, master_own_row,
    master_edge, master_edge_row, master_lane, master_column, weight_out, tab_source, tab_inverse,
    modulus_out,
    connect_ref, node_ref, master_ref, weight_ref, source_ref, inverse_ref, map_ref, tall_ref, sums_ref,
    sems,
):
    copy_in(
        [
            (connect_hbm, connect_ref),
            (node_hbm, node_ref),
            (master_hbm, master_ref),
            (weight_hbm, weight_ref),
            (source_hbm, source_ref),
            (inverse_hbm, inverse_ref),
            (modulus_hbm, modulus_out),
        ],
        sems,
    )
    owned = source_ref.shape[1]
    extent = owned + 2 * REACH * WIDE
    fill_table(source_ref, tab_source)
    fill_table(inverse_ref, tab_inverse)
    codes = master_ref[...]
    master = lax.rem(17 * codes + 8 * lax.broadcasted_iota(i32, codes.shape, 1), extent)
    count = codes.shape[0] // 2
    master = jnp.concatenate([master[:count], master[count:]], 1)
    weight = weight_ref[...]
    weight_out[...] = jnp.concatenate([weight[:count], weight[count:]], 1)
    last = owned // LANES
    where = master >> 7
    master_own[...] = jnp.where(where < last, where, NOWHERE)
    master_edge[...] = jnp.where(where < last, NOWHERE, where - last)
    master_lane[...] = master & 127
    row = master >> 8
    master_own_row[...] = jnp.where(where < last, row, NOWHERE)
    master_edge_row[...] = jnp.where(where < last, NOWHERE, row - last // 2)
    master_column[...] = master & 255

    codes = node_ref[...]
    node = jnp.where(codes == pad_code, extent, lax.rem(13 * codes, owned))
    slot = (lax.broadcasted_iota(i32, codes.shape, 1) + 1).astype(f32)
    map_ref[...] = lax.dot_general(
        spread16(match16(node >> 8, OWN), slot),
        one_hot(node & 255, WIDE),
        (((1,), (1,)), ((), ())),
        preferred_element_type=f32,
    )

    codes = connect_ref[...]
    cells = lax.broadcasted_iota(i32, codes.shape, 1)
    slots = lax.rem(27 * cells + 17 * codes, extent)
    own_where[...] = slots >> 7
    lane_ref[...] = slots & 127
    tall_ref[...] = jnp.zeros_like(tall_ref)
    for half_row in range(last):
        row, half = half_row // 2, half_row % 2
        tall_ref[half_row : half_row + 1, :] = map_ref[
            row : row + 1, half * LANES : (half + 1) * LANES
        ]
    table = jnp.concatenate(pieces(tall_ref[...]), 1)
    gather(table, tall_ref.shape[0], 1, own_where, lane_ref, sums_ref)
    slot = gathered(sums_ref, codes.shape[0], 0).astype(i32)
    where = slots >> 7
    hanging = slot > 0
    outside = where >= last
    lane = jnp.where(hanging, slot - 1, slots & 127)
    lane_ref[...] = lane
    where_own = jnp.where(hanging | outside, NOWHERE, where)
    own_where[...] = where_own
    own_row[...], column_ref[...] = rows_and_columns(where_own, lane)
    where_edge = jnp.where(hanging, 4 * REACH, jnp.where(outside, where - last, NOWHERE))
    edge_where[...] = where_edge
    edge_row[...], edge_column[...] = rows_and_columns(where_edge, lane)


def own_gather(
    half_rows, tab_ref, where_ref, lane_ref, master_where, master_lane, weight_ref, cells_ref,
    hang_ref, *rest,
):
    *final_ref, tall_ref, sums_ref = rest
    table = tall_table([tab_ref], half_rows, tall_ref)
    tall = up8(half_rows)
    found = sum_masters(table, tall, weight_ref[...], master_where, master_lane, sums_ref)
    for part in range(3):
        hang_ref[part : part + 1, :] = found[part]
    gather(table, tall, 3, where_ref, lane_ref, sums_ref)
    count = where_ref.shape[0]
    for part in range(3):
        cells_ref[part * count : (part + 1) * count, :] = gathered(sums_ref, count, part)
    if final_ref:
        final_ref = final_ref[0]
        for row in range(final_ref.shape[1] // WIDE):
            for part in range(3):
                final_ref[part : part + 1, row * WIDE : (row + 1) * WIDE] = tab_ref[
                    part * OWN + row : part * OWN + row + 1, :
                ]


def edge_gather(
    place, got_refs, first, cells_ref, hang_ref, where_ref, lane_ref, master_where, master_lane,
    weight_ref, edge_ref, sums_ref, out_ref,
):
    slots = 2 * REACH
    edge_ref[...] = jnp.zeros_like(edge_ref)
    for part in range(3):
        for half in range(2):
            lines = landed(place, 1, got_refs[part], first[part] + half)
            for slot in range(slots):
                at = part * TALL + 2 * slot + half
                edge_ref[at : at + 1, :] = lines[slot]
    table = jnp.concatenate(pieces(edge_ref[...]), 1)
    found = sum_masters(table, TALL, weight_ref[...], master_where, master_lane, sums_ref)
    for part in range(3):
        at = part * TALL + 2 * slots
        edge_ref[at : at + 1, :] = found[part] + hang_ref[part : part + 1, :]
    table = jnp.concatenate(pieces(edge_ref[...]), 1)
    gather(table, TALL, 3, where_ref, lane_ref, sums_ref)
    count = where_ref.shape[0]
    for part in range(3):
        rows = slice(part * count, (part + 1) * count)
        out_ref[rows, :] = cells_ref[rows, :] + gathered(sums_ref, count, part)


def edge_product(
    primal_part, place_ref, got_ref, cells_ref, hang_ref, where_ref, lane_ref, master_where, master_lane,
    weight_ref, row_ref, column_ref, master_row, master_column, extra_ref, modulus_ref,
    stiffness_ref, out_ref,
    image_ref, held_ref, pack_ref, edge_ref, sums_ref, full_ref, low_ref, sum_ref, *scratch,
):
    place = place_ref[0]
    edge_gather(
        place, [got_ref] * 3, (0, 2, 4), cells_ref, hang_ref, where_ref, lane_ref,
        master_where, master_lane, weight_ref, edge_ref, sums_ref, full_ref,
    )
    image = modulus_ref[...] * lax.dot_general(
        stiffness_ref[...],
        full_ref[...],
        (((0,), (0,)), ((), ())),
        precision=lax.Precision.HIGHEST,
        preferred_element_type=f32,
    )
    image_ref[...] = image
    full_ref[...], low_ref[...] = split32(image)
    scatter(full_ref, low_ref, EDGE, row_ref, column_ref, sum_ref)
    sums = add_pieces(sum_ref[...])
    slots = 2 * REACH
    held = jnp.concatenate(
        [sums[part * EDGE + slots : part * EDGE + slots + 1, :LANES] for part in range(3)], 0
    )
    held_ref[...] = held
    sums += spread_hanging(held, weight_ref[...], EDGE, master_row, master_column, scratch)
    rows = [
        [
            sums[part * EDGE + slot : part * EDGE + slot + 1, half * LANES : (half + 1) * LANES]
            for part in range(3)
            for half in range(2)
        ]
        for slot in range(slots)
    ]
    add_primal(rows, -1, primal_part, extra_ref)
    pack(place, -1, rows, pack_ref, out_ref)


def own_sums(
    image_ref, held_ref, row_ref, column_ref, master_row, master_column, weight_ref,
    tab_ref, source_ref, inverse_ref, out_ref, high_ref, low_ref, sum_ref, *scratch,
):
    high_ref[...], low_ref[...] = split32(image_ref[...])
    scatter(high_ref, low_ref, OWN, row_ref, column_ref, sum_ref)
    applied = add_pieces(sum_ref[...]) + spread_hanging(
        held_ref[...], weight_ref[...], OWN, master_row, master_column, scratch
    )
    out_ref[...] = tab_ref[...] + relaxation * inverse_ref[...] * (source_ref[...] - applied)


def update(
    primal_part, place_ref, got_ref, row_ref, column_ref, partial_ref, inverse_ref, extra_ref,
    out_ref, tab_ref,
    pack_ref, sums_ref, *scratch,
):
    place = place_ref[0]
    values = [landed_wide(place, -1, got_ref, part) for part in range(3)]
    returned = scatter_few(values, OWN, row_ref, column_ref, scratch)
    fresh = partial_ref[...] - relaxation * inverse_ref[...] * returned
    tab_ref[...] = fresh
    rows = rows_of(export_tiles(fresh, 3, row_ref, column_ref, sums_ref))
    if primal_part is not None:
        add_primal(rows, 1, primal_part, extra_ref)
    pack(place, 1, rows, pack_ref, out_ref)


def primal_product(
    place_ref, got_a, got_b, got_c, cells_ref, hang_ref, where_ref, lane_ref, master_where,
    master_lane, weight_ref, modulus_ref, stiffness_ref, out_ref, edge_ref, sums_ref, full_ref,
):
    edge_gather(
        place_ref[0], (got_a, got_b, got_c), (6, 6, 6), cells_ref, hang_ref, where_ref, lane_ref,
        master_where, master_lane, weight_ref, edge_ref, sums_ref, full_ref,
    )
    out_ref[...] = modulus_ref[...] * jnp.dot(
        stiffness_ref[...],
        full_ref[...],
        precision=lax.Precision.HIGHEST,
        preferred_element_type=f32,
    )


def fluxes(
    place_ref, got_ref, cells_ref, hang_ref, where_ref, lane_ref, master_where,
    master_lane, weight_ref, ku_ref, load_ref, sub_cell, sub_face, out_ref,
    term_ref, pack_ref, edge_ref, sums_ref, full_ref, tall_ref, code_ref, few_ref,
):
    place = place_ref[0]
    edge_gather(
        place, [got_ref] * 3, (0, 2, 4), cells_ref, hang_ref, where_ref, lane_ref,
        master_where, master_lane, weight_ref, edge_ref, sums_ref, full_ref,
    )
    cells = full_ref[...]
    ku = ku_ref[...]
    term_ref[...] = jnp.sum(cells * (load_ref[...] - ku), 0, keepdims=True)
    face = lax.broadcasted_iota(i32, (8, ku.shape[0]), 0)
    node = lax.broadcasted_iota(i32, (8, ku.shape[0]), 1) & 63
    index = jnp.where(face < 2, node >> 4, jnp.where(face < 4, (node >> 2) & 3, node & 3))
    member = jnp.where((face < 6) & (index == 3 * (face & 1)), 1.0, 0.0).astype(f32)
    flux = jnp.dot(
        member, ku * cells, precision=lax.Precision.HIGHEST, preferred_element_type=f32
    )
    tall_ref[...] = jnp.zeros_like(tall_ref)
    for number in range(6):
        for half in range(2):
            at = 2 * number + half
            tall_ref[at : at + 1, :] = flux[
                number : number + 1, half * LANES : (half + 1) * LANES
            ]
    cell = sub_cell[...]
    code_ref[:8, :] = 2 * sub_face[...] + (cell >> 7)
    code_ref[8:, :] = cell & 127
    table = jnp.concatenate(pieces(tall_ref[...]), 1)
    gather(table, 16, 1, code_ref.at[:8, :], code_ref.at[8:, :], few_ref)
    found = gathered(few_ref, 8, 0)
    rows = [[found[slot : slot + 1]] for slot in range(2 * REACH)]
    pack(place, 1, rows, pack_ref, out_ref)


def collect(place_ref, got_ref, owner_ref, term_ref, out_ref):
    count = term_ref.shape[1]
    got = jnp.concatenate(landed(place_ref[0], 1, got_ref, 0), 1)
    hot = jnp.concatenate(
        [one_hot(owner_ref[slot : slot + 1, :], count) for slot in range(2 * REACH)], 1
    )
    values = jnp.concatenate(
        [jnp.broadcast_to(x, (16, got.shape[1])).astype(bf16) for x in split32(got)], 0
    )
    sums = lax.dot_general(values, hot, (((1,), (1,)), ((), ())), preferred_element_type=f32)
    face_term = sums[0:1] + sums[16:17]
    out_ref[...] = (jnp.abs(term_ref[...]) + jnp.abs(face_term)) / scale_down


SMALL = pl.BlockSpec(memory_space=pltpu.SMEM)
FAST = pl.BlockSpec(memory_space=pltpu.VMEM)
FAR = pl.BlockSpec(memory_space=pl.ANY)


def away(*arrays):
    return [pltpu.with_memory_space_constraint(x, pltpu.HBM) for x in arrays]


def call(kernel, outs, scratch=(), specs=None, sems=0):
    scratch = [pltpu.VMEM(shape, kind) for shape, kind in scratch]
    if sems:
        scratch.append(pltpu.SemaphoreType.DMA((sems,)))

    def run(*args):
        return pl.pallas_call(
            kernel,
            out_shape=[jax.ShapeDtypeStruct(shape, kind) for shape, kind in outs],
            in_specs=specs or [SMALL] + [FAST] * (len(args) - 1),
            scratch_shapes=scratch,
            compiler_params=pltpu.CompilerParams(vmem_limit_bytes=40 * 1024 * 1024),
        )(*args)

    return run


def local(
    adjoint_start,
    adjoint_source,
    inverse_diagonal,
    primal_field,
    cell_load,
    modulus,
    stiffness,
    connectivity,
    hang_node,
    hang_master,
    hang_weight,
    ghost_lists,
    subface_cell,
    subface_face,
    subface_owner,
):
    slots = 2 * REACH
    local_values, cell_count = cell_load.shape
    nodes = connectivity.shape[0]
    half_rows = adjoint_start.shape[1] // LANES
    place = lax.axis_index("dom").reshape(1).astype(i32)
    table = ((3 * OWN, WIDE), f32)
    index = ((nodes, cell_count), i32)
    cells_shape = ((local_values, cell_count), f32)
    hang_shape = ((3, hang_node.shape[0]), f32)
    master_shape = ((8, WIDE), i32)

    count = lax.axis_size("dom")

    def packed(height):
        return [((count, height, LANES), f32)]

    def room(height):
        return ((count + 1, height, LANES), f32)

    tall = up8(half_rows)
    few_sums = ((2, 3 * 64, LANES), f32)
    many_sums = ((2, local_values * 8, LANES), f32)
    own_tall = ((3 * tall, LANES), f32)
    edge = [((3 * TALL, LANES), f32), many_sums, cells_shape]
    tab, tab_primal, list_row, list_column, extra, blocks = call(
        first_export,
        [table, table]
        + [(ghost_lists.shape, i32)] * 2
        + [((6, slots, LANES), f32)]
        + packed(8),
        [
            room(8),
            (adjoint_start.shape, f32),
            (primal_field.shape, f32),
            (ghost_lists.shape, i32),
            ((2, 6 * 64, LANES), f32),
        ],
        [SMALL, FAR, FAR, FAR],
        sems=3,
    )(place, *away(adjoint_start, primal_field, ghost_lists))
    ghosts = exchange(blocks)
    far = (
        connectivity, hang_node.reshape(1, -1), hang_master, hang_weight, adjoint_source,
        inverse_diagonal,
    )
    (
        own_where, own_row, edge_where, edge_row, lane, own_column, edge_column, master_own,
        master_own_row, master_edge, master_edge_row, master_lane, master_column, weight, source,
        inverse, moduli,
    ) = call(
        setup,
        [index] * 7 + [master_shape] * 6
        + [((8, WIDE), f32), table, table, ((1, cell_count), f32)],
        [(x.shape, x.dtype) for x in far]
        + [((OWN, WIDE), f32), ((tall, LANES), f32), ((2, nodes * 8, LANES), f32)],
        [FAR] * 7,
        sems=7,
    )(*away(*far, modulus.reshape(1, cell_count)))

    def gather_own(values, final=()):
        return call(
            functools.partial(own_gather, half_rows),
            [cells_shape, hang_shape, *final],
            [own_tall, many_sums],
            specs=[FAST] * 6,
        )(values, own_where, lane, master_own, master_lane, weight)

    on_edge = (edge_where, lane, master_edge, master_lane, weight)
    landings = []
    for sweep in range(SWEEPS):
        cells, hang = gather_own(tab)
        if sweep == 1:
            tab_primal, tab = lax.optimization_barrier((tab_primal, tab))
            primal_cells = gather_own(tab_primal)
            cells, *primal_cells = lax.optimization_barrier((cells, *primal_cells))
        blocks, image, held = call(
            functools.partial(edge_product, 2 * sweep),
            packed(8) + [cells_shape, hang_shape],
            [room(8)] + edge + [cells_shape, ((6 * EDGE, WIDE), f32)] + few(EDGE),
        )(
            place, ghosts, cells, hang, *on_edge, edge_row, edge_column, master_edge_row,
            master_column, extra, moduli, stiffness,
        )
        returned = exchange(blocks)
        landings.append(returned)
        (partial,) = call(
            own_sums,
            [table],
            [cells_shape, cells_shape, ((6 * OWN, WIDE), f32)] + few(OWN),
            specs=[FAST] * 10,
        )(
            image, held, own_row, own_column, master_own_row, master_column, weight, tab, source,
            inverse,
        )
        blocks, tab = call(
            functools.partial(update, 1 if sweep == 0 else None),
            packed(8) + [table],
            [room(8), few_sums] + few(OWN),
        )(place, returned, list_row, list_column, partial, inverse, extra)
        ghosts = exchange(blocks)
        landings.append(ghosts)
    cells, hang, adjoint = gather_own(tab, [(adjoint_start.shape, f32)])
    tab, *primal_cells = lax.optimization_barrier((tab, *primal_cells))
    (ku,) = call(primal_product, [cells_shape], edge)(
        place, *landings[:3], *primal_cells, *on_edge, moduli, stiffness
    )
    blocks, term = call(
        fluxes,
        packed(1) + [((1, cell_count), f32)],
        [room(1)]
        + edge
        + [
            ((16, LANES), f32),
            ((16, subface_cell.shape[1]), i32),
            ((1, 64, LANES), f32),
        ],
    )(place, ghosts, cells, hang, *on_edge, ku, cell_load, subface_cell, subface_face)
    received = exchange(blocks)
    (indicator,) = call(collect, [((1, cell_count), f32)])(
        place, received, subface_owner, term
    )
    return (adjoint, indicator.reshape(cell_count))


def solution(mesh):
    placed = (
        P(None, "dom"),
        P(None, "dom"),
        P(None, "dom"),
        P(None, "dom"),
        P(None, "dom"),
        P("dom"),
        P(),
        P(None, "dom"),
        P("dom"),
        P(None, "dom"),
        P(None, "dom"),
        P(None, "dom"),
        P(None, "dom"),
        P(None, "dom"),
        P(None, "dom"),
    )
    return jax.shard_map(
        local, mesh=mesh, in_specs=placed, out_specs=(P(None, "dom"), P("dom")), check_vma=False
    )
```

```python
import functools

import jax
import jax.numpy as jnp
from jax import lax
from jax.experimental import pallas as pl
from jax.experimental.pallas import tpu as pltpu
from jax.sharding import PartitionSpec as P

REACH = 4
SWEEPS = 2
LANES = 128
WIDE = 2 * LANES
OWN = 32
EDGE = 32
TALL = 24
NOWHERE = 126

relaxation = 0.7
scale_down = 16.0
pad_code = 16368

f32 = jnp.float32
bf16 = jnp.bfloat16
i32 = jnp.int32


def neighbour_offsets():
    return [step + 1 for step in range(REACH)] + [-(step + 1) for step in range(REACH)]


def exchange(packed):
    return lax.all_to_all(packed, "dom", 0, 0, tiled=True)


def pack(place, sign, rows, pack_ref, out_ref):
    count = out_ref.shape[0]
    pack_ref[...] = jnp.zeros_like(pack_ref)
    for slot, offset in enumerate(neighbour_offsets()):
        target = place + sign * offset
        at = jnp.where((target >= 0) & (target < count), target, count)
        for number, row in enumerate(rows[slot]):
            pack_ref[at, number : number + 1, :] = row
    out_ref[...] = pack_ref[:count]


def landed(place, sign, got_ref, number):
    count = got_ref.shape[0]
    rows = []
    for offset in neighbour_offsets():
        source = place - sign * offset
        row = got_ref[jnp.clip(source, 0, count - 1), number : number + 1, :]
        there = jnp.broadcast_to((source >= 0) & (source < count), row.shape)
        rows.append(jnp.where(there, row, 0.0))
    return rows


def landed_wide(place, sign, got_ref, part):
    halves = [
        jnp.concatenate(landed(place, sign, got_ref, 2 * part + half), 0) for half in range(2)
    ]
    return jnp.concatenate(halves, 1)


def match16(row, count):
    width = row.shape[1]
    wide = jnp.broadcast_to(row.astype(f32), (16, width)).astype(bf16)
    numbers = lax.broadcasted_iota(i32, (count, width), 0).astype(f32).astype(bf16)
    return numbers.reshape(count // 16, 16, width) == wide[None]


def one_hot(row, count):
    mask = match16(row, count)
    ones = jnp.ones(mask.shape, bf16)
    return jnp.where(mask, ones, jnp.zeros_like(ones)).reshape(count, row.shape[1])


def spread16(mask, row):
    wide = jnp.broadcast_to(row, (16, row.shape[1])).astype(bf16)[None]
    out = jnp.where(mask, jnp.broadcast_to(wide, mask.shape), jnp.zeros(mask.shape, bf16))
    return out.reshape(mask.shape[0] * 16, row.shape[1])


def pieces(x):
    high = x.astype(bf16)
    return high, (x - high.astype(f32)).astype(bf16)


def gather(jobs, column_ref, wide=False):
    count, width = column_ref.shape
    tables = jnp.concatenate([job[0] for job in jobs], 0)
    high = tables.shape[0]
    numbers = lax.broadcasted_iota(i32, (max(job[1] for job in jobs), width), 0)
    step = min(count, 32 if sum(job[1] * job[2] for job in jobs) <= 192 else 16)

    def body(block, carry):
        start = pl.multiple_of(block * step, step)
        for j in range(step):
            hot = one_hot(column_ref[pl.ds(start + j, 1), :], WIDE if wide else LANES)
            if not wide:
                hot = jnp.concatenate([hot, hot], 0)
            all_found = jnp.dot(tables, hot, preferred_element_type=f32)
            if wide:
                all_found = all_found[: high // 2] + all_found[high // 2 :]
            top = 0
            for _, rows, parts, row_ref, sums_ref in jobs:
                found = all_found[top : top + parts * rows]
                top += parts * rows
                mask = numbers[:rows] == jnp.broadcast_to(
                    row_ref[pl.ds(start + j, 1), :], (rows, width)
                )
                for part in range(parts):
                    kept = jnp.where(mask, found[part * rows : (part + 1) * rows], 0.0)
                    kept = jnp.sum(kept.reshape(rows // 8, 8, width), 0)
                    for half in range(width // LANES):
                        sums_ref[half, pl.ds(part * count * 8 + start * 8 + j * 8, 8), :] = kept[
                            :, half * LANES : (half + 1) * LANES
                        ]
        return carry

    if count == step:
        body(0, 0)
    else:
        lax.fori_loop(0, count // step, body, 0)


def gathered(sums_ref, count, part):
    totals = []
    for half in range(sums_ref.shape[0]):
        rows = [sums_ref[half, pl.ds(part * count * 8 + s, count, stride=8), :] for s in range(8)]
        while len(rows) > 1:
            rows = [a + b for a, b in zip(rows[::2], rows[1::2])]
        totals.append(rows[0])
    return jnp.concatenate(totals, 1)


def halves(x):
    return [x[:, :LANES], x[:, LANES:]]


def rows_and_columns(where, lane):
    return where >> 1, (where & 1) * LANES + lane


def scatter(high_ref, low_ref, rows, row_ref, column_ref, sum_ref):
    count = row_ref.shape[0]
    step = min(count, 32)

    def product(start):
        masks = [match16(row_ref[pl.ds(start + j, 1), :], rows) for j in range(8)]
        hot = jnp.concatenate(
            [one_hot(column_ref[pl.ds(start + j, 1), :], sum_ref.shape[1]) for j in range(8)], 1
        )
        stacked = [
            jnp.concatenate(
                [
                    spread16(mask, piece_ref[pl.ds(part * count + start + j, 1), :])
                    for j, mask in enumerate(masks)
                ],
                1,
            )
            for piece_ref in (high_ref, low_ref)
            for part in range(3)
        ]
        return lax.dot_general(
            jnp.concatenate(stacked, 0), hot, (((1,), (1,)), ((), ())), preferred_element_type=f32
        )

    if count == 8:
        sum_ref[...] = product(0)
        return
    sum_ref[...] = jnp.zeros_like(sum_ref)

    def body(block, carry):
        start = pl.multiple_of(block * step, step)
        total = product(start)
        for first in range(8, step, 8):
            total += product(start + first)
        sum_ref[...] += total
        return carry

    lax.fori_loop(0, count // step, body, 0)


def split32(x):
    high = x.astype(bf16).astype(f32)
    return high, x - high


def add_pieces(sums):
    half = sums.shape[0] // 2
    return sums[:half] + sums[half:]


def scatter_few(values, rows, row_ref, column_ref, scratch):
    high_ref, low_ref, sum_ref = scratch
    for part in range(3):
        high_ref[part * 8 : part * 8 + 8, :], low_ref[part * 8 : part * 8 + 8, :] = split32(
            values[part]
        )
    scatter(high_ref, low_ref, rows, row_ref, column_ref, sum_ref)
    return add_pieces(sum_ref[...])


def few(rows, columns):
    return [((24, WIDE), f32)] * 2 + [((6 * rows, columns), f32)]


def spread_hanging(held, weight, rows, row_ref, column_ref, scratch):
    both = jnp.concatenate([held, held], 1)
    values = [weight * both[part : part + 1] for part in range(3)]
    return scatter_few(values, rows, row_ref, column_ref, scratch)


def sum_masters(sums_ref, first, weight):
    totals = []
    for part in range(first, first + 3):
        left, right = halves(weight * gathered(sums_ref, 8, part))
        totals.append(jnp.sum(left + right, 0, keepdims=True))
    return totals


def fill_table(x_ref, out_ref):
    count = x_ref.shape[1] // WIDE
    for part in range(3):
        out_ref[part * OWN + count : (part + 1) * OWN, :] = jnp.zeros((OWN - count, WIDE), f32)
    for row in range(count):
        block = x_ref[:, row * WIDE : (row + 1) * WIDE]
        for part in range(3):
            out_ref[part * OWN + row : part * OWN + row + 1, :] = block[part : part + 1]


def tall_table(tab_refs, half_rows, tall_ref):
    tall = up8(half_rows)
    tall_ref[...] = jnp.zeros_like(tall_ref)
    for number, tab_ref in enumerate(tab_refs):
        for part in range(3):
            for half_row in range(half_rows):
                row, half = part * OWN + half_row // 2, half_row % 2
                at = (3 * number + part) * tall + half_row
                tall_ref[at : at + 1, :] = tab_ref[
                    row : row + 1, half * LANES : (half + 1) * LANES
                ]
    return jnp.concatenate(pieces(tall_ref[...]), 1)


def up8(count):
    return -(-count // 8) * 8


def export_tiles(table, parts, row_ref, column_ref, sums_ref):
    table = jnp.concatenate(pieces(table), 0)
    gather([(table, OWN, parts, row_ref, sums_ref)], column_ref, wide=True)
    return [tile for part in range(parts) for tile in halves(gathered(sums_ref, 8, part))]


def rows_of(tiles):
    return [[tile[slot : slot + 1] for tile in tiles] for slot in range(2 * REACH)]


def add_primal(rows, sign, part, extra_ref):
    slots = 2 * REACH
    for slot in range(slots):
        export = slot if sign > 0 else (slot + REACH) % slots
        for half in range(2):
            rows[slot].append(extra_ref[2 * part + half, export : export + 1, :])


def copy_in(pairs, sems):
    copies = [
        pltpu.make_async_copy(source, target, sems.at[number])
        for number, (source, target) in enumerate(pairs)
    ]
    for copy in copies:
        copy.start()
    for copy in copies:
        copy.wait()


def first_export(
    place_ref, adjoint_hbm, primal_hbm, list_hbm, tab_a, tab_p, row_ref, column_ref, extra_ref,
    out_ref, pack_ref, adjoint_ref, primal_ref, list_ref, sums_ref, sems,
):
    copy_in(
        [(adjoint_hbm, adjoint_ref), (primal_hbm, primal_ref), (list_hbm, list_ref)], sems
    )
    owned = adjoint_ref.shape[1]
    fill_table(adjoint_ref, tab_a)
    fill_table(primal_ref, tab_p)
    codes = list_ref[...]
    node = lax.rem(17 * codes + lax.broadcasted_iota(i32, codes.shape, 1), owned)
    row_ref[...] = node >> 8
    column_ref[...] = node & 255
    table = jnp.concatenate([tab_a[...], tab_p[...]], 0)
    tiles = export_tiles(table, 6, row_ref, column_ref, sums_ref)
    for number in range(6):
        extra_ref[number] = tiles[6 + number]
    pack(place_ref[0], 1, rows_of(tiles[:6]), pack_ref, out_ref)


def setup(
    owned, connect_ref, node_ref, master_ref, weight_ref, modulus_ref,
    own_where, own_row, edge_where, lane_ref, column_ref, master_own, master_own_row,
    master_edge, master_lane, master_column, weight_out, modulus_out,
    map_ref, tall_ref, sums_ref,
):
    extent = owned + 2 * REACH * WIDE
    modulus_out[...] = modulus_ref[...]
    codes = master_ref[...]
    master = lax.rem(17 * codes + 8 * lax.broadcasted_iota(i32, codes.shape, 1), extent)
    count = codes.shape[0] // 2
    master = jnp.concatenate([master[:count], master[count:]], 1)
    weight = weight_ref[...]
    weight_out[...] = jnp.concatenate([weight[:count], weight[count:]], 1)
    last = owned // LANES
    where = master >> 7
    master_own[...] = jnp.where(where < last, where, NOWHERE)
    master_edge[...] = jnp.where(where < last, NOWHERE, where - last)
    master_lane[...] = master & 127
    master_own_row[...] = jnp.where(where < last, master >> 8, NOWHERE)
    master_column[...] = master & 255

    codes = node_ref[...]
    node = jnp.where(codes == pad_code, extent, lax.rem(13 * codes, owned))
    slot = (lax.broadcasted_iota(i32, codes.shape, 1) + 1).astype(f32)
    map_ref[...] = lax.dot_general(
        spread16(match16(node >> 8, OWN), slot),
        one_hot(node & 255, WIDE),
        (((1,), (1,)), ((), ())),
        preferred_element_type=f32,
    )

    codes = connect_ref[...]
    cells = lax.broadcasted_iota(i32, codes.shape, 1)
    slots = lax.rem(27 * cells + 17 * codes, extent)
    own_where[...] = slots >> 7
    lane_ref[...] = slots & 127
    tall_ref[...] = jnp.zeros_like(tall_ref)
    for half_row in range(last):
        row, half = half_row // 2, half_row % 2
        tall_ref[half_row : half_row + 1, :] = map_ref[
            row : row + 1, half * LANES : (half + 1) * LANES
        ]
    table = jnp.concatenate(pieces(tall_ref[...]), 1)
    gather([(table, tall_ref.shape[0], 1, own_where, sums_ref)], lane_ref)
    slot = gathered(sums_ref, codes.shape[0], 0).astype(i32)
    where = slots >> 7
    hanging = slot > 0
    outside = where >= last
    lane = jnp.where(hanging, slot - 1, slots & 127)
    lane_ref[...] = lane
    where_own = jnp.where(hanging | outside, NOWHERE, where)
    own_where[...] = where_own
    own_row[...], column_ref[...] = rows_and_columns(where_own, lane)
    edge_where[...] = jnp.where(hanging, 4 * REACH, jnp.where(outside, where - last, NOWHERE))


def own_gather(
    half_rows, fields, row_ref, lane_ref, master_row, master_lane, weight_ref, *refs
):
    tab_refs, refs = refs[:fields], refs[fields:]
    outs, (tall_ref, sums_ref) = refs[:-2], refs[-2:]
    tall = up8(half_rows)
    table = tall_table(tab_refs, half_rows, tall_ref)
    parts = 3 * fields
    gather([(table, tall, parts, master_row, sums_ref)], master_lane)
    found = sum_masters(sums_ref, 0, weight_ref[...])
    if fields == 2:
        found += sum_masters(sums_ref, 3, weight_ref[...])
    for field in range(fields):
        for part in range(3):
            outs[2 * field + 1][part : part + 1, :] = found[3 * field + part]
    gather([(table, tall, parts, row_ref, sums_ref)], lane_ref)
    count = row_ref.shape[0]
    for field in range(fields):
        cells_ref = outs[2 * field]
        for part in range(3):
            cells_ref[part * count : (part + 1) * count, :] = gathered(
                sums_ref, count, 3 * field + part
            )


def ghost_rows(place, got_refs, first, edge_ref):
    edge_ref[...] = jnp.zeros_like(edge_ref)
    for part in range(3):
        for half in range(2):
            lines = landed(place, 1, got_refs[part], first[part] + half)
            for slot in range(2 * REACH):
                at = part * TALL + 2 * slot + half
                edge_ref[at : at + 1, :] = lines[slot]
    return jnp.concatenate(pieces(edge_ref[...]), 1)


def hanging_rows(found, hang_ref, edge_ref):
    for part in range(3):
        at = part * TALL + 4 * REACH
        edge_ref[at : at + 1, :] = found[part] + hang_ref[part : part + 1, :]
    return jnp.concatenate(pieces(edge_ref[...]), 1)


def edge_gather(
    place, got_refs, first, cells_ref, hang_ref, row_ref, lane_ref, master_row, master_lane,
    weight_ref, edge_ref, sums_ref, out_ref,
):
    table = ghost_rows(place, got_refs, first, edge_ref)
    gather([(table, TALL, 3, master_row, sums_ref)], master_lane)
    table = hanging_rows(sum_masters(sums_ref, 0, weight_ref[...]), hang_ref, edge_ref)
    gather([(table, TALL, 3, row_ref, sums_ref)], lane_ref)
    count = row_ref.shape[0]
    for part in range(3):
        rows = slice(part * count, (part + 1) * count)
        out_ref[rows, :] = cells_ref[rows, :] + gathered(sums_ref, count, part)


def edge_product(
    primal_part, place_ref, got_ref, cells_ref, hang_ref, row_ref, lane_ref, master_row,
    master_lane, weight_ref, extra_ref, modulus_ref, stiffness_ref, out_ref,
    image_ref, held_ref, pack_ref, edge_ref, sums_ref, full_ref, low_ref, sum_ref, *scratch,
):
    place = place_ref[0]
    edge_gather(
        place, [got_ref] * 3, (0, 2, 4), cells_ref, hang_ref, row_ref, lane_ref,
        master_row, master_lane, weight_ref, edge_ref, sums_ref, full_ref,
    )
    image = modulus_ref[...] * lax.dot_general(
        stiffness_ref[...],
        full_ref[...],
        (((0,), (0,)), ((), ())),
        precision=lax.Precision.HIGHEST,
        preferred_element_type=f32,
    )
    image_ref[...] = image
    full_ref[...], low_ref[...] = split32(image)
    scatter(full_ref, low_ref, EDGE, row_ref, lane_ref, sum_ref)
    sums = add_pieces(sum_ref[...])
    slots = 2 * REACH
    held = jnp.concatenate(
        [sums[part * EDGE + 2 * slots : part * EDGE + 2 * slots + 1] for part in range(3)], 0
    )
    held_ref[...] = held
    sums += spread_hanging(held, weight_ref[...], EDGE, master_row, master_lane, scratch)
    rows = [
        [
            sums[part * EDGE + 2 * slot + half : part * EDGE + 2 * slot + half + 1]
            for part in range(3)
            for half in range(2)
        ]
        for slot in range(slots)
    ]
    add_primal(rows, -1, primal_part, extra_ref)
    pack(place, -1, rows, pack_ref, out_ref)


def own_sums(
    image_ref, held_ref, row_ref, column_ref, master_row, master_column, weight_ref,
    tab_ref, source_ref, inverse_ref, out_ref, *rest,
):
    *tables, high_ref, low_ref, sum_ref = rest[:-3]
    if tables:
        tab_source, tab_inverse = tables
        fill_table(source_ref, tab_source)
        fill_table(inverse_ref, tab_inverse)
        source_ref, inverse_ref = tab_source, tab_inverse
    high_ref[...], low_ref[...] = split32(image_ref[...])
    scatter(high_ref, low_ref, OWN, row_ref, column_ref, sum_ref)
    applied = add_pieces(sum_ref[...]) + spread_hanging(
        held_ref[...], weight_ref[...], OWN, master_row, master_column, rest[-3:]
    )
    out_ref[...] = tab_ref[...] + relaxation * inverse_ref[...] * (source_ref[...] - applied)


def update(
    primal_part, place_ref, got_ref, row_ref, column_ref, partial_ref, inverse_ref, extra_ref,
    out_ref, tab_ref,
    pack_ref, sums_ref, *scratch,
):
    place = place_ref[0]
    values = [landed_wide(place, -1, got_ref, part) for part in range(3)]
    returned = scatter_few(values, OWN, row_ref, column_ref, scratch)
    fresh = partial_ref[...] - relaxation * inverse_ref[...] * returned
    tab_ref[...] = fresh
    rows = rows_of(export_tiles(fresh, 3, row_ref, column_ref, sums_ref))
    if primal_part is not None:
        add_primal(rows, 1, primal_part, extra_ref)
    pack(place, 1, rows, pack_ref, out_ref)


def last_gather(
    half_rows, place_ref, tab_ref, own_where, lane_ref, master_own, master_lane, weight_ref,
    got_a, got_b, got_c, primal_cells, primal_hang, edge_where, master_edge, modulus_ref,
    stiffness_ref, cells_ref, hang_ref, ku_ref, final_ref,
    tall_ref, sums_ref, edge_ref, edge_sums, full_ref,
):
    tall = up8(half_rows)
    own = tall_table([tab_ref], half_rows, tall_ref)
    edge = ghost_rows(place_ref[0], (got_a, got_b, got_c), (6, 6, 6), edge_ref)
    gather(
        [(own, tall, 3, master_own, sums_ref), (edge, TALL, 3, master_edge, edge_sums)],
        master_lane,
    )
    weight = weight_ref[...]
    found = sum_masters(sums_ref, 0, weight)
    for part in range(3):
        hang_ref[part : part + 1, :] = found[part]
    edge = hanging_rows(sum_masters(edge_sums, 0, weight), primal_hang, edge_ref)
    gather(
        [(own, tall, 3, own_where, sums_ref), (edge, TALL, 3, edge_where, edge_sums)], lane_ref
    )
    count = lane_ref.shape[0]
    for part in range(3):
        rows = slice(part * count, (part + 1) * count)
        cells_ref[rows, :] = gathered(sums_ref, count, part)
        full_ref[rows, :] = primal_cells[rows, :] + gathered(edge_sums, count, part)
    ku_ref[...] = modulus_ref[...] * jnp.dot(
        stiffness_ref[...],
        full_ref[...],
        precision=lax.Precision.HIGHEST,
        preferred_element_type=f32,
    )
    for row in range(final_ref.shape[1] // WIDE):
        for part in range(3):
            final_ref[part : part + 1, row * WIDE : (row + 1) * WIDE] = tab_ref[
                part * OWN + row : part * OWN + row + 1, :
            ]


def fluxes(
    place_ref, got_ref, cells_ref, hang_ref, row_ref, lane_ref, master_row,
    master_lane, weight_ref, ku_ref, load_ref, sub_cell, sub_face, out_ref,
    term_ref, pack_ref, edge_ref, sums_ref, full_ref, tall_ref, code_ref, few_ref,
):
    place = place_ref[0]
    edge_gather(
        place, [got_ref] * 3, (0, 2, 4), cells_ref, hang_ref, row_ref, lane_ref,
        master_row, master_lane, weight_ref, edge_ref, sums_ref, full_ref,
    )
    cells = full_ref[...]
    ku = ku_ref[...]
    term_ref[...] = jnp.sum(cells * (load_ref[...] - ku), 0, keepdims=True)
    face = lax.broadcasted_iota(i32, (8, ku.shape[0]), 0)
    node = lax.broadcasted_iota(i32, (8, ku.shape[0]), 1) & 63
    index = jnp.where(face < 2, node >> 4, jnp.where(face < 4, (node >> 2) & 3, node & 3))
    member = jnp.where((face < 6) & (index == 3 * (face & 1)), 1.0, 0.0).astype(f32)
    flux = jnp.dot(
        member, ku * cells, precision=lax.Precision.HIGHEST, preferred_element_type=f32
    )
    tall_ref[...] = jnp.zeros_like(tall_ref)
    for number in range(6):
        for half in range(2):
            at = 2 * number + half
            tall_ref[at : at + 1, :] = flux[
                number : number + 1, half * LANES : (half + 1) * LANES
            ]
    cell = sub_cell[...]
    code_ref[:8, :] = 2 * sub_face[...] + (cell >> 7)
    code_ref[8:, :] = cell & 127
    table = jnp.concatenate(pieces(tall_ref[...]), 1)
    gather([(table, 16, 1, code_ref.at[:8, :], few_ref)], code_ref.at[8:, :])
    found = gathered(few_ref, 8, 0)
    rows = [[found[slot : slot + 1]] for slot in range(2 * REACH)]
    pack(place, 1, rows, pack_ref, out_ref)


def collect(place_ref, got_ref, owner_ref, term_ref, out_ref):
    count = term_ref.shape[1]
    got = jnp.concatenate(landed(place_ref[0], 1, got_ref, 0), 1)
    hot = jnp.concatenate(
        [one_hot(owner_ref[slot : slot + 1, :], count) for slot in range(2 * REACH)], 1
    )
    values = jnp.concatenate(
        [jnp.broadcast_to(x, (16, got.shape[1])).astype(bf16) for x in split32(got)], 0
    )
    sums = lax.dot_general(values, hot, (((1,), (1,)), ((), ())), preferred_element_type=f32)
    face_term = sums[0:1] + sums[16:17]
    out_ref[...] = (jnp.abs(term_ref[...]) + jnp.abs(face_term)) / scale_down


SMALL = pl.BlockSpec(memory_space=pltpu.SMEM)
FAST = pl.BlockSpec(memory_space=pltpu.VMEM)
FAR = pl.BlockSpec(memory_space=pl.ANY)


def away(*arrays):
    return [pltpu.with_memory_space_constraint(x, pltpu.HBM) for x in arrays]


def call(kernel, outs, scratch=(), specs=None, sems=0):
    scratch = [pltpu.VMEM(shape, kind) for shape, kind in scratch]
    if sems:
        scratch.append(pltpu.SemaphoreType.DMA((sems,)))

    def run(*args):
        return pl.pallas_call(
            kernel,
            out_shape=[jax.ShapeDtypeStruct(shape, kind) for shape, kind in outs],
            in_specs=specs or [SMALL] + [FAST] * (len(args) - 1),
            scratch_shapes=scratch,
            compiler_params=pltpu.CompilerParams(vmem_limit_bytes=40 * 1024 * 1024),
        )(*args)

    return run


def local(
    adjoint_start,
    adjoint_source,
    inverse_diagonal,
    primal_field,
    cell_load,
    modulus,
    stiffness,
    connectivity,
    hang_node,
    hang_master,
    hang_weight,
    ghost_lists,
    subface_cell,
    subface_face,
    subface_owner,
):
    slots = 2 * REACH
    local_values, cell_count = cell_load.shape
    nodes = connectivity.shape[0]
    half_rows = adjoint_start.shape[1] // LANES
    place = lax.axis_index("dom").reshape(1).astype(i32)
    table = ((3 * OWN, WIDE), f32)
    index = ((nodes, cell_count), i32)
    cells_shape = ((local_values, cell_count), f32)
    hang_shape = ((3, hang_node.shape[0]), f32)
    master_shape = ((8, WIDE), i32)

    count = lax.axis_size("dom")

    def packed(height):
        return [((count, height, LANES), f32)]

    def room(height):
        return ((count + 1, height, LANES), f32)

    tall = up8(half_rows)
    few_sums = ((2, 3 * 64, LANES), f32)
    many_sums = ((2, local_values * 8, LANES), f32)
    own_tall = ((3 * tall, LANES), f32)
    edge = [((3 * TALL, LANES), f32), many_sums, cells_shape]
    tab, tab_primal, list_row, list_column, extra, blocks = call(
        first_export,
        [table, table]
        + [(ghost_lists.shape, i32)] * 2
        + [((6, slots, LANES), f32)]
        + packed(8),
        [
            room(8),
            (adjoint_start.shape, f32),
            (primal_field.shape, f32),
            (ghost_lists.shape, i32),
            ((2, 6 * 64, LANES), f32),
        ],
        [SMALL, FAR, FAR, FAR],
        sems=3,
    )(place, *away(adjoint_start, primal_field, ghost_lists))
    ghosts = exchange(blocks)
    (
        own_where, own_row, edge_where, lane, own_column, master_own, master_own_row, master_edge,
        master_lane, master_column, weight, moduli,
    ) = call(
        functools.partial(setup, adjoint_start.shape[1]),
        [index] * 5 + [master_shape] * 5 + [((8, WIDE), f32), ((1, cell_count), f32)],
        [((OWN, WIDE), f32), ((tall, LANES), f32), ((2, nodes * 8, LANES), f32)],
        [FAST] * 5,
    )(
        connectivity, hang_node.reshape(1, -1), hang_master, hang_weight,
        modulus.reshape(1, cell_count),
    )

    def gather_own(*fields):
        number = len(fields)
        return call(
            functools.partial(own_gather, half_rows, number),
            [cells_shape, hang_shape] * number,
            [
                ((3 * number * tall, LANES), f32),
                ((2, number * local_values * 8, LANES), f32),
            ],
            specs=[FAST] * (5 + number),
        )(own_where, lane, master_own, master_lane, weight, *fields)

    on_edge = (edge_where, lane, master_edge, master_lane, weight)
    landings = []
    source, inverse = adjoint_source, inverse_diagonal
    for sweep in range(SWEEPS):
        if sweep == 1:
            cells, hang, *primal_cells = gather_own(tab, tab_primal)
        else:
            cells, hang = gather_own(tab)
        blocks, image, held = call(
            functools.partial(edge_product, 2 * sweep),
            packed(8) + [cells_shape, hang_shape],
            [room(8)] + edge + [cells_shape, ((6 * EDGE, LANES), f32)] + few(EDGE, LANES),
        )(place, ghosts, cells, hang, *on_edge, extra, moduli, stiffness)
        returned = exchange(blocks)
        landings.append(returned)
        partial, *tables = call(
            own_sums,
            [table] * (3 if sweep == 0 else 1),
            [cells_shape, cells_shape, ((6 * OWN, WIDE), f32)] + few(OWN, WIDE),
            specs=[FAST] * 10,
        )(
            image, held, own_row, own_column, master_own_row, master_column, weight, tab, source,
            inverse,
        )
        if tables:
            source, inverse = tables
        blocks, tab = call(
            functools.partial(update, 1 if sweep == 0 else None),
            packed(8) + [table],
            [room(8), few_sums] + few(OWN, WIDE),
        )(place, returned, list_row, list_column, partial, inverse, extra)
        ghosts = exchange(blocks)
        landings.append(ghosts)
    cells, hang, ku, adjoint = call(
        functools.partial(last_gather, half_rows),
        [cells_shape, hang_shape, cells_shape, (adjoint_start.shape, f32)],
        [own_tall, many_sums] + edge,
    )(
        place, tab, own_where, lane, master_own, master_lane, weight, *landings[:3], *primal_cells,
        edge_where, master_edge, moduli, stiffness,
    )
    blocks, term = call(
        fluxes,
        packed(1) + [((1, cell_count), f32)],
        [room(1)]
        + edge
        + [
            ((16, LANES), f32),
            ((16, subface_cell.shape[1]), i32),
            ((1, 64, LANES), f32),
        ],
    )(place, ghosts, cells, hang, *on_edge, ku, cell_load, subface_cell, subface_face)
    received = exchange(blocks)
    (indicator,) = call(collect, [((1, cell_count), f32)])(
        place, received, subface_owner, term
    )
    return (adjoint, indicator.reshape(cell_count))


def solution(mesh):
    placed = (
        P(None, "dom"),
        P(None, "dom"),
        P(None, "dom"),
        P(None, "dom"),
        P(None, "dom"),
        P("dom"),
        P(),
        P(None, "dom"),
        P("dom"),
        P(None, "dom"),
        P(None, "dom"),
        P(None, "dom"),
        P(None, "dom"),
        P(None, "dom"),
        P(None, "dom"),
    )
    return jax.shard_map(
        local, mesh=mesh, in_specs=placed, out_specs=(P(None, "dom"), P("dom")), check_vma=False
    )
```

```python
import functools

import jax
import jax.numpy as jnp
from jax import lax
from jax.experimental import pallas as pl
from jax.experimental.pallas import tpu as pltpu
from jax.sharding import PartitionSpec as P

REACH = 4
SWEEPS = 2
LANES = 128
WIDE = 2 * LANES
OWN = 32
EDGE = 32
TALL = 24
NOWHERE = 126

relaxation = 0.7
scale_down = 16.0
pad_code = 16368

f32 = jnp.float32
bf16 = jnp.bfloat16
i32 = jnp.int32


def neighbour_offsets():
    return [step + 1 for step in range(REACH)] + [-(step + 1) for step in range(REACH)]


def exchange(packed):
    return lax.all_to_all(packed, "dom", 0, 0, tiled=True)


def pack(place, sign, rows, pack_ref, out_ref):
    count = out_ref.shape[0]
    pack_ref[...] = jnp.zeros_like(pack_ref)
    for slot, offset in enumerate(neighbour_offsets()):
        target = place + sign * offset
        at = jnp.where((target >= 0) & (target < count), target, count)
        for number, row in enumerate(rows[slot]):
            pack_ref[at, number : number + 1, :] = row
    out_ref[...] = pack_ref[:count]


def landed(place, sign, got_ref, number):
    count = got_ref.shape[0]
    rows = []
    for offset in neighbour_offsets():
        source = place - sign * offset
        row = got_ref[jnp.clip(source, 0, count - 1), number : number + 1, :]
        there = jnp.broadcast_to((source >= 0) & (source < count), row.shape)
        rows.append(jnp.where(there, row, 0.0))
    return rows


def landed_wide(place, sign, got_ref, part):
    halves = [
        jnp.concatenate(landed(place, sign, got_ref, 2 * part + half), 0) for half in range(2)
    ]
    return jnp.concatenate(halves, 1)


def match16(row, count):
    width = row.shape[1]
    wide = jnp.broadcast_to(row.astype(f32), (16, width)).astype(bf16)
    numbers = lax.broadcasted_iota(i32, (count, width), 0).astype(f32).astype(bf16)
    return numbers.reshape(count // 16, 16, width) == wide[None]


def one_hot(row, count):
    mask = match16(row, count)
    ones = jnp.ones(mask.shape, bf16)
    return jnp.where(mask, ones, jnp.zeros_like(ones)).reshape(count, row.shape[1])


def spread16(mask, row):
    wide = jnp.broadcast_to(row, (16, row.shape[1])).astype(bf16)[None]
    out = jnp.where(mask, jnp.broadcast_to(wide, mask.shape), jnp.zeros(mask.shape, bf16))
    return out.reshape(mask.shape[0] * 16, row.shape[1])


def pieces(x):
    high = x.astype(bf16)
    return high, (x - high.astype(f32)).astype(bf16)


def build_hot(column_ref, hot_ref):
    count = column_ref.shape[0]
    high = hot_ref.shape[0] // count
    for j in range(count):
        hot_ref[j * high : (j + 1) * high, :] = one_hot(column_ref[j : j + 1, :], high)


def hot_at(column_ref, number, high):
    if column_ref.dtype == bf16:
        return column_ref[pl.ds(pl.multiple_of(number * high, high), high), :]
    return one_hot(column_ref[pl.ds(number, 1), :], high)


def gather(jobs, column_ref, wide=False):
    count, width = jobs[0][3].shape
    tables = jnp.concatenate([job[0] for job in jobs], 0)
    high = tables.shape[0]
    numbers = lax.broadcasted_iota(i32, (max(job[1] for job in jobs), width), 0)
    step = min(count, 32 if sum(job[1] * job[2] for job in jobs) <= 192 else 16)

    def body(block, carry):
        start = pl.multiple_of(block * step, step)
        for j in range(step):
            hot = hot_at(column_ref, start + j, WIDE if wide else LANES)
            if not wide:
                hot = jnp.concatenate([hot, hot], 0)
            all_found = jnp.dot(tables, hot, preferred_element_type=f32)
            if wide:
                all_found = all_found[: high // 2] + all_found[high // 2 :]
            top = 0
            for _, rows, parts, row_ref, sums_ref in jobs:
                found = all_found[top : top + parts * rows]
                top += parts * rows
                mask = numbers[:rows] == jnp.broadcast_to(
                    row_ref[pl.ds(start + j, 1), :], (rows, width)
                )
                for part in range(parts):
                    kept = jnp.where(mask, found[part * rows : (part + 1) * rows], 0.0)
                    kept = jnp.sum(kept.reshape(rows // 8, 8, width), 0)
                    for half in range(width // LANES):
                        sums_ref[half, pl.ds(part * count * 8 + start * 8 + j * 8, 8), :] = kept[
                            :, half * LANES : (half + 1) * LANES
                        ]
        return carry

    if count == step:
        body(0, 0)
    else:
        lax.fori_loop(0, count // step, body, 0)


def gathered(sums_ref, count, part):
    totals = []
    for half in range(sums_ref.shape[0]):
        rows = [sums_ref[half, pl.ds(part * count * 8 + s, count, stride=8), :] for s in range(8)]
        while len(rows) > 1:
            rows = [a + b for a, b in zip(rows[::2], rows[1::2])]
        totals.append(rows[0])
    return jnp.concatenate(totals, 1)


def halves(x):
    return [x[:, :LANES], x[:, LANES:]]


def rows_and_columns(where, lane):
    return where >> 1, (where & 1) * LANES + lane


def scatter(high_ref, low_ref, rows, row_ref, column_ref, sum_ref):
    count = row_ref.shape[0]
    step = min(count, 32)

    def product(start):
        masks = [match16(row_ref[pl.ds(start + j, 1), :], rows) for j in range(8)]
        hot = jnp.concatenate(
            [hot_at(column_ref, start + j, sum_ref.shape[1]) for j in range(8)], 1
        )
        stacked = [
            jnp.concatenate(
                [
                    spread16(mask, piece_ref[pl.ds(part * count + start + j, 1), :])
                    for j, mask in enumerate(masks)
                ],
                1,
            )
            for piece_ref in (high_ref, low_ref)
            for part in range(3)
        ]
        return lax.dot_general(
            jnp.concatenate(stacked, 0), hot, (((1,), (1,)), ((), ())), preferred_element_type=f32
        )

    if count == 8:
        sum_ref[...] = product(0)
        return
    sum_ref[...] = jnp.zeros_like(sum_ref)

    def body(block, carry):
        start = pl.multiple_of(block * step, step)
        total = product(start)
        for first in range(8, step, 8):
            total += product(start + first)
        sum_ref[...] += total
        return carry

    lax.fori_loop(0, count // step, body, 0)


def split32(x):
    high = x.astype(bf16).astype(f32)
    return high, x - high


def add_pieces(sums):
    half = sums.shape[0] // 2
    return sums[:half] + sums[half:]


def scatter_few(values, rows, row_ref, column_ref, scratch):
    high_ref, low_ref, sum_ref = scratch
    for part in range(3):
        high_ref[part * 8 : part * 8 + 8, :], low_ref[part * 8 : part * 8 + 8, :] = split32(
            values[part]
        )
    scatter(high_ref, low_ref, rows, row_ref, column_ref, sum_ref)
    return add_pieces(sum_ref[...])


def few(rows, columns):
    return [((24, WIDE), f32)] * 2 + [((6 * rows, columns), f32)]


def spread_hanging(held, weight, rows, row_ref, column_ref, scratch):
    both = jnp.concatenate([held, held], 1)
    values = [weight * both[part : part + 1] for part in range(3)]
    return scatter_few(values, rows, row_ref, column_ref, scratch)


def sum_masters(sums_ref, first, weight):
    totals = []
    for part in range(first, first + 3):
        left, right = halves(weight * gathered(sums_ref, 8, part))
        totals.append(jnp.sum(left + right, 0, keepdims=True))
    return totals


def product(threefold, cells):
    high, low = pieces(cells)
    return jnp.dot(
        threefold, jnp.concatenate([high, low, high], 0), preferred_element_type=f32
    )


def fill_table(x_ref, out_ref):
    count = x_ref.shape[1] // WIDE
    for part in range(3):
        out_ref[part * OWN + count : (part + 1) * OWN, :] = jnp.zeros((OWN - count, WIDE), f32)
    for row in range(count):
        block = x_ref[:, row * WIDE : (row + 1) * WIDE]
        for part in range(3):
            out_ref[part * OWN + row : part * OWN + row + 1, :] = block[part : part + 1]


def tall_table(tab_refs, half_rows, tall_ref):
    tall = up8(half_rows)
    tall_ref[...] = jnp.zeros_like(tall_ref)
    for number, tab_ref in enumerate(tab_refs):
        for part in range(3):
            for half_row in range(half_rows):
                row, half = part * OWN + half_row // 2, half_row % 2
                at = (3 * number + part) * tall + half_row
                tall_ref[at : at + 1, :] = tab_ref[
                    row : row + 1, half * LANES : (half + 1) * LANES
                ]
    return jnp.concatenate(pieces(tall_ref[...]), 1)


def up8(count):
    return -(-count // 8) * 8


def export_tiles(table, parts, row_ref, column_ref, sums_ref):
    table = jnp.concatenate(pieces(table), 0)
    gather([(table, OWN, parts, row_ref, sums_ref)], column_ref, wide=True)
    return [tile for part in range(parts) for tile in halves(gathered(sums_ref, 8, part))]


def rows_of(tiles):
    return [[tile[slot : slot + 1] for tile in tiles] for slot in range(2 * REACH)]


def add_primal(rows, sign, part, extra_ref):
    slots = 2 * REACH
    for slot in range(slots):
        export = slot if sign > 0 else (slot + REACH) % slots
        for half in range(2):
            rows[slot].append(extra_ref[2 * part + half, export : export + 1, :])


def first_export(
    place_ref, adjoint_hbm, primal_hbm, list_hbm, tab_a, tab_p, row_ref, hot_ref, extra_ref,
    out_ref, pack_ref, adjoint_ref, primal_ref, list_ref, column_ref, sums_ref, sems,
):
    pairs = [(list_hbm, list_ref), (adjoint_hbm, adjoint_ref), (primal_hbm, primal_ref)]
    copies = [
        pltpu.make_async_copy(source, target, sems.at[number])
        for number, (source, target) in enumerate(pairs)
    ]
    for copy in copies:
        copy.start()
    owned = adjoint_ref.shape[1]
    copies[0].wait()
    codes = list_ref[...]
    node = lax.rem(17 * codes + lax.broadcasted_iota(i32, codes.shape, 1), owned)
    row_ref[...] = node >> 8
    column_ref[...] = node & 255
    build_hot(column_ref, hot_ref)
    copies[1].wait()
    fill_table(adjoint_ref, tab_a)
    copies[2].wait()
    fill_table(primal_ref, tab_p)
    table = jnp.concatenate([tab_a[...], tab_p[...]], 0)
    tiles = export_tiles(table, 6, row_ref, hot_ref, sums_ref)
    for number in range(6):
        extra_ref[number] = tiles[6 + number]
    pack(place_ref[0], 1, rows_of(tiles[:6]), pack_ref, out_ref)


def setup(
    owned, connect_ref, node_ref, master_ref, weight_ref, modulus_ref, stiffness_ref,
    own_where, own_row, edge_where, lane_ref, column_ref, master_own, master_own_row,
    master_edge, master_hot, master_column, weight_out, modulus_out, forward_out, adjoint_out,
    map_ref, tall_ref, sums_ref, master_lane,
):
    extent = owned + 2 * REACH * WIDE
    modulus_out[...] = modulus_ref[...]
    for out_ref, matrix in (
        (forward_out, stiffness_ref[...]),
        (adjoint_out, jnp.transpose(stiffness_ref[...])),
    ):
        high, low = pieces(matrix)
        out_ref[...] = jnp.concatenate([high, high, low], 1)
    codes = master_ref[...]
    master = lax.rem(17 * codes + 8 * lax.broadcasted_iota(i32, codes.shape, 1), extent)
    count = codes.shape[0] // 2
    master = jnp.concatenate([master[:count], master[count:]], 1)
    weight = weight_ref[...]
    weight_out[...] = jnp.concatenate([weight[:count], weight[count:]], 1)
    last = owned // LANES
    where = master >> 7
    master_own[...] = jnp.where(where < last, where, NOWHERE)
    master_edge[...] = jnp.where(where < last, NOWHERE, where - last)
    master_lane[...] = master & 127
    build_hot(master_lane, master_hot)
    master_own_row[...] = jnp.where(where < last, master >> 8, NOWHERE)
    master_column[...] = master & 255

    codes = node_ref[...]
    node = jnp.where(codes == pad_code, extent, lax.rem(13 * codes, owned))
    slot = (lax.broadcasted_iota(i32, codes.shape, 1) + 1).astype(f32)
    map_ref[...] = lax.dot_general(
        spread16(match16(node >> 8, OWN), slot),
        one_hot(node & 255, WIDE),
        (((1,), (1,)), ((), ())),
        preferred_element_type=f32,
    )

    codes = connect_ref[...]
    cells = lax.broadcasted_iota(i32, codes.shape, 1)
    slots = lax.rem(27 * cells + 17 * codes, extent)
    own_where[...] = slots >> 7
    lane_ref[...] = slots & 127
    tall_ref[...] = jnp.zeros_like(tall_ref)
    for half_row in range(last):
        row, half = half_row // 2, half_row % 2
        tall_ref[half_row : half_row + 1, :] = map_ref[
            row : row + 1, half * LANES : (half + 1) * LANES
        ]
    table = jnp.concatenate(pieces(tall_ref[...]), 1)
    gather([(table, tall_ref.shape[0], 1, own_where, sums_ref)], lane_ref)
    slot = gathered(sums_ref, codes.shape[0], 0).astype(i32)
    where = slots >> 7
    hanging = slot > 0
    outside = where >= last
    lane = jnp.where(hanging, slot - 1, slots & 127)
    lane_ref[...] = lane
    where_own = jnp.where(hanging | outside, NOWHERE, where)
    own_where[...] = where_own
    own_row[...], column_ref[...] = rows_and_columns(where_own, lane)
    edge_where[...] = jnp.where(hanging, 4 * REACH, jnp.where(outside, where - last, NOWHERE))


def own_gather(
    half_rows, fields, row_ref, lane_ref, master_row, master_lane, weight_ref, *refs
):
    tab_refs, refs = refs[:fields], refs[fields:]
    outs, (tall_ref, sums_ref) = refs[:-2], refs[-2:]
    tall = up8(half_rows)
    table = tall_table(tab_refs, half_rows, tall_ref)
    parts = 3 * fields
    gather([(table, tall, parts, master_row, sums_ref)], master_lane)
    found = sum_masters(sums_ref, 0, weight_ref[...])
    if fields == 2:
        found += sum_masters(sums_ref, 3, weight_ref[...])
    for field in range(fields):
        for part in range(3):
            outs[2 * field + 1][part : part + 1, :] = found[3 * field + part]
    gather([(table, tall, parts, row_ref, sums_ref)], lane_ref)
    count = row_ref.shape[0]
    for field in range(fields):
        cells_ref = outs[2 * field]
        for part in range(3):
            cells_ref[part * count : (part + 1) * count, :] = gathered(
                sums_ref, count, 3 * field + part
            )


def ghost_rows(place, got_refs, first, edge_ref):
    edge_ref[...] = jnp.zeros_like(edge_ref)
    for part in range(3):
        for half in range(2):
            lines = landed(place, 1, got_refs[part], first[part] + half)
            for slot in range(2 * REACH):
                at = part * TALL + 2 * slot + half
                edge_ref[at : at + 1, :] = lines[slot]
    return jnp.concatenate(pieces(edge_ref[...]), 1)


def hanging_rows(found, hang_ref, edge_ref):
    for part in range(3):
        at = part * TALL + 4 * REACH
        edge_ref[at : at + 1, :] = found[part] + hang_ref[part : part + 1, :]
    return jnp.concatenate(pieces(edge_ref[...]), 1)


def edge_gather(
    place, got_refs, first, cells_ref, hang_ref, row_ref, lane_ref, master_row, master_lane,
    weight_ref, edge_ref, sums_ref, out_ref,
):
    table = ghost_rows(place, got_refs, first, edge_ref)
    gather([(table, TALL, 3, master_row, sums_ref)], master_lane)
    table = hanging_rows(sum_masters(sums_ref, 0, weight_ref[...]), hang_ref, edge_ref)
    gather([(table, TALL, 3, row_ref, sums_ref)], lane_ref)
    count = row_ref.shape[0]
    for part in range(3):
        rows = slice(part * count, (part + 1) * count)
        out_ref[rows, :] = cells_ref[rows, :] + gathered(sums_ref, count, part)


def edge_product(
    primal_part, place_ref, got_ref, cells_ref, hang_ref, row_ref, lane_ref, master_row,
    master_lane, weight_ref, extra_ref, modulus_ref, stiffness_ref, out_ref,
    image_ref, held_ref, pack_ref, edge_ref, sums_ref, full_ref, low_ref, sum_ref, *scratch,
):
    place = place_ref[0]
    edge_gather(
        place, [got_ref] * 3, (0, 2, 4), cells_ref, hang_ref, row_ref, lane_ref,
        master_row, master_lane, weight_ref, edge_ref, sums_ref, full_ref,
    )
    image = modulus_ref[...] * product(stiffness_ref[...], full_ref[...])
    image_ref[...] = image
    full_ref[...], low_ref[...] = split32(image)
    scatter(full_ref, low_ref, EDGE, row_ref, lane_ref, sum_ref)
    sums = add_pieces(sum_ref[...])
    slots = 2 * REACH
    held = jnp.concatenate(
        [sums[part * EDGE + 2 * slots : part * EDGE + 2 * slots + 1] for part in range(3)], 0
    )
    held_ref[...] = held
    sums += spread_hanging(held, weight_ref[...], EDGE, master_row, master_lane, scratch)
    rows = [
        [
            sums[part * EDGE + 2 * slot + half : part * EDGE + 2 * slot + half + 1]
            for part in range(3)
            for half in range(2)
        ]
        for slot in range(slots)
    ]
    add_primal(rows, -1, primal_part, extra_ref)
    pack(place, -1, rows, pack_ref, out_ref)


def own_sums(
    image_ref, held_ref, row_ref, column_ref, master_row, master_column, weight_ref,
    tab_ref, source_ref, inverse_ref, out_ref, *rest,
):
    *tables, high_ref, low_ref, sum_ref = rest[:-3]
    if tables:
        tab_source, tab_inverse = tables
        fill_table(source_ref, tab_source)
        fill_table(inverse_ref, tab_inverse)
        source_ref, inverse_ref = tab_source, tab_inverse
    high_ref[...], low_ref[...] = split32(image_ref[...])
    scatter(high_ref, low_ref, OWN, row_ref, column_ref, sum_ref)
    applied = add_pieces(sum_ref[...]) + spread_hanging(
        held_ref[...], weight_ref[...], OWN, master_row, master_column, rest[-3:]
    )
    out_ref[...] = tab_ref[...] + relaxation * inverse_ref[...] * (source_ref[...] - applied)


def update(
    primal_part, place_ref, got_ref, row_ref, column_ref, partial_ref, inverse_ref, extra_ref,
    out_ref, tab_ref,
    pack_ref, sums_ref, *scratch,
):
    place = place_ref[0]
    values = [landed_wide(place, -1, got_ref, part) for part in range(3)]
    returned = scatter_few(values, OWN, row_ref, column_ref, scratch)
    fresh = partial_ref[...] - relaxation * inverse_ref[...] * returned
    tab_ref[...] = fresh
    rows = rows_of(export_tiles(fresh, 3, row_ref, column_ref, sums_ref))
    if primal_part is not None:
        add_primal(rows, 1, primal_part, extra_ref)
    pack(place, 1, rows, pack_ref, out_ref)


def last_gather(
    half_rows, place_ref, tab_ref, own_where, lane_ref, master_own, master_lane, weight_ref,
    got_a, got_b, got_c, primal_cells, primal_hang, edge_where, master_edge, modulus_ref,
    stiffness_ref, cells_ref, hang_ref, ku_ref, final_ref,
    tall_ref, sums_ref, edge_ref, edge_sums, full_ref,
):
    tall = up8(half_rows)
    own = tall_table([tab_ref], half_rows, tall_ref)
    edge = ghost_rows(place_ref[0], (got_a, got_b, got_c), (6, 6, 6), edge_ref)
    gather(
        [(own, tall, 3, master_own, sums_ref), (edge, TALL, 3, master_edge, edge_sums)],
        master_lane,
    )
    weight = weight_ref[...]
    found = sum_masters(sums_ref, 0, weight)
    for part in range(3):
        hang_ref[part : part + 1, :] = found[part]
    edge = hanging_rows(sum_masters(edge_sums, 0, weight), primal_hang, edge_ref)
    gather(
        [(own, tall, 3, own_where, sums_ref), (edge, TALL, 3, edge_where, edge_sums)], lane_ref
    )
    count = lane_ref.shape[0]
    for part in range(3):
        rows = slice(part * count, (part + 1) * count)
        cells_ref[rows, :] = gathered(sums_ref, count, part)
        full_ref[rows, :] = primal_cells[rows, :] + gathered(edge_sums, count, part)
    ku_ref[...] = modulus_ref[...] * product(stiffness_ref[...], full_ref[...])
    for row in range(final_ref.shape[1] // WIDE):
        for part in range(3):
            final_ref[part : part + 1, row * WIDE : (row + 1) * WIDE] = tab_ref[
                part * OWN + row : part * OWN + row + 1, :
            ]


def fluxes(
    place_ref, got_ref, cells_ref, hang_ref, row_ref, lane_ref, master_row,
    master_lane, weight_ref, ku_ref, load_ref, sub_where, sub_hot, out_ref,
    term_ref, pack_ref, edge_ref, sums_ref, full_ref, tall_ref, few_ref,
):
    place = place_ref[0]
    edge_gather(
        place, [got_ref] * 3, (0, 2, 4), cells_ref, hang_ref, row_ref, lane_ref,
        master_row, master_lane, weight_ref, edge_ref, sums_ref, full_ref,
    )
    cells = full_ref[...]
    ku = ku_ref[...]
    term_ref[...] = jnp.sum(cells * (load_ref[...] - ku), 0, keepdims=True)
    face = lax.broadcasted_iota(i32, (8, ku.shape[0]), 0)
    node = lax.broadcasted_iota(i32, (8, ku.shape[0]), 1) & 63
    index = jnp.where(face < 2, node >> 4, jnp.where(face < 4, (node >> 2) & 3, node & 3))
    member = jnp.where((face < 6) & (index == 3 * (face & 1)), 1.0, 0.0).astype(f32)
    flux = jnp.dot(
        member, ku * cells, precision=lax.Precision.HIGHEST, preferred_element_type=f32
    )
    tall_ref[...] = jnp.zeros_like(tall_ref)
    for number in range(6):
        for half in range(2):
            at = 2 * number + half
            tall_ref[at : at + 1, :] = flux[
                number : number + 1, half * LANES : (half + 1) * LANES
            ]
    table = jnp.concatenate(pieces(tall_ref[...]), 1)
    gather([(table, 16, 1, sub_where, few_ref)], sub_hot)
    found = gathered(few_ref, 8, 0)
    rows = [[found[slot : slot + 1]] for slot in range(2 * REACH)]
    pack(place, 1, rows, pack_ref, out_ref)


def keep_subfaces(cell_ref, face_ref, owner_ref, where_ref, hot_ref, owner_hot, lane_ref):
    cell = cell_ref[...]
    where_ref[...] = 2 * face_ref[...] + (cell >> 7)
    lane_ref[...] = cell & 127
    build_hot(lane_ref, hot_ref)
    build_hot(owner_ref, owner_hot)


def collect(place_ref, got_ref, owner_hot, term_ref, out_ref):
    count = term_ref.shape[1]
    got = jnp.concatenate(landed(place_ref[0], 1, got_ref, 0), 1)
    hot = jnp.concatenate(
        [owner_hot[slot * count : (slot + 1) * count, :] for slot in range(2 * REACH)], 1
    )
    values = jnp.concatenate(
        [jnp.broadcast_to(x, (16, got.shape[1])).astype(bf16) for x in split32(got)], 0
    )
    sums = lax.dot_general(values, hot, (((1,), (1,)), ((), ())), preferred_element_type=f32)
    face_term = sums[0:1] + sums[16:17]
    out_ref[...] = (jnp.abs(term_ref[...]) + jnp.abs(face_term)) / scale_down


SMALL = pl.BlockSpec(memory_space=pltpu.SMEM)
FAST = pl.BlockSpec(memory_space=pltpu.VMEM)
FAR = pl.BlockSpec(memory_space=pl.ANY)


def away(*arrays):
    return [pltpu.with_memory_space_constraint(x, pltpu.HBM) for x in arrays]


def call(kernel, outs, scratch=(), specs=None, sems=0):
    scratch = [pltpu.VMEM(shape, kind) for shape, kind in scratch]
    if sems:
        scratch.append(pltpu.SemaphoreType.DMA((sems,)))

    def run(*args):
        return pl.pallas_call(
            kernel,
            out_shape=[jax.ShapeDtypeStruct(shape, kind) for shape, kind in outs],
            in_specs=specs or [SMALL] + [FAST] * (len(args) - 1),
            scratch_shapes=scratch,
            compiler_params=pltpu.CompilerParams(vmem_limit_bytes=40 * 1024 * 1024),
        )(*args)

    return run


def local(
    adjoint_start,
    adjoint_source,
    inverse_diagonal,
    primal_field,
    cell_load,
    modulus,
    stiffness,
    connectivity,
    hang_node,
    hang_master,
    hang_weight,
    ghost_lists,
    subface_cell,
    subface_face,
    subface_owner,
):
    slots = 2 * REACH
    local_values, cell_count = cell_load.shape
    nodes = connectivity.shape[0]
    half_rows = adjoint_start.shape[1] // LANES
    place = lax.axis_index("dom").reshape(1).astype(i32)
    table = ((3 * OWN, WIDE), f32)
    index = ((nodes, cell_count), i32)
    cells_shape = ((local_values, cell_count), f32)
    hang_shape = ((3, hang_node.shape[0]), f32)
    master_shape = ((8, WIDE), i32)

    count = lax.axis_size("dom")

    def packed(height):
        return [((count, height, LANES), f32)]

    def room(height):
        return ((count + 1, height, LANES), f32)

    tall = up8(half_rows)
    few_sums = ((2, 3 * 64, LANES), f32)
    many_sums = ((2, local_values * 8, LANES), f32)
    own_tall = ((3 * tall, LANES), f32)
    edge = [((3 * TALL, LANES), f32), many_sums, cells_shape]
    tab, tab_primal, list_row, list_hot, extra, blocks = call(
        first_export,
        [table, table, (ghost_lists.shape, i32), ((8 * WIDE, WIDE), bf16)]
        + [((6, slots, LANES), f32)]
        + packed(8),
        [
            room(8),
            (adjoint_start.shape, f32),
            (primal_field.shape, f32),
            (ghost_lists.shape, i32),
            (ghost_lists.shape, i32),
            ((2, 6 * 64, LANES), f32),
        ],
        [SMALL, FAR, FAR, FAR],
        sems=3,
    )(place, *away(adjoint_start, primal_field, ghost_lists))
    ghosts = exchange(blocks)
    connectivity, list_row = lax.optimization_barrier((connectivity, list_row))
    (
        own_where, own_row, edge_where, lane, own_column, master_own, master_own_row, master_edge,
        master_hot, master_column, weight, moduli, forward, backward,
    ) = call(
        functools.partial(setup, adjoint_start.shape[1]),
        [index] * 5
        + [master_shape] * 3
        + [((8 * LANES, WIDE), bf16), master_shape, ((8, WIDE), f32), ((1, cell_count), f32)]
        + [((local_values, 3 * local_values), bf16)] * 2,
        [((OWN, WIDE), f32), ((tall, LANES), f32), ((2, nodes * 8, LANES), f32), master_shape],
        [FAST] * 6,
    )(
        connectivity, hang_node.reshape(1, -1), hang_master, hang_weight,
        modulus.reshape(1, cell_count), stiffness,
    )

    def gather_own(*fields):
        number = len(fields)
        return call(
            functools.partial(own_gather, half_rows, number),
            [cells_shape, hang_shape] * number,
            [
                ((3 * number * tall, LANES), f32),
                ((2, number * local_values * 8, LANES), f32),
            ],
            specs=[FAST] * (5 + number),
        )(own_where, lane, master_own, master_hot, weight, *fields)

    on_edge = (edge_where, lane, master_edge, master_hot, weight)
    landings = []
    source, inverse = adjoint_source, inverse_diagonal
    for sweep in range(SWEEPS):
        if sweep == 1:
            cells, hang, *primal_cells = gather_own(tab, tab_primal)
        else:
            cells, hang = gather_own(tab)
        blocks, image, held = call(
            functools.partial(edge_product, 2 * sweep),
            packed(8) + [cells_shape, hang_shape],
            [room(8)] + edge + [cells_shape, ((6 * EDGE, LANES), f32)] + few(EDGE, LANES),
        )(place, ghosts, cells, hang, *on_edge, extra, moduli, backward)
        returned = exchange(blocks)
        landings.append(returned)
        partial, *tables = call(
            own_sums,
            [table] * (3 if sweep == 0 else 1),
            [cells_shape, cells_shape, ((6 * OWN, WIDE), f32)] + few(OWN, WIDE),
            specs=[FAST] * 10,
        )(
            image, held, own_row, own_column, master_own_row, master_column, weight, tab, source,
            inverse,
        )
        if tables:
            source, inverse = tables
        else:
            subs, image = lax.optimization_barrier(
                ((subface_cell, subface_face, subface_owner), image)
            )
            kept = call(
                keep_subfaces,
                [
                    (subface_cell.shape, i32),
                    ((slots * LANES, subface_cell.shape[1]), bf16),
                    ((slots * cell_count, subface_cell.shape[1]), bf16),
                ],
                [(subface_cell.shape, i32)],
                [FAST] * 3,
            )(*subs)
            partial, (sub_where, sub_hot, owner_hot) = lax.optimization_barrier((partial, kept))
        blocks, tab = call(
            functools.partial(update, 1 if sweep == 0 else None),
            packed(8) + [table],
            [room(8), few_sums] + few(OWN, WIDE),
        )(place, returned, list_row, list_hot, partial, inverse, extra)
        ghosts = exchange(blocks)
        landings.append(ghosts)
    cells, hang, ku, adjoint = call(
        functools.partial(last_gather, half_rows),
        [cells_shape, hang_shape, cells_shape, (adjoint_start.shape, f32)],
        [own_tall, many_sums] + edge,
    )(
        place, tab, own_where, lane, master_own, master_hot, weight, *landings[:3], *primal_cells,
        edge_where, master_edge, moduli, forward,
    )
    blocks, term = call(
        fluxes,
        packed(1) + [((1, cell_count), f32)],
        [room(1)]
        + edge
        + [
            ((16, LANES), f32),
            ((1, 64, LANES), f32),
        ],
    )(place, ghosts, cells, hang, *on_edge, ku, cell_load, sub_where, sub_hot)
    received = exchange(blocks)
    (indicator,) = call(collect, [((1, cell_count), f32)])(
        place, received, owner_hot, term
    )
    return (adjoint, indicator.reshape(cell_count))


def solution(mesh):
    placed = (
        P(None, "dom"),
        P(None, "dom"),
        P(None, "dom"),
        P(None, "dom"),
        P(None, "dom"),
        P("dom"),
        P(),
        P(None, "dom"),
        P("dom"),
        P(None, "dom"),
        P(None, "dom"),
        P(None, "dom"),
        P(None, "dom"),
        P(None, "dom"),
        P(None, "dom"),
    )
    return jax.shard_map(
        local, mesh=mesh, in_specs=placed, out_specs=(P(None, "dom"), P("dom")), check_vma=False
    )
```

```python
import functools

import jax
import jax.numpy as jnp
from jax import lax
from jax.experimental import pallas as pl
from jax.experimental.pallas import tpu as pltpu
from jax.sharding import PartitionSpec as P

REACH = 4
SWEEPS = 2
LANES = 128
WIDE = 2 * LANES
OWN = 32
EDGE = 32
TALL = 24
NOWHERE = 126

relaxation = 0.7
scale_down = 16.0
pad_code = 16368

f32 = jnp.float32
bf16 = jnp.bfloat16
i32 = jnp.int32


def neighbour_offsets():
    return [step + 1 for step in range(REACH)] + [-(step + 1) for step in range(REACH)]


def exchange(packed):
    return lax.all_to_all(packed, "dom", 0, 0, tiled=True)


def pack(place, sign, rows, pack_ref, out_ref):
    count = out_ref.shape[0]
    pack_ref[...] = jnp.zeros_like(pack_ref)
    for slot, offset in enumerate(neighbour_offsets()):
        target = place + sign * offset
        at = jnp.where((target >= 0) & (target < count), target, count)
        for number, row in enumerate(rows[slot]):
            pack_ref[at, number : number + 1, :] = row
    out_ref[...] = pack_ref[:count]


def landed(place, sign, got_ref, number):
    count = got_ref.shape[0]
    rows = []
    for offset in neighbour_offsets():
        source = place - sign * offset
        row = got_ref[jnp.clip(source, 0, count - 1), number : number + 1, :]
        there = jnp.broadcast_to((source >= 0) & (source < count), row.shape)
        rows.append(jnp.where(there, row, 0.0))
    return rows


def landed_wide(place, sign, got_ref, part):
    halves = [
        jnp.concatenate(landed(place, sign, got_ref, 2 * part + half), 0) for half in range(2)
    ]
    return jnp.concatenate(halves, 1)


def match16(row, count):
    width = row.shape[1]
    wide = jnp.broadcast_to(row.astype(f32), (16, width)).astype(bf16)
    numbers = lax.broadcasted_iota(i32, (count, width), 0).astype(f32).astype(bf16)
    return numbers.reshape(count // 16, 16, width) == wide[None]


def one_hot(row, count):
    mask = match16(row, count)
    ones = jnp.ones(mask.shape, bf16)
    return jnp.where(mask, ones, jnp.zeros_like(ones)).reshape(count, row.shape[1])


def spread16(mask, row):
    wide = jnp.broadcast_to(row, (16, row.shape[1])).astype(bf16)[None]
    out = jnp.where(mask, jnp.broadcast_to(wide, mask.shape), jnp.zeros(mask.shape, bf16))
    return out.reshape(mask.shape[0] * 16, row.shape[1])


def pieces(x):
    high = x.astype(bf16)
    return high, (x - high.astype(f32)).astype(bf16)


def gather(jobs, column_ref, wide=False):
    count, width = column_ref.shape
    tables = jnp.concatenate([job[0] for job in jobs], 0)
    high = tables.shape[0]
    numbers = lax.broadcasted_iota(i32, (max(job[1] for job in jobs), width), 0)
    step = min(count, 32 if sum(job[1] * job[2] for job in jobs) <= 192 else 16)

    def body(block, carry):
        start = pl.multiple_of(block * step, step)
        for j in range(step):
            hot = one_hot(column_ref[pl.ds(start + j, 1), :], WIDE if wide else LANES)
            if not wide:
                hot = jnp.concatenate([hot, hot], 0)
            all_found = jnp.dot(tables, hot, preferred_element_type=f32)
            if wide:
                all_found = all_found[: high // 2] + all_found[high // 2 :]
            top = 0
            for _, rows, parts, row_ref, sums_ref in jobs:
                found = all_found[top : top + parts * rows]
                top += parts * rows
                mask = numbers[:rows] == jnp.broadcast_to(
                    row_ref[pl.ds(start + j, 1), :], (rows, width)
                )
                for part in range(parts):
                    kept = jnp.where(mask, found[part * rows : (part + 1) * rows], 0.0)
                    kept = jnp.sum(kept.reshape(rows // 8, 8, width), 0)
                    for half in range(width // LANES):
                        sums_ref[half, pl.ds(part * count * 8 + start * 8 + j * 8, 8), :] = kept[
                            :, half * LANES : (half + 1) * LANES
                        ]
        return carry

    if count == step:
        body(0, 0)
    else:
        lax.fori_loop(0, count // step, body, 0)


def gathered(sums_ref, count, part):
    totals = []
    for half in range(sums_ref.shape[0]):
        rows = [sums_ref[half, pl.ds(part * count * 8 + s, count, stride=8), :] for s in range(8)]
        while len(rows) > 1:
            rows = [a + b for a, b in zip(rows[::2], rows[1::2])]
        totals.append(rows[0])
    return jnp.concatenate(totals, 1)


def halves(x):
    return [x[:, :LANES], x[:, LANES:]]


def rows_and_columns(where, lane):
    return where >> 1, (where & 1) * LANES + lane


def scatter(high_ref, low_ref, rows, row_ref, column_ref, sum_ref):
    count = row_ref.shape[0]
    step = min(count, 32)

    def product(start):
        masks = [match16(row_ref[pl.ds(start + j, 1), :], rows) for j in range(8)]
        hot = jnp.concatenate(
            [one_hot(column_ref[pl.ds(start + j, 1), :], sum_ref.shape[1]) for j in range(8)], 1
        )
        stacked = [
            jnp.concatenate(
                [
                    spread16(mask, piece_ref[pl.ds(part * count + start + j, 1), :])
                    for j, mask in enumerate(masks)
                ],
                1,
            )
            for piece_ref in (high_ref, low_ref)
            for part in range(3)
        ]
        return lax.dot_general(
            jnp.concatenate(stacked, 0), hot, (((1,), (1,)), ((), ())), preferred_element_type=f32
        )

    if count == 8:
        sum_ref[...] = product(0)
        return
    sum_ref[...] = jnp.zeros_like(sum_ref)

    def body(block, carry):
        start = pl.multiple_of(block * step, step)
        total = product(start)
        for first in range(8, step, 8):
            total += product(start + first)
        sum_ref[...] += total
        return carry

    lax.fori_loop(0, count // step, body, 0)


def split32(x):
    high = x.astype(bf16).astype(f32)
    return high, x - high


def add_pieces(sums):
    half = sums.shape[0] // 2
    return sums[:half] + sums[half:]


def scatter_few(values, rows, row_ref, column_ref, scratch):
    high_ref, low_ref, sum_ref = scratch
    for part in range(3):
        high_ref[part * 8 : part * 8 + 8, :], low_ref[part * 8 : part * 8 + 8, :] = split32(
            values[part]
        )
    scatter(high_ref, low_ref, rows, row_ref, column_ref, sum_ref)
    return add_pieces(sum_ref[...])


def few(rows, columns):
    return [((24, WIDE), f32)] * 2 + [((6 * rows, columns), f32)]


def spread_hanging(held, weight, rows, row_ref, column_ref, scratch):
    both = jnp.concatenate([held, held], 1)
    values = [weight * both[part : part + 1] for part in range(3)]
    return scatter_few(values, rows, row_ref, column_ref, scratch)


def sum_masters(sums_ref, first, weight):
    totals = []
    for part in range(first, first + 3):
        left, right = halves(weight * gathered(sums_ref, 8, part))
        totals.append(jnp.sum(left + right, 0, keepdims=True))
    return totals


def product(threefold, cells):
    high, low = pieces(cells)
    return jnp.dot(
        threefold, jnp.concatenate([high, low, high], 0), preferred_element_type=f32
    )


def fill_table(x_ref, out_ref):
    count = x_ref.shape[1] // WIDE
    for part in range(3):
        out_ref[part * OWN + count : (part + 1) * OWN, :] = jnp.zeros((OWN - count, WIDE), f32)
    for row in range(count):
        block = x_ref[:, row * WIDE : (row + 1) * WIDE]
        for part in range(3):
            out_ref[part * OWN + row : part * OWN + row + 1, :] = block[part : part + 1]


def tall_table(tab_refs, half_rows, tall_ref):
    tall = up8(half_rows)
    tall_ref[...] = jnp.zeros_like(tall_ref)
    for number, tab_ref in enumerate(tab_refs):
        for part in range(3):
            for half_row in range(half_rows):
                row, half = part * OWN + half_row // 2, half_row % 2
                at = (3 * number + part) * tall + half_row
                tall_ref[at : at + 1, :] = tab_ref[
                    row : row + 1, half * LANES : (half + 1) * LANES
                ]
    return jnp.concatenate(pieces(tall_ref[...]), 1)


def up8(count):
    return -(-count // 8) * 8


def export_tiles(table, parts, row_ref, column_ref, sums_ref):
    table = jnp.concatenate(pieces(table), 0)
    gather([(table, OWN, parts, row_ref, sums_ref)], column_ref, wide=True)
    return [tile for part in range(parts) for tile in halves(gathered(sums_ref, 8, part))]


def rows_of(tiles):
    return [[tile[slot : slot + 1] for tile in tiles] for slot in range(2 * REACH)]


def add_primal(rows, sign, part, extra_ref):
    slots = 2 * REACH
    for slot in range(slots):
        export = slot if sign > 0 else (slot + REACH) % slots
        for half in range(2):
            rows[slot].append(extra_ref[2 * part + half, export : export + 1, :])


def copy_in(pairs, sems):
    copies = [
        pltpu.make_async_copy(source, target, sems.at[number])
        for number, (source, target) in enumerate(pairs)
    ]
    for copy in copies:
        copy.start()
    for copy in copies:
        copy.wait()


def first_export(
    adjoint_hbm, primal_hbm, list_hbm, tab_a, tab_p, row_ref, column_ref, extra_ref,
    out_ref, pack_ref, adjoint_ref, primal_ref, list_ref, sums_ref, sems,
):
    copy_in(
        [(adjoint_hbm, adjoint_ref), (primal_hbm, primal_ref), (list_hbm, list_ref)], sems
    )
    owned = adjoint_ref.shape[1]
    fill_table(adjoint_ref, tab_a)
    fill_table(primal_ref, tab_p)
    codes = list_ref[...]
    node = lax.rem(17 * codes + lax.broadcasted_iota(i32, codes.shape, 1), owned)
    row_ref[...] = node >> 8
    column_ref[...] = node & 255
    table = jnp.concatenate([tab_a[...], tab_p[...]], 0)
    tiles = export_tiles(table, 6, row_ref, column_ref, sums_ref)
    for number in range(6):
        extra_ref[number] = tiles[6 + number]
    pack(lax.axis_index("dom"), 1, rows_of(tiles[:6]), pack_ref, out_ref)


def setup(
    owned, connect_ref, node_ref, master_ref, weight_ref, modulus_ref, stiffness_ref,
    own_where, own_row, edge_where, lane_ref, column_ref, master_own, master_own_row,
    master_edge, master_lane, master_column, weight_out, modulus_out, forward_out, adjoint_out,
    map_ref, tall_ref, sums_ref,
):
    extent = owned + 2 * REACH * WIDE
    modulus_out[...] = modulus_ref[...]
    for out_ref, matrix in (
        (forward_out, stiffness_ref[...]),
        (adjoint_out, jnp.transpose(stiffness_ref[...])),
    ):
        high, low = pieces(matrix)
        out_ref[...] = jnp.concatenate([high, high, low], 1)
    codes = master_ref[...]
    master = lax.rem(17 * codes + 8 * lax.broadcasted_iota(i32, codes.shape, 1), extent)
    count = codes.shape[0] // 2
    master = jnp.concatenate([master[:count], master[count:]], 1)
    weight = weight_ref[...]
    weight_out[...] = jnp.concatenate([weight[:count], weight[count:]], 1)
    last = owned // LANES
    where = master >> 7
    master_own[...] = jnp.where(where < last, where, NOWHERE)
    master_edge[...] = jnp.where(where < last, NOWHERE, where - last)
    master_lane[...] = master & 127
    master_own_row[...] = jnp.where(where < last, master >> 8, NOWHERE)
    master_column[...] = master & 255

    codes = node_ref[...]
    node = jnp.where(codes == pad_code, extent, lax.rem(13 * codes, owned))
    slot = (lax.broadcasted_iota(i32, codes.shape, 1) + 1).astype(f32)
    map_ref[...] = lax.dot_general(
        spread16(match16(node >> 8, OWN), slot),
        one_hot(node & 255, WIDE),
        (((1,), (1,)), ((), ())),
        preferred_element_type=f32,
    )

    codes = connect_ref[...]
    cells = lax.broadcasted_iota(i32, codes.shape, 1)
    slots = lax.rem(27 * cells + 17 * codes, extent)
    own_where[...] = slots >> 7
    lane_ref[...] = slots & 127
    tall_ref[...] = jnp.zeros_like(tall_ref)
    for half_row in range(last):
        row, half = half_row // 2, half_row % 2
        tall_ref[half_row : half_row + 1, :] = map_ref[
            row : row + 1, half * LANES : (half + 1) * LANES
        ]
    table = jnp.concatenate(pieces(tall_ref[...]), 1)
    gather([(table, tall_ref.shape[0], 1, own_where, sums_ref)], lane_ref)
    slot = gathered(sums_ref, codes.shape[0], 0).astype(i32)
    where = slots >> 7
    hanging = slot > 0
    outside = where >= last
    lane = jnp.where(hanging, slot - 1, slots & 127)
    lane_ref[...] = lane
    where_own = jnp.where(hanging | outside, NOWHERE, where)
    own_where[...] = where_own
    own_row[...], column_ref[...] = rows_and_columns(where_own, lane)
    edge_where[...] = jnp.where(hanging, 4 * REACH, jnp.where(outside, where - last, NOWHERE))


def own_gather(
    half_rows, fields, row_ref, lane_ref, master_row, master_lane, weight_ref, *refs
):
    tab_refs, refs = refs[:fields], refs[fields:]
    outs, (tall_ref, sums_ref) = refs[:-2], refs[-2:]
    tall = up8(half_rows)
    table = tall_table(tab_refs, half_rows, tall_ref)
    parts = 3 * fields
    gather([(table, tall, parts, master_row, sums_ref)], master_lane)
    found = sum_masters(sums_ref, 0, weight_ref[...])
    if fields == 2:
        found += sum_masters(sums_ref, 3, weight_ref[...])
    for field in range(fields):
        for part in range(3):
            outs[2 * field + 1][part : part + 1, :] = found[3 * field + part]
    gather([(table, tall, parts, row_ref, sums_ref)], lane_ref)
    count = row_ref.shape[0]
    for field in range(fields):
        cells_ref = outs[2 * field]
        for part in range(3):
            cells_ref[part * count : (part + 1) * count, :] = gathered(
                sums_ref, count, 3 * field + part
            )


def ghost_rows(place, got_refs, first, edge_ref):
    edge_ref[...] = jnp.zeros_like(edge_ref)
    for part in range(3):
        for half in range(2):
            lines = landed(place, 1, got_refs[part], first[part] + half)
            for slot in range(2 * REACH):
                at = part * TALL + 2 * slot + half
                edge_ref[at : at + 1, :] = lines[slot]
    return jnp.concatenate(pieces(edge_ref[...]), 1)


def hanging_rows(found, hang_ref, edge_ref):
    for part in range(3):
        at = part * TALL + 4 * REACH
        edge_ref[at : at + 1, :] = found[part] + hang_ref[part : part + 1, :]
    return jnp.concatenate(pieces(edge_ref[...]), 1)


def edge_gather(
    place, got_refs, first, cells_ref, hang_ref, row_ref, lane_ref, master_row, master_lane,
    weight_ref, edge_ref, sums_ref, out_ref,
):
    table = ghost_rows(place, got_refs, first, edge_ref)
    gather([(table, TALL, 3, master_row, sums_ref)], master_lane)
    table = hanging_rows(sum_masters(sums_ref, 0, weight_ref[...]), hang_ref, edge_ref)
    gather([(table, TALL, 3, row_ref, sums_ref)], lane_ref)
    count = row_ref.shape[0]
    for part in range(3):
        rows = slice(part * count, (part + 1) * count)
        out_ref[rows, :] = cells_ref[rows, :] + gathered(sums_ref, count, part)


def edge_product(
    primal_part, got_ref, cells_ref, hang_ref, row_ref, lane_ref, master_row,
    master_lane, weight_ref, extra_ref, modulus_ref, stiffness_ref, out_ref,
    image_ref, held_ref, pack_ref, edge_ref, sums_ref, full_ref, low_ref, sum_ref, *scratch,
):
    place = lax.axis_index("dom")
    edge_gather(
        place, [got_ref] * 3, (0, 2, 4), cells_ref, hang_ref, row_ref, lane_ref,
        master_row, master_lane, weight_ref, edge_ref, sums_ref, full_ref,
    )
    image = modulus_ref[...] * product(stiffness_ref[...], full_ref[...])
    image_ref[...] = image
    full_ref[...], low_ref[...] = split32(image)
    scatter(full_ref, low_ref, EDGE, row_ref, lane_ref, sum_ref)
    sums = add_pieces(sum_ref[...])
    slots = 2 * REACH
    held = jnp.concatenate(
        [sums[part * EDGE + 2 * slots : part * EDGE + 2 * slots + 1] for part in range(3)], 0
    )
    held_ref[...] = held
    sums += spread_hanging(held, weight_ref[...], EDGE, master_row, master_lane, scratch)
    rows = [
        [
            sums[part * EDGE + 2 * slot + half : part * EDGE + 2 * slot + half + 1]
            for part in range(3)
            for half in range(2)
        ]
        for slot in range(slots)
    ]
    add_primal(rows, -1, primal_part, extra_ref)
    pack(place, -1, rows, pack_ref, out_ref)


def own_sums(
    image_ref, held_ref, row_ref, column_ref, master_row, master_column, weight_ref,
    tab_ref, source_ref, inverse_ref, out_ref, *rest,
):
    *tables, high_ref, low_ref, sum_ref = rest[:-3]
    if tables:
        tab_source, tab_inverse = tables
        fill_table(source_ref, tab_source)
        fill_table(inverse_ref, tab_inverse)
        source_ref, inverse_ref = tab_source, tab_inverse
    high_ref[...], low_ref[...] = split32(image_ref[...])
    scatter(high_ref, low_ref, OWN, row_ref, column_ref, sum_ref)
    applied = add_pieces(sum_ref[...]) + spread_hanging(
        held_ref[...], weight_ref[...], OWN, master_row, master_column, rest[-3:]
    )
    out_ref[...] = tab_ref[...] + relaxation * inverse_ref[...] * (source_ref[...] - applied)


def update(
    primal_part, got_ref, row_ref, column_ref, partial_ref, inverse_ref, extra_ref,
    out_ref, tab_ref,
    pack_ref, sums_ref, *scratch,
):
    place = lax.axis_index("dom")
    values = [landed_wide(place, -1, got_ref, part) for part in range(3)]
    returned = scatter_few(values, OWN, row_ref, column_ref, scratch)
    fresh = partial_ref[...] - relaxation * inverse_ref[...] * returned
    tab_ref[...] = fresh
    rows = rows_of(export_tiles(fresh, 3, row_ref, column_ref, sums_ref))
    if primal_part is not None:
        add_primal(rows, 1, primal_part, extra_ref)
    pack(place, 1, rows, pack_ref, out_ref)


def last_gather(
    half_rows, tab_ref, own_where, lane_ref, master_own, master_lane, weight_ref,
    got_a, got_b, got_c, primal_cells, primal_hang, edge_where, master_edge, modulus_ref,
    stiffness_ref, cells_ref, hang_ref, ku_ref, final_ref,
    tall_ref, sums_ref, edge_ref, edge_sums, full_ref,
):
    tall = up8(half_rows)
    own = tall_table([tab_ref], half_rows, tall_ref)
    edge = ghost_rows(lax.axis_index("dom"), (got_a, got_b, got_c), (6, 6, 6), edge_ref)
    gather(
        [(own, tall, 3, master_own, sums_ref), (edge, TALL, 3, master_edge, edge_sums)],
        master_lane,
    )
    weight = weight_ref[...]
    found = sum_masters(sums_ref, 0, weight)
    for part in range(3):
        hang_ref[part : part + 1, :] = found[part]
    edge = hanging_rows(sum_masters(edge_sums, 0, weight), primal_hang, edge_ref)
    gather(
        [(own, tall, 3, own_where, sums_ref), (edge, TALL, 3, edge_where, edge_sums)], lane_ref
    )
    count = lane_ref.shape[0]
    for part in range(3):
        rows = slice(part * count, (part + 1) * count)
        cells_ref[rows, :] = gathered(sums_ref, count, part)
        full_ref[rows, :] = primal_cells[rows, :] + gathered(edge_sums, count, part)
    ku_ref[...] = modulus_ref[...] * product(stiffness_ref[...], full_ref[...])
    for row in range(final_ref.shape[1] // WIDE):
        for part in range(3):
            final_ref[part : part + 1, row * WIDE : (row + 1) * WIDE] = tab_ref[
                part * OWN + row : part * OWN + row + 1, :
            ]


def fluxes(
    got_ref, cells_ref, hang_ref, row_ref, lane_ref, master_row,
    master_lane, weight_ref, ku_ref, load_ref, sub_cell, sub_face, out_ref,
    term_ref, pack_ref, edge_ref, sums_ref, full_ref, tall_ref, code_ref, few_ref,
):
    place = lax.axis_index("dom")
    edge_gather(
        place, [got_ref] * 3, (0, 2, 4), cells_ref, hang_ref, row_ref, lane_ref,
        master_row, master_lane, weight_ref, edge_ref, sums_ref, full_ref,
    )
    cells = full_ref[...]
    ku = ku_ref[...]
    term_ref[...] = jnp.sum(cells * (load_ref[...] - ku), 0, keepdims=True)
    face = lax.broadcasted_iota(i32, (8, ku.shape[0]), 0)
    node = lax.broadcasted_iota(i32, (8, ku.shape[0]), 1) & 63
    index = jnp.where(face < 2, node >> 4, jnp.where(face < 4, (node >> 2) & 3, node & 3))
    member = jnp.where((face < 6) & (index == 3 * (face & 1)), 1.0, 0.0).astype(f32)
    flux = jnp.dot(
        member, ku * cells, precision=lax.Precision.HIGHEST, preferred_element_type=f32
    )
    tall_ref[...] = jnp.zeros_like(tall_ref)
    for number in range(6):
        for half in range(2):
            at = 2 * number + half
            tall_ref[at : at + 1, :] = flux[
                number : number + 1, half * LANES : (half + 1) * LANES
            ]
    cell = sub_cell[...]
    code_ref[:8, :] = 2 * sub_face[...] + (cell >> 7)
    code_ref[8:, :] = cell & 127
    table = jnp.concatenate(pieces(tall_ref[...]), 1)
    gather([(table, 16, 1, code_ref.at[:8, :], few_ref)], code_ref.at[8:, :])
    found = gathered(few_ref, 8, 0)
    rows = [[found[slot : slot + 1]] for slot in range(2 * REACH)]
    pack(place, 1, rows, pack_ref, out_ref)


def collect(got_ref, owner_ref, term_ref, out_ref):
    count = term_ref.shape[1]
    got = jnp.concatenate(landed(lax.axis_index("dom"), 1, got_ref, 0), 1)
    hot = jnp.concatenate(
        [one_hot(owner_ref[slot : slot + 1, :], count) for slot in range(2 * REACH)], 1
    )
    values = jnp.concatenate(
        [jnp.broadcast_to(x, (16, got.shape[1])).astype(bf16) for x in split32(got)], 0
    )
    sums = lax.dot_general(values, hot, (((1,), (1,)), ((), ())), preferred_element_type=f32)
    face_term = sums[0:1] + sums[16:17]
    out_ref[...] = (jnp.abs(term_ref[...]) + jnp.abs(face_term)) / scale_down


FAST = pl.BlockSpec(memory_space=pltpu.VMEM)
FAR = pl.BlockSpec(memory_space=pl.ANY)


def away(*arrays):
    return [pltpu.with_memory_space_constraint(x, pltpu.HBM) for x in arrays]


def call(kernel, outs, scratch=(), specs=None, sems=0):
    scratch = [pltpu.VMEM(shape, kind) for shape, kind in scratch]
    if sems:
        scratch.append(pltpu.SemaphoreType.DMA((sems,)))

    def run(*args):
        return pl.pallas_call(
            kernel,
            out_shape=[out if hasattr(out, "memory_space") else jax.ShapeDtypeStruct(*out) for out in outs],
            in_specs=specs or [FAST] * len(args),
            scratch_shapes=scratch,
            compiler_params=pltpu.CompilerParams(vmem_limit_bytes=40 * 1024 * 1024),
        )(*args)

    return run


def local(
    adjoint_start,
    adjoint_source,
    inverse_diagonal,
    primal_field,
    cell_load,
    modulus,
    stiffness,
    connectivity,
    hang_node,
    hang_master,
    hang_weight,
    ghost_lists,
    subface_cell,
    subface_face,
    subface_owner,
):
    slots = 2 * REACH
    local_values, cell_count = cell_load.shape
    nodes = connectivity.shape[0]
    half_rows = adjoint_start.shape[1] // LANES
    table = ((3 * OWN, WIDE), f32)
    index = ((nodes, cell_count), i32)
    cells_shape = ((local_values, cell_count), f32)
    hang_shape = ((3, hang_node.shape[0]), f32)
    master_shape = ((8, WIDE), i32)

    count = lax.axis_size("dom")

    def packed(height):
        return [pltpu.VMEM((count, height, LANES), f32)]

    def room(height):
        return ((count + 1, height, LANES), f32)

    tall = up8(half_rows)
    few_sums = ((2, 3 * 64, LANES), f32)
    many_sums = ((2, local_values * 8, LANES), f32)
    own_tall = ((3 * tall, LANES), f32)
    edge = [((3 * TALL, LANES), f32), many_sums, cells_shape]
    tab, tab_primal, list_row, list_column, extra, blocks = call(
        first_export,
        [table, table]
        + [(ghost_lists.shape, i32)] * 2
        + [((6, slots, LANES), f32)]
        + packed(8),
        [
            room(8),
            (adjoint_start.shape, f32),
            (primal_field.shape, f32),
            (ghost_lists.shape, i32),
            ((2, 6 * 64, LANES), f32),
        ],
        [FAR, FAR, FAR],
        sems=3,
    )(*away(adjoint_start, primal_field, ghost_lists))
    ghosts = exchange(blocks)
    (
        own_where, own_row, edge_where, lane, own_column, master_own, master_own_row, master_edge,
        master_lane, master_column, weight, moduli, forward, backward,
    ) = call(
        functools.partial(setup, adjoint_start.shape[1]),
        [index] * 5
        + [master_shape] * 5
        + [((8, WIDE), f32), ((1, cell_count), f32)]
        + [((local_values, 3 * local_values), bf16)] * 2,
        [((OWN, WIDE), f32), ((tall, LANES), f32), ((2, nodes * 8, LANES), f32)],
        [FAST] * 6,
    )(
        connectivity, hang_node.reshape(1, -1), hang_master, hang_weight,
        modulus.reshape(1, cell_count), stiffness,
    )

    def gather_own(*fields):
        number = len(fields)
        return call(
            functools.partial(own_gather, half_rows, number),
            [cells_shape, hang_shape] * number,
            [
                ((3 * number * tall, LANES), f32),
                ((2, number * local_values * 8, LANES), f32),
            ],
            specs=[FAST] * (5 + number),
        )(own_where, lane, master_own, master_lane, weight, *fields)

    on_edge = (edge_where, lane, master_edge, master_lane, weight)
    landings = []
    source, inverse = adjoint_source, inverse_diagonal
    for sweep in range(SWEEPS):
        if sweep == 1:
            cells, hang, *primal_cells = gather_own(tab, tab_primal)
        else:
            cells, hang = gather_own(tab)
        blocks, image, held = call(
            functools.partial(edge_product, 2 * sweep),
            packed(8) + [cells_shape, hang_shape],
            [room(8)] + edge + [cells_shape, ((6 * EDGE, LANES), f32)] + few(EDGE, LANES),
        )(ghosts, cells, hang, *on_edge, extra, moduli, backward)
        returned = exchange(blocks)
        landings.append(returned)
        partial, *tables = call(
            own_sums,
            [table] * (3 if sweep == 0 else 1),
            [cells_shape, cells_shape, ((6 * OWN, WIDE), f32)] + few(OWN, WIDE),
            specs=[FAST] * 10,
        )(
            image, held, own_row, own_column, master_own_row, master_column, weight, tab, source,
            inverse,
        )
        if tables:
            source, inverse = tables
        blocks, tab = call(
            functools.partial(update, 1 if sweep == 0 else None),
            packed(8) + [table],
            [room(8), few_sums] + few(OWN, WIDE),
        )(returned, list_row, list_column, partial, inverse, extra)
        ghosts = exchange(blocks)
        landings.append(ghosts)
    cells, hang, ku, adjoint = call(
        functools.partial(last_gather, half_rows),
        [cells_shape, hang_shape, cells_shape, (adjoint_start.shape, f32)],
        [own_tall, many_sums] + edge,
    )(
        tab, own_where, lane, master_own, master_lane, weight, *landings[:3], *primal_cells,
        edge_where, master_edge, moduli, forward,
    )
    blocks, term = call(
        fluxes,
        packed(1) + [((1, cell_count), f32)],
        [room(1)]
        + edge
        + [
            ((16, LANES), f32),
            ((16, subface_cell.shape[1]), i32),
            ((1, 64, LANES), f32),
        ],
    )(ghosts, cells, hang, *on_edge, ku, cell_load, subface_cell, subface_face)
    received = exchange(blocks)
    (indicator,) = call(collect, [((1, cell_count), f32)])(
        received, subface_owner, term
    )
    return (adjoint, indicator.reshape(cell_count))


def solution(mesh):
    placed = (
        P(None, "dom"),
        P(None, "dom"),
        P(None, "dom"),
        P(None, "dom"),
        P(None, "dom"),
        P("dom"),
        P(),
        P(None, "dom"),
        P("dom"),
        P(None, "dom"),
        P(None, "dom"),
        P(None, "dom"),
        P(None, "dom"),
        P(None, "dom"),
        P(None, "dom"),
    )
    return jax.shard_map(
        local, mesh=mesh, in_specs=placed, out_specs=(P(None, "dom"), P("dom")), check_vma=False
    )
```

```python
import functools

import jax
import jax.numpy as jnp
from jax import lax
from jax.experimental import pallas as pl
from jax.experimental.pallas import tpu as pltpu
from jax.sharding import PartitionSpec as P

REACH = 4
SWEEPS = 2
LANES = 128
WIDE = 2 * LANES
OWN = 32
EDGE = 32
TALL = 24
NOWHERE = 126

relaxation = 0.7
scale_down = 16.0
pad_code = 16368

f32 = jnp.float32
bf16 = jnp.bfloat16
i32 = jnp.int32


def neighbour_offsets():
    return [step + 1 for step in range(REACH)] + [-(step + 1) for step in range(REACH)]


def exchange(packed):
    return lax.all_to_all(packed, "dom", 0, 0, tiled=True)


def pack(place, sign, rows, pack_ref, out_ref):
    count = out_ref.shape[0]
    pack_ref[...] = jnp.zeros_like(pack_ref)
    for slot, offset in enumerate(neighbour_offsets()):
        target = place + sign * offset
        at = jnp.where((target >= 0) & (target < count), target, count)
        for number, row in enumerate(rows[slot]):
            pack_ref[at, number : number + 1, :] = row
    out_ref[...] = pack_ref[:count]


def landed(place, sign, got_ref, number):
    count = got_ref.shape[0]
    rows = []
    for offset in neighbour_offsets():
        source = place - sign * offset
        row = got_ref[jnp.clip(source, 0, count - 1), number : number + 1, :]
        there = jnp.broadcast_to((source >= 0) & (source < count), row.shape)
        rows.append(jnp.where(there, row, 0.0))
    return rows


def landed_wide(place, sign, got_ref, part):
    halves = [
        jnp.concatenate(landed(place, sign, got_ref, 2 * part + half), 0) for half in range(2)
    ]
    return jnp.concatenate(halves, 1)


def match16(row, count):
    width = row.shape[1]
    wide = jnp.broadcast_to(row.astype(f32), (16, width)).astype(bf16)
    numbers = lax.broadcasted_iota(i32, (count, width), 0).astype(f32).astype(bf16)
    return numbers.reshape(count // 16, 16, width) == wide[None]


def one_hot(row, count):
    mask = match16(row, count)
    ones = jnp.ones(mask.shape, bf16)
    return jnp.where(mask, ones, jnp.zeros_like(ones)).reshape(count, row.shape[1])


def spread16(mask, row):
    wide = jnp.broadcast_to(row, (16, row.shape[1])).astype(bf16)[None]
    out = jnp.where(mask, jnp.broadcast_to(wide, mask.shape), jnp.zeros(mask.shape, bf16))
    return out.reshape(mask.shape[0] * 16, row.shape[1])


def pieces(x):
    high = x.astype(bf16)
    return high, (x - high.astype(f32)).astype(bf16)


def hot_at(column_ref, number, high):
    if column_ref.dtype == bf16:
        return column_ref[pl.ds(pl.multiple_of(number * high, high), high), :]
    return one_hot(column_ref[pl.ds(number, 1), :], high)


def gather(jobs, column_ref, wide=False):
    count, width = jobs[0][3].shape
    tables = jnp.concatenate([job[0] for job in jobs], 0)
    high = tables.shape[0]
    numbers = lax.broadcasted_iota(i32, (max(job[1] for job in jobs), width), 0)
    step = min(count, 32 if sum(job[1] * job[2] for job in jobs) <= 192 else 16)

    def body(block, carry):
        start = pl.multiple_of(block * step, step)
        for j in range(step):
            hot = hot_at(column_ref, start + j, WIDE if wide else LANES)
            if not wide:
                hot = jnp.concatenate([hot, hot], 0)
            all_found = jnp.dot(tables, hot, preferred_element_type=f32)
            if wide:
                all_found = all_found[: high // 2] + all_found[high // 2 :]
            top = 0
            for _, rows, parts, row_ref, sums_ref in jobs:
                found = all_found[top : top + parts * rows]
                top += parts * rows
                mask = numbers[:rows] == jnp.broadcast_to(
                    row_ref[pl.ds(start + j, 1), :], (rows, width)
                )
                for part in range(parts):
                    kept = jnp.where(mask, found[part * rows : (part + 1) * rows], 0.0)
                    kept = jnp.sum(kept.reshape(rows // 8, 8, width), 0)
                    for half in range(width // LANES):
                        sums_ref[half, pl.ds(part * count * 8 + start * 8 + j * 8, 8), :] = kept[
                            :, half * LANES : (half + 1) * LANES
                        ]
        return carry

    if count == step:
        body(0, 0)
    else:
        lax.fori_loop(0, count // step, body, 0)


def gathered(sums_ref, count, part):
    totals = []
    for half in range(sums_ref.shape[0]):
        rows = [sums_ref[half, pl.ds(part * count * 8 + s, count, stride=8), :] for s in range(8)]
        while len(rows) > 1:
            rows = [a + b for a, b in zip(rows[::2], rows[1::2])]
        totals.append(rows[0])
    return jnp.concatenate(totals, 1)


def halves(x):
    return [x[:, :LANES], x[:, LANES:]]


def rows_and_columns(where, lane):
    return where >> 1, (where & 1) * LANES + lane


def scatter(high_ref, low_ref, rows, row_ref, column_ref, sum_ref):
    count = row_ref.shape[0]
    step = min(count, 32)

    def product(start):
        masks = [match16(row_ref[pl.ds(start + j, 1), :], rows) for j in range(8)]
        hot = jnp.concatenate(
            [hot_at(column_ref, start + j, sum_ref.shape[1]) for j in range(8)], 1
        )
        stacked = [
            jnp.concatenate(
                [
                    spread16(mask, piece_ref[pl.ds(part * count + start + j, 1), :])
                    for j, mask in enumerate(masks)
                ],
                1,
            )
            for piece_ref in (high_ref, low_ref)
            for part in range(3)
        ]
        return lax.dot_general(
            jnp.concatenate(stacked, 0), hot, (((1,), (1,)), ((), ())), preferred_element_type=f32
        )

    if count == 8:
        sum_ref[...] = product(0)
        return
    sum_ref[...] = jnp.zeros_like(sum_ref)

    def body(block, carry):
        start = pl.multiple_of(block * step, step)
        total = product(start)
        for first in range(8, step, 8):
            total += product(start + first)
        sum_ref[...] += total
        return carry

    lax.fori_loop(0, count // step, body, 0)


def split32(x):
    high = x.astype(bf16).astype(f32)
    return high, x - high


def add_pieces(sums):
    half = sums.shape[0] // 2
    return sums[:half] + sums[half:]


def scatter_few(values, rows, row_ref, column_ref, scratch):
    high_ref, low_ref, sum_ref = scratch
    for part in range(3):
        high_ref[part * 8 : part * 8 + 8, :], low_ref[part * 8 : part * 8 + 8, :] = split32(
            values[part]
        )
    scatter(high_ref, low_ref, rows, row_ref, column_ref, sum_ref)
    return add_pieces(sum_ref[...])


def few(rows, columns):
    return [((24, WIDE), f32)] * 2 + [((6 * rows, columns), f32)]


def spread_hanging(held, weight, rows, row_ref, column_ref, scratch):
    both = jnp.concatenate([held, held], 1)
    values = [weight * both[part : part + 1] for part in range(3)]
    return scatter_few(values, rows, row_ref, column_ref, scratch)


def sum_masters(sums_ref, first, weight):
    totals = []
    for part in range(first, first + 3):
        left, right = halves(weight * gathered(sums_ref, 8, part))
        totals.append(jnp.sum(left + right, 0, keepdims=True))
    return totals


def product(threefold, cells):
    high, low = pieces(cells)
    return jnp.dot(
        threefold, jnp.concatenate([high, low, high], 0), preferred_element_type=f32
    )


def fill_table(x_ref, out_ref):
    count = x_ref.shape[1] // WIDE
    for part in range(3):
        out_ref[part * OWN + count : (part + 1) * OWN, :] = jnp.zeros((OWN - count, WIDE), f32)
    for row in range(count):
        block = x_ref[:, row * WIDE : (row + 1) * WIDE]
        for part in range(3):
            out_ref[part * OWN + row : part * OWN + row + 1, :] = block[part : part + 1]


def tall_table(tab_refs, half_rows, tall_ref):
    tall = up8(half_rows)
    tall_ref[...] = jnp.zeros_like(tall_ref)
    for number, tab_ref in enumerate(tab_refs):
        for part in range(3):
            for half_row in range(half_rows):
                row, half = part * OWN + half_row // 2, half_row % 2
                at = (3 * number + part) * tall + half_row
                tall_ref[at : at + 1, :] = tab_ref[
                    row : row + 1, half * LANES : (half + 1) * LANES
                ]
    return jnp.concatenate(pieces(tall_ref[...]), 1)


def up8(count):
    return -(-count // 8) * 8


def export_tiles(table, parts, row_ref, column_ref, sums_ref):
    table = jnp.concatenate(pieces(table), 0)
    gather([(table, OWN, parts, row_ref, sums_ref)], column_ref, wide=True)
    return [tile for part in range(parts) for tile in halves(gathered(sums_ref, 8, part))]


def rows_of(tiles):
    return [[tile[slot : slot + 1] for tile in tiles] for slot in range(2 * REACH)]


def add_primal(rows, sign, part, extra_ref):
    slots = 2 * REACH
    for slot in range(slots):
        export = slot if sign > 0 else (slot + REACH) % slots
        for half in range(2):
            rows[slot].append(extra_ref[2 * part + half, export : export + 1, :])


def copy_in(pairs, sems):
    copies = [
        pltpu.make_async_copy(source, target, sems.at[number])
        for number, (source, target) in enumerate(pairs)
    ]
    for copy in copies:
        copy.start()
    for copy in copies:
        copy.wait()


def first_export(
    adjoint_hbm, primal_hbm, list_hbm, tab_a, tab_p, row_ref, column_ref, extra_ref,
    out_ref, pack_ref, adjoint_ref, primal_ref, list_ref, sums_ref, sems,
):
    copy_in(
        [(adjoint_hbm, adjoint_ref), (primal_hbm, primal_ref), (list_hbm, list_ref)], sems
    )
    owned = adjoint_ref.shape[1]
    fill_table(adjoint_ref, tab_a)
    fill_table(primal_ref, tab_p)
    codes = list_ref[...]
    node = lax.rem(17 * codes + lax.broadcasted_iota(i32, codes.shape, 1), owned)
    row_ref[...] = node >> 8
    column_ref[...] = node & 255
    table = jnp.concatenate([tab_a[...], tab_p[...]], 0)
    tiles = export_tiles(table, 6, row_ref, column_ref, sums_ref)
    for number in range(6):
        extra_ref[number] = tiles[6 + number]
    pack(lax.axis_index("dom"), 1, rows_of(tiles[:6]), pack_ref, out_ref)


def setup(
    owned, connect_ref, node_ref, master_ref, weight_ref, modulus_hbm, stiffness_ref,
    own_where, own_row, edge_where, hot_ref, column_ref, master_own, master_own_row,
    master_edge, master_lane, master_column, weight_out, modulus_out, forward_out, adjoint_out,
    map_ref, tall_ref, sums_ref, lane_ref, sems,
):
    extent = owned + 2 * REACH * WIDE
    copy = pltpu.make_async_copy(modulus_hbm, modulus_out, sems.at[0])
    copy.start()
    for out_ref, matrix in (
        (forward_out, stiffness_ref[...]),
        (adjoint_out, jnp.transpose(stiffness_ref[...])),
    ):
        high, low = pieces(matrix)
        out_ref[...] = jnp.concatenate([high, high, low], 1)
    codes = master_ref[...]
    master = lax.rem(17 * codes + 8 * lax.broadcasted_iota(i32, codes.shape, 1), extent)
    count = codes.shape[0] // 2
    master = jnp.concatenate([master[:count], master[count:]], 1)
    weight = weight_ref[...]
    weight_out[...] = jnp.concatenate([weight[:count], weight[count:]], 1)
    last = owned // LANES
    where = master >> 7
    master_own[...] = jnp.where(where < last, where, NOWHERE)
    master_edge[...] = jnp.where(where < last, NOWHERE, where - last)
    master_lane[...] = master & 127
    master_own_row[...] = jnp.where(where < last, master >> 8, NOWHERE)
    master_column[...] = master & 255

    codes = node_ref[...]
    node = jnp.where(codes == pad_code, extent, lax.rem(13 * codes, owned))
    slot = (lax.broadcasted_iota(i32, codes.shape, 1) + 1).astype(f32)
    map_ref[...] = lax.dot_general(
        spread16(match16(node >> 8, OWN), slot),
        one_hot(node & 255, WIDE),
        (((1,), (1,)), ((), ())),
        preferred_element_type=f32,
    )

    codes = connect_ref[...]
    cells = lax.broadcasted_iota(i32, codes.shape, 1)
    slots = lax.rem(27 * cells + 17 * codes, extent)
    own_where[...] = slots >> 7
    lane_ref[...] = slots & 127
    tall_ref[...] = jnp.zeros_like(tall_ref)
    for half_row in range(last):
        row, half = half_row // 2, half_row % 2
        tall_ref[half_row : half_row + 1, :] = map_ref[
            row : row + 1, half * LANES : (half + 1) * LANES
        ]
    table = jnp.concatenate(pieces(tall_ref[...]), 1)
    gather([(table, tall_ref.shape[0], 1, own_where, sums_ref)], lane_ref)
    slot = gathered(sums_ref, codes.shape[0], 0).astype(i32)
    where = slots >> 7
    hanging = slot > 0
    outside = where >= last
    lane = jnp.where(hanging, slot - 1, slots & 127)
    lane_ref[...] = lane
    where_own = jnp.where(hanging | outside, NOWHERE, where)
    own_where[...] = where_own
    own_row[...], column_ref[...] = rows_and_columns(where_own, lane)
    edge_where[...] = jnp.where(hanging, 4 * REACH, jnp.where(outside, where - last, NOWHERE))

    def body(block, carry):
        start = pl.multiple_of(block * 16, 16)
        for j in range(16):
            at = pl.multiple_of((start + j) * LANES, LANES)
            hot_ref[pl.ds(at, LANES), :] = one_hot(lane_ref[pl.ds(start + j, 1), :], LANES)
        return carry

    lax.fori_loop(0, codes.shape[0] // 16, body, 0)
    copy.wait()


def own_gather(
    half_rows, fields, row_ref, lane_ref, master_row, master_lane, weight_ref, *refs
):
    tab_refs, refs = refs[:fields], refs[fields:]
    outs, (tall_ref, sums_ref) = refs[:-2], refs[-2:]
    tall = up8(half_rows)
    table = tall_table(tab_refs, half_rows, tall_ref)
    parts = 3 * fields
    gather([(table, tall, parts, master_row, sums_ref)], master_lane)
    found = sum_masters(sums_ref, 0, weight_ref[...])
    if fields == 2:
        found += sum_masters(sums_ref, 3, weight_ref[...])
    for field in range(fields):
        for part in range(3):
            outs[2 * field + 1][part : part + 1, :] = found[3 * field + part]
    gather([(table, tall, parts, row_ref, sums_ref)], lane_ref)
    count = row_ref.shape[0]
    for field in range(fields):
        cells_ref = outs[2 * field]
        for part in range(3):
            cells_ref[part * count : (part + 1) * count, :] = gathered(
                sums_ref, count, 3 * field + part
            )


def ghost_rows(place, got_refs, first, edge_ref):
    edge_ref[...] = jnp.zeros_like(edge_ref)
    for part in range(3):
        for half in range(2):
            lines = landed(place, 1, got_refs[part], first[part] + half)
            for slot in range(2 * REACH):
                at = part * TALL + 2 * slot + half
                edge_ref[at : at + 1, :] = lines[slot]
    return jnp.concatenate(pieces(edge_ref[...]), 1)


def hanging_rows(found, hang_ref, edge_ref):
    for part in range(3):
        at = part * TALL + 4 * REACH
        edge_ref[at : at + 1, :] = found[part] + hang_ref[part : part + 1, :]
    return jnp.concatenate(pieces(edge_ref[...]), 1)


def edge_gather(
    place, got_refs, first, cells_ref, hang_ref, row_ref, lane_ref, master_row, master_lane,
    weight_ref, edge_ref, sums_ref, out_ref,
):
    table = ghost_rows(place, got_refs, first, edge_ref)
    gather([(table, TALL, 3, master_row, sums_ref)], master_lane)
    table = hanging_rows(sum_masters(sums_ref, 0, weight_ref[...]), hang_ref, edge_ref)
    gather([(table, TALL, 3, row_ref, sums_ref)], lane_ref)
    count = row_ref.shape[0]
    for part in range(3):
        rows = slice(part * count, (part + 1) * count)
        out_ref[rows, :] = cells_ref[rows, :] + gathered(sums_ref, count, part)


def edge_product(
    primal_part, got_ref, cells_ref, hang_ref, row_ref, lane_ref, master_row,
    master_lane, weight_ref, extra_ref, modulus_ref, stiffness_ref, out_ref,
    image_ref, held_ref, pack_ref, edge_ref, sums_ref, full_ref, low_ref, sum_ref, *scratch,
):
    place = lax.axis_index("dom")
    edge_gather(
        place, [got_ref] * 3, (0, 2, 4), cells_ref, hang_ref, row_ref, lane_ref,
        master_row, master_lane, weight_ref, edge_ref, sums_ref, full_ref,
    )
    image = modulus_ref[...] * product(stiffness_ref[...], full_ref[...])
    image_ref[...] = image
    full_ref[...], low_ref[...] = split32(image)
    scatter(full_ref, low_ref, EDGE, row_ref, lane_ref, sum_ref)
    sums = add_pieces(sum_ref[...])
    slots = 2 * REACH
    held = jnp.concatenate(
        [sums[part * EDGE + 2 * slots : part * EDGE + 2 * slots + 1] for part in range(3)], 0
    )
    held_ref[...] = held
    sums += spread_hanging(held, weight_ref[...], EDGE, master_row, master_lane, scratch)
    rows = [
        [
            sums[part * EDGE + 2 * slot + half : part * EDGE + 2 * slot + half + 1]
            for part in range(3)
            for half in range(2)
        ]
        for slot in range(slots)
    ]
    add_primal(rows, -1, primal_part, extra_ref)
    pack(place, -1, rows, pack_ref, out_ref)


def own_sums(
    image_ref, held_ref, row_ref, column_ref, master_row, master_column, weight_ref,
    tab_ref, source_ref, inverse_ref, out_ref, *rest,
):
    *tables, high_ref, low_ref, sum_ref = rest[:-3]
    if tables:
        tab_source, tab_inverse = tables
        fill_table(source_ref, tab_source)
        fill_table(inverse_ref, tab_inverse)
        source_ref, inverse_ref = tab_source, tab_inverse
    high_ref[...], low_ref[...] = split32(image_ref[...])
    scatter(high_ref, low_ref, OWN, row_ref, column_ref, sum_ref)
    applied = add_pieces(sum_ref[...]) + spread_hanging(
        held_ref[...], weight_ref[...], OWN, master_row, master_column, rest[-3:]
    )
    out_ref[...] = tab_ref[...] + relaxation * inverse_ref[...] * (source_ref[...] - applied)


def update(
    primal_part, got_ref, row_ref, column_ref, partial_ref, inverse_ref, extra_ref,
    out_ref, tab_ref,
    pack_ref, sums_ref, *scratch,
):
    place = lax.axis_index("dom")
    values = [landed_wide(place, -1, got_ref, part) for part in range(3)]
    returned = scatter_few(values, OWN, row_ref, column_ref, scratch)
    fresh = partial_ref[...] - relaxation * inverse_ref[...] * returned
    tab_ref[...] = fresh
    rows = rows_of(export_tiles(fresh, 3, row_ref, column_ref, sums_ref))
    if primal_part is not None:
        add_primal(rows, 1, primal_part, extra_ref)
    pack(place, 1, rows, pack_ref, out_ref)


def last_gather(
    half_rows, tab_ref, own_where, lane_ref, master_own, master_lane, weight_ref,
    got_a, got_b, got_c, primal_cells, primal_hang, edge_where, master_edge, modulus_ref,
    stiffness_ref, cells_ref, hang_ref, ku_ref, final_ref,
    tall_ref, sums_ref, edge_ref, edge_sums, full_ref,
):
    tall = up8(half_rows)
    own = tall_table([tab_ref], half_rows, tall_ref)
    edge = ghost_rows(lax.axis_index("dom"), (got_a, got_b, got_c), (6, 6, 6), edge_ref)
    gather(
        [(own, tall, 3, master_own, sums_ref), (edge, TALL, 3, master_edge, edge_sums)],
        master_lane,
    )
    weight = weight_ref[...]
    found = sum_masters(sums_ref, 0, weight)
    for part in range(3):
        hang_ref[part : part + 1, :] = found[part]
    edge = hanging_rows(sum_masters(edge_sums, 0, weight), primal_hang, edge_ref)
    gather(
        [(own, tall, 3, own_where, sums_ref), (edge, TALL, 3, edge_where, edge_sums)], lane_ref
    )
    count = own_where.shape[0]
    for part in range(3):
        rows = slice(part * count, (part + 1) * count)
        cells_ref[rows, :] = gathered(sums_ref, count, part)
        full_ref[rows, :] = primal_cells[rows, :] + gathered(edge_sums, count, part)
    ku_ref[...] = modulus_ref[...] * product(stiffness_ref[...], full_ref[...])
    for row in range(final_ref.shape[1] // WIDE):
        for part in range(3):
            final_ref[part : part + 1, row * WIDE : (row + 1) * WIDE] = tab_ref[
                part * OWN + row : part * OWN + row + 1, :
            ]


def fluxes(
    got_ref, cells_ref, hang_ref, row_ref, lane_ref, master_row,
    master_lane, weight_ref, ku_ref, load_ref, sub_cell, sub_face, out_ref,
    term_ref, pack_ref, edge_ref, sums_ref, full_ref, tall_ref, code_ref, few_ref,
):
    place = lax.axis_index("dom")
    edge_gather(
        place, [got_ref] * 3, (0, 2, 4), cells_ref, hang_ref, row_ref, lane_ref,
        master_row, master_lane, weight_ref, edge_ref, sums_ref, full_ref,
    )
    cells = full_ref[...]
    ku = ku_ref[...]
    term_ref[...] = jnp.sum(cells * (load_ref[...] - ku), 0, keepdims=True)
    face = lax.broadcasted_iota(i32, (8, ku.shape[0]), 0)
    node = lax.broadcasted_iota(i32, (8, ku.shape[0]), 1) & 63
    index = jnp.where(face < 2, node >> 4, jnp.where(face < 4, (node >> 2) & 3, node & 3))
    member = jnp.where((face < 6) & (index == 3 * (face & 1)), 1.0, 0.0).astype(f32)
    flux = jnp.dot(
        member, ku * cells, precision=lax.Precision.HIGHEST, preferred_element_type=f32
    )
    tall_ref[...] = jnp.zeros_like(tall_ref)
    for number in range(6):
        for half in range(2):
            at = 2 * number + half
            tall_ref[at : at + 1, :] = flux[
                number : number + 1, half * LANES : (half + 1) * LANES
            ]
    cell = sub_cell[...]
    code_ref[:8, :] = 2 * sub_face[...] + (cell >> 7)
    code_ref[8:, :] = cell & 127
    table = jnp.concatenate(pieces(tall_ref[...]), 1)
    gather([(table, 16, 1, code_ref.at[:8, :], few_ref)], code_ref.at[8:, :])
    found = gathered(few_ref, 8, 0)
    rows = [[found[slot : slot + 1]] for slot in range(2 * REACH)]
    pack(place, 1, rows, pack_ref, out_ref)


def collect(got_ref, owner_ref, term_ref, out_ref):
    count = term_ref.shape[1]
    got = jnp.concatenate(landed(lax.axis_index("dom"), 1, got_ref, 0), 1)
    hot = jnp.concatenate(
        [one_hot(owner_ref[slot : slot + 1, :], count) for slot in range(2 * REACH)], 1
    )
    values = jnp.concatenate(
        [jnp.broadcast_to(x, (16, got.shape[1])).astype(bf16) for x in split32(got)], 0
    )
    sums = lax.dot_general(values, hot, (((1,), (1,)), ((), ())), preferred_element_type=f32)
    face_term = sums[0:1] + sums[16:17]
    out_ref[...] = (jnp.abs(term_ref[...]) + jnp.abs(face_term)) / scale_down


FAST = pl.BlockSpec(memory_space=pltpu.VMEM)
FAR = pl.BlockSpec(memory_space=pl.ANY)


def away(*arrays):
    return [pltpu.with_memory_space_constraint(x, pltpu.HBM) for x in arrays]


def call(kernel, outs, scratch=(), specs=None, sems=0):
    scratch = [pltpu.VMEM(shape, kind) for shape, kind in scratch]
    if sems:
        scratch.append(pltpu.SemaphoreType.DMA((sems,)))

    def run(*args):
        return pl.pallas_call(
            kernel,
            out_shape=[jax.ShapeDtypeStruct(*out) for out in outs],
            in_specs=specs or [FAST] * len(args),
            scratch_shapes=scratch,
            compiler_params=pltpu.CompilerParams(vmem_limit_bytes=16 * 1024 * 1024),
        )(*args)

    return run


def local(
    adjoint_start,
    adjoint_source,
    inverse_diagonal,
    primal_field,
    cell_load,
    modulus,
    stiffness,
    connectivity,
    hang_node,
    hang_master,
    hang_weight,
    ghost_lists,
    subface_cell,
    subface_face,
    subface_owner,
):
    slots = 2 * REACH
    local_values, cell_count = cell_load.shape
    nodes = connectivity.shape[0]
    half_rows = adjoint_start.shape[1] // LANES
    table = ((3 * OWN, WIDE), f32)
    index = ((nodes, cell_count), i32)
    cells_shape = ((local_values, cell_count), f32)
    hang_shape = ((3, hang_node.shape[0]), f32)
    master_shape = ((8, WIDE), i32)

    count = lax.axis_size("dom")

    def packed(height):
        return [((count, height, LANES), f32)]

    def room(height):
        return ((count + 1, height, LANES), f32)

    tall = up8(half_rows)
    few_sums = ((2, 3 * 64, LANES), f32)
    many_sums = ((2, local_values * 8, LANES), f32)
    own_tall = ((3 * tall, LANES), f32)
    edge = [((3 * TALL, LANES), f32), many_sums, cells_shape]
    tab, tab_primal, list_row, list_column, extra, blocks = call(
        first_export,
        [table, table]
        + [(ghost_lists.shape, i32)] * 2
        + [((6, slots, LANES), f32)]
        + packed(8),
        [
            room(8),
            (adjoint_start.shape, f32),
            (primal_field.shape, f32),
            (ghost_lists.shape, i32),
            ((2, 6 * 64, LANES), f32),
        ],
        [FAR, FAR, FAR],
        sems=3,
    )(*away(adjoint_start, primal_field, ghost_lists))
    ghosts = exchange(blocks)
    (
        own_where, own_row, edge_where, hot, own_column, master_own, master_own_row, master_edge,
        master_lane, master_column, weight, moduli, forward, backward,
    ) = call(
        functools.partial(setup, adjoint_start.shape[1]),
        [index] * 3
        + [((nodes * LANES, cell_count), bf16), index]
        + [master_shape] * 5
        + [((8, WIDE), f32), ((1, cell_count), f32)]
        + [((local_values, 3 * local_values), bf16)] * 2,
        [((OWN, WIDE), f32), ((tall, LANES), f32), ((2, nodes * 8, LANES), f32), index],
        [FAST] * 4 + [FAR, FAST],
        sems=1,
    )(
        connectivity, hang_node.reshape(1, -1), hang_master, hang_weight,
        *away(modulus.reshape(1, cell_count)), stiffness,
    )

    def gather_own(*fields):
        number = len(fields)
        return call(
            functools.partial(own_gather, half_rows, number),
            [cells_shape, hang_shape] * number,
            [
                ((3 * number * tall, LANES), f32),
                ((2, number * local_values * 8, LANES), f32),
            ],
            specs=[FAST] * (5 + number),
        )(own_where, hot, master_own, master_lane, weight, *fields)

    on_edge = (edge_where, hot, master_edge, master_lane, weight)
    landings = []
    source, inverse = adjoint_source, inverse_diagonal
    for sweep in range(SWEEPS):
        if sweep == 1:
            cells, hang, *primal_cells = gather_own(tab, tab_primal)
        else:
            cells, hang = gather_own(tab)
        blocks, image, held = call(
            functools.partial(edge_product, 2 * sweep),
            packed(8) + [cells_shape, hang_shape],
            [room(8)] + edge + [cells_shape, ((6 * EDGE, LANES), f32)] + few(EDGE, LANES),
        )(ghosts, cells, hang, *on_edge, extra, moduli, backward)
        returned = exchange(blocks)
        landings.append(returned)
        partial, *tables = call(
            own_sums,
            [table] * (3 if sweep == 0 else 1),
            [cells_shape, cells_shape, ((6 * OWN, WIDE), f32)] + few(OWN, WIDE),
            specs=[FAST] * 10,
        )(
            image, held, own_row, own_column, master_own_row, master_column, weight, tab, source,
            inverse,
        )
        if tables:
            source, inverse = tables
        blocks, tab = call(
            functools.partial(update, 1 if sweep == 0 else None),
            packed(8) + [table],
            [room(8), few_sums] + few(OWN, WIDE),
        )(returned, list_row, list_column, partial, inverse, extra)
        ghosts = exchange(blocks)
        landings.append(ghosts)
    cells, hang, ku, adjoint = call(
        functools.partial(last_gather, half_rows),
        [cells_shape, hang_shape, cells_shape, (adjoint_start.shape, f32)],
        [own_tall, many_sums] + edge,
    )(
        tab, own_where, hot, master_own, master_lane, weight, *landings[:3], *primal_cells,
        edge_where, master_edge, moduli, forward,
    )
    blocks, term = call(
        fluxes,
        packed(1) + [((1, cell_count), f32)],
        [room(1)]
        + edge
        + [
            ((16, LANES), f32),
            ((16, subface_cell.shape[1]), i32),
            ((1, 64, LANES), f32),
        ],
    )(ghosts, cells, hang, *on_edge, ku, cell_load, subface_cell, subface_face)
    received = exchange(blocks)
    (indicator,) = call(collect, [((1, cell_count), f32)])(
        received, subface_owner, term
    )
    return (adjoint, indicator.reshape(cell_count))


def solution(mesh):
    placed = (
        P(None, "dom"),
        P(None, "dom"),
        P(None, "dom"),
        P(None, "dom"),
        P(None, "dom"),
        P("dom"),
        P(),
        P(None, "dom"),
        P("dom"),
        P(None, "dom"),
        P(None, "dom"),
        P(None, "dom"),
        P(None, "dom"),
        P(None, "dom"),
        P(None, "dom"),
    )
    return jax.shard_map(
        local, mesh=mesh, in_specs=placed, out_specs=(P(None, "dom"), P("dom")), check_vma=False
    )
```

```python
import functools

import jax
import jax.numpy as jnp
from jax import lax
from jax.experimental import pallas as pl
from jax.experimental.pallas import tpu as pltpu
from jax.sharding import PartitionSpec as P

REACH = 4
SWEEPS = 2
LANES = 128
WIDE = 2 * LANES
OWN = 32
EDGE = 16
TALL = 24
NOWHERE = 126

relaxation = 0.7
scale_down = 16.0
pad_code = 16368

f32 = jnp.float32
bf16 = jnp.bfloat16
i32 = jnp.int32


def neighbour_offsets():
    return [step + 1 for step in range(REACH)] + [-(step + 1) for step in range(REACH)]


def exchange(packed):
    return lax.all_to_all(packed, "dom", 0, 0, tiled=True)


def pack(place, sign, rows, pack_ref, out_ref):
    count = out_ref.shape[0]
    pack_ref[...] = jnp.zeros_like(pack_ref)
    for slot, offset in enumerate(neighbour_offsets()):
        target = place + sign * offset
        at = jnp.where((target >= 0) & (target < count), target, count)
        for number, row in enumerate(rows[slot]):
            pack_ref[at, number : number + 1, :] = row
    out_ref[...] = pack_ref[:count]


def landed(place, sign, got_ref, number):
    count = got_ref.shape[0]
    rows = []
    for offset in neighbour_offsets():
        source = place - sign * offset
        row = got_ref[jnp.clip(source, 0, count - 1), number : number + 1, :]
        there = jnp.broadcast_to((source >= 0) & (source < count), row.shape)
        rows.append(jnp.where(there, row, 0.0))
    return rows


def landed_wide(place, sign, got_ref, part):
    halves = [
        jnp.concatenate(landed(place, sign, got_ref, 2 * part + half), 0) for half in range(2)
    ]
    return jnp.concatenate(halves, 1)


def match16(row, count):
    width = row.shape[1]
    wide = jnp.broadcast_to(row.astype(f32), (16, width)).astype(bf16)
    numbers = lax.broadcasted_iota(i32, (count, width), 0).astype(f32).astype(bf16)
    return numbers.reshape(count // 16, 16, width) == wide[None]


def one_hot(row, count):
    mask = match16(row, count)
    ones = jnp.ones(mask.shape, bf16)
    return jnp.where(mask, ones, jnp.zeros_like(ones)).reshape(count, row.shape[1])


def spread16(mask, row):
    wide = jnp.broadcast_to(row, (16, row.shape[1])).astype(bf16)[None]
    out = jnp.where(mask, jnp.broadcast_to(wide, mask.shape), jnp.zeros(mask.shape, bf16))
    return out.reshape(mask.shape[0] * 16, row.shape[1])


def pieces(x):
    high = x.astype(bf16)
    return high, (x - high.astype(f32)).astype(bf16)


def gather(jobs, column_ref, high=2 * LANES, stacked=False):
    count, width = column_ref.shape
    tables = jnp.concatenate([job[0] for job in jobs], 0)
    tall = tables.shape[0] // 2
    numbers = lax.broadcasted_iota(i32, (max(job[1] for job in jobs), width), 0)
    step = min(count, 32 if sum(job[1] * job[2] for job in jobs) <= 192 else 16)

    def body(block, carry):
        start = pl.multiple_of(block * step, step)
        for j in range(step):
            hot = one_hot(column_ref[pl.ds(start + j, 1), :], high if stacked else LANES)
            if not stacked:
                hot = jnp.concatenate([hot, hot], 0)
            all_found = jnp.dot(tables, hot, preferred_element_type=f32)
            if stacked:
                all_found = all_found[:tall] + all_found[tall:]
            top = 0
            for _, rows, parts, row_ref, sums_ref in jobs:
                found = all_found[top : top + parts * rows]
                top += parts * rows
                mask = numbers[:rows] == jnp.broadcast_to(
                    row_ref[pl.ds(start + j, 1), :], (rows, width)
                )
                for part in range(parts):
                    kept = jnp.where(mask, found[part * rows : (part + 1) * rows], 0.0)
                    kept = jnp.sum(kept.reshape(rows // 8, 8, width), 0)
                    for half in range(width // LANES):
                        sums_ref[half, pl.ds(part * count * 8 + start * 8 + j * 8, 8), :] = kept[
                            :, half * LANES : (half + 1) * LANES
                        ]
        return carry

    if count == step:
        body(0, 0)
    else:
        lax.fori_loop(0, count // step, body, 0)


def gathered(sums_ref, count, part):
    totals = []
    for half in range(sums_ref.shape[0]):
        rows = [sums_ref[half, pl.ds(part * count * 8 + s, count, stride=8), :] for s in range(8)]
        while len(rows) > 1:
            rows = [a + b for a, b in zip(rows[::2], rows[1::2])]
        totals.append(rows[0])
    return jnp.concatenate(totals, 1)


def halves(x):
    return [x[:, :LANES], x[:, LANES:]]


def rows_and_columns(where, lane):
    return where >> 1, (where & 1) * LANES + lane


def scatter(high_ref, low_ref, rows, row_ref, column_ref, sum_ref, hanging=None):
    count = row_ref.shape[0]
    step = min(count, 32)

    def hanging_tile(number):
        at_row = row_ref[pl.ds(number, 1), :]
        shape = (8, at_row.shape[1])
        numbers = lax.broadcasted_iota(i32, shape, 0)
        tile = jnp.zeros(shape, f32)
        for piece, piece_ref in enumerate((high_ref, low_ref)):
            for part in range(3):
                value = jnp.broadcast_to(piece_ref[pl.ds(part * count + number, 1), :], shape)
                tile = jnp.where(numbers == 3 * piece + part, value, tile)
        tile = jnp.where(jnp.broadcast_to(at_row, shape) == hanging, tile, 0.0)
        return jnp.concatenate([tile, jnp.zeros_like(tile)], 0).astype(bf16)

    def product(start):
        masks = [match16(row_ref[pl.ds(start + j, 1), :], rows) for j in range(8)]
        hot = jnp.concatenate(
            [one_hot(column_ref[pl.ds(start + j, 1), :], sum_ref.shape[1]) for j in range(8)], 1
        )
        stacked = [
            jnp.concatenate(
                [
                    spread16(mask, piece_ref[pl.ds(part * count + start + j, 1), :])
                    for j, mask in enumerate(masks)
                ],
                1,
            )
            for piece_ref in (high_ref, low_ref)
            for part in range(3)
        ]
        if hanging is not None:
            stacked.append(jnp.concatenate([hanging_tile(start + j) for j in range(8)], 1))
        return lax.dot_general(
            jnp.concatenate(stacked, 0), hot, (((1,), (1,)), ((), ())), preferred_element_type=f32
        )

    if count == 8:
        sum_ref[...] = product(0)
        return
    sum_ref[...] = jnp.zeros_like(sum_ref)

    def body(block, carry):
        start = pl.multiple_of(block * step, step)
        total = product(start)
        for first in range(8, step, 8):
            total += product(start + first)
        sum_ref[...] += total
        return carry

    lax.fori_loop(0, count // step, body, 0)


def split32(x):
    high = x.astype(bf16).astype(f32)
    return high, x - high


def add_pieces(sums):
    half = sums.shape[0] // 2
    return sums[:half] + sums[half:]


def scatter_few(values, rows, row_ref, column_ref, scratch):
    high_ref, low_ref, sum_ref = scratch
    for part in range(3):
        high_ref[part * 8 : part * 8 + 8, :], low_ref[part * 8 : part * 8 + 8, :] = split32(
            values[part]
        )
    scatter(high_ref, low_ref, rows, row_ref, column_ref, sum_ref)
    return add_pieces(sum_ref[...])


def few(rows, columns):
    return [((24, WIDE), f32)] * 2 + [((6 * rows, columns), f32)]


def spread_hanging(held, weight, rows, row_ref, column_ref, scratch):
    both = jnp.concatenate([held, held], 1)
    values = [weight * both[part : part + 1] for part in range(3)]
    return scatter_few(values, rows, row_ref, column_ref, scratch)


def sum_masters(sums_ref, first, weight):
    totals = []
    for part in range(first, first + 3):
        left, right = halves(weight * gathered(sums_ref, 8, part))
        totals.append(jnp.sum(left + right, 0, keepdims=True))
    return totals


def product(threefold, cells):
    high, low = pieces(cells)
    return jnp.dot(
        threefold, jnp.concatenate([high, low, high], 0), preferred_element_type=f32
    )


def fill_table(x_ref, out_ref):
    count = x_ref.shape[1] // WIDE
    for part in range(3):
        out_ref[part * OWN + count : (part + 1) * OWN, :] = jnp.zeros((OWN - count, WIDE), f32)
    for row in range(count):
        block = x_ref[:, row * WIDE : (row + 1) * WIDE]
        for part in range(3):
            out_ref[part * OWN + row : part * OWN + row + 1, :] = block[part : part + 1]


def tall_table(tab_refs, half_rows, tall_ref):
    tall = up8(half_rows)
    tall_ref[...] = jnp.zeros_like(tall_ref)
    for number, tab_ref in enumerate(tab_refs):
        for part in range(3):
            for half_row in range(half_rows):
                row, half = part * OWN + half_row // 2, half_row % 2
                at = (3 * number + part) * tall + half_row
                tall_ref[at : at + 1, :] = tab_ref[
                    row : row + 1, half * LANES : (half + 1) * LANES
                ]
    return jnp.concatenate(pieces(tall_ref[...]), 1)


def up8(count):
    return -(-count // 8) * 8


def export_tiles(table, parts, row_ref, column_ref, sums_ref):
    table = jnp.concatenate(pieces(table), 0)
    gather([(table, OWN, parts, row_ref, sums_ref)], column_ref, WIDE, stacked=True)
    return [tile for part in range(parts) for tile in halves(gathered(sums_ref, 8, part))]


def rows_of(tiles):
    return [[tile[slot : slot + 1] for tile in tiles] for slot in range(2 * REACH)]


def add_primal(rows, sign, part, extra_ref):
    slots = 2 * REACH
    for slot in range(slots):
        export = slot if sign > 0 else (slot + REACH) % slots
        for half in range(2):
            rows[slot].append(extra_ref[2 * part + half, export : export + 1, :])


def copy_in(pairs, sems):
    copies = [
        pltpu.make_async_copy(source, target, sems.at[number])
        for number, (source, target) in enumerate(pairs)
    ]
    for copy in copies:
        copy.start()
    for copy in copies:
        copy.wait()


def first_export(
    adjoint_hbm, primal_hbm, list_hbm, modulus_hbm, node_hbm, tab_a, tab_p, row_ref,
    column_ref, extra_ref, modulus_ref, node_ref, out_ref, pack_ref, adjoint_ref, primal_ref, list_ref, sums_ref, sems,
):
    copy_in(
        [
            (adjoint_hbm, adjoint_ref),
            (primal_hbm, primal_ref),
            (list_hbm, list_ref),
            (modulus_hbm, modulus_ref),
            (node_hbm, node_ref),
        ],
        sems,
    )
    owned = adjoint_ref.shape[1]
    fill_table(adjoint_ref, tab_a)
    fill_table(primal_ref, tab_p)
    codes = list_ref[...]
    node = lax.rem(17 * codes + lax.broadcasted_iota(i32, codes.shape, 1), owned)
    row_ref[...] = node >> 8
    column_ref[...] = node & 255
    table = jnp.concatenate([tab_a[...], tab_p[...]], 0)
    tiles = export_tiles(table, 6, row_ref, column_ref, sums_ref)
    for number in range(6):
        extra_ref[number] = tiles[6 + number]
    pack(lax.axis_index("dom"), 1, rows_of(tiles[:6]), pack_ref, out_ref)


def setup(
    owned, connect_ref, node_ref, master_ref, weight_ref, stiffness_ref,
    own_where, own_row, edge_where, lane_ref, column_ref, master_own, master_own_row,
    master_edge, master_lane, master_column, weight_out, forward_out, adjoint_out,
    map_ref, tall_ref, sums_ref,
):
    extent = owned + 2 * REACH * WIDE
    for out_ref, matrix in (
        (forward_out, stiffness_ref[...]),
        (adjoint_out, jnp.transpose(stiffness_ref[...])),
    ):
        high, low = pieces(matrix)
        out_ref[...] = jnp.concatenate([high, high, low], 1)
    codes = master_ref[...]
    master = lax.rem(17 * codes + 8 * lax.broadcasted_iota(i32, codes.shape, 1), extent)
    count = codes.shape[0] // 2
    master = jnp.concatenate([master[:count], master[count:]], 1)
    weight = weight_ref[...]
    weight_out[...] = jnp.concatenate([weight[:count], weight[count:]], 1)
    last = owned // LANES
    where = master >> 7
    master_own[...] = jnp.where(where < last, where, NOWHERE)
    master_edge[...] = jnp.where(where < last, NOWHERE, where - last)
    master_lane[...] = master & 127
    master_own_row[...] = jnp.where(where < last, master >> 8, NOWHERE)
    master_column[...] = master & 255

    codes = node_ref[...]
    node = jnp.where(codes == pad_code, extent, lax.rem(13 * codes, owned))
    slot = (lax.broadcasted_iota(i32, codes.shape, 1) + 1).astype(f32)
    map_ref[...] = lax.dot_general(
        spread16(match16(node >> 8, OWN), slot),
        one_hot(node & 255, WIDE),
        (((1,), (1,)), ((), ())),
        preferred_element_type=f32,
    )

    codes = connect_ref[...]
    cells = lax.broadcasted_iota(i32, codes.shape, 1)
    slots = lax.rem(27 * cells + 17 * codes, extent)
    own_where[...] = slots >> 7
    lane_ref[...] = slots & 127
    tall_ref[...] = jnp.zeros_like(tall_ref)
    for half_row in range(last):
        row, half = half_row // 2, half_row % 2
        tall_ref[half_row : half_row + 1, :] = map_ref[
            row : row + 1, half * LANES : (half + 1) * LANES
        ]
    table = jnp.concatenate(pieces(tall_ref[...]), 1)
    gather([(table, tall_ref.shape[0], 1, own_where, sums_ref)], lane_ref)
    slot = gathered(sums_ref, codes.shape[0], 0).astype(i32)
    where = slots >> 7
    hanging = slot > 0
    outside = where >= last
    lane = jnp.where(hanging, slot - 1, slots & 127)
    lane_ref[...] = lane
    where_own = jnp.where(hanging | outside, NOWHERE, where)
    own_where[...] = where_own
    own_row[...], column_ref[...] = rows_and_columns(where_own, lane)
    edge_where[...] = jnp.where(hanging, 4 * REACH, jnp.where(outside, where - last, NOWHERE))


def own_gather(
    half_rows, fields, row_ref, lane_ref, master_row, master_lane, weight_ref, *refs
):
    tab_refs, refs = refs[:fields], refs[fields:]
    outs, (tall_ref, sums_ref) = refs[:-2], refs[-2:]
    tall = up8(half_rows)
    table = tall_table(tab_refs, half_rows, tall_ref)
    parts = 3 * fields
    gather([(table, tall, parts, master_row, sums_ref)], master_lane)
    found = sum_masters(sums_ref, 0, weight_ref[...])
    if fields == 2:
        found += sum_masters(sums_ref, 3, weight_ref[...])
    for field in range(fields):
        for part in range(3):
            outs[2 * field + 1][part : part + 1, :] = found[3 * field + part]
    gather([(table, tall, parts, row_ref, sums_ref)], lane_ref)
    count = row_ref.shape[0]
    for field in range(fields):
        cells_ref = outs[2 * field]
        for part in range(3):
            cells_ref[part * count : (part + 1) * count, :] = gathered(
                sums_ref, count, 3 * field + part
            )


def ghost_rows(place, got_refs, first, edge_ref, axis=1):
    edge_ref[...] = jnp.zeros_like(edge_ref)
    for part in range(3):
        for half in range(2):
            lines = landed(place, 1, got_refs[part], first[part] + half)
            for slot in range(2 * REACH):
                at = part * TALL + 2 * slot + half
                edge_ref[at : at + 1, :] = lines[slot]
    return jnp.concatenate(pieces(edge_ref[...]), axis)


def hanging_rows(found, hang_ref, edge_ref, axis=1):
    for part in range(3):
        at = part * TALL + 4 * REACH
        edge_ref[at : at + 1, :] = found[part] + hang_ref[part : part + 1, :]
    return jnp.concatenate(pieces(edge_ref[...]), axis)


def edge_gather(
    place, got_refs, first, cells_ref, hang_ref, row_ref, lane_ref, master_row, master_lane,
    weight_ref, edge_ref, sums_ref, out_ref,
):
    table = ghost_rows(place, got_refs, first, edge_ref, 0)
    gather([(table, TALL, 3, master_row, sums_ref)], master_lane, LANES, stacked=True)
    table = hanging_rows(sum_masters(sums_ref, 0, weight_ref[...]), hang_ref, edge_ref, 0)
    gather([(table, TALL, 3, row_ref, sums_ref)], lane_ref, LANES, stacked=True)
    count = row_ref.shape[0]
    for part in range(3):
        rows = slice(part * count, (part + 1) * count)
        out_ref[rows, :] = cells_ref[rows, :] + gathered(sums_ref, count, part)


def edge_product(
    primal_part, got_ref, cells_ref, hang_ref, row_ref, lane_ref, master_row,
    master_lane, weight_ref, extra_ref, modulus_ref, stiffness_ref, out_ref,
    image_ref, held_ref, pack_ref, edge_ref, sums_ref, full_ref, low_ref, sum_ref, *scratch,
):
    place = lax.axis_index("dom")
    edge_gather(
        place, [got_ref] * 3, (0, 2, 4), cells_ref, hang_ref, row_ref, lane_ref,
        master_row, master_lane, weight_ref, edge_ref, sums_ref, full_ref,
    )
    image = modulus_ref[...] * product(stiffness_ref[...], full_ref[...])
    image_ref[...] = image
    full_ref[...], low_ref[...] = split32(image)
    slots = 2 * REACH
    scatter(full_ref, low_ref, EDGE, row_ref, lane_ref, sum_ref, hanging=2 * slots)
    sums = add_pieces(sum_ref[: 6 * EDGE, :])
    held = sum_ref[6 * EDGE : 6 * EDGE + 3, :] + sum_ref[6 * EDGE + 3 : 6 * EDGE + 6, :]
    held_ref[...] = held
    sums += spread_hanging(held, weight_ref[...], EDGE, master_row, master_lane, scratch)
    rows = [
        [
            sums[part * EDGE + 2 * slot + half : part * EDGE + 2 * slot + half + 1]
            for part in range(3)
            for half in range(2)
        ]
        for slot in range(slots)
    ]
    add_primal(rows, -1, primal_part, extra_ref)
    pack(place, -1, rows, pack_ref, out_ref)


def own_sums(
    image_ref, held_ref, row_ref, column_ref, master_row, master_column, weight_ref,
    tab_ref, source_ref, inverse_ref, out_ref, *rest,
):
    *tables, high_ref, low_ref, sum_ref = rest[:-3]
    if tables:
        tab_source, tab_inverse = tables
        fill_table(source_ref, tab_source)
        fill_table(inverse_ref, tab_inverse)
        source_ref, inverse_ref = tab_source, tab_inverse
    high_ref[...], low_ref[...] = split32(image_ref[...])
    scatter(high_ref, low_ref, OWN, row_ref, column_ref, sum_ref)
    applied = add_pieces(sum_ref[...]) + spread_hanging(
        held_ref[...], weight_ref[...], OWN, master_row, master_column, rest[-3:]
    )
    out_ref[...] = tab_ref[...] + relaxation * inverse_ref[...] * (source_ref[...] - applied)


def update(
    primal_part, got_ref, row_ref, column_ref, partial_ref, inverse_ref, extra_ref,
    out_ref, tab_ref,
    pack_ref, sums_ref, *scratch,
):
    place = lax.axis_index("dom")
    values = [landed_wide(place, -1, got_ref, part) for part in range(3)]
    returned = scatter_few(values, OWN, row_ref, column_ref, scratch)
    fresh = partial_ref[...] - relaxation * inverse_ref[...] * returned
    tab_ref[...] = fresh
    rows = rows_of(export_tiles(fresh, 3, row_ref, column_ref, sums_ref))
    if primal_part is not None:
        add_primal(rows, 1, primal_part, extra_ref)
    pack(place, 1, rows, pack_ref, out_ref)


def last_gather(
    half_rows, tab_ref, own_where, lane_ref, master_own, master_lane, weight_ref,
    got_a, got_b, got_c, primal_cells, primal_hang, edge_where, master_edge, modulus_ref,
    stiffness_ref, cells_ref, hang_ref, ku_ref, final_ref,
    tall_ref, sums_ref, edge_ref, edge_sums, full_ref,
):
    tall = up8(half_rows)
    own = tall_table([tab_ref], half_rows, tall_ref)
    edge = ghost_rows(lax.axis_index("dom"), (got_a, got_b, got_c), (6, 6, 6), edge_ref)
    gather(
        [(own, tall, 3, master_own, sums_ref), (edge, TALL, 3, master_edge, edge_sums)],
        master_lane,
    )
    weight = weight_ref[...]
    found = sum_masters(sums_ref, 0, weight)
    for part in range(3):
        hang_ref[part : part + 1, :] = found[part]
    edge = hanging_rows(sum_masters(edge_sums, 0, weight), primal_hang, edge_ref)
    gather(
        [(own, tall, 3, own_where, sums_ref), (edge, TALL, 3, edge_where, edge_sums)], lane_ref
    )
    count = lane_ref.shape[0]
    for part in range(3):
        rows = slice(part * count, (part + 1) * count)
        cells_ref[rows, :] = gathered(sums_ref, count, part)
        full_ref[rows, :] = primal_cells[rows, :] + gathered(edge_sums, count, part)
    ku_ref[...] = modulus_ref[...] * product(stiffness_ref[...], full_ref[...])
    for row in range(final_ref.shape[1] // WIDE):
        for part in range(3):
            final_ref[part : part + 1, row * WIDE : (row + 1) * WIDE] = tab_ref[
                part * OWN + row : part * OWN + row + 1, :
            ]


def fluxes(
    got_ref, cells_ref, hang_ref, row_ref, lane_ref, master_row,
    master_lane, weight_ref, ku_ref, load_ref, sub_cell, sub_face, out_ref,
    term_ref, pack_ref, edge_ref, sums_ref, full_ref, tall_ref, code_ref, few_ref,
):
    place = lax.axis_index("dom")
    edge_gather(
        place, [got_ref] * 3, (0, 2, 4), cells_ref, hang_ref, row_ref, lane_ref,
        master_row, master_lane, weight_ref, edge_ref, sums_ref, full_ref,
    )
    cells = full_ref[...]
    ku = ku_ref[...]
    term_ref[...] = jnp.sum(cells * (load_ref[...] - ku), 0, keepdims=True)
    face = lax.broadcasted_iota(i32, (8, ku.shape[0]), 0)
    node = lax.broadcasted_iota(i32, (8, ku.shape[0]), 1) & 63
    index = jnp.where(face < 2, node >> 4, jnp.where(face < 4, (node >> 2) & 3, node & 3))
    member = jnp.where((face < 6) & (index == 3 * (face & 1)), 1.0, 0.0).astype(f32)
    flux = jnp.dot(
        member, ku * cells, precision=lax.Precision.HIGHEST, preferred_element_type=f32
    )
    tall_ref[...] = jnp.zeros_like(tall_ref)
    for number in range(6):
        for half in range(2):
            at = 2 * number + half
            tall_ref[at : at + 1, :] = flux[
                number : number + 1, half * LANES : (half + 1) * LANES
            ]
    cell = sub_cell[...]
    code_ref[:8, :] = 2 * sub_face[...] + (cell >> 7)
    code_ref[8:, :] = cell & 127
    table = jnp.concatenate(pieces(tall_ref[...]), 1)
    gather([(table, 16, 1, code_ref.at[:8, :], few_ref)], code_ref.at[8:, :])
    found = gathered(few_ref, 8, 0)
    rows = [[found[slot : slot + 1]] for slot in range(2 * REACH)]
    pack(place, 1, rows, pack_ref, out_ref)


def collect(got_ref, owner_ref, term_ref, out_ref):
    count = term_ref.shape[1]
    got = jnp.concatenate(landed(lax.axis_index("dom"), 1, got_ref, 0), 1)
    hot = jnp.concatenate(
        [one_hot(owner_ref[slot : slot + 1, :], count) for slot in range(2 * REACH)], 1
    )
    values = jnp.concatenate(
        [jnp.broadcast_to(x, (16, got.shape[1])).astype(bf16) for x in split32(got)], 0
    )
    sums = lax.dot_general(values, hot, (((1,), (1,)), ((), ())), preferred_element_type=f32)
    face_term = sums[0:1] + sums[16:17]
    out_ref[...] = (jnp.abs(term_ref[...]) + jnp.abs(face_term)) / scale_down


FAST = pl.BlockSpec(memory_space=pltpu.VMEM)
FAR = pl.BlockSpec(memory_space=pl.ANY)


def away(*arrays):
    return [pltpu.with_memory_space_constraint(x, pltpu.HBM) for x in arrays]


def call(kernel, outs, scratch=(), specs=None, sems=0):
    scratch = [pltpu.VMEM(shape, kind) for shape, kind in scratch]
    if sems:
        scratch.append(pltpu.SemaphoreType.DMA((sems,)))

    def run(*args):
        return pl.pallas_call(
            kernel,
            out_shape=[jax.ShapeDtypeStruct(*out) for out in outs],
            in_specs=specs or [FAST] * len(args),
            scratch_shapes=scratch,
            compiler_params=pltpu.CompilerParams(vmem_limit_bytes=40 * 1024 * 1024),
        )(*args)

    return run


def local(
    adjoint_start,
    adjoint_source,
    inverse_diagonal,
    primal_field,
    cell_load,
    modulus,
    stiffness,
    connectivity,
    hang_node,
    hang_master,
    hang_weight,
    ghost_lists,
    subface_cell,
    subface_face,
    subface_owner,
):
    slots = 2 * REACH
    local_values, cell_count = cell_load.shape
    nodes = connectivity.shape[0]
    half_rows = adjoint_start.shape[1] // LANES
    table = ((3 * OWN, WIDE), f32)
    index = ((nodes, cell_count), i32)
    cells_shape = ((local_values, cell_count), f32)
    hang_shape = ((3, hang_node.shape[0]), f32)
    master_shape = ((8, WIDE), i32)

    count = lax.axis_size("dom")

    def packed(height):
        return [((count, height, LANES), f32)]

    def room(height):
        return ((count + 1, height, LANES), f32)

    tall = up8(half_rows)
    few_sums = ((2, 3 * 64, LANES), f32)
    many_sums = ((2, local_values * 8, LANES), f32)
    own_tall = ((3 * tall, LANES), f32)
    edge = [((3 * TALL, LANES), f32), many_sums, cells_shape]
    tab, tab_primal, list_row, list_column, extra, moduli, hang_node, blocks = call(
        first_export,
        [table, table]
        + [(ghost_lists.shape, i32)] * 2
        + [((6, slots, LANES), f32), ((1, cell_count), f32), ((1, hang_node.shape[0]), i32)]
        + packed(8),
        [
            room(8),
            (adjoint_start.shape, f32),
            (primal_field.shape, f32),
            (ghost_lists.shape, i32),
            ((2, 6 * 64, LANES), f32),
        ],
        [FAR] * 5,
        sems=5,
    )(
        *away(
            adjoint_start, primal_field, ghost_lists, modulus.reshape(1, -1),
            hang_node.reshape(1, -1),
        )
    )
    ghosts = exchange(blocks)
    (
        own_where, own_row, edge_where, lane, own_column, master_own, master_own_row, master_edge,
        master_lane, master_column, weight, forward, backward,
    ) = call(
        functools.partial(setup, adjoint_start.shape[1]),
        [index] * 5
        + [master_shape] * 5
        + [((8, WIDE), f32)]
        + [((local_values, 3 * local_values), bf16)] * 2,
        [((OWN, WIDE), f32), ((tall, LANES), f32), ((2, nodes * 8, LANES), f32)],
        [FAST] * 5,
    )(connectivity, hang_node, hang_master, hang_weight, stiffness)

    def gather_own(*fields):
        number = len(fields)
        return call(
            functools.partial(own_gather, half_rows, number),
            [cells_shape, hang_shape] * number,
            [
                ((3 * number * tall, LANES), f32),
                ((2, number * local_values * 8, LANES), f32),
            ],
            specs=[FAST] * (5 + number),
        )(own_where, lane, master_own, master_lane, weight, *fields)

    on_edge = (edge_where, lane, master_edge, master_lane, weight)
    landings = []
    source, inverse = adjoint_source, inverse_diagonal
    for sweep in range(SWEEPS):
        if sweep == 1:
            cells, hang, *primal_cells = gather_own(tab, tab_primal)
        else:
            cells, hang = gather_own(tab)
        blocks, image, held = call(
            functools.partial(edge_product, 2 * sweep),
            packed(8) + [cells_shape, hang_shape],
            [room(8)] + edge + [cells_shape, ((6 * EDGE + 16, LANES), f32)] + few(EDGE, LANES),
        )(ghosts, cells, hang, *on_edge, extra, moduli, backward)
        returned = exchange(blocks)
        landings.append(returned)
        partial, *tables = call(
            own_sums,
            [table] * (3 if sweep == 0 else 1),
            [cells_shape, cells_shape, ((6 * OWN, WIDE), f32)] + few(OWN, WIDE),
            specs=[FAST] * 10,
        )(
            image, held, own_row, own_column, master_own_row, master_column, weight, tab, source,
            inverse,
        )
        if tables:
            source, inverse = tables
        blocks, tab = call(
            functools.partial(update, 1 if sweep == 0 else None),
            packed(8) + [table],
            [room(8), few_sums] + few(OWN, WIDE),
        )(returned, list_row, list_column, partial, inverse, extra)
        ghosts = exchange(blocks)
        landings.append(ghosts)
    cells, hang, ku, adjoint = call(
        functools.partial(last_gather, half_rows),
        [cells_shape, hang_shape, cells_shape, (adjoint_start.shape, f32)],
        [own_tall, many_sums] + edge,
    )(
        tab, own_where, lane, master_own, master_lane, weight, *landings[:3], *primal_cells,
        edge_where, master_edge, moduli, forward,
    )
    blocks, term = call(
        fluxes,
        packed(1) + [((1, cell_count), f32)],
        [room(1)]
        + edge
        + [
            ((16, LANES), f32),
            ((16, subface_cell.shape[1]), i32),
            ((1, 64, LANES), f32),
        ],
    )(ghosts, cells, hang, *on_edge, ku, cell_load, subface_cell, subface_face)
    received = exchange(blocks)
    (indicator,) = call(collect, [((1, cell_count), f32)])(
        received, subface_owner, term
    )
    return (adjoint, indicator.reshape(cell_count))


def solution(mesh):
    placed = (
        P(None, "dom"),
        P(None, "dom"),
        P(None, "dom"),
        P(None, "dom"),
        P(None, "dom"),
        P("dom"),
        P(),
        P(None, "dom"),
        P("dom"),
        P(None, "dom"),
        P(None, "dom"),
        P(None, "dom"),
        P(None, "dom"),
        P(None, "dom"),
        P(None, "dom"),
    )
    return jax.shard_map(
        local, mesh=mesh, in_specs=placed, out_specs=(P(None, "dom"), P("dom")), check_vma=False
    )
```

```python
import functools

import jax
import jax.numpy as jnp
from jax import lax
from jax.experimental import pallas as pl
from jax.experimental.pallas import tpu as pltpu
from jax.sharding import PartitionSpec as P

REACH = 4
SWEEPS = 2
LANES = 128
WIDE = 2 * LANES
OWN = 32
EDGE = 16
TALL = 24
NOWHERE = 126

relaxation = 0.7
scale_down = 16.0
pad_code = 16368

f32 = jnp.float32
bf16 = jnp.bfloat16
i32 = jnp.int32


def neighbour_offsets():
    return [step + 1 for step in range(REACH)] + [-(step + 1) for step in range(REACH)]


def exchange(packed):
    return lax.all_to_all(packed, "dom", 0, 0, tiled=True)


def pack(place, sign, rows, pack_ref, out_ref):
    count = out_ref.shape[0]
    pack_ref[...] = jnp.zeros_like(pack_ref)
    for slot, offset in enumerate(neighbour_offsets()):
        target = place + sign * offset
        at = jnp.where((target >= 0) & (target < count), target, count)
        for number, row in enumerate(rows[slot]):
            pack_ref[at, number : number + 1, :] = row
    out_ref[...] = pack_ref[:count]


def send_off(place, sign, rows, pack_ref, out_ref, sems):
    count = out_ref.shape[0]
    copies = []
    for slot, offset in enumerate(neighbour_offsets()):
        for number, row in enumerate(rows[slot]):
            pack_ref[slot, number : number + 1, :] = row
        target = place + sign * offset
        inside = (target >= 0) & (target < count)
        copy = pltpu.make_async_copy(
            pack_ref.at[slot], out_ref.at[jnp.clip(target, 0, count - 1)], sems.at[slot]
        )
        copies.append((inside, copy))
        pl.when(inside)(copy.start)
    for inside, copy in copies:
        pl.when(inside)(copy.wait)


def landed(place, sign, got_ref, number):
    count = got_ref.shape[0]
    rows = []
    for offset in neighbour_offsets():
        source = place - sign * offset
        row = got_ref[jnp.clip(source, 0, count - 1), number : number + 1, :]
        there = jnp.broadcast_to((source >= 0) & (source < count), row.shape)
        rows.append(jnp.where(there, row, 0.0))
    return rows


def landed_wide(place, sign, got_ref, part):
    halves = [
        jnp.concatenate(landed(place, sign, got_ref, 2 * part + half), 0) for half in range(2)
    ]
    return jnp.concatenate(halves, 1)


def match16(row, count):
    width = row.shape[1]
    wide = jnp.broadcast_to(row.astype(f32), (16, width)).astype(bf16)
    numbers = lax.broadcasted_iota(i32, (count, width), 0).astype(f32).astype(bf16)
    return numbers.reshape(count // 16, 16, width) == wide[None]


def one_hot(row, count):
    mask = match16(row, count)
    ones = jnp.ones(mask.shape, bf16)
    return jnp.where(mask, ones, jnp.zeros_like(ones)).reshape(count, row.shape[1])


def spread16(mask, row):
    wide = jnp.broadcast_to(row, (16, row.shape[1])).astype(bf16)[None]
    out = jnp.where(mask, jnp.broadcast_to(wide, mask.shape), jnp.zeros(mask.shape, bf16))
    return out.reshape(mask.shape[0] * 16, row.shape[1])


def pieces(x):
    high = x.astype(bf16)
    return high, (x - high.astype(f32)).astype(bf16)


def gather(jobs, column_ref, high=2 * LANES, stacked=False):
    count, width = column_ref.shape
    tables = jnp.concatenate([job[0] for job in jobs], 0)
    tall = tables.shape[0] // 2
    numbers = lax.broadcasted_iota(i32, (max(job[1] for job in jobs), width), 0)
    step = min(count, 32 if sum(job[1] * job[2] for job in jobs) <= 192 else 16)

    def body(block, carry):
        start = pl.multiple_of(block * step, step)
        for j in range(step):
            hot = one_hot(column_ref[pl.ds(start + j, 1), :], high if stacked else LANES)
            if not stacked:
                hot = jnp.concatenate([hot, hot], 0)
            all_found = jnp.dot(tables, hot, preferred_element_type=f32)
            if stacked:
                all_found = all_found[:tall] + all_found[tall:]
            top = 0
            for _, rows, parts, row_ref, sums_ref in jobs:
                found = all_found[top : top + parts * rows]
                top += parts * rows
                mask = numbers[:rows] == jnp.broadcast_to(
                    row_ref[pl.ds(start + j, 1), :], (rows, width)
                )
                for part in range(parts):
                    kept = jnp.where(mask, found[part * rows : (part + 1) * rows], 0.0)
                    kept = jnp.sum(kept.reshape(rows // 8, 8, width), 0)
                    for half in range(width // LANES):
                        sums_ref[half, pl.ds(part * count * 8 + start * 8 + j * 8, 8), :] = kept[
                            :, half * LANES : (half + 1) * LANES
                        ]
        return carry

    if count == step:
        body(0, 0)
    else:
        lax.fori_loop(0, count // step, body, 0)


def gathered(sums_ref, count, part):
    totals = []
    for half in range(sums_ref.shape[0]):
        rows = [sums_ref[half, pl.ds(part * count * 8 + s, count, stride=8), :] for s in range(8)]
        while len(rows) > 1:
            rows = [a + b for a, b in zip(rows[::2], rows[1::2])]
        totals.append(rows[0])
    return jnp.concatenate(totals, 1)


def halves(x):
    return [x[:, :LANES], x[:, LANES:]]


def rows_and_columns(where, lane):
    return where >> 1, (where & 1) * LANES + lane


def scatter(high_ref, low_ref, rows, row_ref, column_ref, sum_ref, hanging=None):
    count = row_ref.shape[0]
    step = min(count, 32)

    def hanging_tile(number):
        at_row = row_ref[pl.ds(number, 1), :]
        shape = (8, at_row.shape[1])
        numbers = lax.broadcasted_iota(i32, shape, 0)
        tile = jnp.zeros(shape, f32)
        for piece, piece_ref in enumerate((high_ref, low_ref)):
            for part in range(3):
                value = jnp.broadcast_to(piece_ref[pl.ds(part * count + number, 1), :], shape)
                tile = jnp.where(numbers == 3 * piece + part, value, tile)
        tile = jnp.where(jnp.broadcast_to(at_row, shape) == hanging, tile, 0.0)
        return jnp.concatenate([tile, jnp.zeros_like(tile)], 0).astype(bf16)

    def product(start):
        masks = [match16(row_ref[pl.ds(start + j, 1), :], rows) for j in range(8)]
        hot = jnp.concatenate(
            [one_hot(column_ref[pl.ds(start + j, 1), :], sum_ref.shape[1]) for j in range(8)], 1
        )
        stacked = [
            jnp.concatenate(
                [
                    spread16(mask, piece_ref[pl.ds(part * count + start + j, 1), :])
                    for j, mask in enumerate(masks)
                ],
                1,
            )
            for piece_ref in (high_ref, low_ref)
            for part in range(3)
        ]
        if hanging is not None:
            stacked.append(jnp.concatenate([hanging_tile(start + j) for j in range(8)], 1))
        return lax.dot_general(
            jnp.concatenate(stacked, 0), hot, (((1,), (1,)), ((), ())), preferred_element_type=f32
        )

    if count == 8:
        sum_ref[...] = product(0)
        return
    sum_ref[...] = jnp.zeros_like(sum_ref)

    def body(block, carry):
        start = pl.multiple_of(block * step, step)
        total = product(start)
        for first in range(8, step, 8):
            total += product(start + first)
        sum_ref[...] += total
        return carry

    lax.fori_loop(0, count // step, body, 0)


def split32(x):
    high = x.astype(bf16).astype(f32)
    return high, x - high


def add_pieces(sums):
    half = sums.shape[0] // 2
    return sums[:half] + sums[half:]


def scatter_few(values, rows, row_ref, column_ref, scratch):
    high_ref, low_ref, sum_ref = scratch
    for part in range(3):
        high_ref[part * 8 : part * 8 + 8, :], low_ref[part * 8 : part * 8 + 8, :] = split32(
            values[part]
        )
    scatter(high_ref, low_ref, rows, row_ref, column_ref, sum_ref)
    return add_pieces(sum_ref[...])


def few(rows, columns):
    return [((24, WIDE), f32)] * 2 + [((6 * rows, columns), f32)]


def spread_hanging(held, weight, rows, row_ref, column_ref, scratch):
    both = jnp.concatenate([held, held], 1)
    values = [weight * both[part : part + 1] for part in range(3)]
    return scatter_few(values, rows, row_ref, column_ref, scratch)


def sum_masters(sums_ref, first, weight):
    totals = []
    for part in range(first, first + 3):
        left, right = halves(weight * gathered(sums_ref, 8, part))
        totals.append(jnp.sum(left + right, 0, keepdims=True))
    return totals


def product(threefold, cells):
    high, low = pieces(cells)
    return jnp.dot(
        threefold, jnp.concatenate([high, low, high], 0), preferred_element_type=f32
    )


def fill_table(x_ref, out_ref):
    count = x_ref.shape[1] // WIDE
    for part in range(3):
        out_ref[part * OWN + count : (part + 1) * OWN, :] = jnp.zeros((OWN - count, WIDE), f32)
    for row in range(count):
        block = x_ref[:, row * WIDE : (row + 1) * WIDE]
        for part in range(3):
            out_ref[part * OWN + row : part * OWN + row + 1, :] = block[part : part + 1]


def tall_table(tab_refs, half_rows, tall_ref):
    tall = up8(half_rows)
    tall_ref[...] = jnp.zeros_like(tall_ref)
    for number, tab_ref in enumerate(tab_refs):
        for part in range(3):
            for half_row in range(half_rows):
                row, half = part * OWN + half_row // 2, half_row % 2
                at = (3 * number + part) * tall + half_row
                tall_ref[at : at + 1, :] = tab_ref[
                    row : row + 1, half * LANES : (half + 1) * LANES
                ]
    return jnp.concatenate(pieces(tall_ref[...]), 1)


def up8(count):
    return -(-count // 8) * 8


def export_tiles(table, parts, row_ref, column_ref, sums_ref):
    table = jnp.concatenate(pieces(table), 0)
    gather([(table, OWN, parts, row_ref, sums_ref)], column_ref, WIDE, stacked=True)
    return [tile for part in range(parts) for tile in halves(gathered(sums_ref, 8, part))]


def rows_of(tiles):
    return [[tile[slot : slot + 1] for tile in tiles] for slot in range(2 * REACH)]


def add_primal(rows, sign, part, extra_ref):
    slots = 2 * REACH
    for slot in range(slots):
        export = slot if sign > 0 else (slot + REACH) % slots
        for half in range(2):
            rows[slot].append(extra_ref[2 * part + half, export : export + 1, :])


def copy_in(pairs, sems):
    copies = [
        pltpu.make_async_copy(source, target, sems.at[number])
        for number, (source, target) in enumerate(pairs)
    ]
    for copy in copies:
        copy.start()
    for copy in copies:
        copy.wait()


def first_export(
    adjoint_hbm, primal_hbm, list_hbm, modulus_hbm, node_hbm, tab_a, tab_p, row_ref,
    column_ref, extra_ref, modulus_ref, node_ref, out_ref, pack_ref, adjoint_ref, primal_ref, list_ref, sums_ref, sems,
):
    copy_in(
        [
            (adjoint_hbm, adjoint_ref),
            (primal_hbm, primal_ref),
            (list_hbm, list_ref),
            (modulus_hbm, modulus_ref),
            (node_hbm, node_ref),
        ],
        sems,
    )
    owned = adjoint_ref.shape[1]
    fill_table(adjoint_ref, tab_a)
    fill_table(primal_ref, tab_p)
    codes = list_ref[...]
    node = lax.rem(17 * codes + lax.broadcasted_iota(i32, codes.shape, 1), owned)
    row_ref[...] = node >> 8
    column_ref[...] = node & 255
    table = jnp.concatenate([tab_a[...], tab_p[...]], 0)
    tiles = export_tiles(table, 6, row_ref, column_ref, sums_ref)
    for number in range(6):
        extra_ref[number] = tiles[6 + number]
    sent = sems.at[pl.ds(5, 2 * REACH)]
    send_off(lax.axis_index("dom"), 1, rows_of(tiles[:6]), pack_ref, out_ref, sent)


def setup(
    owned, connect_ref, node_ref, master_ref, weight_ref, stiffness_ref,
    own_where, own_row, edge_where, lane_ref, column_ref, master_own, master_own_row,
    master_edge, master_lane, master_column, weight_out, forward_out, adjoint_out,
    map_ref, tall_ref, sums_ref,
):
    extent = owned + 2 * REACH * WIDE
    for out_ref, matrix in (
        (forward_out, stiffness_ref[...]),
        (adjoint_out, jnp.transpose(stiffness_ref[...])),
    ):
        high, low = pieces(matrix)
        out_ref[...] = jnp.concatenate([high, high, low], 1)
    codes = master_ref[...]
    master = lax.rem(17 * codes + 8 * lax.broadcasted_iota(i32, codes.shape, 1), extent)
    count = codes.shape[0] // 2
    master = jnp.concatenate([master[:count], master[count:]], 1)
    weight = weight_ref[...]
    weight_out[...] = jnp.concatenate([weight[:count], weight[count:]], 1)
    last = owned // LANES
    where = master >> 7
    master_own[...] = jnp.where(where < last, where, NOWHERE)
    master_edge[...] = jnp.where(where < last, NOWHERE, where - last)
    master_lane[...] = master & 127
    master_own_row[...] = jnp.where(where < last, master >> 8, NOWHERE)
    master_column[...] = master & 255

    codes = node_ref[...]
    node = jnp.where(codes == pad_code, extent, lax.rem(13 * codes, owned))
    slot = (lax.broadcasted_iota(i32, codes.shape, 1) + 1).astype(f32)
    map_ref[...] = lax.dot_general(
        spread16(match16(node >> 8, OWN), slot),
        one_hot(node & 255, WIDE),
        (((1,), (1,)), ((), ())),
        preferred_element_type=f32,
    )

    codes = connect_ref[...]
    cells = lax.broadcasted_iota(i32, codes.shape, 1)
    slots = lax.rem(27 * cells + 17 * codes, extent)
    own_where[...] = slots >> 7
    lane_ref[...] = slots & 127
    tall_ref[...] = jnp.zeros_like(tall_ref)
    for half_row in range(last):
        row, half = half_row // 2, half_row % 2
        tall_ref[half_row : half_row + 1, :] = map_ref[
            row : row + 1, half * LANES : (half + 1) * LANES
        ]
    table = jnp.concatenate(pieces(tall_ref[...]), 1)
    gather([(table, tall_ref.shape[0], 1, own_where, sums_ref)], lane_ref)
    slot = gathered(sums_ref, codes.shape[0], 0).astype(i32)
    where = slots >> 7
    hanging = slot > 0
    outside = where >= last
    lane = jnp.where(hanging, slot - 1, slots & 127)
    lane_ref[...] = lane
    where_own = jnp.where(hanging | outside, NOWHERE, where)
    own_where[...] = where_own
    own_row[...], column_ref[...] = rows_and_columns(where_own, lane)
    edge_where[...] = jnp.where(hanging, 4 * REACH, jnp.where(outside, where - last, NOWHERE))


def own_gather(
    half_rows, fields, row_ref, lane_ref, master_row, master_lane, weight_ref, *refs
):
    tab_refs, refs = refs[:fields], refs[fields:]
    outs, (tall_ref, sums_ref) = refs[:-2], refs[-2:]
    tall = up8(half_rows)
    table = tall_table(tab_refs, half_rows, tall_ref)
    parts = 3 * fields
    gather([(table, tall, parts, master_row, sums_ref)], master_lane)
    found = sum_masters(sums_ref, 0, weight_ref[...])
    if fields == 2:
        found += sum_masters(sums_ref, 3, weight_ref[...])
    for field in range(fields):
        for part in range(3):
            outs[2 * field + 1][part : part + 1, :] = found[3 * field + part]
    gather([(table, tall, parts, row_ref, sums_ref)], lane_ref)
    count = row_ref.shape[0]
    for field in range(fields):
        cells_ref = outs[2 * field]
        for part in range(3):
            cells_ref[part * count : (part + 1) * count, :] = gathered(
                sums_ref, count, 3 * field + part
            )


def ghost_rows(place, got_refs, first, edge_ref, axis=1):
    edge_ref[...] = jnp.zeros_like(edge_ref)
    for part in range(3):
        for half in range(2):
            lines = landed(place, 1, got_refs[part], first[part] + half)
            for slot in range(2 * REACH):
                at = part * TALL + 2 * slot + half
                edge_ref[at : at + 1, :] = lines[slot]
    return jnp.concatenate(pieces(edge_ref[...]), axis)


def hanging_rows(found, hang_ref, edge_ref, axis=1):
    for part in range(3):
        at = part * TALL + 4 * REACH
        edge_ref[at : at + 1, :] = found[part] + hang_ref[part : part + 1, :]
    return jnp.concatenate(pieces(edge_ref[...]), axis)


def edge_gather(
    place, got_refs, first, cells_ref, hang_ref, row_ref, lane_ref, master_row, master_lane,
    weight_ref, edge_ref, sums_ref, out_ref,
):
    table = ghost_rows(place, got_refs, first, edge_ref, 0)
    gather([(table, TALL, 3, master_row, sums_ref)], master_lane, LANES, stacked=True)
    table = hanging_rows(sum_masters(sums_ref, 0, weight_ref[...]), hang_ref, edge_ref, 0)
    gather([(table, TALL, 3, row_ref, sums_ref)], lane_ref, LANES, stacked=True)
    count = row_ref.shape[0]
    for part in range(3):
        rows = slice(part * count, (part + 1) * count)
        out_ref[rows, :] = cells_ref[rows, :] + gathered(sums_ref, count, part)


def edge_product(
    primal_part, got_ref, cells_ref, hang_ref, row_ref, lane_ref, master_row,
    master_lane, weight_ref, extra_ref, modulus_ref, stiffness_ref, out_ref,
    image_ref, held_ref, pack_ref, edge_ref, sums_ref, full_ref, low_ref, sum_ref, *scratch,
):
    place = lax.axis_index("dom")
    edge_gather(
        place, [got_ref] * 3, (0, 2, 4), cells_ref, hang_ref, row_ref, lane_ref,
        master_row, master_lane, weight_ref, edge_ref, sums_ref, full_ref,
    )
    image = modulus_ref[...] * product(stiffness_ref[...], full_ref[...])
    image_ref[...] = image
    full_ref[...], low_ref[...] = split32(image)
    slots = 2 * REACH
    scatter(full_ref, low_ref, EDGE, row_ref, lane_ref, sum_ref, hanging=2 * slots)
    sums = add_pieces(sum_ref[: 6 * EDGE, :])
    held = sum_ref[6 * EDGE : 6 * EDGE + 3, :] + sum_ref[6 * EDGE + 3 : 6 * EDGE + 6, :]
    held_ref[...] = held
    sums += spread_hanging(held, weight_ref[...], EDGE, master_row, master_lane, scratch[:-1])
    rows = [
        [
            sums[part * EDGE + 2 * slot + half : part * EDGE + 2 * slot + half + 1]
            for part in range(3)
            for half in range(2)
        ]
        for slot in range(slots)
    ]
    add_primal(rows, -1, primal_part, extra_ref)
    send_off(place, -1, rows, pack_ref, out_ref, scratch[-1])


def own_sums(
    image_ref, held_ref, row_ref, column_ref, master_row, master_column, weight_ref,
    tab_ref, source_ref, inverse_ref, out_ref, *rest,
):
    *tables, high_ref, low_ref, sum_ref = rest[:-3]
    if tables:
        tab_source, tab_inverse = tables
        fill_table(source_ref, tab_source)
        fill_table(inverse_ref, tab_inverse)
        source_ref, inverse_ref = tab_source, tab_inverse
    high_ref[...], low_ref[...] = split32(image_ref[...])
    scatter(high_ref, low_ref, OWN, row_ref, column_ref, sum_ref)
    applied = add_pieces(sum_ref[...]) + spread_hanging(
        held_ref[...], weight_ref[...], OWN, master_row, master_column, rest[-3:]
    )
    out_ref[...] = tab_ref[...] + relaxation * inverse_ref[...] * (source_ref[...] - applied)


def update(
    primal_part, got_ref, row_ref, column_ref, partial_ref, inverse_ref, extra_ref,
    out_ref, tab_ref,
    pack_ref, sums_ref, *scratch,
):
    place = lax.axis_index("dom")
    values = [landed_wide(place, -1, got_ref, part) for part in range(3)]
    returned = scatter_few(values, OWN, row_ref, column_ref, scratch[:-1])
    fresh = partial_ref[...] - relaxation * inverse_ref[...] * returned
    tab_ref[...] = fresh
    rows = rows_of(export_tiles(fresh, 3, row_ref, column_ref, sums_ref))
    if primal_part is not None:
        add_primal(rows, 1, primal_part, extra_ref)
    send_off(place, 1, rows, pack_ref, out_ref, scratch[-1])


def last_gather(
    half_rows, tab_ref, own_where, lane_ref, master_own, master_lane, weight_ref,
    got_a, got_b, got_c, primal_cells, primal_hang, edge_where, master_edge, modulus_ref,
    stiffness_ref, cells_ref, hang_ref, ku_ref, final_ref,
    tall_ref, sums_ref, edge_ref, edge_sums, full_ref, whole_ref, sems,
):
    for row in range(whole_ref.shape[1] // WIDE):
        for part in range(3):
            whole_ref[part : part + 1, row * WIDE : (row + 1) * WIDE] = tab_ref[
                part * OWN + row : part * OWN + row + 1, :
            ]
    copy = pltpu.make_async_copy(whole_ref, final_ref, sems.at[0])
    copy.start()
    tall = up8(half_rows)
    own = tall_table([tab_ref], half_rows, tall_ref)
    edge = ghost_rows(lax.axis_index("dom"), (got_a, got_b, got_c), (6, 6, 6), edge_ref)
    gather(
        [(own, tall, 3, master_own, sums_ref), (edge, TALL, 3, master_edge, edge_sums)],
        master_lane,
    )
    weight = weight_ref[...]
    found = sum_masters(sums_ref, 0, weight)
    for part in range(3):
        hang_ref[part : part + 1, :] = found[part]
    edge = hanging_rows(sum_masters(edge_sums, 0, weight), primal_hang, edge_ref)
    gather(
        [(own, tall, 3, own_where, sums_ref), (edge, TALL, 3, edge_where, edge_sums)], lane_ref
    )
    count = lane_ref.shape[0]
    for part in range(3):
        rows = slice(part * count, (part + 1) * count)
        cells_ref[rows, :] = gathered(sums_ref, count, part)
        full_ref[rows, :] = primal_cells[rows, :] + gathered(edge_sums, count, part)
    ku_ref[...] = modulus_ref[...] * product(stiffness_ref[...], full_ref[...])
    copy.wait()


def fluxes(
    got_ref, cells_ref, hang_ref, row_ref, lane_ref, master_row,
    master_lane, weight_ref, ku_ref, load_ref, sub_cell, sub_face, out_ref,
    term_ref, pack_ref, edge_ref, sums_ref, full_ref, tall_ref, code_ref, few_ref,
):
    place = lax.axis_index("dom")
    edge_gather(
        place, [got_ref] * 3, (0, 2, 4), cells_ref, hang_ref, row_ref, lane_ref,
        master_row, master_lane, weight_ref, edge_ref, sums_ref, full_ref,
    )
    cells = full_ref[...]
    ku = ku_ref[...]
    term_ref[...] = jnp.sum(cells * (load_ref[...] - ku), 0, keepdims=True)
    face = lax.broadcasted_iota(i32, (8, ku.shape[0]), 0)
    node = lax.broadcasted_iota(i32, (8, ku.shape[0]), 1) & 63
    index = jnp.where(face < 2, node >> 4, jnp.where(face < 4, (node >> 2) & 3, node & 3))
    member = jnp.where((face < 6) & (index == 3 * (face & 1)), 1.0, 0.0).astype(f32)
    flux = jnp.dot(
        member, ku * cells, precision=lax.Precision.HIGHEST, preferred_element_type=f32
    )
    tall_ref[...] = jnp.zeros_like(tall_ref)
    for number in range(6):
        for half in range(2):
            at = 2 * number + half
            tall_ref[at : at + 1, :] = flux[
                number : number + 1, half * LANES : (half + 1) * LANES
            ]
    cell = sub_cell[...]
    code_ref[:8, :] = 2 * sub_face[...] + (cell >> 7)
    code_ref[8:, :] = cell & 127
    table = jnp.concatenate(pieces(tall_ref[...]), 1)
    gather([(table, 16, 1, code_ref.at[:8, :], few_ref)], code_ref.at[8:, :])
    found = gathered(few_ref, 8, 0)
    rows = [[found[slot : slot + 1]] for slot in range(2 * REACH)]
    pack(place, 1, rows, pack_ref, out_ref)


def collect(got_ref, owner_ref, term_ref, out_ref):
    count = term_ref.shape[1]
    got = jnp.concatenate(landed(lax.axis_index("dom"), 1, got_ref, 0), 1)
    hot = jnp.concatenate(
        [one_hot(owner_ref[slot : slot + 1, :], count) for slot in range(2 * REACH)], 1
    )
    values = jnp.concatenate(
        [jnp.broadcast_to(x, (16, got.shape[1])).astype(bf16) for x in split32(got)], 0
    )
    sums = lax.dot_general(values, hot, (((1,), (1,)), ((), ())), preferred_element_type=f32)
    face_term = sums[0:1] + sums[16:17]
    out_ref[...] = (jnp.abs(term_ref[...]) + jnp.abs(face_term)) / scale_down


FAST = pl.BlockSpec(memory_space=pltpu.VMEM)
FAR = pl.BlockSpec(memory_space=pl.ANY)


def away(*arrays):
    return [pltpu.with_memory_space_constraint(x, pltpu.HBM) for x in arrays]


def call(kernel, outs, scratch=(), specs=None, sems=0):
    scratch = [pltpu.VMEM(shape, kind) for shape, kind in scratch]
    if sems:
        scratch.append(pltpu.SemaphoreType.DMA((sems,)))

    def run(*args):
        return pl.pallas_call(
            kernel,
            out_shape=[jax.ShapeDtypeStruct(*out[:2]) for out in outs],
            out_specs=[out[2] if len(out) > 2 else FAST for out in outs],
            in_specs=specs or [FAST] * len(args),
            scratch_shapes=scratch,
            compiler_params=pltpu.CompilerParams(vmem_limit_bytes=40 * 1024 * 1024),
        )(*args)

    return run


def local(
    adjoint_start,
    adjoint_source,
    inverse_diagonal,
    primal_field,
    cell_load,
    modulus,
    stiffness,
    connectivity,
    hang_node,
    hang_master,
    hang_weight,
    ghost_lists,
    subface_cell,
    subface_face,
    subface_owner,
):
    slots = 2 * REACH
    local_values, cell_count = cell_load.shape
    nodes = connectivity.shape[0]
    half_rows = adjoint_start.shape[1] // LANES
    table = ((3 * OWN, WIDE), f32)
    index = ((nodes, cell_count), i32)
    cells_shape = ((local_values, cell_count), f32)
    hang_shape = ((3, hang_node.shape[0]), f32)
    master_shape = ((8, WIDE), i32)

    count = lax.axis_size("dom")

    def packed(height, *where):
        return [((count, height, LANES), f32, *where)]

    def room(height):
        return ((count + 1, height, LANES), f32)

    tall = up8(half_rows)
    pack_room = ((slots, 8, LANES), f32)
    few_sums = ((2, 3 * 64, LANES), f32)
    many_sums = ((2, local_values * 8, LANES), f32)
    own_tall = ((3 * tall, LANES), f32)
    edge = [((3 * TALL, LANES), f32), many_sums, cells_shape]
    tab, tab_primal, list_row, list_column, extra, moduli, hang_node, blocks = call(
        first_export,
        [table, table]
        + [(ghost_lists.shape, i32)] * 2
        + [((6, slots, LANES), f32), ((1, cell_count), f32), ((1, hang_node.shape[0]), i32)]
        + packed(8, FAR),
        [
            pack_room,
            (adjoint_start.shape, f32),
            (primal_field.shape, f32),
            (ghost_lists.shape, i32),
            ((2, 6 * 64, LANES), f32),
        ],
        [FAR] * 5,
        sems=5 + slots,
    )(
        *away(
            adjoint_start, primal_field, ghost_lists, modulus.reshape(1, -1),
            hang_node.reshape(1, -1),
        )
    )
    ghosts = exchange(blocks)
    (
        own_where, own_row, edge_where, lane, own_column, master_own, master_own_row, master_edge,
        master_lane, master_column, weight, forward, backward,
    ) = call(
        functools.partial(setup, adjoint_start.shape[1]),
        [index] * 5
        + [master_shape] * 5
        + [((8, WIDE), f32)]
        + [((local_values, 3 * local_values), bf16)] * 2,
        [((OWN, WIDE), f32), ((tall, LANES), f32), ((2, nodes * 8, LANES), f32)],
        [FAST] * 5,
    )(connectivity, hang_node, hang_master, hang_weight, stiffness)

    def gather_own(*fields):
        number = len(fields)
        return call(
            functools.partial(own_gather, half_rows, number),
            [cells_shape, hang_shape] * number,
            [
                ((3 * number * tall, LANES), f32),
                ((2, number * local_values * 8, LANES), f32),
            ],
            specs=[FAST] * (5 + number),
        )(own_where, lane, master_own, master_lane, weight, *fields)

    on_edge = (edge_where, lane, master_edge, master_lane, weight)
    landings = []
    source, inverse = adjoint_source, inverse_diagonal
    for sweep in range(SWEEPS):
        if sweep == 1:
            cells, hang, *primal_cells = gather_own(tab, tab_primal)
        else:
            cells, hang = gather_own(tab)
        blocks, image, held = call(
            functools.partial(edge_product, 2 * sweep),
            packed(8, FAR) + [cells_shape, hang_shape],
            [pack_room] + edge + [cells_shape, ((6 * EDGE + 16, LANES), f32)] + few(EDGE, LANES),
            sems=slots,
        )(ghosts, cells, hang, *on_edge, extra, moduli, backward)
        returned = exchange(blocks)
        landings.append(returned)
        partial, *tables = call(
            own_sums,
            [table] * (3 if sweep == 0 else 1),
            [cells_shape, cells_shape, ((6 * OWN, WIDE), f32)] + few(OWN, WIDE),
            specs=[FAST] * 10,
        )(
            image, held, own_row, own_column, master_own_row, master_column, weight, tab, source,
            inverse,
        )
        if tables:
            source, inverse = tables
        blocks, tab = call(
            functools.partial(update, 1 if sweep == 0 else None),
            packed(8, FAR) + [table],
            [pack_room, few_sums] + few(OWN, WIDE),
            sems=slots,
        )(returned, list_row, list_column, partial, inverse, extra)
        ghosts = exchange(blocks)
        landings.append(ghosts)
    cells, hang, ku, adjoint = call(
        functools.partial(last_gather, half_rows),
        [cells_shape, hang_shape, cells_shape, (adjoint_start.shape, f32, FAR)],
        [own_tall, many_sums] + edge + [(adjoint_start.shape, f32)],
        sems=1,
    )(
        tab, own_where, lane, master_own, master_lane, weight, *landings[:3], *primal_cells,
        edge_where, master_edge, moduli, forward,
    )
    blocks, term = call(
        fluxes,
        packed(1) + [((1, cell_count), f32)],
        [room(1)]
        + edge
        + [
            ((16, LANES), f32),
            ((16, subface_cell.shape[1]), i32),
            ((1, 64, LANES), f32),
        ],
    )(ghosts, cells, hang, *on_edge, ku, cell_load, subface_cell, subface_face)
    received = exchange(blocks)
    (indicator,) = call(collect, [((1, cell_count), f32)])(
        received, subface_owner, term
    )
    return (adjoint, indicator.reshape(cell_count))


def solution(mesh):
    placed = (
        P(None, "dom"),
        P(None, "dom"),
        P(None, "dom"),
        P(None, "dom"),
        P(None, "dom"),
        P("dom"),
        P(),
        P(None, "dom"),
        P("dom"),
        P(None, "dom"),
        P(None, "dom"),
        P(None, "dom"),
        P(None, "dom"),
        P(None, "dom"),
        P(None, "dom"),
    )
    return jax.shard_map(
        local, mesh=mesh, in_specs=placed, out_specs=(P(None, "dom"), P("dom")), check_vma=False
    )
```
